32 devices in a mesh: gx: 4 (over z), gy: 8 (over y, x, core).
Axes of the slice: x: 2, y: 2, z: 4, core: 2. Of those that a mesh axis runs over, the one named last changes fastest.
Arguments:
- cotangent: float32 [6, 128, 128, 128], P(None, 'gx', 'gy'), may hold values from -3000 to 3000
- diffusion: float32 [128, 128, 128], P('gx', 'gy'), may hold values from 50 to 2000
- phase: int32 [128, 128, 128], P('gx', 'gy'), may hold values 0 or 1
- courant: float32 [3, 128, 128, 128], P(None, 'gx', 'gy'), may hold values from 0.02 to 0.3
- upwind: int32 [3, 128, 128, 128], P(None, 'gx', 'gy'), may hold values 0 or 1
Outputs:
- grad: float32 [6, 128, 128, 128], P(None, 'gx', 'gy')
The draws below stay inside these ranges and needn't reach their ends.
All inputs are finite; a program needn't handle non-finite values. No bound on the sum of `phase` or of `upwind` on one device may be relied on, other than what follows from the above.
Results may differ from the reference program's by a relative error of at most 0.00019.
Values sent between devices are 32-bit elements; how exact they have to be, the bound alone decides.
No kernel may reach another device: no remote copies, remote signals or barrier semaphores. Data moves between devices by JAX's collectives and lax.ppermute only.
A program may use at most 128 MiB of HBM per device.

```python
import math
import jax
import jax.numpy as jnp
from jax import lax

COMPS = 6
NX = 128
NY = 128
NZ = 128


def draw_cotangent(key, part):
    key = jax.random.fold_in(key, 11)
    shape = (COMPS, NX, NY, NZ)
    return jax.random.truncated_normal(key, -6.0, 6.0, shape, jnp.float32) * 500.0


def place_ends(values, own_key, least, high):
    place = [jax.random.randint(jax.random.fold_in(own_key, axis), (), 0, length) for axis, length in enumerate(values.shape)]
    main_axis = values.shape.index(max(values.shape))
    next_to = place[:main_axis] + [(place[main_axis] + 1) % values.shape[main_axis]] + place[main_axis + 1:]
    return values.at[tuple(place)].set(least).at[tuple(next_to)].set(high)


def levels(key, shape, shards, smallest, largest):
    def one(dim, blocks):
        steps = jax.random.uniform(jax.random.fold_in(jax.random.fold_in(key, 6), dim), (blocks,), jnp.float32, smallest / len(shards), largest / len(shards))
        return jnp.repeat(jnp.exp(steps), shape[dim] // blocks).reshape((-1,) + (1,) * (len(shape) - dim - 1))

    gain = one(*shards[0])
    for cut in shards[1:]:
        gain = gain * one(*cut)
    return gain


def setup_inputs(seed: int = 0) -> dict:
    arg_keys = jax.random.split(jax.random.key(seed), 6)
    cotangent = draw_cotangent(jax.random.fold_in(arg_keys[5], 71), 0)
    diffusion = jnp.clip(jnp.exp(math.log(2000.0) - 3.6888795 * jax.random.uniform(arg_keys[1], (NX, NY, NZ), jnp.float32) ** levels(arg_keys[1], (NX, NY, NZ), ((0, 4), (1, 8)), -0.2, 0.2)), 50.0, 2000.0)
    phase = place_ends((jax.random.randint(arg_keys[2], (NX, NY, NZ), 0, 4) < 1).astype(jnp.int32), jax.random.fold_in(arg_keys[2], 1), 0, 1)
    courant = jnp.clip(jnp.exp(math.log(0.3) - 2.7080503 * jax.random.uniform(arg_keys[3], (3, NX, NY, NZ), jnp.float32) ** levels(arg_keys[3], (3, NX, NY, NZ), ((1, 4), (2, 8)), -0.2, 0.2)), 0.02, 0.3)
    upwind = place_ends((jax.random.randint(arg_keys[4], (3, NX, NY, NZ), 0, 2) < 1).astype(jnp.int32), jax.random.fold_in(arg_keys[4], 1), 0, 1)
    return {"cotangent": cotangent, "diffusion": diffusion, "phase": phase, "courant": courant, "upwind": upwind}


def tridiag_solve(diag, rhs):
    def forward(carry, entry):
        carry_c, carry_d = carry
        diag_row, rhs_row = entry
        denom = diag_row + carry_c
        new_c = -1.0 / denom
        new_d = (rhs_row + carry_d) / denom[None]
        return (new_c, new_d), (new_c, new_d)

    start = (jnp.zeros(diag.shape[1:], diag.dtype), jnp.zeros(rhs.shape[1:], rhs.dtype))
    ending, sweeps = lax.scan(forward, start, (diag, rhs))

    def backward(later, entry):
        sweep_c, sweep_d = entry
        current = sweep_d - sweep_c[None] * later
        return current, current

    ending, solved = lax.scan(backward, jnp.zeros(rhs.shape[1:], rhs.dtype), sweeps, reverse=True)
    return solved


def line_solve(field, coeff, axis):
    moved = jnp.moveaxis(field, axis + 1, 0)
    scales = jnp.moveaxis(coeff, axis, 0)
    solved = tridiag_solve(2.0 + 1.0 / scales, moved)
    return jnp.moveaxis(solved / scales[:, None], 0, axis + 1)


def next_along(array, dim):
    extent = array.shape[dim]
    zero_face = jnp.zeros_like(lax.slice_in_dim(array, 0, 1, axis=dim))
    return jnp.concatenate([lax.slice_in_dim(array, 1, extent, axis=dim), zero_face], axis=dim)


def prev_along(array, dim):
    extent = array.shape[dim]
    zero_face = jnp.zeros_like(lax.slice_in_dim(array, 0, 1, axis=dim))
    return jnp.concatenate([zero_face, lax.slice_in_dim(array, 0, extent - 1, axis=dim)], axis=dim)


def adjoint_advect(field, courant, upwind):
    result = field
    for direction in range(3):
        flux = courant[direction][None] * field
        ahead = upwind[direction].astype(field.dtype)[None] * flux
        behind = flux - ahead
        result = result - ahead + behind + next_along(ahead, direction + 1) - prev_along(behind, direction + 1)
    return result


def reference(cotangent, diffusion, phase, courant, upwind):
    coeff = diffusion * (1.0 + 3.0 * phase.astype(diffusion.dtype))
    along_z = line_solve(cotangent, coeff, 2)
    along_y = line_solve(along_z, coeff, 1)
    along_x = line_solve(along_y, coeff, 0)
    return adjoint_advect(along_x, courant, upwind)
```

```python
import functools

import jax
import jax.numpy as jnp
from jax import lax
from jax.experimental import pallas as pl
from jax.experimental.pallas import tpu as pltpu
from jax.sharding import PartitionSpec as P

COMPS = 6
LANES = 128
TILE = 8
VMEM_BYTES = 24 * 1024 * 1024


def round_up(count, step):
    return (count + step - 1) // step * step


def weight_of(diffusion, phase):
    return 1.0 / (diffusion * (1.0 + 3.0 * phase.astype(jnp.float32)))


def growing_step(value, slope, weight):
    slope = slope + weight * value
    return value + slope, slope


def split3(cells):
    high = cells.astype(jnp.bfloat16)
    rest = cells - high.astype(jnp.float32)
    middle = rest.astype(jnp.bfloat16)
    low = (rest - middle.astype(jnp.float32)).astype(jnp.bfloat16)
    return high, middle, low


def sum_matrix():
    row = lax.broadcasted_iota(jnp.int32, (2 * LANES, 2 * LANES), 0)
    col = lax.broadcasted_iota(jnp.int32, (2 * LANES, 2 * LANES), 1)
    before = (row < LANES) & (col < LANES) & (row <= col)
    after = (row >= LANES) & (col >= LANES) & (row > col)
    return jnp.where(before | after, 1.0, 0.0).astype(jnp.bfloat16)


def z_kernel(
    dims, cot_any, diffusion, phase, az_any, send, w_out, inv_out,
    cot, az, wt, pht, pst, phi, psi, left, right, in_sems, out_sems,
):
    nx, ny, py, width = dims
    rows = nx * ny
    tiles = rows // LANES
    owned = nx // py
    for c in range(COMPS):
        pltpu.make_async_copy(cot_any.at[c], cot.at[c], in_sems.at[c]).start()

    w_out[...] = weight_of(diffusion[...], phase[...])
    for t in range(tiles):
        span = pl.ds(t * LANES, LANES)
        wt[span, :] = w_out[span, :].T
    ones = jnp.ones((tiles, LANES), jnp.float32)
    value, slope = ones, ones
    back, fall = ones, ones
    for k in range(LANES):
        here = pl.ds(k, tiles, stride=LANES)
        pht[here, :] = value
        value, slope = growing_step(value, slope, wt[here, :])
        there = pl.ds(LANES - 1 - k, tiles, stride=LANES)
        pst[there, :] = back
        back, fall = growing_step(back, fall, wt[there, :])
    scale = 1.0 / value
    for t in range(tiles):
        span = pl.ds(t * LANES, LANES)
        phi[span, :] = pht[span, :].T
        psi[span, :] = (pst[span, :] * scale[t : t + 1]).T

    one = jnp.ones((nx, LANES), jnp.float32)
    value, slope, chain = one, one, []
    weights = [w_out[pl.ds(y, nx, stride=ny), :] for y in range(ny)]
    for y in range(ny):
        chain.append(value)
        value, slope = growing_step(value, slope, weights[y])
    total = 1.0 / value
    chain.append(value)
    back, fall = one, one
    for y in reversed(range(ny)):
        span = pl.ds(y * nx, nx)
        left[span, :] = back * total
        right[span, :] = chain[y] * total
        inv_out[span, :] = chain[y] / chain[y + 1]
        back, fall = growing_step(back, fall, weights[y])

    def post(index, cells):
        for r in range(owned):
            send[pl.ds(index * owned + r, py, stride=width), :] = cells[r * py : (r + 1) * py]

    post(2 * COMPS, left[pl.ds(0, nx), :])
    post(2 * COMPS + 1, right[pl.ds(0, nx), :])
    post(2 * COMPS + 2, right[pl.ds((ny - 1) * nx, nx), :])

    sums = sum_matrix()
    for c in range(COMPS):
        pltpu.make_async_copy(cot_any.at[c], cot.at[c], in_sems.at[c]).wait()
        for t in range(tiles):
            span = pl.ds(t * LANES, LANES)
            cells, up, down = cot[c, span, :], phi[span, :], psi[span, :]
            wide = jnp.concatenate([up * cells, down * cells], axis=1)
            found = sum(
                jnp.dot(part, sums, preferred_element_type=jnp.float32) for part in split3(wide)
            )
            az[c, span, :] = w_out[span, :] * (down * found[:, :LANES] + up * found[:, LANES:])
        pltpu.make_async_copy(az.at[c], az_any.at[c], out_sems.at[c]).start()
        first = jnp.zeros((nx, LANES), jnp.float32)
        last = jnp.zeros((nx, LANES), jnp.float32)
        for y in range(ny):
            cells = az[c, pl.ds(y, nx, stride=ny), :]
            span = pl.ds(y * nx, nx)
            first = first + left[span, :] * cells
            last = last + right[span, :] * cells
        post(c, first)
        post(COMPS + c, last)
    for c in range(COMPS):
        pltpu.make_async_copy(az.at[c], az_any.at[c], out_sems.at[c]).wait()


def owner_kernel(dims, got, send):
    owned, py, width, out_width = dims
    group = COMPS * owned

    def spread(row, p):
        piece = got[pl.ds(p * width + row, owned), :]
        return jnp.concatenate([piece] * COMPS, axis=0)

    zero = jnp.zeros((group, LANES), jnp.float32)
    tail, tail_edge = zero, zero
    chains = []
    for p in range(py):
        yfirst = got[pl.ds(p * width, group), :]
        ylast = got[pl.ds(p * width + group, group), :]
        corner = spread(2 * group, p)
        cross = spread(2 * group + owned, p)
        far = spread(2 * group + 2 * owned, p)
        pivot = 1.0 / (1.0 - corner * tail_edge)
        lead = (yfirst + corner * tail) * pivot
        lead_edge = cross * pivot
        linked = cross * tail_edge
        tail, tail_edge = ylast + cross * tail + linked * lead, far + linked * lead_edge
        chains.append((lead, lead_edge, tail, tail_edge))
    later = zero
    for p in reversed(range(py)):
        lead, lead_edge, tail, tail_edge = chains[p]
        send[pl.ds(p * out_width + group, group), :] = later
        if p + 1 < py:
            send[pl.ds((p + 1) * out_width, group), :] = tail + tail_edge * later
        later = lead + lead_edge * later
    send[pl.ds(0, group), :] = zero


def sides(before, after, x):
    return jnp.concatenate(
        [
            jnp.broadcast_to(before[pl.ds(x, 1), :], (TILE, LANES)),
            jnp.broadcast_to(after[pl.ds(x, 1), :], (TILE, LANES)),
        ],
        axis=0,
    )


def state_kernel(dims, me_ref, w, before, after, xend, send):
    nx, ny, px, width = dims
    me = me_ref[0]
    rows = ny + 2 * TILE
    one = jnp.ones((rows, LANES), jnp.float32)
    zero = jnp.zeros((rows, LANES), jnp.float32)
    states = [(one, zero), (zero, one)]
    for x in range(nx):
        weight = jnp.concatenate([w[pl.ds(x * ny, ny), :], sides(before, after, x)], axis=0)
        states = [growing_step(value, slope, weight) for value, slope in states]
    entries = [states[0][0], states[1][0], states[0][1], states[1][1]]
    for p in range(px):
        base = p * width
        for e, entry in enumerate(entries):
            send[pl.ds(base + e * ny, ny), :] = entry[:ny]
            send[pl.ds(base + 4 * ny + 2 * e, 1), :] = entry[ny : ny + 1]
            send[pl.ds(base + 4 * ny + 2 * e + 1, 1), :] = entry[ny + TILE : ny + TILE + 1]
        send[pl.ds(base + 4 * ny + TILE, ny), :] = jnp.where(
            jnp.full((ny, LANES), p, jnp.int32) < me, xend[pl.ds(0, ny), :], xend[pl.ds(ny, ny), :]
        )


def y_kernel(
    dims, me_ref, az, got, w, inv, before, after, states,
    ay, ghost, send, total_out, xinv, misc, back_all,
):
    nx, ny, py, px, out_width, state_width, x_width = dims
    me = me_ref[0]
    owned = nx // py
    rows = ny + 2 * TILE
    gbase = COMPS * ny

    ghost[...] = jnp.zeros(ghost.shape, jnp.float32)
    for c in range(COMPS):
        for r in range(owned):
            part = pl.ds(r * py, py)
            fb = got[pl.ds(c * owned + r, py, stride=out_width), :]
            fa = got[pl.ds((COMPS + c) * owned + r, py, stride=out_width), :]
            ghost[pl.ds(r * py * 2 * TILE + c, py, stride=2 * TILE), :] = before[part, :] * fb
            ghost[pl.ds(r * py * 2 * TILE + TILE + c, py, stride=2 * TILE), :] = after[part, :] * fa
            swept = fb
            chain = []
            for y in range(ny):
                cells = az[c, pl.ds(r * py * ny + y, py, stride=ny), :]
                swept = (cells + swept) * inv[pl.ds(y * nx + r * py, py), :]
                chain.append(swept)
            later = fa
            for y in reversed(range(ny)):
                where = pl.ds(r * py * ny + y, py, stride=ny)
                later = chain[y] + inv[pl.ds(y * nx + r * py, py), :] * later
                ay[c, where, :] = later * w[where, :]

    def entry(p, e):
        base = p * state_width
        row = base + 4 * ny + 2 * e
        return jnp.concatenate(
            [
                states[pl.ds(base + e * ny, ny), :],
                jnp.broadcast_to(states[pl.ds(row, 1), :], (TILE, LANES)),
                jnp.broadcast_to(states[pl.ds(row + 1, 1), :], (TILE, LANES)),
            ],
            axis=0,
        )

    maps = [[entry(p, e) for e in range(4)] for p in range(px)]
    one = jnp.ones((rows, LANES), jnp.float32)
    value, slope = one, one
    start_value, start_slope = one, one
    for p in range(px):
        a, b, c, d = maps[p]
        keep = jnp.full((rows, LANES), p, jnp.int32) == me
        start_value = jnp.where(keep, value, start_value)
        start_slope = jnp.where(keep, slope, start_slope)
        value, slope = a * value + b * slope, c * value + d * slope
    scale = 1.0 / value
    back, fall = scale, scale
    for p in reversed(range(px)):
        a, b, c, d = maps[p]
        past = jnp.full((rows, LANES), p, jnp.int32) > me
        new_back = (c + d) * back + (a + b - c - d) * fall
        new_fall = c * back + (a - c) * fall
        back = jnp.where(past, new_back, back)
        fall = jnp.where(past, new_fall, fall)

    inverse = 1.0 / start_value
    misc[pl.ds(0, rows), :] = inverse
    misc[pl.ds(rows, rows), :] = (start_value - start_slope) * inverse
    misc[pl.ds(2 * rows, rows), :] = back - fall

    def weight_at(x):
        return jnp.concatenate([w[pl.ds(x * ny, ny), :], sides(before, after, x)], axis=0)

    for x in reversed(range(nx)):
        back_all[pl.ds(x * rows, rows), :] = back
        back, fall = growing_step(back, fall, weight_at(x))
    value, slope = start_value, start_slope
    zero = jnp.zeros((ny, LANES), jnp.float32)
    ups = [zero] * COMPS
    downs = [zero] * COMPS
    gup = jnp.zeros((2 * TILE, LANES), jnp.float32)
    gdown = gup
    for x in range(nx):
        down = back_all[pl.ds(x * rows, rows), :]
        for c in range(COMPS):
            cells = ay[c, pl.ds(x * ny, ny), :]
            ups[c] = ups[c] + value[:ny] * cells
            downs[c] = downs[c] + down[:ny] * cells
        cells = ghost[pl.ds(x * 2 * TILE, 2 * TILE), :]
        gup = gup + value[ny:] * cells
        gdown = gdown + down[ny:] * cells
        new_value, slope = growing_step(value, slope, weight_at(x))
        xinv[pl.ds(x * rows, rows), :] = value / new_value
        value = new_value
    misc[pl.ds(3 * rows, rows), :] = value
    for c in range(COMPS):
        total_out[pl.ds(c * ny, ny), :] = ups[c]
    total_out[pl.ds(gbase, 2 * TILE), :] = gup
    for p in range(px):
        base = p * x_width
        later = jnp.full((ny, LANES), p, jnp.int32) > me
        for c in range(COMPS):
            send[pl.ds(base + c * ny, ny), :] = jnp.where(later, ups[c], downs[c])
        later = jnp.full((2 * TILE, LANES), p, jnp.int32) > me
        send[pl.ds(base + gbase, 2 * TILE), :] = jnp.where(later, gup, gdown)


def x_kernel(
    dims, me_ref, got, total, misc, xinv, ay, ghost, w, before, after, states, courant, upwind,
    out, swept_all, gswept, sums,
):
    nx, ny, px, state_width, x_width = dims
    me = me_ref[0]
    rows = ny + 2 * TILE
    gbase = COMPS * ny

    pre = jnp.zeros((x_width, LANES), jnp.float32)
    suf = pre
    for p in range(px):
        chunk = got[pl.ds(p * x_width, x_width), :]
        index = jnp.full((x_width, LANES), p, jnp.int32)
        pre = pre + jnp.where(index < me, chunk, 0.0)
        suf = suf + jnp.where(index > me, chunk, 0.0)
    sums[pl.ds(0, x_width), :] = pre
    sums[pl.ds(x_width, x_width), :] = suf

    inverse = misc[pl.ds(0, ny), :]
    reach = misc[pl.ds(rows, ny), :]
    psi_next = misc[pl.ds(2 * rows, ny), :]
    phi_next = misc[pl.ds(3 * rows, ny), :]
    g_inverse = misc[pl.ds(ny, 2 * TILE), :]
    g_psi_next = misc[pl.ds(2 * rows + ny, 2 * TILE), :]
    g_phi_next = misc[pl.ds(3 * rows + ny, 2 * TILE), :]

    starts = [sums[pl.ds(c * ny, ny), :] * inverse for c in range(COMPS)]
    gstart = sums[pl.ds(gbase, 2 * TILE), :] * g_inverse
    nexts = [
        psi_next * (sums[pl.ds(c * ny, ny), :] + total[pl.ds(c * ny, ny), :])
        + phi_next * sums[pl.ds(x_width + c * ny, ny), :]
        for c in range(COMPS)
    ]
    gnext = g_psi_next * (
        sums[pl.ds(gbase, 2 * TILE), :] + total[pl.ds(gbase, 2 * TILE), :]
    ) + g_phi_next * sums[pl.ds(x_width + gbase, 2 * TILE), :]

    def sweep(x, carry):
        cells, gcells = carry
        factor = xinv[pl.ds(x * rows, rows), :]
        span = pl.ds(x * ny, ny)
        new = []
        for c in range(COMPS):
            value = (ay[c, span, :] + cells[c]) * factor[:ny]
            swept_all[c, span, :] = value
            new.append(value)
        gspan = pl.ds(x * 2 * TILE, 2 * TILE)
        gvalue = (ghost[gspan, :] + gcells) * factor[ny:]
        gswept[gspan, :] = gvalue
        return tuple(new), gvalue

    lax.fori_loop(0, nx, sweep, (tuple(starts), gstart), unroll=4)

    lane = lax.broadcasted_iota(jnp.int32, (ny, LANES), 1)
    line = lax.broadcasted_iota(jnp.int32, (ny, LANES), 0)
    has_left = jnp.where(me > 0, 1.0, 0.0)
    has_right = jnp.where(me < px - 1, 1.0, 0.0)
    left_row = jnp.maximum(me - 1, 0) * state_width + 4 * ny + TILE
    right_row = jnp.minimum(me + 1, px - 1) * state_width + 4 * ny + TILE
    near = states[pl.ds(pl.multiple_of(left_row, TILE), ny), :] * has_left
    far = states[pl.ds(pl.multiple_of(right_row, TILE), ny), :] * has_right

    def finish(step, carry):
        cells, fluxes, gcells = carry
        x = nx - 1 - step
        span = pl.ds(x * ny, ny)
        factor = xinv[pl.ds(x * rows, rows), :]
        weight = w[span, :]
        ahead, behind = [], []
        own = jnp.ones((ny, LANES), jnp.float32)
        for d in range(3):
            flow = courant[d, span, :]
            up = flow * upwind[d, span, :].astype(jnp.float32)
            down = flow - up
            own = own + (down - up)
            ahead.append(up)
            behind.append(down)
        ahead_y = jnp.where(line == 0, 0.0, ahead[1])
        behind_y = jnp.where(line == ny - 1, 0.0, behind[1])
        ahead_z = jnp.where(lane == 0, 0.0, ahead[2])
        behind_z = jnp.where(lane == LANES - 1, 0.0, behind[2])
        gspan = pl.ds(x * 2 * TILE, 2 * TILE)
        gvalue = gswept[gspan, :] + factor[ny:] * gcells
        gflux = gvalue * sides_of(before, after, x)
        new_cells, new_fluxes = [], []
        for c in range(COMPS):
            solved = swept_all[c, span, :] + factor[:ny] * cells[c]
            grad = weight * solved
            part = own * grad + fluxes[c]
            part = part + pltpu.roll(ahead_y * grad, ny - 1, 0) - pltpu.roll(behind_y * grad, 1, 0)
            part = part + pltpu.roll(ahead_z * grad, LANES - 1, 1) - pltpu.roll(behind_z * grad, 1, 1)
            part = part - jnp.where(line == 0, gflux[c : c + 1], 0.0)
            part = part + jnp.where(line == ny - 1, gflux[TILE + c : TILE + c + 1], 0.0)
            out[c, span, :] = part
            upper = pl.ds((x + 1) * ny, ny)
            out[c, upper, :] = out[c, upper, :] - behind[0] * grad
            new_cells.append(solved)
            new_fluxes.append(ahead[0] * grad)
        return tuple(new_cells), tuple(new_fluxes), gvalue

    def sides_of(lower, upper, x):
        return jnp.concatenate(
            [
                jnp.broadcast_to(lower[pl.ds(nx + x, 1), :], (TILE, LANES)),
                jnp.broadcast_to(upper[pl.ds(nx + x, 1), :], (TILE, LANES)),
            ],
            axis=0,
        )

    fluxes = tuple(far * nexts[c] for c in range(COMPS))
    solved, _, _ = lax.fori_loop(0, nx, finish, (tuple(nexts), fluxes, gnext))
    top = pl.ds(0, ny)
    for c in range(COMPS):
        entering = starts[c] + reach * solved[c]
        out[c, top, :] = out[c, top, :] - near * entering


def call(kernel, name, operands, outs, scratch=(), spaces=None, out_spaces=None, ops=0):
    params = pltpu.CompilerParams(vmem_limit_bytes=VMEM_BYTES)
    vmem = pl.BlockSpec(memory_space=pltpu.VMEM)
    anywhere = pl.BlockSpec(memory_space=pl.ANY)
    smem = pl.BlockSpec(memory_space=pltpu.SMEM)
    pick = {"v": vmem, "a": anywhere, "s": smem}
    spaces = spaces or "v" * len(operands)
    out_spaces = out_spaces or "v" * len(outs)
    moved = sum(4 * math_prod(shape) for shape in outs) + sum(4 * o.size for o in operands)
    return pl.pallas_call(
        kernel,
        name=name,
        out_shape=[jax.ShapeDtypeStruct(shape, jnp.float32) for shape in outs],
        in_specs=[pick[s] for s in spaces],
        out_specs=[pick[s] for s in out_spaces],
        scratch_shapes=list(scratch),
        compiler_params=params,
        cost_estimate=pl.CostEstimate(flops=ops, bytes_accessed=moved, transcendentals=0),
    )(*operands)


def math_prod(shape):
    size = 1
    for extent in shape:
        size *= extent
    return size


def on_device(cotangent, diffusion, phase, courant, upwind):
    comps, nx, ny, nz = cotangent.shape
    px, py = lax.axis_size("gx"), lax.axis_size("gy")
    rows = nx * ny
    owned = nx // py
    group = comps * owned
    width = round_up(2 * group + 3 * owned, TILE)
    out_width = round_up(2 * group, TILE)
    state_width = 5 * ny + TILE
    x_width = comps * ny + 2 * TILE
    wide = ny + 2 * TILE
    me = lax.axis_index("gx").astype(jnp.int32).reshape(1)
    f32 = jnp.float32
    vmem = lambda *shape: pltpu.VMEM(shape, f32)

    flat_w = (diffusion.reshape(rows, nz), phase.reshape(rows, nz))
    cot = cotangent.reshape(comps, rows, nz)
    cour = courant.reshape(3, rows, nz)
    upw = upwind.reshape(3, rows, nz)

    def y_edge(y, toward):
        weight = weight_of(diffusion[:, y], phase[:, y])
        up = courant[1, :, y] * upwind[1, :, y].astype(f32)
        flow = up if toward else courant[1, :, y] - up
        return jnp.concatenate([weight, weight * flow], axis=0)

    after = lax.ppermute(y_edge(0, True), "gy", [(i + 1, i) for i in range(py - 1)])
    before = lax.ppermute(y_edge(ny - 1, False), "gy", [(i, i + 1) for i in range(py - 1)])

    def x_edge(x, toward):
        weight = weight_of(diffusion[x], phase[x])
        up = courant[0, x] * upwind[0, x].astype(f32)
        return weight * (up if toward else courant[0, x] - up)

    xend = jnp.concatenate([x_edge(0, True), x_edge(nx - 1, False)], axis=0)

    az, posted, w, inv = call(
        functools.partial(z_kernel, (nx, ny, py, width)),
        "z_solve",
        (cot,) + flat_w,
        [(comps, rows, nz), (py * width, nz), (rows, nz), (rows, nz)],
        [
            vmem(comps, rows, nz), vmem(comps, rows, nz), vmem(rows, nz), vmem(rows, nz),
            vmem(rows, nz), vmem(rows, nz), vmem(rows, nz), vmem(rows, nz), vmem(rows, nz),
            pltpu.SemaphoreType.DMA((comps,)), pltpu.SemaphoreType.DMA((comps,)),
        ],
        spaces="avv",
        out_spaces="avvv",
    )
    got = lax.all_to_all(posted, "gy", 0, 0, tiled=True)
    (states_send,) = call(
        functools.partial(state_kernel, (nx, ny, px, state_width)),
        "x_states",
        (me, w, before, after, xend),
        [(px * state_width, nz)],
        spaces="svvvv",
    )
    states = lax.all_to_all(states_send, "gx", 0, 0, tiled=True)
    (answers,) = call(
        functools.partial(owner_kernel, (owned, py, width, out_width)),
        "y_reduced",
        (got,),
        [(py * out_width, nz)],
    )
    edges = lax.all_to_all(answers, "gy", 0, 0, tiled=True)
    ay, ghost, x_send, total, xinv, misc = call(
        functools.partial(y_kernel, (nx, ny, py, px, out_width, state_width, x_width)),
        "y_solve",
        (me, az, edges, w, inv, before, after, states),
        [
            (comps, rows, nz), (nx * 2 * TILE, nz), (px * x_width, nz), (x_width, nz),
            (nx * wide, nz), (4 * wide, nz),
        ],
        [vmem(nx * wide, nz)],
        spaces="svvvvvvv",
    )
    x_got = lax.all_to_all(x_send, "gx", 0, 0, tiled=True)
    (grad,) = call(
        functools.partial(x_kernel, (nx, ny, px, state_width, x_width)),
        "x_solve",
        (me, x_got, total, misc, xinv, ay, ghost, w, before, after, states, cour, upw),
        [(comps, rows + ny, nz)],
        [vmem(comps, rows, nz), vmem(nx * 2 * TILE, nz), vmem(2 * x_width, nz)],
        spaces="s" + "v" * 12,
    )
    return grad[:, :rows].reshape(comps, nx, ny, nz)


def solution(mesh):
    placed = (
        P(None, "gx", "gy", None),
        P("gx", "gy", None),
        P("gx", "gy", None),
        P(None, "gx", "gy", None),
        P(None, "gx", "gy", None),
    )
    return jax.shard_map(
        on_device, mesh=mesh, in_specs=placed, out_specs=P(None, "gx", "gy", None), check_vma=False
    )
```

```python
import functools

import jax
import jax.numpy as jnp
from jax import lax
from jax.experimental import pallas as pl
from jax.experimental.pallas import tpu as pltpu
from jax.sharding import PartitionSpec as P

COMPS = 6
LANES = 128
TILE = 8
VMEM_BYTES = 24 * 1024 * 1024


def weight_of(diffusion, phase):
    return 1.0 / (diffusion * (1.0 + 3.0 * phase.astype(jnp.float32)))


def growing_step(value, slope, weight):
    slope = slope + weight * value
    return value + slope, slope


def split3(cells):
    high = cells.astype(jnp.bfloat16)
    rest = cells - high.astype(jnp.float32)
    middle = rest.astype(jnp.bfloat16)
    low = (rest - middle.astype(jnp.float32)).astype(jnp.bfloat16)
    return high, middle, low


def sum_matrix():
    row = lax.broadcasted_iota(jnp.int32, (2 * LANES, 2 * LANES), 0)
    col = lax.broadcasted_iota(jnp.int32, (2 * LANES, 2 * LANES), 1)
    before = (row < LANES) & (col < LANES) & (row <= col)
    after = (row >= LANES) & (col >= LANES) & (row > col)
    return jnp.where(before | after, 1.0, 0.0).astype(jnp.bfloat16)


class Layout:
    def __init__(self, pieces, groups, edges, lines):
        self.pieces, self.groups, self.edges, self.lines = pieces, groups, edges, lines
        self.couple = pieces * lines * 2
        self.packed = self.couple + 3 * lines
        self.edge = self.packed + (TILE if groups > 1 else 0)
        self.rows = self.edge + 2 * edges * lines
        self.side_couple = pieces * lines
        self.side_packed = self.side_couple + lines
        self.side_edge = self.side_packed + (TILE if groups > 1 else 0)
        self.side_rows = self.side_edge + edges * lines
        self.answer_rows = 2 * (pieces + edges) * lines

    def group(self, piece):
        return 0 if piece < COMPS else 1


def read_rows(ref, base, count, lines):
    return [ref[pl.ds(base + i * lines, lines), :] for i in range(count)]


def write_rows(ref, base, values, lines):
    for i, value in enumerate(values):
        ref[pl.ds(base + i * lines, lines), :] = value


def read_pair(ref, row):
    return jnp.concatenate(
        [jnp.broadcast_to(ref[pl.ds(row + i, 1), :], (TILE, LANES)) for i in range(2)], axis=0
    )


def write_pair(ref, row, value):
    ref[pl.ds(row, 1), :] = value[:1]
    ref[pl.ds(row + 1, 1), :] = value[TILE : TILE + 1]


def read_block(lay, ref, base=0):
    n, m = lay.lines, lay.pieces
    couple = []
    for e in range(3):
        entry = [ref[pl.ds(base + lay.couple + e * n, n), :]]
        if lay.groups > 1:
            entry.append(read_pair(ref, base + lay.packed + 2 * e))
        couple.append(entry)
    return {
        "first": read_rows(ref, base, m, n),
        "last": read_rows(ref, base + m * n, m, n),
        "near": couple[0],
        "cross": couple[1],
        "far": couple[2],
        "head": read_rows(ref, base + lay.edge, lay.edges, n),
        "tail": read_rows(ref, base + lay.edge + lay.edges * n, lay.edges, n),
    }


def write_block(lay, ref, block, base=0):
    n, m = lay.lines, lay.pieces
    write_rows(ref, base, block["first"], n)
    write_rows(ref, base + m * n, block["last"], n)
    for e, name in enumerate(("near", "cross", "far")):
        ref[pl.ds(base + lay.couple + e * n, n), :] = block[name][0]
        if lay.groups > 1:
            write_pair(ref, base + lay.packed + 2 * e, block[name][1])
    write_rows(ref, base + lay.edge, block["head"], n)
    write_rows(ref, base + lay.edge + lay.edges * n, block["tail"], n)


def write_side(lay, ref, block, upper):
    n = lay.lines

    def facing(low, high):
        return jnp.where(jnp.full(low.shape, upper, jnp.int32) == 1, high, low)

    write_rows(ref, 0, [facing(a, b) for a, b in zip(block["last"], block["first"])], n)
    pair = [facing(a, b) for a, b in zip(block["far"], block["near"])]
    ref[pl.ds(lay.side_couple, n), :] = pair[0]
    if lay.groups > 1:
        write_pair(ref, lay.side_packed, pair[1])
    write_rows(ref, lay.side_edge, [facing(a, b) for a, b in zip(block["tail"], block["head"])], n)


def read_side(lay, ref):
    n = lay.lines
    couple = [ref[pl.ds(lay.side_couple, n), :]]
    if lay.groups > 1:
        couple.append(read_pair(ref, lay.side_packed))
    return (
        read_rows(ref, 0, lay.pieces, n),
        couple,
        read_rows(ref, lay.side_edge, lay.edges, n),
    )


def pick(upper, low, high):
    if isinstance(low, list):
        return [pick(upper, a, b) for a, b in zip(low, high)]
    return jnp.where(jnp.full(low.shape, upper, jnp.int32) == 1, high, low)


def ordered(upper, own, other):
    low = {name: pick(upper, own[name], other[name]) for name in own}
    high = {name: pick(upper, other[name], own[name]) for name in own}
    return low, high


def joint(lay, low, high):
    return [
        1.0 / (1.0 - low["far"][g] * high["near"][g]) for g in range(lay.groups)
    ]


def merge(lay, low, high):
    shrink = joint(lay, low, high)
    to_low = [low["cross"][g] * shrink[g] for g in range(lay.groups)]
    to_high = [high["cross"][g] * shrink[g] for g in range(lay.groups)]
    span = range(lay.pieces)
    of = lay.group
    return {
        "first": [
            low["first"][i]
            + to_low[of(i)] * (high["first"][i] + high["near"][of(i)] * low["last"][i])
            for i in span
        ],
        "last": [
            high["last"][i]
            + to_high[of(i)] * (low["last"][i] + low["far"][of(i)] * high["first"][i])
            for i in span
        ],
        "near": [
            low["near"][g] + to_low[g] * low["cross"][g] * high["near"][g]
            for g in range(lay.groups)
        ],
        "cross": [to_low[g] * high["cross"][g] for g in range(lay.groups)],
        "far": [
            high["far"][g] + to_high[g] * high["cross"][g] * low["far"][g]
            for g in range(lay.groups)
        ],
        "head": low["head"],
        "tail": high["tail"],
    }


def inner(lay, low, high, before, after):
    shrink = joint(lay, low, high)
    low_last, high_first = [], []
    for i in range(lay.pieces):
        g = lay.group(i)
        left = low["last"][i] + low["cross"][g] * before[i]
        right = high["first"][i] + high["cross"][g] * after[i]
        low_last.append((left + low["far"][g] * right) * shrink[g])
        high_first.append((right + high["near"][g] * left) * shrink[g])
    return low_last, high_first


def merge_kernel(lay, bit, top, me_ref, own, other, out, *side):
    upper = (me_ref[0] >> bit) & 1
    low, high = ordered(upper, read_block(lay, own), read_block(lay, other))
    block = merge(lay, low, high)
    write_block(lay, out, block)
    if top:
        write_side(lay, side[0], block, (me_ref[0] >> (bit + 1)) & 1)


def descend(lay, me, levels, own_refs, got_refs):
    top = levels - 1
    upper = (me >> top) & 1
    own = read_block(lay, own_refs[top])
    met, met_couple, met_edge = read_side(lay, got_refs[top])
    facing = pick(upper, own["last"], own["first"])
    couple = pick(upper, own["far"], own["near"])
    found = []
    for i in range(lay.pieces):
        g = lay.group(i)
        found.append((met[i] + met_couple[g] * facing[i]) / (1.0 - met_couple[g] * couple[g]))
    zeros = [jnp.zeros_like(v) for v in found]
    edge_zeros = [jnp.zeros_like(v) for v in met_edge]
    before, after = pick(upper, zeros, found), pick(upper, found, zeros)
    behind, ahead = pick(upper, edge_zeros, met_edge), pick(upper, met_edge, edge_zeros)
    return before, after, behind, ahead


def narrow(lay, upper, low, high, before, after, behind, ahead):
    low_last, high_first = inner(lay, low, high, before, after)
    return (
        pick(upper, before, low_last),
        pick(upper, high_first, after),
        pick(upper, behind, low["tail"]),
        pick(upper, high["head"], ahead),
    )


def write_answer(lay, ref, before, after, behind, ahead):
    write_rows(ref, 0, before + after + behind + ahead, lay.lines)


def solve_kernel(lay, levels, split, me_ref, *refs):
    me = me_ref[0]
    own_refs, got_refs = refs[:levels], refs[levels : 2 * levels]
    outs = refs[2 * levels :]
    state = descend(lay, me, levels, own_refs, got_refs)
    for level in reversed(range(levels - 1)):
        upper = (me >> level) & 1
        low, high = ordered(
            upper, read_block(lay, own_refs[level]), read_block(lay, got_refs[level])
        )
        if level == 0 and split:
            write_answer(lay, outs[1], *narrow(lay, 1 - upper, low, high, *state))
        state = narrow(lay, upper, low, high, *state)
    write_answer(lay, outs[0], *state)


def corners(weights):
    one = jnp.ones_like(weights[0])
    value, slope, chain = one, one, [one]
    for weight in weights:
        value, slope = growing_step(value, slope, weight)
        chain.append(value)
    total = 1.0 / value
    back, fall, backs = one, one, []
    for weight in reversed(weights):
        backs.append(back)
        back, fall = growing_step(back, fall, weight)
    backs.reverse()
    return chain, backs, total


def z_kernel(
    dims, lay, me_ref, cot_any, diff_any, phase_any, cour_any, upw_any, az, w_out, inv_out, keep, send,
    cot, diff, phase, cour, upw, wt, pht, pst, phi, psi, left, right, both, in_sems, sems,
):
    nx, ny = dims
    rows = nx * ny
    tiles = rows // LANES
    half = nx // 2
    small = [(diff_any, diff), (phase_any, phase), (cour_any.at[1], cour), (upw_any.at[1], upw)]
    for i, (source, target) in enumerate(small):
        pltpu.make_async_copy(source, target, sems.at[i]).start()
    for c in range(COMPS):
        pltpu.make_async_copy(cot_any.at[c], cot.at[c], in_sems.at[c]).start()

    for i, (source, target) in enumerate(small[:2]):
        pltpu.make_async_copy(source, target, sems.at[i]).wait()
    w_out[...] = weight_of(diff[...], phase[...])
    for t in range(tiles):
        span = pl.ds(t * LANES, LANES)
        wt[span, :] = w_out[span, :].T
    ones = jnp.ones((tiles, LANES), jnp.float32)
    value, slope = ones, ones
    back, fall = ones, ones
    for k in range(LANES):
        here = pl.ds(k, tiles, stride=LANES)
        pht[here, :] = value
        value, slope = growing_step(value, slope, wt[here, :])
        there = pl.ds(LANES - 1 - k, tiles, stride=LANES)
        pst[there, :] = back
        back, fall = growing_step(back, fall, wt[there, :])
    scale = 1.0 / value
    for t in range(tiles):
        span = pl.ds(t * LANES, LANES)
        phi[span, :] = pht[span, :].T
        psi[span, :] = (pst[span, :] * scale[t : t + 1]).T

    chain, backs, total = corners([w_out[pl.ds(y, nx, stride=ny), :] for y in range(ny)])
    for y in range(ny):
        span = pl.ds(y * nx, nx)
        left[span, :] = backs[y] * total
        right[span, :] = chain[y] * total
        inv_out[span, :] = chain[y] / chain[y + 1]

    def post(row, cells):
        for h in range(2):
            both[pl.ds(h * lay.rows + row, half), :] = cells[h * half : (h + 1) * half]

    post(lay.couple, left[pl.ds(0, nx), :])
    post(lay.couple + half, total)
    post(lay.couple + 2 * half, right[pl.ds((ny - 1) * nx, nx), :])
    for i, (source, target) in enumerate(small[2:]):
        pltpu.make_async_copy(source, target, sems.at[2 + i]).wait()
    for e, y in enumerate((0, ny - 1)):
        edge = pl.ds(y, nx, stride=ny)
        weight = w_out[edge, :]
        up = cour[edge, :] * upw[edge, :].astype(jnp.float32)
        flow = up if e == 0 else cour[edge, :] - up
        post(lay.edge + 2 * e * half, weight)
        post(lay.edge + (2 * e + 1) * half, weight * flow)

    sums = sum_matrix()
    for c in range(COMPS):
        pltpu.make_async_copy(cot_any.at[c], cot.at[c], in_sems.at[c]).wait()
        for t in range(tiles):
            span = pl.ds(t * LANES, LANES)
            cells, up, down = cot[c, span, :], phi[span, :], psi[span, :]
            wide = jnp.concatenate([up * cells, down * cells], axis=1)
            found = sum(
                jnp.dot(part, sums, preferred_element_type=jnp.float32) for part in split3(wide)
            )
            az[c, span, :] = w_out[span, :] * (down * found[:, :LANES] + up * found[:, LANES:])
        first = jnp.zeros((nx, LANES), jnp.float32)
        last = jnp.zeros((nx, LANES), jnp.float32)
        for y in range(ny):
            cells = az[c, pl.ds(y, nx, stride=ny), :]
            span = pl.ds(y * nx, nx)
            first = first + left[span, :] * cells
            last = last + right[span, :] * cells
        post(c * half, first)
        post((COMPS + c) * half, last)
    mine = me_ref[0] & 1
    keep[...] = both[pl.ds(pl.multiple_of(mine * lay.rows, TILE), lay.rows), :]
    send[...] = both[pl.ds(pl.multiple_of((1 - mine) * lay.rows, TILE), lay.rows), :]


def sides(before, after, x):
    return jnp.concatenate(
        [
            jnp.broadcast_to(before[pl.ds(x, 1), :], (TILE, LANES)),
            jnp.broadcast_to(after[pl.ds(x, 1), :], (TILE, LANES)),
        ],
        axis=0,
    )


def y_kernel(
    dims, ylay, xlay, me_ref, az, own, got, w, inv, cour, upw,
    ay, ghost, block, xinv, before, after, joined, left_all,
):
    nx, ny = dims
    half = nx // 2
    rows = ny + 2 * TILE
    mine = me_ref[0] & 1
    span = ylay.answer_rows
    joined[pl.ds(pl.multiple_of(mine * span, TILE), span), :] = own[...]
    joined[pl.ds(pl.multiple_of((1 - mine) * span, TILE), span), :] = got[...]
    for h in range(2):
        for e in range(2):
            where = pl.ds(e * nx + h * half, half)
            row = h * span + 2 * COMPS * half + e * half
            before[where, :] = joined[pl.ds(row, half), :]
            after[where, :] = joined[pl.ds(row + 2 * half, half), :]

    ghost[...] = jnp.zeros(ghost.shape, jnp.float32)
    for c in range(COMPS):
        for h in range(2):
            part = pl.ds(h * half, half)
            fb = joined[pl.ds(h * span + c * half, half), :]
            fa = joined[pl.ds(h * span + (COMPS + c) * half, half), :]
            deep = 2 * TILE
            ghost[pl.ds(h * half * deep + c, half, stride=deep), :] = before[part, :] * fb
            ghost[pl.ds(h * half * deep + TILE + c, half, stride=deep), :] = after[part, :] * fa
            swept, chain = fb, []
            for y in range(ny):
                cells = az[c, pl.ds(h * half * ny + y, half, stride=ny), :]
                swept = (cells + swept) * inv[pl.ds(y * nx + h * half, half), :]
                chain.append(swept)
            later = fa
            for y in reversed(range(ny)):
                where = pl.ds(h * half * ny + y, half, stride=ny)
                later = chain[y] + inv[pl.ds(y * nx + h * half, half), :] * later
                ay[c, where, :] = later * w[where, :]

    def weight_at(x):
        return jnp.concatenate([w[pl.ds(x * ny, ny), :], sides(before, after, x)], axis=0)

    one = jnp.ones((rows, LANES), jnp.float32)
    back, fall = one, one
    for x in reversed(range(nx)):
        left_all[pl.ds(x * rows, rows), :] = back
        back, fall = growing_step(back, fall, weight_at(x))
    total = 1.0 / back
    value, slope = one, one
    zero = jnp.zeros((ny, LANES), jnp.float32)
    pieces = xlay.pieces
    firsts, lasts = [zero] * pieces, [zero] * pieces
    corner = left_all[pl.ds(0, rows), :]
    for x in range(nx):
        down = left_all[pl.ds(x * rows, rows), :]
        for i in range(pieces):
            part = slice(0, ny) if i < COMPS else slice(ny, rows)
            cells = ay[i, pl.ds(x * ny, ny), :] if i < COMPS else ghost[pl.ds(x * 2 * TILE, 2 * TILE), :]
            lasts[i] = lasts[i] + value[part] * cells
            firsts[i] = firsts[i] + down[part] * cells
        new_value, slope = growing_step(value, slope, weight_at(x))
        xinv[pl.ds(x * rows, rows), :] = value / new_value
        end, value = value, new_value

    def halves(cells):
        return [cells[:ny], cells[ny:]]

    scale = halves(total)
    edges = []
    for e, x in enumerate((0, nx - 1)):
        where = pl.ds(x * ny, ny)
        up = cour[0, where, :] * upw[0, where, :].astype(jnp.float32)
        edges.append(w[where, :] * (up if e == 0 else cour[0, where, :] - up))
    write_block(
        xlay,
        block,
        {
            "first": [v * scale[xlay.group(i)] for i, v in enumerate(firsts)],
            "last": [v * scale[xlay.group(i)] for i, v in enumerate(lasts)],
            "near": halves(corner * total),
            "cross": scale,
            "far": halves(end * total),
            "head": edges[:1],
            "tail": edges[1:],
        },
    )
    if xlay.edge > xlay.packed + 6:
        block[pl.ds(xlay.packed + 6, 2), :] = jnp.zeros((2, LANES), jnp.float32)


def x_kernel(
    dims, lay, levels, me_ref, *refs
):
    nx, ny = dims
    own_refs, got_refs = refs[:levels], refs[levels : 2 * levels]
    (xinv, ay, ghost, w, lower, upper_edge, courant, upwind,
     out_any, out, swept_all, gswept, answer, sems) = refs[2 * levels :]
    rows = ny + 2 * TILE
    solve_kernel(lay, levels, False, me_ref, *own_refs, *got_refs, answer)
    n = lay.pieces
    starts = read_rows(answer, 0, n, ny)
    nexts = read_rows(answer, n * ny, n, ny)
    near = answer[pl.ds(2 * n * ny, ny), :]
    far = answer[pl.ds((2 * n + 1) * ny, ny), :]

    def sweep(x, carry):
        factor = xinv[pl.ds(x * rows, rows), :]
        span = pl.ds(x * ny, ny)
        new = []
        for c in range(COMPS):
            value = (ay[c, span, :] + carry[c]) * factor[:ny]
            swept_all[c, span, :] = value
            new.append(value)
        gspan = pl.ds(x * 2 * TILE, 2 * TILE)
        gvalue = (ghost[gspan, :] + carry[COMPS]) * factor[ny:]
        gswept[gspan, :] = gvalue
        return tuple(new) + (gvalue,)

    lax.fori_loop(0, nx, sweep, tuple(starts), unroll=4)

    lane = lax.broadcasted_iota(jnp.int32, (ny, LANES), 1)
    line = lax.broadcasted_iota(jnp.int32, (ny, LANES), 0)

    def finish(step, carry):
        cells, fluxes, gcells = carry
        x = nx - 1 - step
        span = pl.ds(x * ny, ny)
        factor = xinv[pl.ds(x * rows, rows), :]
        weight = w[span, :]
        ahead, behind = [], []
        own = jnp.ones((ny, LANES), jnp.float32)
        for d in range(3):
            flow = courant[d, span, :]
            up = flow * upwind[d, span, :].astype(jnp.float32)
            down = flow - up
            own = own + (down - up)
            ahead.append(up)
            behind.append(down)
        ahead_y = jnp.where(line == 0, 0.0, ahead[1])
        behind_y = jnp.where(line == ny - 1, 0.0, behind[1])
        ahead_z = jnp.where(lane == 0, 0.0, ahead[2])
        behind_z = jnp.where(lane == LANES - 1, 0.0, behind[2])
        gspan = pl.ds(x * 2 * TILE, 2 * TILE)
        gvalue = gswept[gspan, :] + factor[ny:] * gcells
        gflux = gvalue * jnp.concatenate(
            [
                jnp.broadcast_to(lower[pl.ds(nx + x, 1), :], (TILE, LANES)),
                jnp.broadcast_to(upper_edge[pl.ds(nx + x, 1), :], (TILE, LANES)),
            ],
            axis=0,
        )
        new_cells, new_fluxes = [], []
        for c in range(COMPS):
            solved = swept_all[c, span, :] + factor[:ny] * cells[c]
            grad = weight * solved
            part = own * grad + fluxes[c]
            part = part + pltpu.roll(ahead_y * grad, ny - 1, 0) - pltpu.roll(behind_y * grad, 1, 0)
            part = part + pltpu.roll(ahead_z * grad, LANES - 1, 1) - pltpu.roll(behind_z * grad, 1, 1)
            part = part - jnp.where(line == 0, gflux[c : c + 1], 0.0)
            part = part + jnp.where(line == ny - 1, gflux[TILE + c : TILE + c + 1], 0.0)
            out[c, span, :] = part
            above = pl.ds((x + 1) * ny, ny)
            out[c, above, :] = out[c, above, :] - behind[0] * grad
            new_cells.append(solved)
            new_fluxes.append(ahead[0] * grad)
        return tuple(new_cells), tuple(new_fluxes), gvalue

    out[:, pl.ds(nx * ny, ny), :] = jnp.zeros((COMPS, ny, LANES), jnp.float32)
    state = (tuple(nexts[:COMPS]), tuple(far * nexts[c] for c in range(COMPS)), nexts[COMPS])
    parts = 4
    deep = nx // parts

    def copy(part):
        span = pl.ds(part * deep * ny, deep * ny)
        return pltpu.make_async_copy(out.at[:, span, :], out_any.at[:, span, :], sems.at[part])

    for part in reversed(range(parts)):
        first = (parts - 1 - part) * deep
        state = lax.fori_loop(first, first + deep, finish, state)
        if part + 1 < parts:
            copy(part + 1).start()
    top = pl.ds(0, ny)
    for c in range(COMPS):
        out[c, top, :] = out[c, top, :] - near * starts[c]
    copy(0).start()
    for part in range(parts):
        copy(part).wait()


def call(kernel, name, operands, outs, scratch=(), spaces=None, out_spaces=None):
    params = pltpu.CompilerParams(vmem_limit_bytes=VMEM_BYTES)
    pick_space = {
        "v": pl.BlockSpec(memory_space=pltpu.VMEM),
        "h": pl.BlockSpec(memory_space=pltpu.HBM),
        "s": pl.BlockSpec(memory_space=pltpu.SMEM),
    }
    spaces = spaces or "s" + "v" * (len(operands) - 1)
    out_spaces = out_spaces or "v" * len(outs)
    return pl.pallas_call(
        kernel,
        name=name,
        out_shape=[jax.ShapeDtypeStruct(shape, jnp.float32) for shape in outs],
        in_specs=[pick_space[s] for s in spaces],
        out_specs=[pick_space[s] for s in out_spaces],
        scratch_shapes=list(scratch),
        compiler_params=params,
    )(*operands)


def exchange(rows, axis, bit):
    count = lax.axis_size(axis)
    return lax.ppermute(rows, axis, [(i, i ^ (1 << bit)) for i in range(count)])


def climb(lay, axis, levels, me, own):
    owns, gots = [own], []
    for level in range(levels - 1):
        gots.append(exchange(owns[-1][0], axis, level))
        top = level == levels - 2
        shapes = [(lay.rows, LANES)] + ([(lay.side_rows, LANES)] if top else [])
        merged = call(
            functools.partial(merge_kernel, lay, level, top),
            axis + "_merge_" + str(level),
            (me, owns[-1][1], gots[-1]),
            shapes,
        )
        owns.append((merged[-1], merged[0]))
    gots.append(exchange(owns[-1][0], axis, levels - 1))
    return [block for _, block in owns], gots


def on_device(cotangent, diffusion, phase, courant, upwind):
    comps, nx, ny, nz = cotangent.shape
    x_levels = (lax.axis_size("gx") - 1).bit_length()
    y_levels = (lax.axis_size("gy") - 1).bit_length()
    rows = nx * ny
    half = nx // 2
    wide = ny + 2 * TILE
    ylay = Layout(comps, 1, 2, half)
    xlay = Layout(comps + 1, 2, 1, ny)
    me_x = lax.axis_index("gx").astype(jnp.int32).reshape(1)
    me_y = lax.axis_index("gy").astype(jnp.int32).reshape(1)

    def vmem(*shape, dtype=jnp.float32):
        return pltpu.VMEM(shape, dtype)

    cot = cotangent.reshape(comps, rows, nz)
    cour = courant.reshape(3, rows, nz)
    upw = upwind.reshape(3, rows, nz)
    az, w, inv, keep, send = call(
        functools.partial(z_kernel, (nx, ny), ylay),
        "z_solve",
        (me_y, cot, diffusion.reshape(rows, nz), phase.reshape(rows, nz), cour, upw),
        [(comps, rows, nz), (rows, nz), (rows, nz), (ylay.rows, nz), (ylay.rows, nz)],
        [
            vmem(comps, rows, nz), vmem(rows, nz), vmem(rows, nz, dtype=jnp.int32),
            vmem(rows, nz), vmem(rows, nz, dtype=jnp.int32),
            vmem(rows, nz), vmem(rows, nz), vmem(rows, nz), vmem(rows, nz), vmem(rows, nz),
            vmem(rows, nz), vmem(rows, nz), vmem(2 * ylay.rows, nz),
            pltpu.SemaphoreType.DMA((comps,)), pltpu.SemaphoreType.DMA((4,)),
        ],
        spaces="shhhhh",
    )
    y_owns, y_gots = climb(ylay, "gy", y_levels, me_y, (send, keep))
    answer, passed = call(
        functools.partial(solve_kernel, ylay, y_levels, True),
        "y_reduced",
        (me_y, *y_owns, *y_gots),
        [(ylay.answer_rows, nz), (ylay.answer_rows, nz)],
    )
    met = exchange(passed, "gy", 0)
    ay, ghost, block, xinv, before, after = call(
        functools.partial(y_kernel, (nx, ny), ylay, xlay),
        "y_solve",
        (me_y, az, answer, met, w, inv, cour, upw),
        [
            (comps, rows, nz), (nx * 2 * TILE, nz), (xlay.rows, nz), (nx * wide, nz),
            (2 * nx, nz), (2 * nx, nz),
        ],
        [vmem(2 * ylay.answer_rows, nz), vmem(nx * wide, nz)],
    )
    x_owns, x_gots = climb(xlay, "gx", x_levels, me_x, (block, block))
    (grad,) = call(
        functools.partial(x_kernel, (nx, ny), xlay, x_levels),
        "x_solve",
        (me_x, *x_owns, *x_gots, xinv, ay, ghost, w, before, after, cour, upw),
        [(comps, rows, nz)],
        [
            vmem(comps, rows + ny, nz), vmem(comps, rows, nz), vmem(nx * 2 * TILE, nz),
            vmem(xlay.answer_rows, nz), pltpu.SemaphoreType.DMA((4,)),
        ],
        out_spaces="h",
    )
    return grad.reshape(comps, nx, ny, nz)


def solution(mesh):
    placed = (
        P(None, "gx", "gy", None),
        P("gx", "gy", None),
        P("gx", "gy", None),
        P(None, "gx", "gy", None),
        P(None, "gx", "gy", None),
    )
    return jax.shard_map(
        on_device, mesh=mesh, in_specs=placed, out_specs=P(None, "gx", "gy", None), check_vma=False
    )
```

```python
import functools

import jax
import jax.numpy as jnp
from jax import lax
from jax.experimental import pallas as pl
from jax.experimental.pallas import tpu as pltpu
from jax.sharding import PartitionSpec as P

COMPS = 6
LANES = 128
TILE = 8


def weight_of(diffusion, phase):
    return 1.0 / (diffusion * (1.0 + 3.0 * phase.astype(jnp.float32)))


def growing_step(value, slope, weight):
    slope = slope + weight * value
    return value + slope, slope


def split3(cells):
    high = cells.astype(jnp.bfloat16)
    rest = cells - high.astype(jnp.float32)
    middle = rest.astype(jnp.bfloat16)
    low = (rest - middle.astype(jnp.float32)).astype(jnp.bfloat16)
    return high, middle, low


def sum_matrix():
    row = lax.broadcasted_iota(jnp.int32, (2 * LANES, 2 * LANES), 0)
    col = lax.broadcasted_iota(jnp.int32, (2 * LANES, 2 * LANES), 1)
    before = (row < LANES) & (col < LANES) & (row <= col)
    after = (row >= LANES) & (col >= LANES) & (row > col)
    return jnp.where(before | after, 1.0, 0.0).astype(jnp.bfloat16)


class Layout:
    def __init__(self, pieces, groups, edges, lines):
        self.pieces, self.groups, self.edges, self.lines = pieces, groups, edges, lines
        self.couple = pieces * lines * 2
        self.packed = self.couple + 3 * lines
        self.edge = self.packed + (TILE if groups > 1 else 0)
        self.rows = self.edge + 2 * edges * lines
        self.side_couple = pieces * lines
        self.side_packed = self.side_couple + lines
        self.side_edge = self.side_packed + (TILE if groups > 1 else 0)
        self.side_rows = self.side_edge + edges * lines
        self.answer_rows = 2 * (pieces + edges) * lines

    def group(self, piece):
        return 0 if piece < COMPS else 1


def read_rows(ref, base, count, lines):
    return [ref[pl.ds(base + i * lines, lines), :] for i in range(count)]


def write_rows(ref, base, values, lines):
    for i, value in enumerate(values):
        ref[pl.ds(base + i * lines, lines), :] = value


def read_pair(ref, row):
    return jnp.concatenate(
        [jnp.broadcast_to(ref[pl.ds(row + i, 1), :], (TILE, LANES)) for i in range(2)], axis=0
    )


def write_pair(ref, row, value):
    ref[pl.ds(row, 1), :] = value[:1]
    ref[pl.ds(row + 1, 1), :] = value[TILE : TILE + 1]


def read_block(lay, ref, base=0):
    n, m = lay.lines, lay.pieces
    couple = []
    for e in range(3):
        entry = [ref[pl.ds(base + lay.couple + e * n, n), :]]
        if lay.groups > 1:
            entry.append(read_pair(ref, base + lay.packed + 2 * e))
        couple.append(entry)
    return {
        "first": read_rows(ref, base, m, n),
        "last": read_rows(ref, base + m * n, m, n),
        "near": couple[0],
        "cross": couple[1],
        "far": couple[2],
        "head": read_rows(ref, base + lay.edge, lay.edges, n),
        "tail": read_rows(ref, base + lay.edge + lay.edges * n, lay.edges, n),
    }


def write_block(lay, ref, block, base=0):
    n, m = lay.lines, lay.pieces
    write_rows(ref, base, block["first"], n)
    write_rows(ref, base + m * n, block["last"], n)
    for e, name in enumerate(("near", "cross", "far")):
        ref[pl.ds(base + lay.couple + e * n, n), :] = block[name][0]
        if lay.groups > 1:
            write_pair(ref, base + lay.packed + 2 * e, block[name][1])
    write_rows(ref, base + lay.edge, block["head"], n)
    write_rows(ref, base + lay.edge + lay.edges * n, block["tail"], n)


def write_side(lay, ref, block, upper):
    n = lay.lines

    def facing(low, high):
        return jnp.where(jnp.full(low.shape, upper, jnp.int32) == 1, high, low)

    write_rows(ref, 0, [facing(a, b) for a, b in zip(block["last"], block["first"])], n)
    pair = [facing(a, b) for a, b in zip(block["far"], block["near"])]
    ref[pl.ds(lay.side_couple, n), :] = pair[0]
    if lay.groups > 1:
        write_pair(ref, lay.side_packed, pair[1])
    write_rows(ref, lay.side_edge, [facing(a, b) for a, b in zip(block["tail"], block["head"])], n)


def read_side(lay, ref):
    n = lay.lines
    couple = [ref[pl.ds(lay.side_couple, n), :]]
    if lay.groups > 1:
        couple.append(read_pair(ref, lay.side_packed))
    return (
        read_rows(ref, 0, lay.pieces, n),
        couple,
        read_rows(ref, lay.side_edge, lay.edges, n),
    )


def pick(upper, low, high):
    if isinstance(low, list):
        return [pick(upper, a, b) for a, b in zip(low, high)]
    return jnp.where(jnp.full(low.shape, upper, jnp.int32) == 1, high, low)


def ordered(upper, own, other):
    low = {name: pick(upper, own[name], other[name]) for name in own}
    high = {name: pick(upper, other[name], own[name]) for name in own}
    return low, high


def joint(lay, low, high):
    return [
        1.0 / (1.0 - low["far"][g] * high["near"][g]) for g in range(lay.groups)
    ]


def merge(lay, low, high):
    shrink = joint(lay, low, high)
    to_low = [low["cross"][g] * shrink[g] for g in range(lay.groups)]
    to_high = [high["cross"][g] * shrink[g] for g in range(lay.groups)]
    span = range(lay.pieces)
    of = lay.group
    return {
        "first": [
            low["first"][i]
            + to_low[of(i)] * (high["first"][i] + high["near"][of(i)] * low["last"][i])
            for i in span
        ],
        "last": [
            high["last"][i]
            + to_high[of(i)] * (low["last"][i] + low["far"][of(i)] * high["first"][i])
            for i in span
        ],
        "near": [
            low["near"][g] + to_low[g] * low["cross"][g] * high["near"][g]
            for g in range(lay.groups)
        ],
        "cross": [to_low[g] * high["cross"][g] for g in range(lay.groups)],
        "far": [
            high["far"][g] + to_high[g] * high["cross"][g] * low["far"][g]
            for g in range(lay.groups)
        ],
        "head": low["head"],
        "tail": high["tail"],
    }


def inner(lay, low, high, before, after):
    shrink = joint(lay, low, high)
    low_last, high_first = [], []
    for i in range(lay.pieces):
        g = lay.group(i)
        left = low["last"][i] + low["cross"][g] * before[i]
        right = high["first"][i] + high["cross"][g] * after[i]
        low_last.append((left + low["far"][g] * right) * shrink[g])
        high_first.append((right + high["near"][g] * left) * shrink[g])
    return low_last, high_first


def merge_kernel(lay, bit, top, me_ref, own, other, *refs):
    out, *side = refs[-2:] if top else refs[-1:]
    upper = (me_ref[0] >> bit) & 1
    low, high = ordered(upper, read_block(lay, own), read_block(lay, other))
    block = merge(lay, low, high)
    write_block(lay, out, block)
    if top:
        write_side(lay, side[0], block, (me_ref[0] >> (bit + 1)) & 1)


def descend(lay, me, levels, own_refs, got_refs):
    top = levels - 1
    upper = (me >> top) & 1
    own = read_block(lay, own_refs[top])
    met, met_couple, met_edge = read_side(lay, got_refs[top])
    facing = pick(upper, own["last"], own["first"])
    couple = pick(upper, own["far"], own["near"])
    found = []
    for i in range(lay.pieces):
        g = lay.group(i)
        found.append((met[i] + met_couple[g] * facing[i]) / (1.0 - met_couple[g] * couple[g]))
    zeros = [jnp.zeros_like(v) for v in found]
    edge_zeros = [jnp.zeros_like(v) for v in met_edge]
    before, after = pick(upper, zeros, found), pick(upper, found, zeros)
    behind, ahead = pick(upper, edge_zeros, met_edge), pick(upper, met_edge, edge_zeros)
    return before, after, behind, ahead


def narrow(lay, upper, low, high, before, after, behind, ahead):
    low_last, high_first = inner(lay, low, high, before, after)
    return (
        pick(upper, before, low_last),
        pick(upper, high_first, after),
        pick(upper, behind, low["tail"]),
        pick(upper, high["head"], ahead),
    )


def write_answer(lay, ref, before, after, behind, ahead):
    write_rows(ref, 0, before + after + behind + ahead, lay.lines)


def solve_kernel(lay, levels, split, me_ref, *refs):
    me = me_ref[0]
    own_refs, got_refs = refs[:levels], refs[levels : 2 * levels]
    outs = refs[2 * levels :]
    state = descend(lay, me, levels, own_refs, got_refs)
    for level in reversed(range(levels - 1)):
        upper = (me >> level) & 1
        low, high = ordered(
            upper, read_block(lay, own_refs[level]), read_block(lay, got_refs[level])
        )
        if level == 0 and split:
            write_answer(lay, outs[1], *narrow(lay, 1 - upper, low, high, *state))
        state = narrow(lay, upper, low, high, *state)
    write_answer(lay, outs[0], *state)


def corners(weights):
    one = jnp.ones_like(weights[0])
    value, slope, chain = one, one, [one]
    for weight in weights:
        value, slope = growing_step(value, slope, weight)
        chain.append(value)
    total = 1.0 / value
    back, fall, backs = one, one, []
    for weight in reversed(weights):
        backs.append(back)
        back, fall = growing_step(back, fall, weight)
    backs.reverse()
    return chain, backs, total


def z_kernel(
    dims, lay, me_ref, cot_any, diff_any, phase_any, cour_any, upw_any, az, w_out, inv_out, keep, send,
    cot, diff, phase, cour, upw, wt, pht, pst, phi, psi, left, right, both, in_sems, sems,
):
    nx, ny = dims
    rows = nx * ny
    tiles = rows // LANES
    half = nx // 2
    small = [(diff_any, diff), (phase_any, phase), (cour_any.at[1], cour), (upw_any.at[1], upw)]
    for i, (source, target) in enumerate(small):
        pltpu.make_async_copy(source, target, sems.at[i]).start()
    for c in range(COMPS):
        pltpu.make_async_copy(cot_any.at[c], cot.at[c], in_sems.at[c]).start()

    for i, (source, target) in enumerate(small[:2]):
        pltpu.make_async_copy(source, target, sems.at[i]).wait()
    w_out[...] = weight_of(diff[...], phase[...])
    for t in range(tiles):
        span = pl.ds(t * LANES, LANES)
        wt[span, :] = w_out[span, :].T
    ones = jnp.ones((tiles, LANES), jnp.float32)
    value, slope = ones, ones
    back, fall = ones, ones
    for k in range(LANES):
        here = pl.ds(k, tiles, stride=LANES)
        pht[here, :] = value
        value, slope = growing_step(value, slope, wt[here, :])
        there = pl.ds(LANES - 1 - k, tiles, stride=LANES)
        pst[there, :] = back
        back, fall = growing_step(back, fall, wt[there, :])
    scale = 1.0 / value
    for t in range(tiles):
        span = pl.ds(t * LANES, LANES)
        phi[span, :] = pht[span, :].T
        psi[span, :] = (pst[span, :] * scale[t : t + 1]).T

    chain, backs, total = corners([w_out[pl.ds(y, nx, stride=ny), :] for y in range(ny)])
    for y in range(ny):
        span = pl.ds(y * nx, nx)
        left[span, :] = backs[y] * total
        right[span, :] = chain[y] * total
        inv_out[span, :] = chain[y] / chain[y + 1]

    def post(row, cells):
        for h in range(2):
            both[pl.ds(h * lay.rows + row, half), :] = cells[h * half : (h + 1) * half]

    post(lay.couple, left[pl.ds(0, nx), :])
    post(lay.couple + half, total)
    post(lay.couple + 2 * half, right[pl.ds((ny - 1) * nx, nx), :])
    for i, (source, target) in enumerate(small[2:]):
        pltpu.make_async_copy(source, target, sems.at[2 + i]).wait()
    for e, y in enumerate((0, ny - 1)):
        edge = pl.ds(y, nx, stride=ny)
        weight = w_out[edge, :]
        up = cour[edge, :] * upw[edge, :].astype(jnp.float32)
        flow = up if e == 0 else cour[edge, :] - up
        post(lay.edge + 2 * e * half, weight)
        post(lay.edge + (2 * e + 1) * half, weight * flow)

    sums = sum_matrix()
    for c in range(COMPS):
        pltpu.make_async_copy(cot_any.at[c], cot.at[c], in_sems.at[c]).wait()
        for t in range(tiles):
            span = pl.ds(t * LANES, LANES)
            cells, up, down = cot[c, span, :], phi[span, :], psi[span, :]
            wide = jnp.concatenate([up * cells, down * cells], axis=1)
            found = sum(
                jnp.dot(part, sums, preferred_element_type=jnp.float32) for part in split3(wide)
            )
            az[c, span, :] = w_out[span, :] * (down * found[:, :LANES] + up * found[:, LANES:])
        first = jnp.zeros((nx, LANES), jnp.float32)
        last = jnp.zeros((nx, LANES), jnp.float32)
        for y in range(ny):
            cells = az[c, pl.ds(y, nx, stride=ny), :]
            span = pl.ds(y * nx, nx)
            first = first + left[span, :] * cells
            last = last + right[span, :] * cells
        post(c * half, first)
        post((COMPS + c) * half, last)
    mine = me_ref[0] & 1
    keep[...] = both[pl.ds(pl.multiple_of(mine * lay.rows, TILE), lay.rows), :]
    send[...] = both[pl.ds(pl.multiple_of((1 - mine) * lay.rows, TILE), lay.rows), :]


def sides(before, after, x):
    return jnp.concatenate(
        [
            jnp.broadcast_to(before[pl.ds(x, 1), :], (TILE, LANES)),
            jnp.broadcast_to(after[pl.ds(x, 1), :], (TILE, LANES)),
        ],
        axis=0,
    )


def coef_kernel(dims, w, courant, upwind, after, block, xinv, left, right, flows):
    del after
    nx, ny = dims
    rows = nx * ny
    one = jnp.ones((ny, LANES), jnp.float32)
    value, slope, back, fall = one, one, one, one
    for k in range(nx):
        low, high = pl.ds(k * ny, ny), pl.ds((nx - 1 - k) * ny, ny)
        right[low, :] = value
        left[high, :] = back
        new_value, slope = growing_step(value, slope, w[low, :])
        xinv[low, :] = value / new_value
        end, value = value, new_value
        corner = back
        back, fall = growing_step(back, fall, w[high, :])
    total = 1.0 / value
    block[pl.ds(0, ny), :] = corner * total
    block[pl.ds(ny, ny), :] = total
    block[pl.ds(2 * ny, ny), :] = end * total

    lane = lax.broadcasted_iota(jnp.int32, (ny, LANES), 1)

    def plane(x, carry):
        span = pl.ds(x * ny, ny)
        left[span, :] = left[span, :] * total
        right[span, :] = right[span, :] * total
        own = one
        for d in range(3):
            flow = courant[d, span, :]
            up = flow * upwind[d, span, :].astype(jnp.float32)
            down = flow - up
            own = own + (down - up)
            if d == 2:
                up = jnp.where(lane == 0, 0.0, up)
                down = jnp.where(lane == LANES - 1, 0.0, down)
            flows[pl.ds((1 + 2 * d) * rows + x * ny, ny), :] = up
            flows[pl.ds((2 + 2 * d) * rows + x * ny, ny), :] = down
        flows[span, :] = own
        return carry

    lax.fori_loop(0, nx, plane, 0, unroll=4)
    first, last = pl.ds(0, ny), pl.ds(rows - ny, ny)
    block[pl.ds(3 * ny, ny), :] = w[first, :] * flows[pl.ds(rows, ny), :]
    block[pl.ds(4 * ny, ny), :] = w[last, :] * flows[pl.ds(2 * rows + rows - ny, ny), :]


def y_kernel(
    dims, ylay, xlay, me_ref, az, own, got, w, inv, left, right, part,
    ay, ghost, block, ginv, before, after, joined, back_all,
):
    nx, ny = dims
    half = nx // 2
    deep = 2 * TILE
    mine = me_ref[0] & 1
    span = ylay.answer_rows
    joined[pl.ds(pl.multiple_of(mine * span, TILE), span), :] = own[...]
    joined[pl.ds(pl.multiple_of((1 - mine) * span, TILE), span), :] = got[...]
    for h in range(2):
        for e in range(2):
            where = pl.ds(e * nx + h * half, half)
            row = h * span + 2 * COMPS * half + e * half
            before[where, :] = joined[pl.ds(row, half), :]
            after[where, :] = joined[pl.ds(row + 2 * half, half), :]

    ghost[...] = jnp.zeros(ghost.shape, jnp.float32)
    for c in range(COMPS):
        for h in range(2):
            piece = pl.ds(h * half, half)
            fb = joined[pl.ds(h * span + c * half, half), :]
            fa = joined[pl.ds(h * span + (COMPS + c) * half, half), :]
            ghost[pl.ds(h * half * deep + c, half, stride=deep), :] = before[piece, :] * fb
            ghost[pl.ds(h * half * deep + TILE + c, half, stride=deep), :] = after[piece, :] * fa
            swept, chain = fb, []
            for y in range(ny):
                cells = az[c, pl.ds(h * half * ny + y, half, stride=ny), :]
                swept = (cells + swept) * inv[pl.ds(y * nx + h * half, half), :]
                chain.append(swept)
            later = fa
            for y in reversed(range(ny)):
                where = pl.ds(h * half * ny + y, half, stride=ny)
                later = chain[y] + inv[pl.ds(y * nx + h * half, half), :] * later
                ay[c, where, :] = later * w[where, :]

    one = jnp.ones((deep, LANES), jnp.float32)
    back, fall = one, one
    for x in reversed(range(nx)):
        back_all[pl.ds(x * deep, deep), :] = back
        corner = back
        back, fall = growing_step(back, fall, sides(before, after, x))
    total = 1.0 / back
    value, slope = one, one
    zero = jnp.zeros((ny, LANES), jnp.float32)
    firsts, lasts = [zero] * xlay.pieces, [zero] * xlay.pieces
    for x in range(nx):
        here = pl.ds(x * ny, ny)
        near, far = left[here, :], right[here, :]
        for c in range(COMPS):
            cells = ay[c, here, :]
            firsts[c] = firsts[c] + near * cells
            lasts[c] = lasts[c] + far * cells
        here = pl.ds(x * deep, deep)
        cells = ghost[here, :]
        firsts[COMPS] = firsts[COMPS] + back_all[here, :] * cells
        lasts[COMPS] = lasts[COMPS] + value * cells
        new_value, slope = growing_step(value, slope, sides(before, after, x))
        ginv[here, :] = value / new_value
        end, value = value, new_value
    firsts[COMPS] = firsts[COMPS] * total
    lasts[COMPS] = lasts[COMPS] * total
    pieces = [part[pl.ds(i * ny, ny), :] for i in range(5)]
    write_block(
        xlay,
        block,
        {
            "first": firsts,
            "last": lasts,
            "near": [pieces[0], corner * total],
            "cross": [pieces[1], total],
            "far": [pieces[2], end * total],
            "head": pieces[3:4],
            "tail": pieces[4:5],
        },
    )
    block[pl.ds(xlay.packed + 6, 2), :] = jnp.zeros((2, LANES), jnp.float32)


def x_kernel(dims, lay, levels, me_ref, *refs):
    nx, ny = dims
    own_refs, got_refs = refs[:levels], refs[levels : 2 * levels]
    (xinv, ginv, ay, ghost, w, lower, higher, flows,
     out_any, out, field, fluxes, answer, sems) = refs[2 * levels :]
    rows = nx * ny
    deep = 2 * TILE
    tiles = ny // TILE
    solve_kernel(lay, levels, False, me_ref, *own_refs, *got_refs, answer)
    n = lay.pieces
    starts = read_rows(answer, 0, n, ny)
    nexts = read_rows(answer, n * ny, n, ny)
    near = answer[pl.ds(2 * n * ny, ny), :]
    far = answer[pl.ds((2 * n + 1) * ny, ny), :]

    def sweep(x, carry):
        span, above = pl.ds(x * ny, ny), pl.ds((x + 1) * ny, ny)
        factor = xinv[span, :]
        new = []
        for c in range(COMPS):
            value = (ay[c, span, :] + carry[c]) * factor
            field[c, above, :] = value
            new.append(value)
        here = pl.ds(x * deep, deep)
        edge = (ghost[here, :] + carry[COMPS]) * ginv[here, :]
        fluxes[here, :] = edge
        return tuple(new) + (edge,)

    lax.fori_loop(0, nx, sweep, tuple(starts), unroll=8)

    def back(step, carry):
        x = nx - 1 - step
        span, above = pl.ds(x * ny, ny), pl.ds((x + 1) * ny, ny)
        factor = xinv[span, :]
        weight = w[span, :]
        new = []
        for c in range(COMPS):
            value = field[c, above, :] + factor * carry[c]
            field[c, above, :] = value * weight
            new.append(value)
        here = pl.ds(x * deep, deep)
        edge = fluxes[here, :] + ginv[here, :] * carry[COMPS]
        scale = jnp.concatenate(
            [
                jnp.broadcast_to(lower[pl.ds(nx + x, 1), :], (TILE, LANES)),
                jnp.broadcast_to(higher[pl.ds(nx + x, 1), :], (TILE, LANES)),
            ],
            axis=0,
        )
        fluxes[here, :] = edge * scale
        return tuple(new) + (edge,)

    lax.fori_loop(0, nx, back, tuple(nexts), unroll=8)
    blank = jnp.zeros((COMPS, ny, LANES), jnp.float32)
    field[:, pl.ds(0, ny), :] = blank
    field[:, pl.ds((nx + 1) * ny, ny), :] = blank

    line = lax.broadcasted_iota(jnp.int32, (TILE, LANES), 0)

    def advect(x, carry):
        before = jnp.maximum(x - 1, 0)
        beyond = jnp.minimum(x + 1, nx - 1)

        def flow(kind, plane, t):
            start = pl.multiple_of(kind * rows + plane * ny + t * TILE, TILE)
            return flows[pl.ds(start, TILE), :]

        own = [flow(0, x, t) for t in range(tiles)]
        ahead_x = [flow(1, beyond, t) for t in range(tiles)]
        behind_x = [flow(2, before, t) for t in range(tiles)]
        ahead_y = [flow(3, x, t) for t in range(tiles)]
        behind_y = [flow(4, x, t) for t in range(tiles)]
        ahead_z = [flow(5, x, t) for t in range(tiles)]
        behind_z = [flow(6, x, t) for t in range(tiles)]
        for c in range(COMPS):

            def cells(plane, t):
                start = pl.multiple_of((plane + 1) * ny + t * TILE, TILE)
                return field[c, pl.ds(start, TILE), :]

            grad = [cells(x, t) for t in range(tiles)]
            ups = [pltpu.roll(ahead_y[t] * grad[t], TILE - 1, 0) for t in range(tiles)]
            downs = [pltpu.roll(behind_y[t] * grad[t], 1, 0) for t in range(tiles)]
            lowest = fluxes[pl.ds(x * deep + c, 1), :]
            highest = fluxes[pl.ds(x * deep + TILE + c, 1), :]
            for t in range(tiles):
                part = own[t] * grad[t]
                part = part + ahead_x[t] * cells(x + 1, t) - behind_x[t] * cells(x - 1, t)
                enter = ups[t + 1] if t + 1 < tiles else jnp.broadcast_to(highest, (TILE, LANES))
                part = part + jnp.where(line == TILE - 1, enter, ups[t])
                enter = downs[t - 1] if t > 0 else jnp.broadcast_to(lowest, (TILE, LANES))
                part = part - jnp.where(line == 0, enter, downs[t])
                part = part + pltpu.roll(ahead_z[t] * grad[t], LANES - 1, 1)
                part = part - pltpu.roll(behind_z[t] * grad[t], 1, 1)
                start = pl.multiple_of(x * ny + t * TILE, TILE)
                out[c, pl.ds(start, TILE), :] = part
        return carry

    parts = 4
    share = nx // parts

    def copy(part):
        span = pl.ds(part * share * ny, share * ny)
        return pltpu.make_async_copy(out.at[:, span, :], out_any.at[:, span, :], sems.at[part])

    top, bottom = pl.ds(0, ny), pl.ds(rows - ny, ny)
    for part in range(parts):
        lax.fori_loop(part * share, (part + 1) * share, advect, 0, unroll=2)
        for c in range(COMPS):
            if part == 0:
                out[c, top, :] = out[c, top, :] - near * starts[c]
            if part == parts - 1:
                out[c, bottom, :] = out[c, bottom, :] + far * nexts[c]
        copy(part).start()
    for part in range(parts):
        copy(part).wait()


def call(kernel, name, operands, outs, scratch=(), spaces=None, out_spaces=None, mebibytes=4):
    params = pltpu.CompilerParams(vmem_limit_bytes=mebibytes * 1024 * 1024)
    pick_space = {
        "v": pl.BlockSpec(memory_space=pltpu.VMEM),
        "h": pl.BlockSpec(memory_space=pltpu.HBM),
        "s": pl.BlockSpec(memory_space=pltpu.SMEM),
    }
    spaces = spaces or "s" + "v" * (len(operands) - 1)
    out_spaces = out_spaces or "v" * len(outs)
    operands = [
        pltpu.with_memory_space_constraint(o, pltpu.HBM) if s == "h" else o
        for o, s in zip(operands, spaces)
    ]
    return pl.pallas_call(
        kernel,
        name=name,
        out_shape=[jax.ShapeDtypeStruct(shape, jnp.float32) for shape in outs],
        in_specs=[pick_space[s] for s in spaces],
        out_specs=[pick_space[s] for s in out_spaces],
        scratch_shapes=list(scratch),
        compiler_params=params,
    )(*operands)


def exchange(rows, axis, bit):
    count = lax.axis_size(axis)
    return lax.ppermute(rows, axis, [(i, i ^ (1 << bit)) for i in range(count)])


def climb(lay, axis, levels, me, own, beside=None):
    owns, gots, extra = [own], [], ()
    for level in range(levels - 1):
        gots.append(exchange(owns[-1][0], axis, level))
        top = level == levels - 2
        if beside is not None and top:
            extra = beside(owns[-1][1])
        shapes = [(lay.rows, LANES)] + ([(lay.side_rows, LANES)] if top else [])
        merged = call(
            functools.partial(merge_kernel, lay, level, top),
            axis + "_merge_" + str(level),
            (me, owns[-1][1], gots[-1]) + tuple(extra[:1]),
            shapes,
        )
        owns.append((merged[-1], merged[0]))
    gots.append(exchange(owns[-1][0], axis, levels - 1))
    return [block for _, block in owns], gots, extra


def on_device(cotangent, diffusion, phase, courant, upwind):
    comps, nx, ny, nz = cotangent.shape
    x_levels = (lax.axis_size("gx") - 1).bit_length()
    y_levels = (lax.axis_size("gy") - 1).bit_length()
    rows = nx * ny
    half = nx // 2
    ylay = Layout(comps, 1, 2, half)
    xlay = Layout(comps + 1, 2, 1, ny)
    me_x = lax.axis_index("gx").astype(jnp.int32).reshape(1)
    me_y = lax.axis_index("gy").astype(jnp.int32).reshape(1)

    def vmem(*shape, dtype=jnp.float32):
        return pltpu.VMEM(shape, dtype)

    cot = cotangent.reshape(comps, rows, nz)
    cour = courant.reshape(3, rows, nz)
    upw = upwind.reshape(3, rows, nz)
    az, w, inv, keep, send = call(
        functools.partial(z_kernel, (nx, ny), ylay),
        "z_solve",
        (me_y, cot, diffusion.reshape(rows, nz), phase.reshape(rows, nz), cour, upw),
        [(comps, rows, nz), (rows, nz), (rows, nz), (ylay.rows, nz), (ylay.rows, nz)],
        [
            vmem(comps, rows, nz), vmem(rows, nz), vmem(rows, nz, dtype=jnp.int32),
            vmem(rows, nz), vmem(rows, nz, dtype=jnp.int32),
            vmem(rows, nz), vmem(rows, nz), vmem(rows, nz), vmem(rows, nz), vmem(rows, nz),
            vmem(rows, nz), vmem(rows, nz), vmem(2 * ylay.rows, nz),
            pltpu.SemaphoreType.DMA((comps,)), pltpu.SemaphoreType.DMA((4,)),
        ],
        spaces="shhhhh",
        mebibytes=16,
    )
    def coefficients(after):
        return call(
            functools.partial(coef_kernel, (nx, ny)),
            "x_coefficients",
            (w, cour, upw, after),
            [(5 * ny, nz), (rows, nz), (rows, nz), (rows, nz), (7 * rows, nz)],
            spaces="vvvv",
            mebibytes=8,
        )

    y_owns, y_gots, found = climb(ylay, "gy", y_levels, me_y, (send, keep), coefficients)
    part, xinv, left, right, flows = found
    answer, passed = call(
        functools.partial(solve_kernel, ylay, y_levels, True),
        "y_reduced",
        (me_y, *y_owns, *y_gots),
        [(ylay.answer_rows, nz), (ylay.answer_rows, nz)],
    )
    met = exchange(passed, "gy", 0)
    ay, ghost, block, ginv, before, after = call(
        functools.partial(y_kernel, (nx, ny), ylay, xlay),
        "y_solve",
        (me_y, az, answer, met, w, inv, left, right, part),
        [
            (comps, rows, nz), (nx * 2 * TILE, nz), (xlay.rows, nz), (nx * 2 * TILE, nz),
            (2 * nx, nz), (2 * nx, nz),
        ],
        [vmem(2 * ylay.answer_rows, nz), vmem(nx * 2 * TILE, nz)],
        mebibytes=8,
    )
    x_owns, x_gots, _ = climb(xlay, "gx", x_levels, me_x, (block, block))
    (grad,) = call(
        functools.partial(x_kernel, (nx, ny), xlay, x_levels),
        "x_solve",
        (me_x, *x_owns, *x_gots, xinv, ginv, ay, ghost, w, before, after, flows),
        [(comps, rows, nz)],
        [
            vmem(comps, rows, nz), vmem(comps, rows + 2 * ny, nz), vmem(nx * 2 * TILE, nz),
            vmem(xlay.answer_rows, nz), pltpu.SemaphoreType.DMA((4,)),
        ],
        out_spaces="h",
        mebibytes=12,
    )
    return grad.reshape(comps, nx, ny, nz)


def solution(mesh):
    placed = (
        P(None, "gx", "gy", None),
        P("gx", "gy", None),
        P("gx", "gy", None),
        P(None, "gx", "gy", None),
        P(None, "gx", "gy", None),
    )
    return jax.shard_map(
        on_device, mesh=mesh, in_specs=placed, out_specs=P(None, "gx", "gy", None), check_vma=False
    )
```

```python
import functools

import jax
import jax.numpy as jnp
from jax import lax
from jax.experimental import pallas as pl
from jax.experimental.pallas import tpu as pltpu
from jax.sharding import PartitionSpec as P

COMPS = 6
LANES = 128
TILE = 8


def weight_of(diffusion, phase):
    return 1.0 / (diffusion * (1.0 + 3.0 * phase.astype(jnp.float32)))


def growing_step(value, slope, weight):
    slope = slope + weight * value
    return value + slope, slope


def split3(cells):
    high = cells.astype(jnp.bfloat16)
    rest = cells - high.astype(jnp.float32)
    middle = rest.astype(jnp.bfloat16)
    low = (rest - middle.astype(jnp.float32)).astype(jnp.bfloat16)
    return high, middle, low


def sum_matrix():
    row = lax.broadcasted_iota(jnp.int32, (2 * LANES, 2 * LANES), 0)
    col = lax.broadcasted_iota(jnp.int32, (2 * LANES, 2 * LANES), 1)
    before = (row < LANES) & (col < LANES) & (row <= col)
    after = (row >= LANES) & (col >= LANES) & (row > col)
    return jnp.where(before | after, 1.0, 0.0).astype(jnp.bfloat16)


class Layout:
    def __init__(self, pieces, groups, edges, lines):
        self.pieces, self.groups, self.edges, self.lines = pieces, groups, edges, lines
        self.couple = pieces * lines * 2
        self.packed = self.couple + 3 * lines
        self.edge = self.packed + (TILE if groups > 1 else 0)
        self.rows = self.edge + 2 * edges * lines
        self.side_couple = pieces * lines
        self.side_packed = self.side_couple + lines
        self.side_edge = self.side_packed + (TILE if groups > 1 else 0)
        self.side_rows = self.side_edge + edges * lines
        self.answer_rows = 2 * (pieces + edges) * lines

    def group(self, piece):
        return 0 if piece < COMPS else 1


def read_rows(ref, base, count, lines):
    return [ref[pl.ds(base + i * lines, lines), :] for i in range(count)]


def write_rows(ref, base, values, lines):
    for i, value in enumerate(values):
        ref[pl.ds(base + i * lines, lines), :] = value


def read_pair(ref, row):
    return jnp.concatenate(
        [jnp.broadcast_to(ref[pl.ds(row + i, 1), :], (TILE, LANES)) for i in range(2)], axis=0
    )


def write_pair(ref, row, value):
    ref[pl.ds(row, 1), :] = value[:1]
    ref[pl.ds(row + 1, 1), :] = value[TILE : TILE + 1]


def read_block(lay, ref, base=0):
    n, m = lay.lines, lay.pieces
    couple = []
    for e in range(3):
        entry = [ref[pl.ds(base + lay.couple + e * n, n), :]]
        if lay.groups > 1:
            entry.append(read_pair(ref, base + lay.packed + 2 * e))
        couple.append(entry)
    return {
        "first": read_rows(ref, base, m, n),
        "last": read_rows(ref, base + m * n, m, n),
        "near": couple[0],
        "cross": couple[1],
        "far": couple[2],
        "head": read_rows(ref, base + lay.edge, lay.edges, n),
        "tail": read_rows(ref, base + lay.edge + lay.edges * n, lay.edges, n),
    }


def write_block(lay, ref, block, base=0):
    n, m = lay.lines, lay.pieces
    write_rows(ref, base, block["first"], n)
    write_rows(ref, base + m * n, block["last"], n)
    for e, name in enumerate(("near", "cross", "far")):
        ref[pl.ds(base + lay.couple + e * n, n), :] = block[name][0]
        if lay.groups > 1:
            write_pair(ref, base + lay.packed + 2 * e, block[name][1])
    write_rows(ref, base + lay.edge, block["head"], n)
    write_rows(ref, base + lay.edge + lay.edges * n, block["tail"], n)


def write_side(lay, ref, block, upper):
    n = lay.lines

    def facing(low, high):
        return jnp.where(jnp.full(low.shape, upper, jnp.int32) == 1, high, low)

    write_rows(ref, 0, [facing(a, b) for a, b in zip(block["last"], block["first"])], n)
    pair = [facing(a, b) for a, b in zip(block["far"], block["near"])]
    ref[pl.ds(lay.side_couple, n), :] = pair[0]
    if lay.groups > 1:
        write_pair(ref, lay.side_packed, pair[1])
    write_rows(ref, lay.side_edge, [facing(a, b) for a, b in zip(block["tail"], block["head"])], n)


def read_side(lay, ref):
    n = lay.lines
    couple = [ref[pl.ds(lay.side_couple, n), :]]
    if lay.groups > 1:
        couple.append(read_pair(ref, lay.side_packed))
    return (
        read_rows(ref, 0, lay.pieces, n),
        couple,
        read_rows(ref, lay.side_edge, lay.edges, n),
    )


def pick(upper, low, high):
    if isinstance(low, list):
        return [pick(upper, a, b) for a, b in zip(low, high)]
    return jnp.where(jnp.full(low.shape, upper, jnp.int32) == 1, high, low)


def ordered(upper, own, other):
    low = {name: pick(upper, own[name], other[name]) for name in own}
    high = {name: pick(upper, other[name], own[name]) for name in own}
    return low, high


def joint(lay, low, high):
    return [
        1.0 / (1.0 - low["far"][g] * high["near"][g]) for g in range(lay.groups)
    ]


def merge(lay, low, high):
    shrink = joint(lay, low, high)
    to_low = [low["cross"][g] * shrink[g] for g in range(lay.groups)]
    to_high = [high["cross"][g] * shrink[g] for g in range(lay.groups)]
    span = range(lay.pieces)
    of = lay.group
    return {
        "first": [
            low["first"][i]
            + to_low[of(i)] * (high["first"][i] + high["near"][of(i)] * low["last"][i])
            for i in span
        ],
        "last": [
            high["last"][i]
            + to_high[of(i)] * (low["last"][i] + low["far"][of(i)] * high["first"][i])
            for i in span
        ],
        "near": [
            low["near"][g] + to_low[g] * low["cross"][g] * high["near"][g]
            for g in range(lay.groups)
        ],
        "cross": [to_low[g] * high["cross"][g] for g in range(lay.groups)],
        "far": [
            high["far"][g] + to_high[g] * high["cross"][g] * low["far"][g]
            for g in range(lay.groups)
        ],
        "head": low["head"],
        "tail": high["tail"],
    }


def inner(lay, low, high, before, after):
    shrink = joint(lay, low, high)
    low_last, high_first = [], []
    for i in range(lay.pieces):
        g = lay.group(i)
        left = low["last"][i] + low["cross"][g] * before[i]
        right = high["first"][i] + high["cross"][g] * after[i]
        low_last.append((left + low["far"][g] * right) * shrink[g])
        high_first.append((right + high["near"][g] * left) * shrink[g])
    return low_last, high_first


def merge_kernel(lay, bit, top, me_ref, own, other, *refs):
    out, *side = refs[-2:] if top else refs[-1:]
    upper = (me_ref[0] >> bit) & 1
    low, high = ordered(upper, read_block(lay, own), read_block(lay, other))
    block = merge(lay, low, high)
    write_block(lay, out, block)
    if top:
        write_side(lay, side[0], block, (me_ref[0] >> (bit + 1)) & 1)


def descend(lay, me, levels, own_refs, got_refs):
    top = levels - 1
    upper = (me >> top) & 1
    own = read_block(lay, own_refs[top])
    met, met_couple, met_edge = read_side(lay, got_refs[top])
    facing = pick(upper, own["last"], own["first"])
    couple = pick(upper, own["far"], own["near"])
    found = []
    for i in range(lay.pieces):
        g = lay.group(i)
        found.append((met[i] + met_couple[g] * facing[i]) / (1.0 - met_couple[g] * couple[g]))
    zeros = [jnp.zeros_like(v) for v in found]
    edge_zeros = [jnp.zeros_like(v) for v in met_edge]
    before, after = pick(upper, zeros, found), pick(upper, found, zeros)
    behind, ahead = pick(upper, edge_zeros, met_edge), pick(upper, met_edge, edge_zeros)
    return before, after, behind, ahead


def narrow(lay, upper, low, high, before, after, behind, ahead):
    low_last, high_first = inner(lay, low, high, before, after)
    return (
        pick(upper, before, low_last),
        pick(upper, high_first, after),
        pick(upper, behind, low["tail"]),
        pick(upper, high["head"], ahead),
    )


def write_answer(lay, ref, before, after, behind, ahead):
    write_rows(ref, 0, before + after + behind + ahead, lay.lines)


def solve_kernel(lay, levels, split, me_ref, *refs):
    me = me_ref[0]
    own_refs, got_refs = refs[:levels], refs[levels : 2 * levels]
    outs = refs[2 * levels :]
    state = descend(lay, me, levels, own_refs, got_refs)
    for level in reversed(range(levels - 1)):
        upper = (me >> level) & 1
        low, high = ordered(
            upper, read_block(lay, own_refs[level]), read_block(lay, got_refs[level])
        )
        if level == 0 and split:
            write_answer(lay, outs[1], *narrow(lay, 1 - upper, low, high, *state))
        state = narrow(lay, upper, low, high, *state)
    write_answer(lay, outs[0], *state)


def corners(weights):
    one = jnp.ones_like(weights[0])
    value, slope, chain = one, one, [one]
    for weight in weights:
        value, slope = growing_step(value, slope, weight)
        chain.append(value)
    total = 1.0 / value
    back, fall, backs = one, one, []
    for weight in reversed(weights):
        backs.append(back)
        back, fall = growing_step(back, fall, weight)
    backs.reverse()
    return chain, backs, total


def z_kernel(
    dims, lay, me_ref, cot_any, diff_any, phase_any, cour_any, upw_any, az, w_out, inv_out, keep, send,
    cot, diff, phase, cour, upw, wt, pht, pst, phi, psi, left, right, both, in_sems, sems,
):
    nx, ny = dims
    rows = nx * ny
    tiles = rows // LANES
    half = nx // 2
    small = [(diff_any, diff), (phase_any, phase), (cour_any.at[1], cour), (upw_any.at[1], upw)]
    for i, (source, target) in enumerate(small):
        pltpu.make_async_copy(source, target, sems.at[i]).start()
    for c in range(COMPS):
        pltpu.make_async_copy(cot_any.at[c], cot.at[c], in_sems.at[c]).start()

    for i, (source, target) in enumerate(small[:2]):
        pltpu.make_async_copy(source, target, sems.at[i]).wait()
    w_out[...] = weight_of(diff[...], phase[...])
    for t in range(tiles):
        span = pl.ds(t * LANES, LANES)
        wt[span, :] = w_out[span, :].T
    ones = jnp.ones((tiles, LANES), jnp.float32)
    value, slope = ones, ones
    back, fall = ones, ones
    for k in range(LANES):
        here = pl.ds(k, tiles, stride=LANES)
        pht[here, :] = value
        value, slope = growing_step(value, slope, wt[here, :])
        there = pl.ds(LANES - 1 - k, tiles, stride=LANES)
        pst[there, :] = back
        back, fall = growing_step(back, fall, wt[there, :])
    scale = 1.0 / value
    for t in range(tiles):
        span = pl.ds(t * LANES, LANES)
        phi[span, :] = pht[span, :].T
        psi[span, :] = (pst[span, :] * scale[t : t + 1]).T

    chain, backs, total = corners([w_out[pl.ds(y, nx, stride=ny), :] for y in range(ny)])
    for y in range(ny):
        span = pl.ds(y * nx, nx)
        left[span, :] = backs[y] * total
        right[span, :] = chain[y] * total
        inv_out[span, :] = chain[y] / chain[y + 1]

    def post(row, cells):
        for h in range(2):
            both[pl.ds(h * lay.rows + row, half), :] = cells[h * half : (h + 1) * half]

    post(lay.couple, left[pl.ds(0, nx), :])
    post(lay.couple + half, total)
    post(lay.couple + 2 * half, right[pl.ds((ny - 1) * nx, nx), :])
    for i, (source, target) in enumerate(small[2:]):
        pltpu.make_async_copy(source, target, sems.at[2 + i]).wait()
    for e, y in enumerate((0, ny - 1)):
        edge = pl.ds(y, nx, stride=ny)
        weight = w_out[edge, :]
        up = cour[edge, :] * upw[edge, :].astype(jnp.float32)
        flow = up if e == 0 else cour[edge, :] - up
        post(lay.edge + 2 * e * half, weight)
        post(lay.edge + (2 * e + 1) * half, weight * flow)

    sums = jnp.concatenate([sum_matrix()] * 3, axis=0)
    for c in range(COMPS):
        pltpu.make_async_copy(cot_any.at[c], cot.at[c], in_sems.at[c]).wait()
        cells, up, down = cot[c], phi[...], psi[...]
        high, middle, low = split3(jnp.concatenate([up * cells, down * cells], axis=1))
        found = jnp.dot(
            jnp.concatenate([high, middle, low], axis=1), sums, preferred_element_type=jnp.float32
        )
        az[c] = w_out[...] * (down * found[:, :LANES] + up * found[:, LANES:])
        first = jnp.zeros((nx, LANES), jnp.float32)
        last = jnp.zeros((nx, LANES), jnp.float32)
        for y in range(ny):
            cells = az[c, pl.ds(y, nx, stride=ny), :]
            span = pl.ds(y * nx, nx)
            first = first + left[span, :] * cells
            last = last + right[span, :] * cells
        post(c * half, first)
        post((COMPS + c) * half, last)
    mine = me_ref[0] & 1
    keep[...] = both[pl.ds(pl.multiple_of(mine * lay.rows, TILE), lay.rows), :]
    send[...] = both[pl.ds(pl.multiple_of((1 - mine) * lay.rows, TILE), lay.rows), :]


def sides(before, after, x):
    return jnp.concatenate(
        [
            jnp.broadcast_to(before[pl.ds(x, 1), :], (TILE, LANES)),
            jnp.broadcast_to(after[pl.ds(x, 1), :], (TILE, LANES)),
        ],
        axis=0,
    )


def coef_kernel(dims, w, courant, upwind, after, block, xinv, left, right, flows):
    del after
    nx, ny = dims
    rows = nx * ny
    one = jnp.ones((ny, LANES), jnp.float32)
    value, slope, back, fall = one, one, one, one
    for k in range(nx):
        low, high = pl.ds(k * ny, ny), pl.ds((nx - 1 - k) * ny, ny)
        right[low, :] = value
        left[high, :] = back
        new_value, slope = growing_step(value, slope, w[low, :])
        xinv[low, :] = value / new_value
        end, value = value, new_value
        corner = back
        back, fall = growing_step(back, fall, w[high, :])
    total = 1.0 / value
    block[pl.ds(0, ny), :] = corner * total
    block[pl.ds(ny, ny), :] = total
    block[pl.ds(2 * ny, ny), :] = end * total

    lane = lax.broadcasted_iota(jnp.int32, (ny, LANES), 1)

    def plane(x, carry):
        span = pl.ds(x * ny, ny)
        left[span, :] = left[span, :] * total
        right[span, :] = right[span, :] * total
        own = one
        for d in range(3):
            flow = courant[d, span, :]
            up = flow * upwind[d, span, :].astype(jnp.float32)
            down = flow - up
            own = own + (down - up)
            if d == 2:
                up = jnp.where(lane == 0, 0.0, up)
                down = jnp.where(lane == LANES - 1, 0.0, down)
            flows[pl.ds((1 + 2 * d) * rows + x * ny, ny), :] = up
            flows[pl.ds((2 + 2 * d) * rows + x * ny, ny), :] = down
        flows[span, :] = own
        return carry

    lax.fori_loop(0, nx, plane, 0, unroll=4)
    first, last = pl.ds(0, ny), pl.ds(rows - ny, ny)
    block[pl.ds(3 * ny, ny), :] = w[first, :] * flows[pl.ds(rows, ny), :]
    block[pl.ds(4 * ny, ny), :] = w[last, :] * flows[pl.ds(2 * rows + rows - ny, ny), :]


def y_kernel(
    dims, ylay, xlay, me_ref, az, own, got, w, inv, left, right, part,
    ay, ghost, block, ginv, before, after, joined, back_all,
):
    nx, ny = dims
    half = nx // 2
    deep = 2 * TILE
    mine = me_ref[0] & 1
    span = ylay.answer_rows
    joined[pl.ds(pl.multiple_of(mine * span, TILE), span), :] = own[...]
    joined[pl.ds(pl.multiple_of((1 - mine) * span, TILE), span), :] = got[...]
    for h in range(2):
        for e in range(2):
            where = pl.ds(e * nx + h * half, half)
            row = h * span + 2 * COMPS * half + e * half
            before[where, :] = joined[pl.ds(row, half), :]
            after[where, :] = joined[pl.ds(row + 2 * half, half), :]

    ghost[...] = jnp.zeros(ghost.shape, jnp.float32)
    for c in range(COMPS):
        for h in range(2):
            piece = pl.ds(h * half, half)
            fb = joined[pl.ds(h * span + c * half, half), :]
            fa = joined[pl.ds(h * span + (COMPS + c) * half, half), :]
            ghost[pl.ds(h * half * deep + c, half, stride=deep), :] = before[piece, :] * fb
            ghost[pl.ds(h * half * deep + TILE + c, half, stride=deep), :] = after[piece, :] * fa
            swept, chain = fb, []
            for y in range(ny):
                cells = az[c, pl.ds(h * half * ny + y, half, stride=ny), :]
                swept = (cells + swept) * inv[pl.ds(y * nx + h * half, half), :]
                chain.append(swept)
            later = fa
            for y in reversed(range(ny)):
                where = pl.ds(h * half * ny + y, half, stride=ny)
                later = chain[y] + inv[pl.ds(y * nx + h * half, half), :] * later
                ay[c, where, :] = later * w[where, :]

    one = jnp.ones((deep, LANES), jnp.float32)
    back, fall = one, one
    for x in reversed(range(nx)):
        back_all[pl.ds(x * deep, deep), :] = back
        corner = back
        back, fall = growing_step(back, fall, sides(before, after, x))
    total = 1.0 / back
    value, slope = one, one
    zero = jnp.zeros((ny, LANES), jnp.float32)
    firsts, lasts = [zero] * xlay.pieces, [zero] * xlay.pieces
    for x in range(nx):
        here = pl.ds(x * ny, ny)
        near, far = left[here, :], right[here, :]
        for c in range(COMPS):
            cells = ay[c, here, :]
            firsts[c] = firsts[c] + near * cells
            lasts[c] = lasts[c] + far * cells
        here = pl.ds(x * deep, deep)
        cells = ghost[here, :]
        firsts[COMPS] = firsts[COMPS] + back_all[here, :] * cells
        lasts[COMPS] = lasts[COMPS] + value * cells
        new_value, slope = growing_step(value, slope, sides(before, after, x))
        ginv[here, :] = value / new_value
        end, value = value, new_value
    firsts[COMPS] = firsts[COMPS] * total
    lasts[COMPS] = lasts[COMPS] * total
    pieces = [part[pl.ds(i * ny, ny), :] for i in range(5)]
    write_block(
        xlay,
        block,
        {
            "first": firsts,
            "last": lasts,
            "near": [pieces[0], corner * total],
            "cross": [pieces[1], total],
            "far": [pieces[2], end * total],
            "head": pieces[3:4],
            "tail": pieces[4:5],
        },
    )
    block[pl.ds(xlay.packed + 6, 2), :] = jnp.zeros((2, LANES), jnp.float32)


def x_kernel(dims, lay, levels, me_ref, *refs):
    nx, ny = dims
    own_refs, got_refs = refs[:levels], refs[levels : 2 * levels]
    (xinv, ginv, ay, ghost, w, lower, higher, flows,
     out_any, out, field, fluxes, answer, sems) = refs[2 * levels :]
    rows = nx * ny
    deep = 2 * TILE
    tiles = ny // TILE
    solve_kernel(lay, levels, False, me_ref, *own_refs, *got_refs, answer)
    n = lay.pieces
    starts = read_rows(answer, 0, n, ny)
    nexts = read_rows(answer, n * ny, n, ny)
    near = answer[pl.ds(2 * n * ny, ny), :]
    far = answer[pl.ds((2 * n + 1) * ny, ny), :]

    def sweep(x, carry):
        span, above = pl.ds(x * ny, ny), pl.ds((x + 1) * ny, ny)
        factor = xinv[span, :]
        new = []
        for c in range(COMPS):
            value = (ay[c, span, :] + carry[c]) * factor
            field[c, above, :] = value
            new.append(value)
        here = pl.ds(x * deep, deep)
        edge = (ghost[here, :] + carry[COMPS]) * ginv[here, :]
        fluxes[here, :] = edge
        return tuple(new) + (edge,)

    lax.fori_loop(0, nx, sweep, tuple(starts), unroll=8)

    def back(step, carry):
        x = nx - 1 - step
        span, above = pl.ds(x * ny, ny), pl.ds((x + 1) * ny, ny)
        factor = xinv[span, :]
        weight = w[span, :]
        new = []
        for c in range(COMPS):
            value = field[c, above, :] + factor * carry[c]
            field[c, above, :] = value * weight
            new.append(value)
        here = pl.ds(x * deep, deep)
        edge = fluxes[here, :] + ginv[here, :] * carry[COMPS]
        scale = jnp.concatenate(
            [
                jnp.broadcast_to(lower[pl.ds(nx + x, 1), :], (TILE, LANES)),
                jnp.broadcast_to(higher[pl.ds(nx + x, 1), :], (TILE, LANES)),
            ],
            axis=0,
        )
        fluxes[here, :] = edge * scale
        return tuple(new) + (edge,)

    lax.fori_loop(0, nx, back, tuple(nexts), unroll=8)
    blank = jnp.zeros((COMPS, ny, LANES), jnp.float32)
    field[:, pl.ds(0, ny), :] = blank
    field[:, pl.ds((nx + 1) * ny, ny), :] = blank

    line = lax.broadcasted_iota(jnp.int32, (TILE, LANES), 0)

    def advect(x, carry):
        before = jnp.maximum(x - 1, 0)
        beyond = jnp.minimum(x + 1, nx - 1)

        def flow(kind, plane, t):
            start = pl.multiple_of(kind * rows + plane * ny + t * TILE, TILE)
            return flows[pl.ds(start, TILE), :]

        own = [flow(0, x, t) for t in range(tiles)]
        ahead_x = [flow(1, beyond, t) for t in range(tiles)]
        behind_x = [flow(2, before, t) for t in range(tiles)]
        ahead_y = [flow(3, x, t) for t in range(tiles)]
        behind_y = [flow(4, x, t) for t in range(tiles)]
        ahead_z = [flow(5, x, t) for t in range(tiles)]
        behind_z = [flow(6, x, t) for t in range(tiles)]
        for c in range(COMPS):

            def cells(plane, t):
                start = pl.multiple_of((plane + 1) * ny + t * TILE, TILE)
                return field[c, pl.ds(start, TILE), :]

            grad = [cells(x, t) for t in range(tiles)]
            ups = [pltpu.roll(ahead_y[t] * grad[t], TILE - 1, 0) for t in range(tiles)]
            downs = [pltpu.roll(behind_y[t] * grad[t], 1, 0) for t in range(tiles)]
            lowest = fluxes[pl.ds(x * deep + c, 1), :]
            highest = fluxes[pl.ds(x * deep + TILE + c, 1), :]
            for t in range(tiles):
                part = own[t] * grad[t]
                part = part + ahead_x[t] * cells(x + 1, t) - behind_x[t] * cells(x - 1, t)
                enter = ups[t + 1] if t + 1 < tiles else jnp.broadcast_to(highest, (TILE, LANES))
                part = part + jnp.where(line == TILE - 1, enter, ups[t])
                enter = downs[t - 1] if t > 0 else jnp.broadcast_to(lowest, (TILE, LANES))
                part = part - jnp.where(line == 0, enter, downs[t])
                part = part + pltpu.roll(ahead_z[t] * grad[t], LANES - 1, 1)
                part = part - pltpu.roll(behind_z[t] * grad[t], 1, 1)
                start = pl.multiple_of(x * ny + t * TILE, TILE)
                out[c, pl.ds(start, TILE), :] = part
        return carry

    parts = 4
    share = nx // parts

    def copy(part):
        span = pl.ds(part * share * ny, share * ny)
        return pltpu.make_async_copy(out.at[:, span, :], out_any.at[:, span, :], sems.at[part])

    top, bottom = pl.ds(0, ny), pl.ds(rows - ny, ny)
    for part in range(parts):
        lax.fori_loop(part * share, (part + 1) * share, advect, 0, unroll=2)
        for c in range(COMPS):
            if part == 0:
                out[c, top, :] = out[c, top, :] - near * starts[c]
            if part == parts - 1:
                out[c, bottom, :] = out[c, bottom, :] + far * nexts[c]
        copy(part).start()
    for part in range(parts):
        copy(part).wait()


def call(kernel, name, operands, outs, scratch=(), spaces=None, out_spaces=None, mebibytes=4):
    params = pltpu.CompilerParams(vmem_limit_bytes=mebibytes * 1024 * 1024)
    pick_space = {
        "v": pl.BlockSpec(memory_space=pltpu.VMEM),
        "h": pl.BlockSpec(memory_space=pltpu.HBM),
        "s": pl.BlockSpec(memory_space=pltpu.SMEM),
        "k": pl.BlockSpec(memory_space=pltpu.VMEM),
    }
    held = {"h": pltpu.HBM, "k": pltpu.VMEM}
    spaces = spaces or "s" + "v" * (len(operands) - 1)
    out_spaces = out_spaces or "v" * len(outs)
    operands = [
        pltpu.with_memory_space_constraint(o, held[s]) if s in held else o
        for o, s in zip(operands, spaces)
    ]
    return pl.pallas_call(
        kernel,
        name=name,
        out_shape=[
            held[s](shape, jnp.float32) if s in held else jax.ShapeDtypeStruct(shape, jnp.float32)
            for shape, s in zip(outs, out_spaces)
        ],
        in_specs=[pick_space[s] for s in spaces],
        out_specs=[pick_space[s] for s in out_spaces],
        scratch_shapes=list(scratch),
        compiler_params=params,
    )(*operands)


def exchange(rows, axis, bit):
    count = lax.axis_size(axis)
    return lax.ppermute(rows, axis, [(i, i ^ (1 << bit)) for i in range(count)])


def climb(lay, axis, levels, me, own, beside=None):
    owns, gots, extra = [own], [], ()
    for level in range(levels - 1):
        gots.append(exchange(owns[-1][0], axis, level))
        top = level == levels - 2
        if beside is not None and top:
            extra = beside(owns[-1][1])
        shapes = [(lay.rows, LANES)] + ([(lay.side_rows, LANES)] if top else [])
        merged = call(
            functools.partial(merge_kernel, lay, level, top),
            axis + "_merge_" + str(level),
            (me, owns[-1][1], gots[-1]) + tuple(extra[:1]),
            shapes,
        )
        owns.append((merged[-1], merged[0]))
    gots.append(exchange(owns[-1][0], axis, levels - 1))
    return [block for _, block in owns], gots, extra


def on_device(cotangent, diffusion, phase, courant, upwind):
    comps, nx, ny, nz = cotangent.shape
    x_levels = (lax.axis_size("gx") - 1).bit_length()
    y_levels = (lax.axis_size("gy") - 1).bit_length()
    rows = nx * ny
    half = nx // 2
    ylay = Layout(comps, 1, 2, half)
    xlay = Layout(comps + 1, 2, 1, ny)
    me_x = lax.axis_index("gx").astype(jnp.int32).reshape(1)
    me_y = lax.axis_index("gy").astype(jnp.int32).reshape(1)

    def vmem(*shape, dtype=jnp.float32):
        return pltpu.VMEM(shape, dtype)

    cot = cotangent.reshape(comps, rows, nz)
    cour = courant.reshape(3, rows, nz)
    upw = upwind.reshape(3, rows, nz)
    az, w, inv, keep, send = call(
        functools.partial(z_kernel, (nx, ny), ylay),
        "z_solve",
        (me_y, cot, diffusion.reshape(rows, nz), phase.reshape(rows, nz), cour, upw),
        [(comps, rows, nz), (rows, nz), (rows, nz), (ylay.rows, nz), (ylay.rows, nz)],
        [
            vmem(comps, rows, nz), vmem(rows, nz), vmem(rows, nz, dtype=jnp.int32),
            vmem(rows, nz), vmem(rows, nz, dtype=jnp.int32),
            vmem(rows, nz), vmem(rows, nz), vmem(rows, nz), vmem(rows, nz), vmem(rows, nz),
            vmem(rows, nz), vmem(rows, nz), vmem(2 * ylay.rows, nz),
            pltpu.SemaphoreType.DMA((comps,)), pltpu.SemaphoreType.DMA((4,)),
        ],
        spaces="shhhhh",
        mebibytes=16,
    )
    def coefficients(after):
        return call(
            functools.partial(coef_kernel, (nx, ny)),
            "x_coefficients",
            (w, cour, upw, after),
            [(5 * ny, nz), (rows, nz), (rows, nz), (rows, nz), (7 * rows, nz)],
            spaces="vvvv",
            mebibytes=8,
        )

    y_owns, y_gots, found = climb(ylay, "gy", y_levels, me_y, (send, keep), coefficients)
    part, xinv, left, right, flows = found
    answer, passed = call(
        functools.partial(solve_kernel, ylay, y_levels, True),
        "y_reduced",
        (me_y, *y_owns, *y_gots),
        [(ylay.answer_rows, nz), (ylay.answer_rows, nz)],
    )
    met = exchange(passed, "gy", 0)
    ay, ghost, block, ginv, before, after = call(
        functools.partial(y_kernel, (nx, ny), ylay, xlay),
        "y_solve",
        (me_y, az, answer, met, w, inv, left, right, part),
        [
            (comps, rows, nz), (nx * 2 * TILE, nz), (xlay.rows, nz), (nx * 2 * TILE, nz),
            (2 * nx, nz), (2 * nx, nz),
        ],
        [vmem(2 * ylay.answer_rows, nz), vmem(nx * 2 * TILE, nz)],
        out_spaces="kvvvvv",
        mebibytes=8,
    )
    x_owns, x_gots, _ = climb(xlay, "gx", x_levels, me_x, (block, block))
    (grad,) = call(
        functools.partial(x_kernel, (nx, ny), xlay, x_levels),
        "x_solve",
        (me_x, *x_owns, *x_gots, xinv, ginv, ay, ghost, w, before, after, flows),
        [(comps, rows, nz)],
        [
            vmem(comps, rows, nz), vmem(comps, rows + 2 * ny, nz), vmem(nx * 2 * TILE, nz),
            vmem(xlay.answer_rows, nz), pltpu.SemaphoreType.DMA((4,)),
        ],
        spaces="s" + "v" * (2 * x_levels + 2) + "k" + "v" * 5,
        out_spaces="h",
        mebibytes=12,
    )
    return grad.reshape(comps, nx, ny, nz)


def solution(mesh):
    placed = (
        P(None, "gx", "gy", None),
        P("gx", "gy", None),
        P("gx", "gy", None),
        P(None, "gx", "gy", None),
        P(None, "gx", "gy", None),
    )
    return jax.shard_map(
        on_device, mesh=mesh, in_specs=placed, out_specs=P(None, "gx", "gy", None), check_vma=False
    )
```

```python
import functools

import jax
import jax.numpy as jnp
from jax import lax
from jax.experimental import pallas as pl
from jax.experimental.pallas import tpu as pltpu
from jax.sharding import PartitionSpec as P

COMPS = 6
LANES = 128
TILE = 8
SIDE = TILE // 2


def weight_of(diffusion, phase):
    return 1.0 / (diffusion * (1.0 + 3.0 * phase.astype(jnp.float32)))


def growing_step(value, slope, weight):
    slope = slope + weight * value
    return value + slope, slope


def split3(cells):
    high = cells.astype(jnp.bfloat16)
    rest = cells - high.astype(jnp.float32)
    middle = rest.astype(jnp.bfloat16)
    low = (rest - middle.astype(jnp.float32)).astype(jnp.bfloat16)
    return high, middle, low


def sum_matrix():
    row = lax.broadcasted_iota(jnp.int32, (2 * LANES, 2 * LANES), 0)
    col = lax.broadcasted_iota(jnp.int32, (2 * LANES, 2 * LANES), 1)
    before = (row < LANES) & (col < LANES) & (row <= col)
    after = (row >= LANES) & (col >= LANES) & (row > col)
    return jnp.where(before | after, 1.0, 0.0).astype(jnp.bfloat16)


class Layout:
    def __init__(self, sizes, groups, edges, lines, leads):
        self.sizes, self.groups, self.edges, self.lines, self.leads = sizes, groups, edges, lines, leads
        self.offsets = [sum(sizes[:i]) for i in range(len(sizes))]
        self.total = sum(sizes)
        packed = TILE if groups > 1 else 0
        self.couple = 2 * self.total
        self.packed = self.couple + 3 * lines
        self.edge = self.packed + packed
        self.side_couple = self.total
        self.side_packed = self.side_couple + lines
        self.side_edge = self.side_packed + packed
        extra = 2 * edges * lines
        self.rows = self.edge + extra if leads else self.couple
        self.side_rows = self.side_edge + extra // 2 if leads else self.total
        self.answer_rows = 2 * self.total + (extra if leads else 0)

    def group(self, piece):
        return 1 if self.groups > 1 and piece == len(self.sizes) - 1 else 0


def read_pieces(lay, ref, base=0):
    return [ref[pl.ds(base + o, n), :] for o, n in zip(lay.offsets, lay.sizes)]


def write_pieces(lay, ref, values, base=0):
    for o, n, value in zip(lay.offsets, lay.sizes, values):
        ref[pl.ds(base + o, n), :] = value


def read_rows(ref, base, count, lines):
    return [ref[pl.ds(base + i * lines, lines), :] for i in range(count)]


def write_rows(ref, base, values, lines):
    for i, value in enumerate(values):
        ref[pl.ds(base + i * lines, lines), :] = value


def two_sides(low, high):
    return jnp.concatenate(
        [jnp.broadcast_to(low, (SIDE, LANES)), jnp.broadcast_to(high, (SIDE, LANES))], axis=0
    )


def read_pair(ref, row):
    return two_sides(ref[pl.ds(row, 1), :], ref[pl.ds(row + 1, 1), :])


def write_pair(ref, row, value):
    ref[pl.ds(row, 1), :] = value[:1]
    ref[pl.ds(row + 1, 1), :] = value[SIDE : SIDE + 1]


def read_block(lay, ref, lead, lead_ref):
    n = lead.lines
    block = {"first": read_pieces(lay, ref), "last": read_pieces(lay, ref, lay.total)}
    for e, name in enumerate(("near", "cross", "far")):
        entry = [lead_ref[pl.ds(lead.couple + e * n, n), :]]
        if lead.groups > 1:
            entry.append(read_pair(lead_ref, lead.packed + 2 * e))
        block[name] = entry
    block["head"] = read_rows(lead_ref, lead.edge, lead.edges, n)
    block["tail"] = read_rows(lead_ref, lead.edge + lead.edges * n, lead.edges, n)
    return block


def write_block(lay, ref, block):
    n = lay.lines
    write_pieces(lay, ref, block["first"])
    write_pieces(lay, ref, block["last"], lay.total)
    if not lay.leads:
        return
    for e, name in enumerate(("near", "cross", "far")):
        ref[pl.ds(lay.couple + e * n, n), :] = block[name][0]
        if lay.groups > 1:
            write_pair(ref, lay.packed + 2 * e, block[name][1])
    if lay.groups > 1:
        ref[pl.ds(lay.packed + 6, 2), :] = jnp.zeros((2, LANES), jnp.float32)
    write_rows(ref, lay.edge, block["head"], n)
    write_rows(ref, lay.edge + lay.edges * n, block["tail"], n)


def pick(upper, low, high):
    if isinstance(low, list):
        return [pick(upper, a, b) for a, b in zip(low, high)]
    return jnp.where(jnp.full(low.shape, upper, jnp.int32) == 1, high, low)


def write_side(lay, ref, block, upper):
    n = lay.lines
    write_pieces(lay, ref, pick(upper, block["last"], block["first"]))
    if not lay.leads:
        return
    pair = pick(upper, block["far"], block["near"])
    ref[pl.ds(lay.side_couple, n), :] = pair[0]
    if lay.groups > 1:
        ref[pl.ds(lay.side_packed, TILE), :] = pair[1]
    write_rows(ref, lay.side_edge, pick(upper, block["tail"], block["head"]), n)


def read_side(lay, ref, lead, lead_ref):
    n = lead.lines
    couple = [lead_ref[pl.ds(lead.side_couple, n), :]]
    if lead.groups > 1:
        couple.append(lead_ref[pl.ds(lead.side_packed, TILE), :])
    return read_pieces(lay, ref), couple, read_rows(lead_ref, lead.side_edge, lead.edges, n)


def ordered(upper, own, other):
    low = {name: pick(upper, own[name], other[name]) for name in own}
    high = {name: pick(upper, other[name], own[name]) for name in own}
    return low, high


def joint(low, high):
    return [1.0 / (1.0 - far * near) for far, near in zip(low["far"], high["near"])]


def merge(lay, low, high):
    shrink = joint(low, high)
    groups = range(len(shrink))
    to_low = [low["cross"][g] * shrink[g] for g in groups]
    to_high = [high["cross"][g] * shrink[g] for g in groups]
    span = range(len(lay.sizes))
    of = lay.group
    block = {
        "first": [
            low["first"][i]
            + to_low[of(i)] * (high["first"][i] + high["near"][of(i)] * low["last"][i])
            for i in span
        ],
        "last": [
            high["last"][i]
            + to_high[of(i)] * (low["last"][i] + low["far"][of(i)] * high["first"][i])
            for i in span
        ],
    }
    block["near"] = [low["near"][g] + to_low[g] * low["cross"][g] * high["near"][g] for g in groups]
    block["cross"] = [to_low[g] * high["cross"][g] for g in groups]
    block["far"] = [high["far"][g] + to_high[g] * high["cross"][g] * low["far"][g] for g in groups]
    block["head"] = low["head"]
    block["tail"] = high["tail"]
    return block


def inner(lay, low, high, before, after):
    shrink = joint(low, high)
    low_last, high_first = [], []
    for i in range(len(lay.sizes)):
        g = lay.group(i)
        left = low["last"][i] + low["cross"][g] * before[i]
        right = high["first"][i] + high["cross"][g] * after[i]
        low_last.append((left + low["far"][g] * right) * shrink[g])
        high_first.append((right + high["near"][g] * left) * shrink[g])
    return low_last, high_first


def merge_kernel(lay, lead, bit, top, me_ref, own, other, *refs):
    out, *side = refs[-2:] if top else refs[-1:]
    lead_own, lead_other = (own, other) if lay.leads else refs[:2]
    upper = (me_ref[0] >> bit) & 1
    low, high = ordered(
        upper, read_block(lay, own, lead, lead_own), read_block(lay, other, lead, lead_other)
    )
    block = merge(lay, low, high)
    write_block(lay, out, block)
    if top:
        write_side(lay, side[0], block, (me_ref[0] >> (bit + 1)) & 1)


def solve_lines(lay, lead, levels, me, refs):
    owns, gots = refs[:levels], refs[levels : 2 * levels]
    lead_owns, lead_gots = owns, gots
    if not lay.leads:
        lead_owns, lead_gots = refs[2 * levels : 3 * levels], refs[3 * levels : 4 * levels]
    top = levels - 1
    upper = (me >> top) & 1
    own = read_block(lay, owns[top], lead, lead_owns[top])
    met, met_couple, met_edge = read_side(lay, gots[top], lead, lead_gots[top])
    facing = pick(upper, own["last"], own["first"])
    couple = pick(upper, own["far"], own["near"])
    shrink = [1.0 / (1.0 - a * b) for a, b in zip(met_couple, couple)]
    found = []
    for i in range(len(lay.sizes)):
        g = lay.group(i)
        found.append((met[i] + met_couple[g] * facing[i]) * shrink[g])
    zeros = [jnp.zeros_like(v) for v in found]
    blank = [jnp.zeros_like(v) for v in met_edge]
    state = (
        pick(upper, zeros, found), pick(upper, found, zeros),
        pick(upper, blank, met_edge), pick(upper, met_edge, blank),
    )
    partner = None
    for level in reversed(range(top)):
        upper = (me >> level) & 1
        low, high = ordered(
            upper,
            read_block(lay, owns[level], lead, lead_owns[level]),
            read_block(lay, gots[level], lead, lead_gots[level]),
        )
        before, after, behind, ahead = state
        low_last, high_first = inner(lay, low, high, before, after)
        lower = (before, high_first, behind, high["head"])
        higher = (low_last, after, low["tail"], ahead)
        state = tuple(pick(upper, a, b) for a, b in zip(lower, higher))
        partner = tuple(pick(upper, a, b) for a, b in zip(higher, lower))
    return state, partner


def write_answer(lay, ref, state):
    before, after, behind, ahead = state
    write_pieces(lay, ref, before)
    write_pieces(lay, ref, after, lay.total)
    if lay.leads:
        write_rows(ref, 2 * lay.total, behind + ahead, lay.lines)


def solve_kernel(lay, lead, levels, me_ref, *refs):
    state, partner = solve_lines(lay, lead, levels, me_ref[0], refs[:-2])
    write_answer(lay, refs[-2], state)
    write_answer(lay, refs[-1], partner)


def corners(weights):
    one = jnp.ones_like(weights[0])
    value, slope, chain = one, one, [one]
    for weight in weights:
        value, slope = growing_step(value, slope, weight)
        chain.append(value)
    back, fall, backs = one, one, []
    for weight in reversed(weights):
        backs.append(back)
        back, fall = growing_step(back, fall, weight)
    backs.reverse()
    return chain, backs, 1.0 / value


def post(lay, both, row, cells):
    half = cells.shape[0] // 2
    for h in range(2):
        both[pl.ds(h * lay.rows + row, half), :] = cells[h * half : (h + 1) * half]


def z_part(dims, lay, me_ref, cot, phi, psi, w, left, right, arrived, az, both, keep, send):
    nx, ny = dims
    tiles = nx * ny // LANES
    sums = sum_matrix()
    for c in range(len(lay.sizes)):
        arrived(c)
        for t in range(tiles):
            span = pl.ds(t * LANES, LANES)
            cells, up, down = cot[c, span, :], phi[span, :], psi[span, :]
            wide = jnp.concatenate([up * cells, down * cells], axis=1)
            found = sum(
                jnp.dot(part, sums, preferred_element_type=jnp.float32) for part in split3(wide)
            )
            az[c, span, :] = w[span, :] * (down * found[:, :LANES] + up * found[:, LANES:])
        first = jnp.zeros((nx, LANES), jnp.float32)
        last = jnp.zeros((nx, LANES), jnp.float32)
        for y in range(ny):
            cells = az[c, pl.ds(y, nx, stride=ny), :]
            span = pl.ds(y * nx, nx)
            first = first + left[span, :] * cells
            last = last + right[span, :] * cells
        post(lay, both, lay.offsets[c], first)
        post(lay, both, lay.total + lay.offsets[c], last)
    mine = me_ref[0] & 1
    keep[...] = both[pl.ds(pl.multiple_of(mine * lay.rows, TILE), lay.rows), :]
    send[...] = both[pl.ds(pl.multiple_of((1 - mine) * lay.rows, TILE), lay.rows), :]


def lead_z_kernel(
    dims, lay, me_ref, cot_any, diff_any, phase_any, cour_any, upw_any,
    keep, send, az, w, inv, left, right, phi, psi,
    cot, diff, phase, cour, upw, wt, pht, pst, both, in_sems, sems,
):
    nx, ny = dims
    tiles = nx * ny // LANES
    half = nx // 2
    small = [(diff_any, diff), (phase_any, phase), (cour_any.at[1], cour), (upw_any.at[1], upw)]
    for i, (source, target) in enumerate(small):
        pltpu.make_async_copy(source, target, sems.at[i]).start()
    for c in range(len(lay.sizes)):
        pltpu.make_async_copy(cot_any.at[c], cot.at[c], in_sems.at[c]).start()

    for i, (source, target) in enumerate(small[:2]):
        pltpu.make_async_copy(source, target, sems.at[i]).wait()
    w[...] = weight_of(diff[...], phase[...])
    for t in range(tiles):
        span = pl.ds(t * LANES, LANES)
        wt[span, :] = w[span, :].T
    ones = jnp.ones((tiles, LANES), jnp.float32)
    value, slope = ones, ones
    back, fall = ones, ones
    for k in range(LANES):
        here = pl.ds(k, tiles, stride=LANES)
        pht[here, :] = value
        value, slope = growing_step(value, slope, wt[here, :])
        there = pl.ds(LANES - 1 - k, tiles, stride=LANES)
        pst[there, :] = back
        back, fall = growing_step(back, fall, wt[there, :])
    scale = 1.0 / value
    for t in range(tiles):
        span = pl.ds(t * LANES, LANES)
        phi[span, :] = pht[span, :].T
        psi[span, :] = (pst[span, :] * scale[t : t + 1]).T

    chain, backs, total = corners([w[pl.ds(y, nx, stride=ny), :] for y in range(ny)])
    for y in range(ny):
        span = pl.ds(y * nx, nx)
        left[span, :] = backs[y] * total
        right[span, :] = chain[y] * total
        inv[span, :] = chain[y] / chain[y + 1]
    post(lay, both, lay.couple, backs[0] * total)
    post(lay, both, lay.couple + half, total)
    post(lay, both, lay.couple + 2 * half, chain[ny - 1] * total)
    for i, (source, target) in enumerate(small[2:]):
        pltpu.make_async_copy(source, target, sems.at[2 + i]).wait()
    for e, y in enumerate((0, ny - 1)):
        edge = pl.ds(y, nx, stride=ny)
        weight = w[edge, :]
        up = cour[edge, :] * upw[edge, :].astype(jnp.float32)
        flow = up if e == 0 else cour[edge, :] - up
        post(lay, both, lay.edge + 2 * e * half, weight)
        post(lay, both, lay.edge + (2 * e + 1) * half, weight * flow)

    def arrived(c):
        pltpu.make_async_copy(cot_any.at[c], cot.at[c], in_sems.at[c]).wait()

    z_part(dims, lay, me_ref, cot, phi, psi, w, left, right, arrived, az, both, keep, send)


def next_z_kernel(
    dims, lay, start, me_ref, cot_any, phi, psi, w, left, right, keep, send, az, cot, both, in_sems,
):
    def copy(c):
        return pltpu.make_async_copy(cot_any.at[start + c], cot.at[c], in_sems.at[c])

    for c in range(len(lay.sizes)):
        copy(c).start()
    z_part(
        dims, lay, me_ref, cot, phi, psi, w, left, right, lambda c: copy(c).wait(), az, both, keep, send
    )


def coef_kernel(dims, w, courant, upwind, after, block, xinv, left, right, flows):
    del after
    nx, ny = dims
    rows = nx * ny
    one = jnp.ones((ny, LANES), jnp.float32)
    value, slope, back, fall = one, one, one, one
    for k in range(nx):
        low, high = pl.ds(k * ny, ny), pl.ds((nx - 1 - k) * ny, ny)
        right[low, :] = value
        left[high, :] = back
        new_value, slope = growing_step(value, slope, w[low, :])
        xinv[low, :] = value / new_value
        end, value = value, new_value
        corner = back
        back, fall = growing_step(back, fall, w[high, :])
    total = 1.0 / value
    block[pl.ds(0, ny), :] = corner * total
    block[pl.ds(ny, ny), :] = total
    block[pl.ds(2 * ny, ny), :] = end * total

    lane = lax.broadcasted_iota(jnp.int32, (ny, LANES), 1)

    def plane(x, carry):
        span = pl.ds(x * ny, ny)
        left[span, :] = left[span, :] * total
        right[span, :] = right[span, :] * total
        own = one
        for d in range(3):
            flow = courant[d, span, :]
            up = flow * upwind[d, span, :].astype(jnp.float32)
            down = flow - up
            own = own + (down - up)
            if d == 2:
                up = jnp.where(lane == 0, 0.0, up)
                down = jnp.where(lane == LANES - 1, 0.0, down)
            flows[pl.ds((1 + 2 * d) * rows + x * ny, ny), :] = up
            flows[pl.ds((2 + 2 * d) * rows + x * ny, ny), :] = down
        flows[span, :] = own
        return carry

    lax.fori_loop(0, nx, plane, 0, unroll=4)
    first, last = pl.ds(0, ny), pl.ds(rows - ny, ny)
    block[pl.ds(3 * ny, ny), :] = w[first, :] * flows[pl.ds(rows, ny), :]
    block[pl.ds(4 * ny, ny), :] = w[last, :] * flows[pl.ds(2 * rows + rows - ny, ny), :]


def sides(before, after, x):
    return two_sides(before[pl.ds(x, 1), :], after[pl.ds(x, 1), :])


def y_kernel(dims, ylay, xlay, me_ref, az, own, got, w, inv, left, right, *refs):
    nx, ny = dims
    half = nx // 2
    comps = len(ylay.sizes)
    if xlay.leads:
        part, _, block, ay, ghost, ginv, gleft, gright, before, after, joined = refs
    else:
        before, after, gleft, gright, block, ay, ghost, joined = refs
    mine = me_ref[0] & 1
    span = ylay.answer_rows
    joined[pl.ds(pl.multiple_of(mine * span, TILE), span), :] = own[...]
    joined[pl.ds(pl.multiple_of((1 - mine) * span, TILE), span), :] = got[...]
    if xlay.leads:
        for h in range(2):
            for e in range(2):
                where = pl.ds(e * nx + h * half, half)
                row = h * span + 2 * ylay.total + e * half
                before[where, :] = joined[pl.ds(row, half), :]
                after[where, :] = joined[pl.ds(row + 2 * half, half), :]
        one = jnp.ones((TILE, LANES), jnp.float32)
        value, slope, back, fall = one, one, one, one
        for k in range(nx):
            low, high = pl.ds(k * TILE, TILE), pl.ds((nx - 1 - k) * TILE, TILE)
            gright[low, :] = value
            gleft[high, :] = back
            new_value, slope = growing_step(value, slope, sides(before, after, k))
            ginv[low, :] = value / new_value
            end, value = value, new_value
            corner = back
            back, fall = growing_step(back, fall, sides(before, after, nx - 1 - k))
        total = 1.0 / value
        gleft[...] = (gleft[...].reshape(nx, TILE, LANES) * total).reshape(nx * TILE, LANES)
        gright[...] = (gright[...].reshape(nx, TILE, LANES) * total).reshape(nx * TILE, LANES)

    ghost[...] = jnp.zeros(ghost.shape, jnp.float32)
    for c in range(comps):
        for h in range(2):
            piece = pl.ds(h * half, half)
            fb = joined[pl.ds(h * span + c * half, half), :]
            fa = joined[pl.ds(h * span + ylay.total + c * half, half), :]
            ghost[pl.ds(h * half * TILE + c, half, stride=TILE), :] = before[piece, :] * fb
            ghost[pl.ds(h * half * TILE + SIDE + c, half, stride=TILE), :] = after[piece, :] * fa
            swept, chain = fb, []
            for y in range(ny):
                cells = az[c, pl.ds(h * half * ny + y, half, stride=ny), :]
                swept = (cells + swept) * inv[pl.ds(y * nx + h * half, half), :]
                chain.append(swept)
            later = fa
            for y in reversed(range(ny)):
                where = pl.ds(h * half * ny + y, half, stride=ny)
                later = chain[y] + inv[pl.ds(y * nx + h * half, half), :] * later
                ay[c, where, :] = later * w[where, :]

    firsts = [jnp.zeros((n, LANES), jnp.float32) for n in xlay.sizes]
    lasts = list(firsts)
    for x in range(nx):
        here = pl.ds(x * ny, ny)
        near, far = left[here, :], right[here, :]
        for c in range(comps):
            cells = ay[c, here, :]
            firsts[c] = firsts[c] + near * cells
            lasts[c] = lasts[c] + far * cells
        here = pl.ds(x * TILE, TILE)
        cells = ghost[here, :]
        firsts[comps] = firsts[comps] + gleft[here, :] * cells
        lasts[comps] = lasts[comps] + gright[here, :] * cells
    record = {"first": firsts, "last": lasts}
    if xlay.leads:
        pieces = [part[pl.ds(i * ny, ny), :] for i in range(5)]
        record["near"] = [pieces[0], corner * total]
        record["cross"] = [pieces[1], total]
        record["far"] = [pieces[2], end * total]
        record["head"], record["tail"] = pieces[3:4], pieces[4:5]
    write_block(xlay, block, record)


def x_kernel(dims, lay, lead, levels, shift, start, me_ref, *refs):
    nx, ny = dims
    count = (2 if lay.leads else 4) * levels
    state, _ = solve_lines(lay, lead, levels, me_ref[0] >> shift, refs[:count])
    xinv, ginv, ay, ghost, w, lower, higher, flows, *rest = refs[count:]
    out_any, out, field, fluxes, sems = rest[-5:]
    rows = nx * ny
    comps = len(lay.sizes) - 1
    tiles = ny // TILE
    starts, nexts, behind, ahead = state
    near, far = behind[0], ahead[0]

    def sweep(x, carry):
        span, above = pl.ds(x * ny, ny), pl.ds((x + 1) * ny, ny)
        factor = xinv[span, :]
        new = []
        for c in range(comps):
            value = (ay[c, span, :] + carry[c]) * factor
            field[c, above, :] = value
            new.append(value)
        here = pl.ds(x * TILE, TILE)
        edge = (ghost[here, :] + carry[comps]) * ginv[here, :]
        fluxes[here, :] = edge
        return tuple(new) + (edge,)

    lax.fori_loop(0, nx, sweep, tuple(starts), unroll=8)

    def back(step, carry):
        x = nx - 1 - step
        span, above = pl.ds(x * ny, ny), pl.ds((x + 1) * ny, ny)
        factor = xinv[span, :]
        weight = w[span, :]
        new = []
        for c in range(comps):
            value = field[c, above, :] + factor * carry[c]
            field[c, above, :] = value * weight
            new.append(value)
        here = pl.ds(x * TILE, TILE)
        edge = fluxes[here, :] + ginv[here, :] * carry[comps]
        fluxes[here, :] = edge * two_sides(lower[pl.ds(nx + x, 1), :], higher[pl.ds(nx + x, 1), :])
        return tuple(new) + (edge,)

    lax.fori_loop(0, nx, back, tuple(nexts), unroll=8)
    blank = jnp.zeros((comps, ny, LANES), jnp.float32)
    field[:, pl.ds(0, ny), :] = blank
    field[:, pl.ds((nx + 1) * ny, ny), :] = blank

    line = lax.broadcasted_iota(jnp.int32, (TILE, LANES), 0)

    def advect(x, carry):
        before = jnp.maximum(x - 1, 0)
        beyond = jnp.minimum(x + 1, nx - 1)

        def flow(kind, plane, t):
            begin = pl.multiple_of(kind * rows + plane * ny + t * TILE, TILE)
            return flows[pl.ds(begin, TILE), :]

        own = [flow(0, x, t) for t in range(tiles)]
        ahead_x = [flow(1, beyond, t) for t in range(tiles)]
        behind_x = [flow(2, before, t) for t in range(tiles)]
        ahead_y = [flow(3, x, t) for t in range(tiles)]
        behind_y = [flow(4, x, t) for t in range(tiles)]
        ahead_z = [flow(5, x, t) for t in range(tiles)]
        behind_z = [flow(6, x, t) for t in range(tiles)]
        for c in range(comps):

            def cells(plane, t):
                begin = pl.multiple_of((plane + 1) * ny + t * TILE, TILE)
                return field[c, pl.ds(begin, TILE), :]

            grad = [cells(x, t) for t in range(tiles)]
            ups = [pltpu.roll(ahead_y[t] * grad[t], TILE - 1, 0) for t in range(tiles)]
            downs = [pltpu.roll(behind_y[t] * grad[t], 1, 0) for t in range(tiles)]
            lowest = fluxes[pl.ds(x * TILE + c, 1), :]
            highest = fluxes[pl.ds(x * TILE + SIDE + c, 1), :]
            for t in range(tiles):
                part = own[t] * grad[t]
                part = part + ahead_x[t] * cells(x + 1, t) - behind_x[t] * cells(x - 1, t)
                enter = ups[t + 1] if t + 1 < tiles else jnp.broadcast_to(highest, (TILE, LANES))
                part = part + jnp.where(line == TILE - 1, enter, ups[t])
                enter = downs[t - 1] if t > 0 else jnp.broadcast_to(lowest, (TILE, LANES))
                part = part - jnp.where(line == 0, enter, downs[t])
                part = part + pltpu.roll(ahead_z[t] * grad[t], LANES - 1, 1)
                part = part - pltpu.roll(behind_z[t] * grad[t], 1, 1)
                out[c, pl.ds(pl.multiple_of(x * ny + t * TILE, TILE), TILE), :] = part
        return carry

    parts = 4
    share = nx // parts

    def copy(part):
        span = pl.ds(part * share * ny, share * ny)
        target = out_any.at[pl.ds(start, comps), span, :]
        return pltpu.make_async_copy(out.at[:, span, :], target, sems.at[part])

    top, bottom = pl.ds(0, ny), pl.ds(rows - ny, ny)
    for part in range(parts):
        lax.fori_loop(part * share, (part + 1) * share, advect, 0, unroll=2)
        for c in range(comps):
            if part == 0:
                out[c, top, :] = out[c, top, :] - near * starts[c]
            if part == parts - 1:
                out[c, bottom, :] = out[c, bottom, :] + far * nexts[c]
        copy(part).start()
    for part in range(parts):
        copy(part).wait()


def call(
    kernel, name, operands, outs, scratch=(), spaces=None, out_spaces=None, mebibytes=4, aliases=None
):
    params = pltpu.CompilerParams(vmem_limit_bytes=mebibytes * 1024 * 1024)
    memory = {"v": pltpu.VMEM, "k": pltpu.VMEM, "h": pltpu.HBM, "s": pltpu.SMEM}
    held = {"h": pltpu.HBM, "k": pltpu.VMEM}
    spaces = spaces or "s" + "v" * (len(operands) - 1)
    out_spaces = out_spaces or "v" * len(outs)
    operands = [
        pltpu.with_memory_space_constraint(o, held[s]) if s in held else o
        for o, s in zip(operands, spaces)
    ]
    return pl.pallas_call(
        kernel,
        name=name,
        out_shape=[
            held[s](shape, jnp.float32) if s in held else jax.ShapeDtypeStruct(shape, jnp.float32)
            for shape, s in zip(outs, out_spaces)
        ],
        in_specs=[pl.BlockSpec(memory_space=memory[s]) for s in spaces],
        out_specs=[pl.BlockSpec(memory_space=memory[s]) for s in out_spaces],
        scratch_shapes=list(scratch),
        input_output_aliases=aliases or {},
        compiler_params=params,
    )(*operands)


def exchange(rows, axis, bit):
    count = lax.axis_size(axis)
    return lax.ppermute(rows, axis, [(i, i ^ (1 << bit)) for i in range(count)])


class Ladder:
    def __init__(self, lay, axis, shift, me, send, keep, lead=None):
        self.lay, self.axis, self.shift, self.me, self.lead = lay, axis, shift, me, lead
        self.levels = (lax.axis_size(axis) - 1).bit_length()
        self.owns, self.gots, self.outgoing = [keep], [], send

    def send(self):
        self.gots.append(exchange(self.outgoing, self.axis, len(self.gots)))

    def merge(self, beside=()):
        level = len(self.owns) - 1
        top = level == self.levels - 2
        leader = self.lead or self
        coupled = () if self.lay.leads else (leader.owns[level], leader.gots[level])
        shapes = [(self.lay.rows, LANES)] + ([(self.lay.side_rows, LANES)] if top else [])
        merged = call(
            functools.partial(merge_kernel, self.lay, leader.lay, self.shift + level, top),
            "merge_" + self.axis,
            (self.me, self.owns[-1], self.gots[-1]) + coupled + tuple(beside),
            shapes,
        )
        self.owns.append(merged[0])
        self.outgoing = merged[-1]

    def records(self):
        found = (*self.owns, *self.gots)
        return found if self.lay.leads else found + (*self.lead.owns, *self.lead.gots)


def on_device(cotangent, diffusion, phase, courant, upwind):
    comps, nx, ny, nz = cotangent.shape
    shift = (lax.axis_size("gy") - 1).bit_length()
    rows = nx * ny
    half = nx // 2
    size = comps // 2
    starts = (0, size)
    counts = (size, comps - size)
    ylays = [Layout([half] * n, 1, 2, half, g == 0) for g, n in enumerate(counts)]
    xlays = [Layout([ny] * n + [TILE], 2, 1, ny, g == 0) for g, n in enumerate(counts)]
    me = lax.axis_index(("gx", "gy")).astype(jnp.int32).reshape(1)

    def vmem(*shape, dtype=jnp.float32):
        return pltpu.VMEM(shape, dtype)

    flat = (rows, nz)
    cot = cotangent.reshape(comps, rows, nz)
    cour = courant.reshape(3, rows, nz)
    upw = upwind.reshape(3, rows, nz)
    n = counts[0]
    keep, send, az, w, inv, left, right, phi, psi = call(
        functools.partial(lead_z_kernel, (nx, ny), ylays[0]),
        "z_solve_lead",
        (me, cot, diffusion.reshape(flat), phase.reshape(flat), cour, upw),
        [(ylays[0].rows, nz)] * 2 + [(n, rows, nz)] + [flat] * 6,
        [
            vmem(n, rows, nz), vmem(*flat), vmem(*flat, dtype=jnp.int32),
            vmem(*flat), vmem(*flat, dtype=jnp.int32),
            vmem(*flat), vmem(*flat), vmem(*flat), vmem(2 * ylays[0].rows, nz),
            pltpu.SemaphoreType.DMA((n,)), pltpu.SemaphoreType.DMA((4,)),
        ],
        spaces="shhhhh",
        mebibytes=12,
    )
    lead = Ladder(ylays[0], "gy", 0, me, send, keep)
    lead.send()
    azs = [az]
    n = counts[1]
    keep, send, az = call(
        functools.partial(next_z_kernel, (nx, ny), ylays[1], starts[1]),
        "z_solve_next",
        (me, cot, phi, psi, w, left, right),
        [(ylays[1].rows, nz)] * 2 + [(n, rows, nz)],
        [
            vmem(n, rows, nz), vmem(2 * ylays[1].rows, nz), pltpu.SemaphoreType.DMA((n,)),
        ],
        spaces="shvvvvv",
        mebibytes=8,
    )
    azs.append(az)
    follow = Ladder(ylays[1], "gy", 0, me, send, keep, lead)
    follow.send()
    beside = (send,)
    for level in range(lead.levels - 1):
        lead.merge(beside)
        lead.send()
        follow.merge()
        follow.send()
        beside = (follow.outgoing,)
        if level == 0:
            part, xinv, xleft, xright, flows = call(
                functools.partial(coef_kernel, (nx, ny)),
                "x_coefficients",
                (w, cour, upw, lead.owns[1]),
                [(5 * ny, nz), flat, flat, flat, (7 * rows, nz)],
                spaces="vvvv",
                mebibytes=8,
            )
            beside = (part, follow.outgoing)
    ladders, mets, answers = (lead, follow), [], []
    for g, ladder in enumerate(ladders):
        answer, passed = call(
            functools.partial(solve_kernel, ylays[g], ylays[0], ladder.levels),
            "y_reduced",
            (me,) + ladder.records() + (beside if g == 0 else ()),
            [(ylays[g].answer_rows, nz)] * 2,
        )
        answers.append(answer)
        mets.append(exchange(passed, "gy", 0))
    ays, ghosts, climbs = [], [], []
    for g in range(2):
        common = (me, azs[g], answers[g], mets[g], w, inv, xleft, xright)
        outs = [(xlays[g].rows, nz), (counts[g], rows, nz), (nx * TILE, nz)]
        scratch = [vmem(2 * ylays[g].answer_rows, nz)]
        body = functools.partial(y_kernel, (nx, ny), ylays[g], xlays[g])
        if g == 0:
            block, ay, ghost, ginv, gleft, gright, before, after = call(
                body,
                "y_solve_lead",
                common + (part, answers[1]),
                outs + [(nx * TILE, nz)] * 3 + [(2 * nx, nz)] * 2,
                scratch,
                mebibytes=6,
            )
        else:
            block, ay, ghost = call(
                body,
                "y_solve_next",
                common + (before, after, gleft, gright),
                outs,
                scratch,
                mebibytes=6,
            )
        ays.append(ay)
        ghosts.append(ghost)
        climbs.append(Ladder(xlays[g], "gx", shift, me, block, block, climbs[0] if g else None))
        climbs[g].send()
    beside = (block,)
    for level in range(climbs[0].levels - 1):
        for ladder in climbs:
            ladder.merge(beside if ladder.lay.leads else ())
            ladder.send()
        beside = (climbs[1].outgoing,)
    grad = None
    for g, ladder in enumerate(climbs):
        operands = (me,) + ladder.records() + (
            xinv, ginv, ays[g], ghosts[g], w, before, after, flows,
        )
        spaces = "s" + "v" * (len(operands) - 1)
        aliases = None
        if g:
            aliases = {len(operands): 0}
            operands, spaces = operands + (grad,), spaces + "h"
        (grad,) = call(
            functools.partial(
                x_kernel, (nx, ny), xlays[g], xlays[0], ladder.levels, shift, starts[g]
            ),
            "x_solve",
            operands,
            [(comps, rows, nz)],
            [
                vmem(counts[g], rows, nz), vmem(counts[g], rows + 2 * ny, nz), vmem(nx * TILE, nz),
                pltpu.SemaphoreType.DMA((4,)),
            ],
            spaces=spaces,
            out_spaces="h",
            mebibytes=8,
            aliases=aliases,
        )
    return grad.reshape(comps, nx, ny, nz)


def solution(mesh):
    placed = (
        P(None, "gx", "gy", None),
        P("gx", "gy", None),
        P("gx", "gy", None),
        P(None, "gx", "gy", None),
        P(None, "gx", "gy", None),
    )
    return jax.shard_map(
        on_device, mesh=mesh, in_specs=placed, out_specs=P(None, "gx", "gy", None), check_vma=False
    )
```

```python
import functools

import jax
import jax.numpy as jnp
from jax import lax
from jax.experimental import pallas as pl
from jax.experimental.pallas import tpu as pltpu
from jax.sharding import PartitionSpec as P

COMPS = 6
LANES = 128
TILE = 8
SIDE = TILE // 2


def weight_of(diffusion, phase):
    return 1.0 / (diffusion * (1.0 + 3.0 * phase.astype(jnp.float32)))


def growing_step(value, slope, weight):
    slope = slope + weight * value
    return value + slope, slope


def split3(cells):
    high = cells.astype(jnp.bfloat16)
    rest = cells - high.astype(jnp.float32)
    middle = rest.astype(jnp.bfloat16)
    low = (rest - middle.astype(jnp.float32)).astype(jnp.bfloat16)
    return high, middle, low


def sum_matrix():
    row = lax.broadcasted_iota(jnp.int32, (2 * LANES, 2 * LANES), 0)
    col = lax.broadcasted_iota(jnp.int32, (2 * LANES, 2 * LANES), 1)
    before = (row < LANES) & (col < LANES) & (row <= col)
    after = (row >= LANES) & (col >= LANES) & (row > col)
    return jnp.where(before | after, 1.0, 0.0).astype(jnp.bfloat16)


class Layout:
    def __init__(self, sizes, groups, edges, lines, leads):
        self.sizes, self.groups, self.edges, self.lines, self.leads = sizes, groups, edges, lines, leads
        self.offsets = [sum(sizes[:i]) for i in range(len(sizes))]
        self.total = sum(sizes)
        packed = TILE if groups > 1 else 0
        self.couple = 2 * self.total
        self.packed = self.couple + 3 * lines
        self.edge = self.packed + packed
        self.side_couple = self.total
        self.side_packed = self.side_couple + lines
        self.side_edge = self.side_packed + packed
        extra = 2 * edges * lines
        self.rows = self.edge + extra if leads else self.couple
        self.side_rows = self.side_edge + extra // 2 if leads else self.total
        self.answer_rows = 2 * self.total + (extra if leads else 0)

    def group(self, piece):
        return 1 if self.groups > 1 and piece == len(self.sizes) - 1 else 0


def read_pieces(lay, ref, base=0):
    return [ref[pl.ds(base + o, n), :] for o, n in zip(lay.offsets, lay.sizes)]


def write_pieces(lay, ref, values, base=0):
    for o, n, value in zip(lay.offsets, lay.sizes, values):
        ref[pl.ds(base + o, n), :] = value


def read_rows(ref, base, count, lines):
    return [ref[pl.ds(base + i * lines, lines), :] for i in range(count)]


def write_rows(ref, base, values, lines):
    for i, value in enumerate(values):
        ref[pl.ds(base + i * lines, lines), :] = value


def two_sides(low, high):
    return jnp.concatenate(
        [jnp.broadcast_to(low, (SIDE, LANES)), jnp.broadcast_to(high, (SIDE, LANES))], axis=0
    )


def read_pair(ref, row):
    return two_sides(ref[pl.ds(row, 1), :], ref[pl.ds(row + 1, 1), :])


def write_pair(ref, row, value):
    ref[pl.ds(row, 1), :] = value[:1]
    ref[pl.ds(row + 1, 1), :] = value[SIDE : SIDE + 1]


def read_block(lay, ref, lead, lead_ref):
    n = lead.lines
    block = {"first": read_pieces(lay, ref), "last": read_pieces(lay, ref, lay.total)}
    for e, name in enumerate(("near", "cross", "far")):
        entry = [lead_ref[pl.ds(lead.couple + e * n, n), :]]
        if lead.groups > 1:
            entry.append(read_pair(lead_ref, lead.packed + 2 * e))
        block[name] = entry
    block["head"] = read_rows(lead_ref, lead.edge, lead.edges, n)
    block["tail"] = read_rows(lead_ref, lead.edge + lead.edges * n, lead.edges, n)
    return block


def write_block(lay, ref, block):
    n = lay.lines
    write_pieces(lay, ref, block["first"])
    write_pieces(lay, ref, block["last"], lay.total)
    if not lay.leads:
        return
    for e, name in enumerate(("near", "cross", "far")):
        ref[pl.ds(lay.couple + e * n, n), :] = block[name][0]
        if lay.groups > 1:
            write_pair(ref, lay.packed + 2 * e, block[name][1])
    if lay.groups > 1:
        ref[pl.ds(lay.packed + 6, 2), :] = jnp.zeros((2, LANES), jnp.float32)
    write_rows(ref, lay.edge, block["head"], n)
    write_rows(ref, lay.edge + lay.edges * n, block["tail"], n)


def pick(upper, low, high):
    if isinstance(low, list):
        return [pick(upper, a, b) for a, b in zip(low, high)]
    return jnp.where(jnp.full(low.shape, upper, jnp.int32) == 1, high, low)


def write_side(lay, ref, block, upper):
    n = lay.lines
    write_pieces(lay, ref, pick(upper, block["last"], block["first"]))
    if not lay.leads:
        return
    pair = pick(upper, block["far"], block["near"])
    ref[pl.ds(lay.side_couple, n), :] = pair[0]
    if lay.groups > 1:
        ref[pl.ds(lay.side_packed, TILE), :] = pair[1]
    write_rows(ref, lay.side_edge, pick(upper, block["tail"], block["head"]), n)


def read_side(lay, ref, lead, lead_ref):
    n = lead.lines
    couple = [lead_ref[pl.ds(lead.side_couple, n), :]]
    if lead.groups > 1:
        couple.append(lead_ref[pl.ds(lead.side_packed, TILE), :])
    return read_pieces(lay, ref), couple, read_rows(lead_ref, lead.side_edge, lead.edges, n)


def ordered(upper, own, other):
    low = {name: pick(upper, own[name], other[name]) for name in own}
    high = {name: pick(upper, other[name], own[name]) for name in own}
    return low, high


def joint(low, high):
    return [1.0 / (1.0 - far * near) for far, near in zip(low["far"], high["near"])]


def merge(lay, low, high):
    shrink = joint(low, high)
    groups = range(len(shrink))
    to_low = [low["cross"][g] * shrink[g] for g in groups]
    to_high = [high["cross"][g] * shrink[g] for g in groups]
    span = range(len(lay.sizes))
    of = lay.group
    block = {
        "first": [
            low["first"][i]
            + to_low[of(i)] * (high["first"][i] + high["near"][of(i)] * low["last"][i])
            for i in span
        ],
        "last": [
            high["last"][i]
            + to_high[of(i)] * (low["last"][i] + low["far"][of(i)] * high["first"][i])
            for i in span
        ],
    }
    block["near"] = [low["near"][g] + to_low[g] * low["cross"][g] * high["near"][g] for g in groups]
    block["cross"] = [to_low[g] * high["cross"][g] for g in groups]
    block["far"] = [high["far"][g] + to_high[g] * high["cross"][g] * low["far"][g] for g in groups]
    block["head"] = low["head"]
    block["tail"] = high["tail"]
    return block


def inner(lay, low, high, before, after):
    shrink = joint(low, high)
    low_last, high_first = [], []
    for i in range(len(lay.sizes)):
        g = lay.group(i)
        left = low["last"][i] + low["cross"][g] * before[i]
        right = high["first"][i] + high["cross"][g] * after[i]
        low_last.append((left + low["far"][g] * right) * shrink[g])
        high_first.append((right + high["near"][g] * left) * shrink[g])
    return low_last, high_first


def merge_kernel(lay, lead, bit, top, me_ref, own, other, *refs):
    out, *side = refs[-2:] if top else refs[-1:]
    lead_own, lead_other = (own, other) if lay.leads else refs[:2]
    upper = (me_ref[0] >> bit) & 1
    low, high = ordered(
        upper, read_block(lay, own, lead, lead_own), read_block(lay, other, lead, lead_other)
    )
    block = merge(lay, low, high)
    write_block(lay, out, block)
    if top:
        write_side(lay, side[0], block, (me_ref[0] >> (bit + 1)) & 1)


def solve_lines(lay, lead, levels, me, refs):
    owns, gots = refs[:levels], refs[levels : 2 * levels]
    lead_owns, lead_gots = owns, gots
    if not lay.leads:
        lead_owns, lead_gots = refs[2 * levels : 3 * levels], refs[3 * levels : 4 * levels]
    top = levels - 1
    upper = (me >> top) & 1
    own = read_block(lay, owns[top], lead, lead_owns[top])
    met, met_couple, met_edge = read_side(lay, gots[top], lead, lead_gots[top])
    facing = pick(upper, own["last"], own["first"])
    couple = pick(upper, own["far"], own["near"])
    shrink = [1.0 / (1.0 - a * b) for a, b in zip(met_couple, couple)]
    found = []
    for i in range(len(lay.sizes)):
        g = lay.group(i)
        found.append((met[i] + met_couple[g] * facing[i]) * shrink[g])
    zeros = [jnp.zeros_like(v) for v in found]
    blank = [jnp.zeros_like(v) for v in met_edge]
    state = (
        pick(upper, zeros, found), pick(upper, found, zeros),
        pick(upper, blank, met_edge), pick(upper, met_edge, blank),
    )
    partner = None
    for level in reversed(range(top)):
        upper = (me >> level) & 1
        low, high = ordered(
            upper,
            read_block(lay, owns[level], lead, lead_owns[level]),
            read_block(lay, gots[level], lead, lead_gots[level]),
        )
        before, after, behind, ahead = state
        low_last, high_first = inner(lay, low, high, before, after)
        lower = (before, high_first, behind, high["head"])
        higher = (low_last, after, low["tail"], ahead)
        state = tuple(pick(upper, a, b) for a, b in zip(lower, higher))
        partner = tuple(pick(upper, a, b) for a, b in zip(higher, lower))
    return state, partner


def write_answer(lay, ref, state):
    before, after, behind, ahead = state
    write_pieces(lay, ref, before)
    write_pieces(lay, ref, after, lay.total)
    if lay.leads:
        write_rows(ref, 2 * lay.total, behind + ahead, lay.lines)


def solve_kernel(lay, lead, levels, me_ref, *refs):
    state, partner = solve_lines(lay, lead, levels, me_ref[0], refs[:-2])
    write_answer(lay, refs[-2], state)
    write_answer(lay, refs[-1], partner)


def corners(weights):
    one = jnp.ones_like(weights[0])
    value, slope, chain = one, one, [one]
    for weight in weights:
        value, slope = growing_step(value, slope, weight)
        chain.append(value)
    back, fall, backs = one, one, []
    for weight in reversed(weights):
        backs.append(back)
        back, fall = growing_step(back, fall, weight)
    backs.reverse()
    return chain, backs, 1.0 / value


def post(lay, both, row, cells):
    half = cells.shape[0] // 2
    for h in range(2):
        both[pl.ds(h * lay.rows + row, half), :] = cells[h * half : (h + 1) * half]


def z_part(dims, lay, me_ref, cot, phi, psi, w, left, right, arrived, az, both, keep, send):
    nx, ny = dims
    tiles = nx * ny // LANES
    sums = sum_matrix()
    for c in range(len(lay.sizes)):
        arrived(c)
        for t in range(tiles):
            span = pl.ds(t * LANES, LANES)
            cells, up, down = cot[c, span, :], phi[span, :], psi[span, :]
            wide = jnp.concatenate([up * cells, down * cells], axis=1)
            found = jnp.dot(
                jnp.concatenate(split3(wide), axis=0), sums, preferred_element_type=jnp.float32
            )
            found = found[:LANES] + (found[LANES : 2 * LANES] + found[2 * LANES :])
            az[c, span, :] = w[span, :] * (down * found[:, :LANES] + up * found[:, LANES:])
        first = jnp.zeros((nx, LANES), jnp.float32)
        last = jnp.zeros((nx, LANES), jnp.float32)
        for y in range(ny):
            cells = az[c, pl.ds(y, nx, stride=ny), :]
            span = pl.ds(y * nx, nx)
            first = first + left[span, :] * cells
            last = last + right[span, :] * cells
        post(lay, both, lay.offsets[c], first)
        post(lay, both, lay.total + lay.offsets[c], last)
    mine = me_ref[0] & 1
    keep[...] = both[pl.ds(pl.multiple_of(mine * lay.rows, TILE), lay.rows), :]
    send[...] = both[pl.ds(pl.multiple_of((1 - mine) * lay.rows, TILE), lay.rows), :]


def lead_z_kernel(
    dims, lay, me_ref, cot_any, diff_any, phase_any, cour_any, upw_any,
    keep, send, az, w, inv, left, right, phi, psi,
    cot, diff, phase, cour, upw, wt, pht, pst, both, in_sems, sems,
):
    nx, ny = dims
    tiles = nx * ny // LANES
    half = nx // 2
    small = [(diff_any, diff), (phase_any, phase), (cour_any.at[1], cour), (upw_any.at[1], upw)]
    for i, (source, target) in enumerate(small):
        pltpu.make_async_copy(source, target, sems.at[i]).start()
    for c in range(len(lay.sizes)):
        pltpu.make_async_copy(cot_any.at[c], cot.at[c], in_sems.at[c]).start()

    for i, (source, target) in enumerate(small[:2]):
        pltpu.make_async_copy(source, target, sems.at[i]).wait()
    w[...] = weight_of(diff[...], phase[...])
    for t in range(tiles):
        span = pl.ds(t * LANES, LANES)
        wt[span, :] = w[span, :].T
    ones = jnp.ones((tiles, LANES), jnp.float32)
    value, slope = ones, ones
    back, fall = ones, ones
    for k in range(LANES):
        here = pl.ds(k, tiles, stride=LANES)
        pht[here, :] = value
        value, slope = growing_step(value, slope, wt[here, :])
        there = pl.ds(LANES - 1 - k, tiles, stride=LANES)
        pst[there, :] = back
        back, fall = growing_step(back, fall, wt[there, :])
    scale = 1.0 / value
    for t in range(tiles):
        span = pl.ds(t * LANES, LANES)
        phi[span, :] = pht[span, :].T
        psi[span, :] = (pst[span, :] * scale[t : t + 1]).T

    chain, backs, total = corners([w[pl.ds(y, nx, stride=ny), :] for y in range(ny)])
    for y in range(ny):
        span = pl.ds(y * nx, nx)
        left[span, :] = backs[y] * total
        right[span, :] = chain[y] * total
        inv[span, :] = chain[y] / chain[y + 1]
    post(lay, both, lay.couple, backs[0] * total)
    post(lay, both, lay.couple + half, total)
    post(lay, both, lay.couple + 2 * half, chain[ny - 1] * total)
    for i, (source, target) in enumerate(small[2:]):
        pltpu.make_async_copy(source, target, sems.at[2 + i]).wait()
    for e, y in enumerate((0, ny - 1)):
        edge = pl.ds(y, nx, stride=ny)
        weight = w[edge, :]
        up = cour[edge, :] * upw[edge, :].astype(jnp.float32)
        flow = up if e == 0 else cour[edge, :] - up
        post(lay, both, lay.edge + 2 * e * half, weight)
        post(lay, both, lay.edge + (2 * e + 1) * half, weight * flow)

    def arrived(c):
        pltpu.make_async_copy(cot_any.at[c], cot.at[c], in_sems.at[c]).wait()

    z_part(dims, lay, me_ref, cot, phi, psi, w, left, right, arrived, az, both, keep, send)


def next_z_kernel(
    dims, lay, start, me_ref, cot_any, phi, psi, w, left, right, keep, send, az, cot, both, in_sems,
):
    def copy(c):
        return pltpu.make_async_copy(cot_any.at[start + c], cot.at[c], in_sems.at[c])

    for c in range(len(lay.sizes)):
        copy(c).start()
    z_part(
        dims, lay, me_ref, cot, phi, psi, w, left, right, lambda c: copy(c).wait(), az, both, keep, send
    )


def coef_kernel(dims, w, courant, upwind, after, block, xinv, left, right, flows):
    del after
    nx, ny = dims
    rows = nx * ny
    one = jnp.ones((ny, LANES), jnp.float32)
    value, slope, back, fall = one, one, one, one
    for k in range(nx):
        low, high = pl.ds(k * ny, ny), pl.ds((nx - 1 - k) * ny, ny)
        right[low, :] = value
        left[high, :] = back
        new_value, slope = growing_step(value, slope, w[low, :])
        xinv[low, :] = value / new_value
        end, value = value, new_value
        corner = back
        back, fall = growing_step(back, fall, w[high, :])
    total = 1.0 / value
    block[pl.ds(0, ny), :] = corner * total
    block[pl.ds(ny, ny), :] = total
    block[pl.ds(2 * ny, ny), :] = end * total

    lane = lax.broadcasted_iota(jnp.int32, (ny, LANES), 1)

    def plane(x, carry):
        span = pl.ds(x * ny, ny)
        left[span, :] = left[span, :] * total
        right[span, :] = right[span, :] * total
        own = one
        for d in range(3):
            flow = courant[d, span, :]
            up = flow * upwind[d, span, :].astype(jnp.float32)
            down = flow - up
            own = own + (down - up)
            if d == 2:
                up = jnp.where(lane == 0, 0.0, up)
                down = jnp.where(lane == LANES - 1, 0.0, down)
            flows[pl.ds((1 + 2 * d) * rows + x * ny, ny), :] = up
            flows[pl.ds((2 + 2 * d) * rows + x * ny, ny), :] = down
        flows[span, :] = own
        return carry

    lax.fori_loop(0, nx, plane, 0, unroll=4)
    first, last = pl.ds(0, ny), pl.ds(rows - ny, ny)
    block[pl.ds(3 * ny, ny), :] = w[first, :] * flows[pl.ds(rows, ny), :]
    block[pl.ds(4 * ny, ny), :] = w[last, :] * flows[pl.ds(2 * rows + rows - ny, ny), :]


def sides(before, after, x):
    return two_sides(before[pl.ds(x, 1), :], after[pl.ds(x, 1), :])


def y_kernel(dims, ylay, xlay, me_ref, az, own, got, w, inv, left, right, *refs):
    nx, ny = dims
    half = nx // 2
    comps = len(ylay.sizes)
    if xlay.leads:
        part, block, ay, ghost, ginv, gleft, gright, before, after, joined = refs
    else:
        before, after, gleft, gright, block, ay, ghost, joined = refs
    mine = me_ref[0] & 1
    span = ylay.answer_rows
    joined[pl.ds(pl.multiple_of(mine * span, TILE), span), :] = own[...]
    joined[pl.ds(pl.multiple_of((1 - mine) * span, TILE), span), :] = got[...]
    if xlay.leads:
        for h in range(2):
            for e in range(2):
                where = pl.ds(e * nx + h * half, half)
                row = h * span + 2 * ylay.total + e * half
                before[where, :] = joined[pl.ds(row, half), :]
                after[where, :] = joined[pl.ds(row + 2 * half, half), :]
        one = jnp.ones((TILE, LANES), jnp.float32)
        value, slope, back, fall = one, one, one, one
        for k in range(nx):
            low, high = pl.ds(k * TILE, TILE), pl.ds((nx - 1 - k) * TILE, TILE)
            gright[low, :] = value
            gleft[high, :] = back
            new_value, slope = growing_step(value, slope, sides(before, after, k))
            ginv[low, :] = value / new_value
            end, value = value, new_value
            corner = back
            back, fall = growing_step(back, fall, sides(before, after, nx - 1 - k))
        total = 1.0 / value
        gleft[...] = (gleft[...].reshape(nx, TILE, LANES) * total).reshape(nx * TILE, LANES)
        gright[...] = (gright[...].reshape(nx, TILE, LANES) * total).reshape(nx * TILE, LANES)

    ghost[...] = jnp.zeros(ghost.shape, jnp.float32)
    for c in range(comps):
        for h in range(2):
            piece = pl.ds(h * half, half)
            fb = joined[pl.ds(h * span + c * half, half), :]
            fa = joined[pl.ds(h * span + ylay.total + c * half, half), :]
            ghost[pl.ds(h * half * TILE + c, half, stride=TILE), :] = before[piece, :] * fb
            ghost[pl.ds(h * half * TILE + SIDE + c, half, stride=TILE), :] = after[piece, :] * fa
            swept, chain = fb, []
            for y in range(ny):
                cells = az[c, pl.ds(h * half * ny + y, half, stride=ny), :]
                swept = (cells + swept) * inv[pl.ds(y * nx + h * half, half), :]
                chain.append(swept)
            later = fa
            for y in reversed(range(ny)):
                where = pl.ds(h * half * ny + y, half, stride=ny)
                later = chain[y] + inv[pl.ds(y * nx + h * half, half), :] * later
                ay[c, where, :] = later * w[where, :]

    firsts = [jnp.zeros((n, LANES), jnp.float32) for n in xlay.sizes]
    lasts = list(firsts)
    for x in range(nx):
        here = pl.ds(x * ny, ny)
        near, far = left[here, :], right[here, :]
        for c in range(comps):
            cells = ay[c, here, :]
            firsts[c] = firsts[c] + near * cells
            lasts[c] = lasts[c] + far * cells
        here = pl.ds(x * TILE, TILE)
        cells = ghost[here, :]
        firsts[comps] = firsts[comps] + gleft[here, :] * cells
        lasts[comps] = lasts[comps] + gright[here, :] * cells
    record = {"first": firsts, "last": lasts}
    if xlay.leads:
        pieces = [part[pl.ds(i * ny, ny), :] for i in range(5)]
        record["near"] = [pieces[0], corner * total]
        record["cross"] = [pieces[1], total]
        record["far"] = [pieces[2], end * total]
        record["head"], record["tail"] = pieces[3:4], pieces[4:5]
    write_block(xlay, block, record)


def x_kernel(dims, lay, lead, levels, shift, start, me_ref, *refs):
    nx, ny = dims
    count = (2 if lay.leads else 4) * levels
    state, _ = solve_lines(lay, lead, levels, me_ref[0] >> shift, refs[:count])
    xinv, ginv, ay, ghost, w, lower, higher, flows, *rest = refs[count:]
    out_any, out, field, fluxes, sems = rest[-5:]
    rows = nx * ny
    comps = len(lay.sizes) - 1
    tiles = ny // TILE
    starts, nexts, behind, ahead = state
    near, far = behind[0], ahead[0]

    def sweep(x, carry):
        span, above = pl.ds(x * ny, ny), pl.ds((x + 1) * ny, ny)
        factor = xinv[span, :]
        new = []
        for c in range(comps):
            value = (ay[c, span, :] + carry[c]) * factor
            field[c, above, :] = value
            new.append(value)
        here = pl.ds(x * TILE, TILE)
        edge = (ghost[here, :] + carry[comps]) * ginv[here, :]
        fluxes[here, :] = edge
        return tuple(new) + (edge,)

    lax.fori_loop(0, nx, sweep, tuple(starts), unroll=8)

    def back(step, carry):
        x = nx - 1 - step
        span, above = pl.ds(x * ny, ny), pl.ds((x + 1) * ny, ny)
        factor = xinv[span, :]
        weight = w[span, :]
        new = []
        for c in range(comps):
            value = field[c, above, :] + factor * carry[c]
            field[c, above, :] = value * weight
            new.append(value)
        here = pl.ds(x * TILE, TILE)
        edge = fluxes[here, :] + ginv[here, :] * carry[comps]
        fluxes[here, :] = edge * two_sides(lower[pl.ds(nx + x, 1), :], higher[pl.ds(nx + x, 1), :])
        return tuple(new) + (edge,)

    lax.fori_loop(0, nx, back, tuple(nexts), unroll=8)
    blank = jnp.zeros((comps, ny, LANES), jnp.float32)
    field[:, pl.ds(0, ny), :] = blank
    field[:, pl.ds((nx + 1) * ny, ny), :] = blank

    line = lax.broadcasted_iota(jnp.int32, (TILE, LANES), 0)

    def advect(x, carry):
        before = jnp.maximum(x - 1, 0)
        beyond = jnp.minimum(x + 1, nx - 1)

        def flow(kind, plane, t):
            begin = pl.multiple_of(kind * rows + plane * ny + t * TILE, TILE)
            return flows[pl.ds(begin, TILE), :]

        own = [flow(0, x, t) for t in range(tiles)]
        ahead_x = [flow(1, beyond, t) for t in range(tiles)]
        behind_x = [flow(2, before, t) for t in range(tiles)]
        ahead_y = [flow(3, x, t) for t in range(tiles)]
        behind_y = [flow(4, x, t) for t in range(tiles)]
        ahead_z = [flow(5, x, t) for t in range(tiles)]
        behind_z = [flow(6, x, t) for t in range(tiles)]
        for c in range(comps):

            def cells(plane, t):
                begin = pl.multiple_of((plane + 1) * ny + t * TILE, TILE)
                return field[c, pl.ds(begin, TILE), :]

            grad = [cells(x, t) for t in range(tiles)]
            ups = [pltpu.roll(ahead_y[t] * grad[t], TILE - 1, 0) for t in range(tiles)]
            downs = [pltpu.roll(behind_y[t] * grad[t], 1, 0) for t in range(tiles)]
            lowest = fluxes[pl.ds(x * TILE + c, 1), :]
            highest = fluxes[pl.ds(x * TILE + SIDE + c, 1), :]
            for t in range(tiles):
                part = own[t] * grad[t]
                part = part + ahead_x[t] * cells(x + 1, t) - behind_x[t] * cells(x - 1, t)
                enter = ups[t + 1] if t + 1 < tiles else jnp.broadcast_to(highest, (TILE, LANES))
                part = part + jnp.where(line == TILE - 1, enter, ups[t])
                enter = downs[t - 1] if t > 0 else jnp.broadcast_to(lowest, (TILE, LANES))
                part = part - jnp.where(line == 0, enter, downs[t])
                part = part + pltpu.roll(ahead_z[t] * grad[t], LANES - 1, 1)
                part = part - pltpu.roll(behind_z[t] * grad[t], 1, 1)
                out[c, pl.ds(pl.multiple_of(x * ny + t * TILE, TILE), TILE), :] = part
        return carry

    parts = 4
    share = nx // parts

    def copy(part):
        span = pl.ds(part * share * ny, share * ny)
        target = out_any.at[pl.ds(start, comps), span, :]
        return pltpu.make_async_copy(out.at[:, span, :], target, sems.at[part])

    top, bottom = pl.ds(0, ny), pl.ds(rows - ny, ny)
    for part in range(parts):
        lax.fori_loop(part * share, (part + 1) * share, advect, 0, unroll=share)
        for c in range(comps):
            if part == 0:
                out[c, top, :] = out[c, top, :] - near * starts[c]
            if part == parts - 1:
                out[c, bottom, :] = out[c, bottom, :] + far * nexts[c]
        copy(part).start()
    for part in range(parts):
        copy(part).wait()


def call(
    kernel, name, operands, outs, scratch=(), spaces=None, out_spaces=None, mebibytes=4, aliases=None
):
    params = pltpu.CompilerParams(vmem_limit_bytes=mebibytes * 1024 * 1024)
    memory = {"v": pltpu.VMEM, "k": pltpu.VMEM, "h": pltpu.HBM, "s": pltpu.SMEM}
    held = {"h": pltpu.HBM, "k": pltpu.VMEM}
    spaces = spaces or "s" + "v" * (len(operands) - 1)
    out_spaces = out_spaces or "v" * len(outs)
    operands = [
        pltpu.with_memory_space_constraint(o, held[s]) if s in held else o
        for o, s in zip(operands, spaces)
    ]
    return pl.pallas_call(
        kernel,
        name=name,
        out_shape=[
            held[s](shape, jnp.float32) if s in held else jax.ShapeDtypeStruct(shape, jnp.float32)
            for shape, s in zip(outs, out_spaces)
        ],
        in_specs=[pl.BlockSpec(memory_space=memory[s]) for s in spaces],
        out_specs=[pl.BlockSpec(memory_space=memory[s]) for s in out_spaces],
        scratch_shapes=list(scratch),
        input_output_aliases=aliases or {},
        compiler_params=params,
    )(*operands)


def exchange(rows, axis, bit):
    count = lax.axis_size(axis)
    return lax.ppermute(rows, axis, [(i, i ^ (1 << bit)) for i in range(count)])


class Ladder:
    def __init__(self, lay, axis, shift, me, send, keep, lead=None):
        self.lay, self.axis, self.shift, self.me, self.lead = lay, axis, shift, me, lead
        self.levels = (lax.axis_size(axis) - 1).bit_length()
        self.owns, self.gots, self.outgoing = [keep], [], send

    def send(self):
        self.gots.append(exchange(self.outgoing, self.axis, len(self.gots)))

    def merge(self, beside=()):
        level = len(self.owns) - 1
        top = level == self.levels - 2
        leader = self.lead or self
        coupled = () if self.lay.leads else (leader.owns[level], leader.gots[level])
        shapes = [(self.lay.rows, LANES)] + ([(self.lay.side_rows, LANES)] if top else [])
        merged = call(
            functools.partial(merge_kernel, self.lay, leader.lay, self.shift + level, top),
            "merge_" + self.axis,
            (self.me, self.owns[-1], self.gots[-1]) + coupled + tuple(beside),
            shapes,
        )
        self.owns.append(merged[0])
        self.outgoing = merged[-1]

    def records(self):
        found = (*self.owns, *self.gots)
        return found if self.lay.leads else found + (*self.lead.owns, *self.lead.gots)


def on_device(cotangent, diffusion, phase, courant, upwind):
    comps, nx, ny, nz = cotangent.shape
    shift = (lax.axis_size("gy") - 1).bit_length()
    rows = nx * ny
    half = nx // 2
    size = comps // 2
    starts = (0, size)
    counts = (size, comps - size)
    ylays = [Layout([half] * n, 1, 2, half, g == 0) for g, n in enumerate(counts)]
    xlays = [Layout([ny] * n + [TILE], 2, 1, ny, g == 0) for g, n in enumerate(counts)]
    me = lax.axis_index(("gx", "gy")).astype(jnp.int32).reshape(1)

    def vmem(*shape, dtype=jnp.float32):
        return pltpu.VMEM(shape, dtype)

    flat = (rows, nz)
    cot = cotangent.reshape(comps, rows, nz)
    cour = courant.reshape(3, rows, nz)
    upw = upwind.reshape(3, rows, nz)
    n = counts[0]
    keep, send, az, w, inv, left, right, phi, psi = call(
        functools.partial(lead_z_kernel, (nx, ny), ylays[0]),
        "z_solve_lead",
        (me, cot, diffusion.reshape(flat), phase.reshape(flat), cour, upw),
        [(ylays[0].rows, nz)] * 2 + [(n, rows, nz)] + [flat] * 6,
        [
            vmem(n, rows, nz), vmem(*flat), vmem(*flat, dtype=jnp.int32),
            vmem(*flat), vmem(*flat, dtype=jnp.int32),
            vmem(*flat), vmem(*flat), vmem(*flat), vmem(2 * ylays[0].rows, nz),
            pltpu.SemaphoreType.DMA((n,)), pltpu.SemaphoreType.DMA((4,)),
        ],
        spaces="shhhhh",
        mebibytes=12,
    )
    lead = Ladder(ylays[0], "gy", 0, me, send, keep)
    lead.send()
    azs = [az]
    n = counts[1]
    keep, send, az = call(
        functools.partial(next_z_kernel, (nx, ny), ylays[1], starts[1]),
        "z_solve_next",
        (me, cot, phi, psi, w, left, right),
        [(ylays[1].rows, nz)] * 2 + [(n, rows, nz)],
        [
            vmem(n, rows, nz), vmem(2 * ylays[1].rows, nz), pltpu.SemaphoreType.DMA((n,)),
        ],
        spaces="shvvvvv",
        mebibytes=8,
    )
    azs.append(az)
    follow = Ladder(ylays[1], "gy", 0, me, send, keep, lead)
    follow.send()
    beside = (send,)
    for level in range(lead.levels - 1):
        lead.merge(beside)
        lead.send()
        follow.merge()
        follow.send()
        beside = (follow.outgoing,)
        if level == 0:
            part, xinv, xleft, xright, flows = call(
                functools.partial(coef_kernel, (nx, ny)),
                "x_coefficients",
                (w, cour, upw, lead.owns[1]),
                [(5 * ny, nz), flat, flat, flat, (7 * rows, nz)],
                spaces="vvvv",
                mebibytes=8,
            )
            beside = (part, follow.outgoing)
    ladders, mets, answers = (lead, follow), [], []
    for g, ladder in enumerate(ladders):
        answer, passed = call(
            functools.partial(solve_kernel, ylays[g], ylays[0], ladder.levels),
            "y_reduced",
            (me,) + ladder.records() + (beside if g == 0 else ()),
            [(ylays[g].answer_rows, nz)] * 2,
        )
        answers.append(answer)
        mets.append(exchange(passed, "gy", 0))
    ays, ghosts, climbs = [], [], []
    for g in range(2):
        common = (me, azs[g], answers[g], mets[g], w, inv, xleft, xright)
        outs = [(xlays[g].rows, nz), (counts[g], rows, nz), (nx * TILE, nz)]
        scratch = [vmem(2 * ylays[g].answer_rows, nz)]
        body = functools.partial(y_kernel, (nx, ny), ylays[g], xlays[g])
        if g == 0:
            block, ay, ghost, ginv, gleft, gright, before, after = call(
                body,
                "y_solve_lead",
                common + (part,),
                outs + [(nx * TILE, nz)] * 3 + [(2 * nx, nz)] * 2,
                scratch,
                mebibytes=6,
            )
        else:
            block, ay, ghost = call(
                body,
                "y_solve_next",
                common + (before, after, gleft, gright),
                outs,
                scratch,
                mebibytes=6,
            )
        ays.append(ay)
        ghosts.append(ghost)
        climbs.append(Ladder(xlays[g], "gx", shift, me, block, block, climbs[0] if g else None))
        climbs[g].send()
    beside = (block,)
    for level in range(climbs[0].levels - 1):
        for ladder in climbs:
            ladder.merge(beside if ladder.lay.leads else ())
            ladder.send()
        beside = (climbs[1].outgoing,)
    grad = None
    for g, ladder in enumerate(climbs):
        operands = (me,) + ladder.records() + (
            xinv, ginv, ays[g], ghosts[g], w, before, after, flows,
        )
        spaces = "s" + "v" * (len(operands) - 1)
        aliases = None
        if g:
            aliases = {len(operands): 0}
            operands, spaces = operands + (grad,), spaces + "h"
        (grad,) = call(
            functools.partial(
                x_kernel, (nx, ny), xlays[g], xlays[0], ladder.levels, shift, starts[g]
            ),
            "x_solve",
            operands,
            [(comps, rows, nz)],
            [
                vmem(counts[g], rows, nz), vmem(counts[g], rows + 2 * ny, nz), vmem(nx * TILE, nz),
                pltpu.SemaphoreType.DMA((4,)),
            ],
            spaces=spaces,
            out_spaces="h",
            mebibytes=8,
            aliases=aliases,
        )
    return grad.reshape(comps, nx, ny, nz)


def solution(mesh):
    placed = (
        P(None, "gx", "gy", None),
        P("gx", "gy", None),
        P("gx", "gy", None),
        P(None, "gx", "gy", None),
        P(None, "gx", "gy", None),
    )
    return jax.shard_map(
        on_device, mesh=mesh, in_specs=placed, out_specs=P(None, "gx", "gy", None), check_vma=False
    )
```

```python
import functools

import jax
import jax.numpy as jnp
from jax import lax
from jax.experimental import pallas as pl
from jax.experimental.pallas import tpu as pltpu
from jax.sharding import PartitionSpec as P

COMPS = 6
LANES = 128
TILE = 8
SIDE = TILE // 2


def weight_of(diffusion, phase):
    return 1.0 / (diffusion * (1.0 + 3.0 * phase.astype(jnp.float32)))


def growing_step(value, slope, weight):
    slope = slope + weight * value
    return value + slope, slope


def split3(cells):
    high = cells.astype(jnp.bfloat16)
    rest = cells - high.astype(jnp.float32)
    middle = rest.astype(jnp.bfloat16)
    low = (rest - middle.astype(jnp.float32)).astype(jnp.bfloat16)
    return high, middle, low


def sum_matrix():
    row = lax.broadcasted_iota(jnp.int32, (2 * LANES, 2 * LANES), 0)
    col = lax.broadcasted_iota(jnp.int32, (2 * LANES, 2 * LANES), 1)
    before = (row < LANES) & (col < LANES) & (row <= col)
    after = (row >= LANES) & (col >= LANES) & (row > col)
    return jnp.where(before | after, 1.0, 0.0).astype(jnp.bfloat16)


class Layout:
    def __init__(self, sizes, groups, edges, lines, leads):
        self.sizes, self.groups, self.edges, self.lines, self.leads = sizes, groups, edges, lines, leads
        self.offsets = [sum(sizes[:i]) for i in range(len(sizes))]
        self.total = sum(sizes)
        packed = TILE if groups > 1 else 0
        self.couple = 2 * self.total
        self.packed = self.couple + 3 * lines
        self.edge = self.packed + packed
        self.side_couple = self.total
        self.side_packed = self.side_couple + lines
        self.side_edge = self.side_packed + packed
        extra = 2 * edges * lines
        self.rows = self.edge + extra if leads else self.couple
        self.side_rows = self.side_edge + extra // 2 if leads else self.total
        self.answer_rows = 2 * self.total + (extra if leads else 0)

    def group(self, piece):
        return 1 if self.groups > 1 and piece == len(self.sizes) - 1 else 0


def read_pieces(lay, ref, base=0):
    return [ref[pl.ds(base + o, n), :] for o, n in zip(lay.offsets, lay.sizes)]


def write_pieces(lay, ref, values, base=0):
    for o, n, value in zip(lay.offsets, lay.sizes, values):
        ref[pl.ds(base + o, n), :] = value


def read_rows(ref, base, count, lines):
    return [ref[pl.ds(base + i * lines, lines), :] for i in range(count)]


def write_rows(ref, base, values, lines):
    for i, value in enumerate(values):
        ref[pl.ds(base + i * lines, lines), :] = value


def two_sides(low, high):
    return jnp.concatenate(
        [jnp.broadcast_to(low, (SIDE, LANES)), jnp.broadcast_to(high, (SIDE, LANES))], axis=0
    )


def read_pair(ref, row):
    return two_sides(ref[pl.ds(row, 1), :], ref[pl.ds(row + 1, 1), :])


def write_pair(ref, row, value):
    ref[pl.ds(row, 1), :] = value[:1]
    ref[pl.ds(row + 1, 1), :] = value[SIDE : SIDE + 1]


def read_block(lay, ref, lead, lead_ref):
    n = lead.lines
    block = {"first": read_pieces(lay, ref), "last": read_pieces(lay, ref, lay.total)}
    for e, name in enumerate(("near", "cross", "far")):
        entry = [lead_ref[pl.ds(lead.couple + e * n, n), :]]
        if lead.groups > 1:
            entry.append(read_pair(lead_ref, lead.packed + 2 * e))
        block[name] = entry
    block["head"] = read_rows(lead_ref, lead.edge, lead.edges, n)
    block["tail"] = read_rows(lead_ref, lead.edge + lead.edges * n, lead.edges, n)
    return block


def write_block(lay, ref, block):
    n = lay.lines
    write_pieces(lay, ref, block["first"])
    write_pieces(lay, ref, block["last"], lay.total)
    if not lay.leads:
        return
    for e, name in enumerate(("near", "cross", "far")):
        ref[pl.ds(lay.couple + e * n, n), :] = block[name][0]
        if lay.groups > 1:
            write_pair(ref, lay.packed + 2 * e, block[name][1])
    if lay.groups > 1:
        ref[pl.ds(lay.packed + 6, 2), :] = jnp.zeros((2, LANES), jnp.float32)
    write_rows(ref, lay.edge, block["head"], n)
    write_rows(ref, lay.edge + lay.edges * n, block["tail"], n)


def pick(upper, low, high):
    if isinstance(low, list):
        return [pick(upper, a, b) for a, b in zip(low, high)]
    return jnp.where(jnp.full(low.shape, upper, jnp.int32) == 1, high, low)


def write_side(lay, ref, block, upper):
    n = lay.lines
    write_pieces(lay, ref, pick(upper, block["last"], block["first"]))
    if not lay.leads:
        return
    pair = pick(upper, block["far"], block["near"])
    ref[pl.ds(lay.side_couple, n), :] = pair[0]
    if lay.groups > 1:
        ref[pl.ds(lay.side_packed, TILE), :] = pair[1]
    write_rows(ref, lay.side_edge, pick(upper, block["tail"], block["head"]), n)


def read_side(lay, ref, lead, lead_ref):
    n = lead.lines
    couple = [lead_ref[pl.ds(lead.side_couple, n), :]]
    if lead.groups > 1:
        couple.append(lead_ref[pl.ds(lead.side_packed, TILE), :])
    return read_pieces(lay, ref), couple, read_rows(lead_ref, lead.side_edge, lead.edges, n)


def ordered(upper, own, other):
    low = {name: pick(upper, own[name], other[name]) for name in own}
    high = {name: pick(upper, other[name], own[name]) for name in own}
    return low, high


def joint(low, high):
    return [1.0 / (1.0 - far * near) for far, near in zip(low["far"], high["near"])]


def merge(lay, low, high):
    shrink = joint(low, high)
    groups = range(len(shrink))
    to_low = [low["cross"][g] * shrink[g] for g in groups]
    to_high = [high["cross"][g] * shrink[g] for g in groups]
    span = range(len(lay.sizes))
    of = lay.group
    block = {
        "first": [
            low["first"][i]
            + to_low[of(i)] * (high["first"][i] + high["near"][of(i)] * low["last"][i])
            for i in span
        ],
        "last": [
            high["last"][i]
            + to_high[of(i)] * (low["last"][i] + low["far"][of(i)] * high["first"][i])
            for i in span
        ],
    }
    block["near"] = [low["near"][g] + to_low[g] * low["cross"][g] * high["near"][g] for g in groups]
    block["cross"] = [to_low[g] * high["cross"][g] for g in groups]
    block["far"] = [high["far"][g] + to_high[g] * high["cross"][g] * low["far"][g] for g in groups]
    block["head"] = low["head"]
    block["tail"] = high["tail"]
    return block


def inner(lay, low, high, before, after):
    shrink = joint(low, high)
    low_last, high_first = [], []
    for i in range(len(lay.sizes)):
        g = lay.group(i)
        left = low["last"][i] + low["cross"][g] * before[i]
        right = high["first"][i] + high["cross"][g] * after[i]
        low_last.append((left + low["far"][g] * right) * shrink[g])
        high_first.append((right + high["near"][g] * left) * shrink[g])
    return low_last, high_first


def merge_kernel(lay, lead, bit, top, me_ref, own, other, *refs):
    out, *side = refs[-2:] if top else refs[-1:]
    lead_own, lead_other = (own, other) if lay.leads else refs[:2]
    upper = (me_ref[0] >> bit) & 1
    low, high = ordered(
        upper, read_block(lay, own, lead, lead_own), read_block(lay, other, lead, lead_other)
    )
    block = merge(lay, low, high)
    write_block(lay, out, block)
    if top:
        write_side(lay, side[0], block, (me_ref[0] >> (bit + 1)) & 1)


def solve_lines(lay, lead, levels, me, refs):
    owns, gots = refs[:levels], refs[levels : 2 * levels]
    lead_owns, lead_gots = owns, gots
    if not lay.leads:
        lead_owns, lead_gots = refs[2 * levels : 3 * levels], refs[3 * levels : 4 * levels]
    top = levels - 1
    upper = (me >> top) & 1
    own = read_block(lay, owns[top], lead, lead_owns[top])
    met, met_couple, met_edge = read_side(lay, gots[top], lead, lead_gots[top])
    facing = pick(upper, own["last"], own["first"])
    couple = pick(upper, own["far"], own["near"])
    shrink = [1.0 / (1.0 - a * b) for a, b in zip(met_couple, couple)]
    found = []
    for i in range(len(lay.sizes)):
        g = lay.group(i)
        found.append((met[i] + met_couple[g] * facing[i]) * shrink[g])
    zeros = [jnp.zeros_like(v) for v in found]
    blank = [jnp.zeros_like(v) for v in met_edge]
    state = (
        pick(upper, zeros, found), pick(upper, found, zeros),
        pick(upper, blank, met_edge), pick(upper, met_edge, blank),
    )
    partner = None
    for level in reversed(range(top)):
        upper = (me >> level) & 1
        low, high = ordered(
            upper,
            read_block(lay, owns[level], lead, lead_owns[level]),
            read_block(lay, gots[level], lead, lead_gots[level]),
        )
        before, after, behind, ahead = state
        low_last, high_first = inner(lay, low, high, before, after)
        lower = (before, high_first, behind, high["head"])
        higher = (low_last, after, low["tail"], ahead)
        state = tuple(pick(upper, a, b) for a, b in zip(lower, higher))
        partner = tuple(pick(upper, a, b) for a, b in zip(higher, lower))
    return state, partner


def write_answer(lay, ref, state):
    before, after, behind, ahead = state
    write_pieces(lay, ref, before)
    write_pieces(lay, ref, after, lay.total)
    if lay.leads:
        write_rows(ref, 2 * lay.total, behind + ahead, lay.lines)


def solve_kernel(lay, lead, levels, me_ref, *refs):
    state, partner = solve_lines(lay, lead, levels, me_ref[0], refs[:-2])
    write_answer(lay, refs[-2], state)
    write_answer(lay, refs[-1], partner)


def corners(weights):
    one = jnp.ones_like(weights[0])
    value, slope, chain = one, one, [one]
    for weight in weights:
        value, slope = growing_step(value, slope, weight)
        chain.append(value)
    back, fall, backs = one, one, []
    for weight in reversed(weights):
        backs.append(back)
        back, fall = growing_step(back, fall, weight)
    backs.reverse()
    return chain, backs, 1.0 / value


def post(lay, both, row, cells):
    half = cells.shape[0] // 2
    for h in range(2):
        both[pl.ds(h * lay.rows + row, half), :] = cells[h * half : (h + 1) * half]


def z_part(dims, lay, me_ref, cot, phi, psi, w, left, right, arrived, az, both, keep, send):
    nx, ny = dims
    tiles = nx * ny // LANES
    sums = sum_matrix()
    for c in range(len(lay.sizes)):
        arrived(c)
        for t in range(tiles):
            span = pl.ds(t * LANES, LANES)
            cells, up, down = cot[c, span, :], phi[span, :], psi[span, :]
            wide = jnp.concatenate([up * cells, down * cells], axis=1)
            found = jnp.dot(
                jnp.concatenate(split3(wide), axis=0), sums, preferred_element_type=jnp.float32
            )
            found = found[:LANES] + (found[LANES : 2 * LANES] + found[2 * LANES :])
            az[c, span, :] = w[span, :] * (down * found[:, :LANES] + up * found[:, LANES:])
        first = jnp.zeros((nx, LANES), jnp.float32)
        last = jnp.zeros((nx, LANES), jnp.float32)
        for y in range(ny):
            cells = az[c, pl.ds(y, nx, stride=ny), :]
            span = pl.ds(y * nx, nx)
            first = first + left[span, :] * cells
            last = last + right[span, :] * cells
        post(lay, both, lay.offsets[c], first)
        post(lay, both, lay.total + lay.offsets[c], last)
    mine = me_ref[0] & 1
    keep[...] = both[pl.ds(pl.multiple_of(mine * lay.rows, TILE), lay.rows), :]
    send[...] = both[pl.ds(pl.multiple_of((1 - mine) * lay.rows, TILE), lay.rows), :]


def lead_z_kernel(
    dims, lay, me_ref, cot_any, diff_any, phase_any, cour_any, upw_any,
    keep, send, az, w, inv, left, right, phi, psi, later,
    cot, diff, phase, cour, upw, wt, pht, pst, both, in_sems, sems,
):
    nx, ny = dims
    tiles = nx * ny // LANES
    half = nx // 2
    count = len(lay.sizes)
    ahead = pltpu.make_async_copy(cot_any.at[pl.ds(count, later.shape[0])], later, sems.at[4])
    small = [(diff_any, diff), (phase_any, phase), (cour_any.at[1], cour), (upw_any.at[1], upw)]
    for i, (source, target) in enumerate(small):
        pltpu.make_async_copy(source, target, sems.at[i]).start()
    for c in range(count):
        pltpu.make_async_copy(cot_any.at[c], cot.at[c], in_sems.at[c]).start()
    ahead.start()

    for i, (source, target) in enumerate(small[:2]):
        pltpu.make_async_copy(source, target, sems.at[i]).wait()
    w[...] = weight_of(diff[...], phase[...])
    for t in range(tiles):
        span = pl.ds(t * LANES, LANES)
        wt[span, :] = w[span, :].T
    ones = jnp.ones((tiles, LANES), jnp.float32)
    value, slope = ones, ones
    back, fall = ones, ones
    for k in range(LANES):
        here = pl.ds(k, tiles, stride=LANES)
        pht[here, :] = value
        value, slope = growing_step(value, slope, wt[here, :])
        there = pl.ds(LANES - 1 - k, tiles, stride=LANES)
        pst[there, :] = back
        back, fall = growing_step(back, fall, wt[there, :])
    scale = 1.0 / value
    for t in range(tiles):
        span = pl.ds(t * LANES, LANES)
        phi[span, :] = pht[span, :].T
        psi[span, :] = (pst[span, :] * scale[t : t + 1]).T

    chain, backs, total = corners([w[pl.ds(y, nx, stride=ny), :] for y in range(ny)])
    for y in range(ny):
        span = pl.ds(y * nx, nx)
        left[span, :] = backs[y] * total
        right[span, :] = chain[y] * total
        inv[span, :] = chain[y] / chain[y + 1]
    post(lay, both, lay.couple, backs[0] * total)
    post(lay, both, lay.couple + half, total)
    post(lay, both, lay.couple + 2 * half, chain[ny - 1] * total)
    for i, (source, target) in enumerate(small[2:]):
        pltpu.make_async_copy(source, target, sems.at[2 + i]).wait()
    for e, y in enumerate((0, ny - 1)):
        edge = pl.ds(y, nx, stride=ny)
        weight = w[edge, :]
        up = cour[edge, :] * upw[edge, :].astype(jnp.float32)
        flow = up if e == 0 else cour[edge, :] - up
        post(lay, both, lay.edge + 2 * e * half, weight)
        post(lay, both, lay.edge + (2 * e + 1) * half, weight * flow)

    def arrived(c):
        pltpu.make_async_copy(cot_any.at[c], cot.at[c], in_sems.at[c]).wait()

    z_part(dims, lay, me_ref, cot, phi, psi, w, left, right, arrived, az, both, keep, send)
    ahead.wait()


def next_z_kernel(dims, lay, me_ref, cot, phi, psi, w, left, right, keep, send, az, both):
    z_part(
        dims, lay, me_ref, cot, phi, psi, w, left, right, lambda c: None, az, both, keep, send
    )


def coef_kernel(dims, w, courant, upwind, after, block, xinv, left, right, flows):
    del after
    nx, ny = dims
    rows = nx * ny
    one = jnp.ones((ny, LANES), jnp.float32)
    value, slope, back, fall = one, one, one, one
    for k in range(nx):
        low, high = pl.ds(k * ny, ny), pl.ds((nx - 1 - k) * ny, ny)
        right[low, :] = value
        left[high, :] = back
        new_value, slope = growing_step(value, slope, w[low, :])
        xinv[low, :] = value / new_value
        end, value = value, new_value
        corner = back
        back, fall = growing_step(back, fall, w[high, :])
    total = 1.0 / value
    block[pl.ds(0, ny), :] = corner * total
    block[pl.ds(ny, ny), :] = total
    block[pl.ds(2 * ny, ny), :] = end * total

    lane = lax.broadcasted_iota(jnp.int32, (ny, LANES), 1)

    def plane(x, carry):
        span = pl.ds(x * ny, ny)
        left[span, :] = left[span, :] * total
        right[span, :] = right[span, :] * total
        own = one
        for d in range(3):
            flow = courant[d, span, :]
            up = flow * upwind[d, span, :].astype(jnp.float32)
            down = flow - up
            own = own + (down - up)
            if d == 2:
                up = jnp.where(lane == 0, 0.0, up)
                down = jnp.where(lane == LANES - 1, 0.0, down)
            flows[pl.ds((1 + 2 * d) * rows + x * ny, ny), :] = up
            flows[pl.ds((2 + 2 * d) * rows + x * ny, ny), :] = down
        flows[span, :] = own
        return carry

    lax.fori_loop(0, nx, plane, 0, unroll=4)
    first, last = pl.ds(0, ny), pl.ds(rows - ny, ny)
    block[pl.ds(3 * ny, ny), :] = w[first, :] * flows[pl.ds(rows, ny), :]
    block[pl.ds(4 * ny, ny), :] = w[last, :] * flows[pl.ds(2 * rows + rows - ny, ny), :]


def sides(before, after, x):
    return two_sides(before[pl.ds(x, 1), :], after[pl.ds(x, 1), :])


def y_kernel(dims, ylay, xlay, me_ref, az, own, got, w, inv, left, right, *refs):
    nx, ny = dims
    half = nx // 2
    comps = len(ylay.sizes)
    if xlay.leads:
        part, block, ay, ghost, ginv, gleft, gright, before, after, joined = refs
    else:
        before, after, gleft, gright, block, ay, ghost, joined = refs
    mine = me_ref[0] & 1
    span = ylay.answer_rows
    joined[pl.ds(pl.multiple_of(mine * span, TILE), span), :] = own[...]
    joined[pl.ds(pl.multiple_of((1 - mine) * span, TILE), span), :] = got[...]
    if xlay.leads:
        for h in range(2):
            for e in range(2):
                where = pl.ds(e * nx + h * half, half)
                row = h * span + 2 * ylay.total + e * half
                before[where, :] = joined[pl.ds(row, half), :]
                after[where, :] = joined[pl.ds(row + 2 * half, half), :]
        one = jnp.ones((TILE, LANES), jnp.float32)
        value, slope, back, fall = one, one, one, one
        for k in range(nx):
            low, high = pl.ds(k * TILE, TILE), pl.ds((nx - 1 - k) * TILE, TILE)
            gright[low, :] = value
            gleft[high, :] = back
            new_value, slope = growing_step(value, slope, sides(before, after, k))
            ginv[low, :] = value / new_value
            end, value = value, new_value
            corner = back
            back, fall = growing_step(back, fall, sides(before, after, nx - 1 - k))
        total = 1.0 / value
        gleft[...] = (gleft[...].reshape(nx, TILE, LANES) * total).reshape(nx * TILE, LANES)
        gright[...] = (gright[...].reshape(nx, TILE, LANES) * total).reshape(nx * TILE, LANES)

    ghost[...] = jnp.zeros(ghost.shape, jnp.float32)
    for c in range(comps):
        for h in range(2):
            piece = pl.ds(h * half, half)
            fb = joined[pl.ds(h * span + c * half, half), :]
            fa = joined[pl.ds(h * span + ylay.total + c * half, half), :]
            ghost[pl.ds(h * half * TILE + c, half, stride=TILE), :] = before[piece, :] * fb
            ghost[pl.ds(h * half * TILE + SIDE + c, half, stride=TILE), :] = after[piece, :] * fa
            swept, chain = fb, []
            for y in range(ny):
                cells = az[c, pl.ds(h * half * ny + y, half, stride=ny), :]
                swept = (cells + swept) * inv[pl.ds(y * nx + h * half, half), :]
                chain.append(swept)
            later = fa
            for y in reversed(range(ny)):
                where = pl.ds(h * half * ny + y, half, stride=ny)
                later = chain[y] + inv[pl.ds(y * nx + h * half, half), :] * later
                ay[c, where, :] = later * w[where, :]

    firsts = [jnp.zeros((n, LANES), jnp.float32) for n in xlay.sizes]
    lasts = list(firsts)
    for x in range(nx):
        here = pl.ds(x * ny, ny)
        near, far = left[here, :], right[here, :]
        for c in range(comps):
            cells = ay[c, here, :]
            firsts[c] = firsts[c] + near * cells
            lasts[c] = lasts[c] + far * cells
        here = pl.ds(x * TILE, TILE)
        cells = ghost[here, :]
        firsts[comps] = firsts[comps] + gleft[here, :] * cells
        lasts[comps] = lasts[comps] + gright[here, :] * cells
    record = {"first": firsts, "last": lasts}
    if xlay.leads:
        pieces = [part[pl.ds(i * ny, ny), :] for i in range(5)]
        record["near"] = [pieces[0], corner * total]
        record["cross"] = [pieces[1], total]
        record["far"] = [pieces[2], end * total]
        record["head"], record["tail"] = pieces[3:4], pieces[4:5]
    write_block(xlay, block, record)


def x_kernel(dims, lay, lead, levels, shift, start, me_ref, *refs):
    nx, ny = dims
    count = (2 if lay.leads else 4) * levels
    state, _ = solve_lines(lay, lead, levels, me_ref[0] >> shift, refs[:count])
    xinv, ginv, ay, ghost, w, lower, higher, flows, *rest = refs[count:]
    out_any, out, field, fluxes, sems = rest[-5:]
    rows = nx * ny
    comps = len(lay.sizes) - 1
    tiles = ny // TILE
    starts, nexts, behind, ahead = state
    near, far = behind[0], ahead[0]

    def sweep(x, carry):
        span, above = pl.ds(x * ny, ny), pl.ds((x + 1) * ny, ny)
        factor = xinv[span, :]
        new = []
        for c in range(comps):
            value = (ay[c, span, :] + carry[c]) * factor
            field[c, above, :] = value
            new.append(value)
        here = pl.ds(x * TILE, TILE)
        edge = (ghost[here, :] + carry[comps]) * ginv[here, :]
        fluxes[here, :] = edge
        return tuple(new) + (edge,)

    lax.fori_loop(0, nx, sweep, tuple(starts), unroll=16)

    def back(step, carry):
        x = nx - 1 - step
        span, above = pl.ds(x * ny, ny), pl.ds((x + 1) * ny, ny)
        factor = xinv[span, :]
        weight = w[span, :]
        new = []
        for c in range(comps):
            value = field[c, above, :] + factor * carry[c]
            field[c, above, :] = value * weight
            new.append(value)
        here = pl.ds(x * TILE, TILE)
        edge = fluxes[here, :] + ginv[here, :] * carry[comps]
        fluxes[here, :] = edge * two_sides(lower[pl.ds(nx + x, 1), :], higher[pl.ds(nx + x, 1), :])
        return tuple(new) + (edge,)

    lax.fori_loop(0, nx, back, tuple(nexts), unroll=16)
    blank = jnp.zeros((comps, ny, LANES), jnp.float32)
    field[:, pl.ds(0, ny), :] = blank
    field[:, pl.ds((nx + 1) * ny, ny), :] = blank

    line = lax.broadcasted_iota(jnp.int32, (TILE, LANES), 0)

    def advect(x, carry):
        before = jnp.maximum(x - 1, 0)
        beyond = jnp.minimum(x + 1, nx - 1)

        def flow(kind, plane, t):
            begin = pl.multiple_of(kind * rows + plane * ny + t * TILE, TILE)
            return flows[pl.ds(begin, TILE), :]

        own = [flow(0, x, t) for t in range(tiles)]
        ahead_x = [flow(1, beyond, t) for t in range(tiles)]
        behind_x = [flow(2, before, t) for t in range(tiles)]
        ahead_y = [flow(3, x, t) for t in range(tiles)]
        behind_y = [flow(4, x, t) for t in range(tiles)]
        ahead_z = [flow(5, x, t) for t in range(tiles)]
        behind_z = [flow(6, x, t) for t in range(tiles)]
        for c in range(comps):

            def cells(plane, t):
                begin = pl.multiple_of((plane + 1) * ny + t * TILE, TILE)
                return field[c, pl.ds(begin, TILE), :]

            grad = [cells(x, t) for t in range(tiles)]
            ups = [pltpu.roll(ahead_y[t] * grad[t], TILE - 1, 0) for t in range(tiles)]
            downs = [pltpu.roll(behind_y[t] * grad[t], 1, 0) for t in range(tiles)]
            lowest = fluxes[pl.ds(x * TILE + c, 1), :]
            highest = fluxes[pl.ds(x * TILE + SIDE + c, 1), :]
            for t in range(tiles):
                part = own[t] * grad[t]
                part = part + ahead_x[t] * cells(x + 1, t) - behind_x[t] * cells(x - 1, t)
                enter = ups[t + 1] if t + 1 < tiles else jnp.broadcast_to(highest, (TILE, LANES))
                part = part + jnp.where(line == TILE - 1, enter, ups[t])
                enter = downs[t - 1] if t > 0 else jnp.broadcast_to(lowest, (TILE, LANES))
                part = part - jnp.where(line == 0, enter, downs[t])
                part = part + pltpu.roll(ahead_z[t] * grad[t], LANES - 1, 1)
                part = part - pltpu.roll(behind_z[t] * grad[t], 1, 1)
                out[c, pl.ds(pl.multiple_of(x * ny + t * TILE, TILE), TILE), :] = part
        return carry

    parts = 4
    share = nx // parts

    def copy(part):
        span = pl.ds(part * share * ny, share * ny)
        target = out_any.at[pl.ds(start, comps), span, :]
        return pltpu.make_async_copy(out.at[:, span, :], target, sems.at[part])

    top, bottom = pl.ds(0, ny), pl.ds(rows - ny, ny)
    for part in range(parts):
        lax.fori_loop(part * share, (part + 1) * share, advect, 0, unroll=share)
        for c in range(comps):
            if part == 0:
                out[c, top, :] = out[c, top, :] - near * starts[c]
            if part == parts - 1:
                out[c, bottom, :] = out[c, bottom, :] + far * nexts[c]
        copy(part).start()
    for part in range(parts):
        copy(part).wait()


def call(
    kernel, name, operands, outs, scratch=(), spaces=None, out_spaces=None, mebibytes=4, aliases=None
):
    params = pltpu.CompilerParams(vmem_limit_bytes=mebibytes * 1024 * 1024)
    memory = {"v": pltpu.VMEM, "k": pltpu.VMEM, "h": pltpu.HBM, "s": pltpu.SMEM}
    held = {"h": pltpu.HBM, "k": pltpu.VMEM}
    spaces = spaces or "s" + "v" * (len(operands) - 1)
    out_spaces = out_spaces or "v" * len(outs)
    operands = [
        pltpu.with_memory_space_constraint(o, held[s]) if s in held else o
        for o, s in zip(operands, spaces)
    ]
    return pl.pallas_call(
        kernel,
        name=name,
        out_shape=[
            held[s](shape, jnp.float32) if s in held else jax.ShapeDtypeStruct(shape, jnp.float32)
            for shape, s in zip(outs, out_spaces)
        ],
        in_specs=[pl.BlockSpec(memory_space=memory[s]) for s in spaces],
        out_specs=[pl.BlockSpec(memory_space=memory[s]) for s in out_spaces],
        scratch_shapes=list(scratch),
        input_output_aliases=aliases or {},
        compiler_params=params,
        cost_estimate=pl.CostEstimate(flops=1024, bytes_accessed=1024, transcendentals=0),
    )(*operands)


def exchange(rows, axis, bit):
    count = lax.axis_size(axis)
    return lax.ppermute(rows, axis, [(i, i ^ (1 << bit)) for i in range(count)])


class Ladder:
    def __init__(self, lay, axis, shift, me, send, keep, lead=None):
        self.lay, self.axis, self.shift, self.me, self.lead = lay, axis, shift, me, lead
        self.levels = (lax.axis_size(axis) - 1).bit_length()
        self.owns, self.gots, self.outgoing = [keep], [], send

    def send(self):
        self.gots.append(exchange(self.outgoing, self.axis, len(self.gots)))

    def merge(self, beside=()):
        level = len(self.owns) - 1
        top = level == self.levels - 2
        leader = self.lead or self
        coupled = () if self.lay.leads else (leader.owns[level], leader.gots[level])
        shapes = [(self.lay.rows, LANES)] + ([(self.lay.side_rows, LANES)] if top else [])
        merged = call(
            functools.partial(merge_kernel, self.lay, leader.lay, self.shift + level, top),
            "merge_" + self.axis,
            (self.me, self.owns[-1], self.gots[-1]) + coupled + tuple(beside),
            shapes,
        )
        self.owns.append(merged[0])
        self.outgoing = merged[-1]

    def records(self):
        found = (*self.owns, *self.gots)
        return found if self.lay.leads else found + (*self.lead.owns, *self.lead.gots)


def on_device(cotangent, diffusion, phase, courant, upwind):
    comps, nx, ny, nz = cotangent.shape
    shift = (lax.axis_size("gy") - 1).bit_length()
    rows = nx * ny
    half = nx // 2
    size = comps // 2
    starts = (0, size)
    counts = (size, comps - size)
    ylays = [Layout([half] * n, 1, 2, half, g == 0) for g, n in enumerate(counts)]
    xlays = [Layout([ny] * n + [TILE], 2, 1, ny, g == 0) for g, n in enumerate(counts)]
    me = lax.axis_index(("gx", "gy")).astype(jnp.int32).reshape(1)

    def vmem(*shape, dtype=jnp.float32):
        return pltpu.VMEM(shape, dtype)

    flat = (rows, nz)
    cot = cotangent.reshape(comps, rows, nz)
    cour = courant.reshape(3, rows, nz)
    upw = upwind.reshape(3, rows, nz)
    n = counts[0]
    keep, send, az, w, inv, left, right, phi, psi, cot_next = call(
        functools.partial(lead_z_kernel, (nx, ny), ylays[0]),
        "z_solve_lead",
        (me, cot, diffusion.reshape(flat), phase.reshape(flat), cour, upw),
        [(ylays[0].rows, nz)] * 2 + [(n, rows, nz)] + [flat] * 6 + [(counts[1], rows, nz)],
        [
            vmem(n, rows, nz), vmem(*flat), vmem(*flat, dtype=jnp.int32),
            vmem(*flat), vmem(*flat, dtype=jnp.int32),
            vmem(*flat), vmem(*flat), vmem(*flat), vmem(2 * ylays[0].rows, nz),
            pltpu.SemaphoreType.DMA((n,)), pltpu.SemaphoreType.DMA((5,)),
        ],
        spaces="shhhhh",
        mebibytes=12,
    )
    lead = Ladder(ylays[0], "gy", 0, me, send, keep)
    lead.send()
    azs = [az]
    n = counts[1]
    keep, send, az = call(
        functools.partial(next_z_kernel, (nx, ny), ylays[1]),
        "z_solve_next",
        (me, cot_next, phi, psi, w, left, right),
        [(ylays[1].rows, nz)] * 2 + [(n, rows, nz)],
        [vmem(2 * ylays[1].rows, nz)],
        mebibytes=8,
    )
    azs.append(az)
    follow = Ladder(ylays[1], "gy", 0, me, send, keep, lead)
    follow.send()
    beside = (send,)
    for level in range(lead.levels - 1):
        lead.merge(beside)
        lead.send()
        follow.merge()
        follow.send()
        beside = (follow.outgoing,)
        if level == 0:
            part, xinv, xleft, xright, flows = call(
                functools.partial(coef_kernel, (nx, ny)),
                "x_coefficients",
                (w, cour, upw, lead.owns[1]),
                [(5 * ny, nz), flat, flat, flat, (7 * rows, nz)],
                spaces="vvvv",
                mebibytes=8,
            )
            beside = (part, follow.outgoing)
    ladders, mets, answers = (lead, follow), [], []
    for g, ladder in enumerate(ladders):
        answer, passed = call(
            functools.partial(solve_kernel, ylays[g], ylays[0], ladder.levels),
            "y_reduced",
            (me,) + ladder.records() + (beside if g == 0 else ()),
            [(ylays[g].answer_rows, nz)] * 2,
        )
        answers.append(answer)
        mets.append(exchange(passed, "gy", 0))
    ays, ghosts, climbs = [], [], []
    for g in range(2):
        common = (me, azs[g], answers[g], mets[g], w, inv, xleft, xright)
        outs = [(xlays[g].rows, nz), (counts[g], rows, nz), (nx * TILE, nz)]
        scratch = [vmem(2 * ylays[g].answer_rows, nz)]
        body = functools.partial(y_kernel, (nx, ny), ylays[g], xlays[g])
        if g == 0:
            block, ay, ghost, ginv, gleft, gright, before, after = call(
                body,
                "y_solve_lead",
                common + (part,),
                outs + [(nx * TILE, nz)] * 3 + [(2 * nx, nz)] * 2,
                scratch,
                mebibytes=6,
            )
        else:
            block, ay, ghost = call(
                body,
                "y_solve_next",
                common + (before, after, gleft, gright),
                outs,
                scratch,
                mebibytes=6,
            )
        ays.append(ay)
        ghosts.append(ghost)
        climbs.append(Ladder(xlays[g], "gx", shift, me, block, block, climbs[0] if g else None))
        climbs[g].send()
    beside = (block,)
    for level in range(climbs[0].levels - 1):
        for ladder in climbs:
            ladder.merge(beside if ladder.lay.leads else ())
            ladder.send()
        beside = (climbs[1].outgoing,)
    grad = None
    for g, ladder in enumerate(climbs):
        operands = (me,) + ladder.records() + (
            xinv, ginv, ays[g], ghosts[g], w, before, after, flows,
        )
        spaces = "s" + "v" * (len(operands) - 1)
        aliases = None
        if g:
            aliases = {len(operands): 0}
            operands, spaces = operands + (grad,), spaces + "h"
        (grad,) = call(
            functools.partial(
                x_kernel, (nx, ny), xlays[g], xlays[0], ladder.levels, shift, starts[g]
            ),
            "x_solve",
            operands,
            [(comps, rows, nz)],
            [
                vmem(counts[g], rows, nz), vmem(counts[g], rows + 2 * ny, nz), vmem(nx * TILE, nz),
                pltpu.SemaphoreType.DMA((4,)),
            ],
            spaces=spaces,
            out_spaces="h",
            mebibytes=8,
            aliases=aliases,
        )
    return grad.reshape(comps, nx, ny, nz)


def solution(mesh):
    placed = (
        P(None, "gx", "gy", None),
        P("gx", "gy", None),
        P("gx", "gy", None),
        P(None, "gx", "gy", None),
        P(None, "gx", "gy", None),
    )
    return jax.shard_map(
        on_device, mesh=mesh, in_specs=placed, out_specs=P(None, "gx", "gy", None), check_vma=False
    )
```

```python
import functools

import jax
import jax.numpy as jnp
from jax import lax
from jax.experimental import pallas as pl
from jax.experimental.pallas import tpu as pltpu
from jax.sharding import PartitionSpec as P

COMPS = 6
LANES = 128
TILE = 8
SIDE = TILE // 2


def weight_of(diffusion, phase):
    return 1.0 / (diffusion * (1.0 + 3.0 * phase.astype(jnp.float32)))


def growing_step(value, slope, weight):
    slope = slope + weight * value
    return value + slope, slope


def split3(cells):
    high = cells.astype(jnp.bfloat16)
    rest = cells - high.astype(jnp.float32)
    middle = rest.astype(jnp.bfloat16)
    low = (rest - middle.astype(jnp.float32)).astype(jnp.bfloat16)
    return high, middle, low


def sum_matrix():
    row = lax.broadcasted_iota(jnp.int32, (2 * LANES, 2 * LANES), 0)
    col = lax.broadcasted_iota(jnp.int32, (2 * LANES, 2 * LANES), 1)
    before = (row < LANES) & (col < LANES) & (row <= col)
    after = (row >= LANES) & (col >= LANES) & (row > col)
    return jnp.where(before | after, 1.0, 0.0).astype(jnp.bfloat16)


class Layout:
    def __init__(self, sizes, groups, edges, lines, leads):
        self.sizes, self.groups, self.edges, self.lines, self.leads = sizes, groups, edges, lines, leads
        self.offsets = [sum(sizes[:i]) for i in range(len(sizes))]
        self.total = sum(sizes)
        packed = TILE if groups > 1 else 0
        self.couple = 2 * self.total
        self.packed = self.couple + 3 * lines
        self.edge = self.packed + packed
        self.side_couple = self.total
        self.side_packed = self.side_couple + lines
        self.side_edge = self.side_packed + packed
        extra = 2 * edges * lines
        self.rows = self.edge + extra if leads else self.couple
        self.side_rows = self.side_edge + extra // 2 if leads else self.total
        self.answer_rows = 2 * self.total + (extra if leads else 0)

    def group(self, piece):
        return 1 if self.groups > 1 and piece == len(self.sizes) - 1 else 0


def read_pieces(lay, ref, base=0):
    return [ref[pl.ds(base + o, n), :] for o, n in zip(lay.offsets, lay.sizes)]


def write_pieces(lay, ref, values, base=0):
    for o, n, value in zip(lay.offsets, lay.sizes, values):
        ref[pl.ds(base + o, n), :] = value


def read_rows(ref, base, count, lines):
    return [ref[pl.ds(base + i * lines, lines), :] for i in range(count)]


def write_rows(ref, base, values, lines):
    for i, value in enumerate(values):
        ref[pl.ds(base + i * lines, lines), :] = value


def two_sides(low, high):
    return jnp.concatenate(
        [jnp.broadcast_to(low, (SIDE, LANES)), jnp.broadcast_to(high, (SIDE, LANES))], axis=0
    )


def read_pair(ref, row):
    return two_sides(ref[pl.ds(row, 1), :], ref[pl.ds(row + 1, 1), :])


def write_pair(ref, row, value):
    ref[pl.ds(row, 1), :] = value[:1]
    ref[pl.ds(row + 1, 1), :] = value[SIDE : SIDE + 1]


def read_block(lay, ref, lead, lead_ref):
    n = lead.lines
    block = {"first": read_pieces(lay, ref), "last": read_pieces(lay, ref, lay.total)}
    for e, name in enumerate(("near", "cross", "far")):
        entry = [lead_ref[pl.ds(lead.couple + e * n, n), :]]
        if lead.groups > 1:
            entry.append(read_pair(lead_ref, lead.packed + 2 * e))
        block[name] = entry
    block["head"] = read_rows(lead_ref, lead.edge, lead.edges, n)
    block["tail"] = read_rows(lead_ref, lead.edge + lead.edges * n, lead.edges, n)
    return block


def write_block(lay, ref, block):
    n = lay.lines
    write_pieces(lay, ref, block["first"])
    write_pieces(lay, ref, block["last"], lay.total)
    if not lay.leads:
        return
    for e, name in enumerate(("near", "cross", "far")):
        ref[pl.ds(lay.couple + e * n, n), :] = block[name][0]
        if lay.groups > 1:
            write_pair(ref, lay.packed + 2 * e, block[name][1])
    if lay.groups > 1:
        ref[pl.ds(lay.packed + 6, 2), :] = jnp.zeros((2, LANES), jnp.float32)
    write_rows(ref, lay.edge, block["head"], n)
    write_rows(ref, lay.edge + lay.edges * n, block["tail"], n)


def pick(upper, low, high):
    if isinstance(low, list):
        return [pick(upper, a, b) for a, b in zip(low, high)]
    return jnp.where(jnp.full(low.shape, upper, jnp.int32) == 1, high, low)


def write_side(lay, ref, block, upper):
    n = lay.lines
    write_pieces(lay, ref, pick(upper, block["last"], block["first"]))
    if not lay.leads:
        return
    pair = pick(upper, block["far"], block["near"])
    ref[pl.ds(lay.side_couple, n), :] = pair[0]
    if lay.groups > 1:
        ref[pl.ds(lay.side_packed, TILE), :] = pair[1]
    write_rows(ref, lay.side_edge, pick(upper, block["tail"], block["head"]), n)


def read_side(lay, ref, lead, lead_ref):
    n = lead.lines
    couple = [lead_ref[pl.ds(lead.side_couple, n), :]]
    if lead.groups > 1:
        couple.append(lead_ref[pl.ds(lead.side_packed, TILE), :])
    return read_pieces(lay, ref), couple, read_rows(lead_ref, lead.side_edge, lead.edges, n)


def ordered(upper, own, other):
    low = {name: pick(upper, own[name], other[name]) for name in own}
    high = {name: pick(upper, other[name], own[name]) for name in own}
    return low, high


def joint(low, high):
    return [1.0 / (1.0 - far * near) for far, near in zip(low["far"], high["near"])]


def merge(lay, low, high):
    shrink = joint(low, high)
    groups = range(len(shrink))
    to_low = [low["cross"][g] * shrink[g] for g in groups]
    to_high = [high["cross"][g] * shrink[g] for g in groups]
    span = range(len(lay.sizes))
    of = lay.group
    block = {
        "first": [
            low["first"][i]
            + to_low[of(i)] * (high["first"][i] + high["near"][of(i)] * low["last"][i])
            for i in span
        ],
        "last": [
            high["last"][i]
            + to_high[of(i)] * (low["last"][i] + low["far"][of(i)] * high["first"][i])
            for i in span
        ],
    }
    block["near"] = [low["near"][g] + to_low[g] * low["cross"][g] * high["near"][g] for g in groups]
    block["cross"] = [to_low[g] * high["cross"][g] for g in groups]
    block["far"] = [high["far"][g] + to_high[g] * high["cross"][g] * low["far"][g] for g in groups]
    block["head"] = low["head"]
    block["tail"] = high["tail"]
    return block


def inner(lay, low, high, before, after):
    shrink = joint(low, high)
    low_last, high_first = [], []
    for i in range(len(lay.sizes)):
        g = lay.group(i)
        left = low["last"][i] + low["cross"][g] * before[i]
        right = high["first"][i] + high["cross"][g] * after[i]
        low_last.append((left + low["far"][g] * right) * shrink[g])
        high_first.append((right + high["near"][g] * left) * shrink[g])
    return low_last, high_first


def merge_kernel(lay, lead, bit, top, me_ref, own, other, *refs):
    out, *side = refs[-2:] if top else refs[-1:]
    lead_own, lead_other = (own, other) if lay.leads else refs[:2]
    upper = (me_ref[0] >> bit) & 1
    low, high = ordered(
        upper, read_block(lay, own, lead, lead_own), read_block(lay, other, lead, lead_other)
    )
    block = merge(lay, low, high)
    write_block(lay, out, block)
    if top:
        write_side(lay, side[0], block, (me_ref[0] >> (bit + 1)) & 1)


def first_merge_kernel(lay, bit, top, me_ref, own, slim, apart, *refs):
    out, joined, *side = refs[-3:] if top else refs[-2:]
    joined[pl.ds(0, lay.couple), :] = slim[pl.ds(0, lay.couple), :]
    joined[pl.ds(lay.packed, TILE), :] = slim[pl.ds(lay.couple, TILE), :]
    joined[pl.ds(lay.couple, 3 * lay.lines), :] = apart[pl.ds(0, 3 * lay.lines), :]
    edges = 2 * lay.edges * lay.lines
    joined[pl.ds(lay.edge, edges), :] = apart[pl.ds(3 * lay.lines, edges), :]
    merge_kernel(lay, lay, bit, top, me_ref, own, joined, out, *side)


def solve_lines(lay, lead, levels, me, refs):
    owns, gots = refs[:levels], refs[levels : 2 * levels]
    lead_owns, lead_gots = owns, gots
    if not lay.leads:
        lead_owns, lead_gots = refs[2 * levels : 3 * levels], refs[3 * levels : 4 * levels]
    top = levels - 1
    upper = (me >> top) & 1
    own = read_block(lay, owns[top], lead, lead_owns[top])
    met, met_couple, met_edge = read_side(lay, gots[top], lead, lead_gots[top])
    facing = pick(upper, own["last"], own["first"])
    couple = pick(upper, own["far"], own["near"])
    shrink = [1.0 / (1.0 - a * b) for a, b in zip(met_couple, couple)]
    found = []
    for i in range(len(lay.sizes)):
        g = lay.group(i)
        found.append((met[i] + met_couple[g] * facing[i]) * shrink[g])
    zeros = [jnp.zeros_like(v) for v in found]
    blank = [jnp.zeros_like(v) for v in met_edge]
    state = (
        pick(upper, zeros, found), pick(upper, found, zeros),
        pick(upper, blank, met_edge), pick(upper, met_edge, blank),
    )
    partner = None
    for level in reversed(range(top)):
        upper = (me >> level) & 1
        low, high = ordered(
            upper,
            read_block(lay, owns[level], lead, lead_owns[level]),
            read_block(lay, gots[level], lead, lead_gots[level]),
        )
        before, after, behind, ahead = state
        low_last, high_first = inner(lay, low, high, before, after)
        lower = (before, high_first, behind, high["head"])
        higher = (low_last, after, low["tail"], ahead)
        state = tuple(pick(upper, a, b) for a, b in zip(lower, higher))
        partner = tuple(pick(upper, a, b) for a, b in zip(higher, lower))
    return state, partner


def write_answer(lay, ref, state):
    before, after, behind, ahead = state
    write_pieces(lay, ref, before)
    write_pieces(lay, ref, after, lay.total)
    if lay.leads:
        write_rows(ref, 2 * lay.total, behind + ahead, lay.lines)


def solve_kernel(lay, lead, levels, me_ref, *refs):
    state, partner = solve_lines(lay, lead, levels, me_ref[0], refs[:-2])
    write_answer(lay, refs[-2], state)
    write_answer(lay, refs[-1], partner)


def corners(weights):
    one = jnp.ones_like(weights[0])
    value, slope, chain = one, one, [one]
    for weight in weights:
        value, slope = growing_step(value, slope, weight)
        chain.append(value)
    back, fall, backs = one, one, []
    for weight in reversed(weights):
        backs.append(back)
        back, fall = growing_step(back, fall, weight)
    backs.reverse()
    return chain, backs, 1.0 / value


def post(lay, both, row, cells):
    half = cells.shape[0] // 2
    for h in range(2):
        both[pl.ds(h * lay.rows + row, half), :] = cells[h * half : (h + 1) * half]


def z_part(dims, lay, me_ref, cot, phi, psi, w, left, right, arrived, az, both, keep, send):
    nx, ny = dims
    tiles = nx * ny // LANES
    sums = sum_matrix()
    for c in range(len(lay.sizes)):
        arrived(c)
        for t in range(tiles):
            span = pl.ds(t * LANES, LANES)
            cells, up, down = cot[c, span, :], phi[span, :], psi[span, :]
            wide = jnp.concatenate([up * cells, down * cells], axis=1)
            found = jnp.dot(
                jnp.concatenate(split3(wide), axis=0), sums, preferred_element_type=jnp.float32
            )
            found = found[:LANES] + (found[LANES : 2 * LANES] + found[2 * LANES :])
            az[c, span, :] = w[span, :] * (down * found[:, :LANES] + up * found[:, LANES:])
        first = jnp.zeros((nx, LANES), jnp.float32)
        last = jnp.zeros((nx, LANES), jnp.float32)
        for y in range(ny):
            cells = az[c, pl.ds(y, nx, stride=ny), :]
            span = pl.ds(y * nx, nx)
            first = first + left[span, :] * cells
            last = last + right[span, :] * cells
        post(lay, both, lay.offsets[c], first)
        post(lay, both, lay.total + lay.offsets[c], last)
    mine = me_ref[0] & 1
    keep[...] = both[pl.ds(pl.multiple_of(mine * lay.rows, TILE), lay.rows), :]
    send[...] = both[pl.ds(pl.multiple_of((1 - mine) * lay.rows, TILE), lay.rows), :]


def lead_z_kernel(
    dims, lay, me_ref, cot_any, diff_any, phase_any, cour_any, upw_any,
    keep, send, az, w, inv, left, right, phi, psi, later,
    cot, diff, phase, cour, upw, wt, pht, pst, both, in_sems, sems,
):
    nx, ny = dims
    tiles = nx * ny // LANES
    half = nx // 2
    count = len(lay.sizes)
    ahead = pltpu.make_async_copy(cot_any.at[pl.ds(count, later.shape[0])], later, sems.at[4])
    small = [(diff_any, diff), (phase_any, phase), (cour_any.at[1], cour), (upw_any.at[1], upw)]
    for i, (source, target) in enumerate(small):
        pltpu.make_async_copy(source, target, sems.at[i]).start()
    for c in range(count):
        pltpu.make_async_copy(cot_any.at[c], cot.at[c], in_sems.at[c]).start()
    ahead.start()

    for i, (source, target) in enumerate(small[:2]):
        pltpu.make_async_copy(source, target, sems.at[i]).wait()
    w[...] = weight_of(diff[...], phase[...])
    for t in range(tiles):
        span = pl.ds(t * LANES, LANES)
        wt[span, :] = w[span, :].T
    ones = jnp.ones((tiles, LANES), jnp.float32)
    value, slope = ones, ones
    back, fall = ones, ones
    for k in range(LANES):
        here = pl.ds(k, tiles, stride=LANES)
        pht[here, :] = value
        value, slope = growing_step(value, slope, wt[here, :])
        there = pl.ds(LANES - 1 - k, tiles, stride=LANES)
        pst[there, :] = back
        back, fall = growing_step(back, fall, wt[there, :])
    scale = 1.0 / value
    for t in range(tiles):
        span = pl.ds(t * LANES, LANES)
        phi[span, :] = pht[span, :].T
        psi[span, :] = (pst[span, :] * scale[t : t + 1]).T

    chain, backs, total = corners([w[pl.ds(y, nx, stride=ny), :] for y in range(ny)])
    for y in range(ny):
        span = pl.ds(y * nx, nx)
        left[span, :] = backs[y] * total
        right[span, :] = chain[y] * total
        inv[span, :] = chain[y] / chain[y + 1]
    post(lay, both, lay.couple, backs[0] * total)
    post(lay, both, lay.couple + half, total)
    post(lay, both, lay.couple + 2 * half, chain[ny - 1] * total)
    for i, (source, target) in enumerate(small[2:]):
        pltpu.make_async_copy(source, target, sems.at[2 + i]).wait()
    for e, y in enumerate((0, ny - 1)):
        edge = pl.ds(y, nx, stride=ny)
        weight = w[edge, :]
        up = cour[edge, :] * upw[edge, :].astype(jnp.float32)
        flow = up if e == 0 else cour[edge, :] - up
        post(lay, both, lay.edge + 2 * e * half, weight)
        post(lay, both, lay.edge + (2 * e + 1) * half, weight * flow)

    def arrived(c):
        pltpu.make_async_copy(cot_any.at[c], cot.at[c], in_sems.at[c]).wait()

    z_part(dims, lay, me_ref, cot, phi, psi, w, left, right, arrived, az, both, keep, send)
    ahead.wait()


def next_z_kernel(dims, lay, me_ref, cot, phi, psi, w, left, right, keep, send, az, both):
    z_part(
        dims, lay, me_ref, cot, phi, psi, w, left, right, lambda c: None, az, both, keep, send
    )


def coef_kernel(dims, w, courant, upwind, after, block, xinv, left, right, flows):
    del after
    nx, ny = dims
    rows = nx * ny
    one = jnp.ones((ny, LANES), jnp.float32)
    value, slope, back, fall = one, one, one, one
    for k in range(nx):
        low, high = pl.ds(k * ny, ny), pl.ds((nx - 1 - k) * ny, ny)
        right[low, :] = value
        left[high, :] = back
        new_value, slope = growing_step(value, slope, w[low, :])
        xinv[low, :] = value / new_value
        end, value = value, new_value
        corner = back
        back, fall = growing_step(back, fall, w[high, :])
    total = 1.0 / value
    block[pl.ds(0, ny), :] = corner * total
    block[pl.ds(ny, ny), :] = total
    block[pl.ds(2 * ny, ny), :] = end * total

    lane = lax.broadcasted_iota(jnp.int32, (ny, LANES), 1)

    def plane(x, carry):
        span = pl.ds(x * ny, ny)
        left[span, :] = left[span, :] * total
        right[span, :] = right[span, :] * total
        own = one
        for d in range(3):
            flow = courant[d, span, :]
            up = flow * upwind[d, span, :].astype(jnp.float32)
            down = flow - up
            own = own + (down - up)
            if d == 2:
                up = jnp.where(lane == 0, 0.0, up)
                down = jnp.where(lane == LANES - 1, 0.0, down)
            flows[pl.ds((1 + 2 * d) * rows + x * ny, ny), :] = up
            flows[pl.ds((2 + 2 * d) * rows + x * ny, ny), :] = down
        flows[span, :] = own
        return carry

    lax.fori_loop(0, nx, plane, 0, unroll=4)
    first, last = pl.ds(0, ny), pl.ds(rows - ny, ny)
    block[pl.ds(3 * ny, ny), :] = w[first, :] * flows[pl.ds(rows, ny), :]
    block[pl.ds(4 * ny, ny), :] = w[last, :] * flows[pl.ds(2 * rows + rows - ny, ny), :]


def sides(before, after, x):
    return two_sides(before[pl.ds(x, 1), :], after[pl.ds(x, 1), :])


def y_kernel(dims, ylay, xlay, me_ref, az, own, got, w, inv, left, right, *refs):
    nx, ny = dims
    half = nx // 2
    comps = len(ylay.sizes)
    if xlay.leads:
        part, block, slim, ay, ghost, ginv, gleft, gright, before, after, joined = refs
    else:
        before, after, gleft, gright, block, ay, ghost, joined = refs
    mine = me_ref[0] & 1
    span = ylay.answer_rows
    joined[pl.ds(pl.multiple_of(mine * span, TILE), span), :] = own[...]
    joined[pl.ds(pl.multiple_of((1 - mine) * span, TILE), span), :] = got[...]
    if xlay.leads:
        for h in range(2):
            for e in range(2):
                where = pl.ds(e * nx + h * half, half)
                row = h * span + 2 * ylay.total + e * half
                before[where, :] = joined[pl.ds(row, half), :]
                after[where, :] = joined[pl.ds(row + 2 * half, half), :]
        one = jnp.ones((TILE, LANES), jnp.float32)
        value, slope, back, fall = one, one, one, one
        for k in range(nx):
            low, high = pl.ds(k * TILE, TILE), pl.ds((nx - 1 - k) * TILE, TILE)
            gright[low, :] = value
            gleft[high, :] = back
            new_value, slope = growing_step(value, slope, sides(before, after, k))
            ginv[low, :] = value / new_value
            end, value = value, new_value
            corner = back
            back, fall = growing_step(back, fall, sides(before, after, nx - 1 - k))
        total = 1.0 / value
        gleft[...] = (gleft[...].reshape(nx, TILE, LANES) * total).reshape(nx * TILE, LANES)
        gright[...] = (gright[...].reshape(nx, TILE, LANES) * total).reshape(nx * TILE, LANES)

    ghost[...] = jnp.zeros(ghost.shape, jnp.float32)
    for c in range(comps):
        for h in range(2):
            piece = pl.ds(h * half, half)
            fb = joined[pl.ds(h * span + c * half, half), :]
            fa = joined[pl.ds(h * span + ylay.total + c * half, half), :]
            ghost[pl.ds(h * half * TILE + c, half, stride=TILE), :] = before[piece, :] * fb
            ghost[pl.ds(h * half * TILE + SIDE + c, half, stride=TILE), :] = after[piece, :] * fa
            swept, chain = fb, []
            for y in range(ny):
                cells = az[c, pl.ds(h * half * ny + y, half, stride=ny), :]
                swept = (cells + swept) * inv[pl.ds(y * nx + h * half, half), :]
                chain.append(swept)
            later = fa
            for y in reversed(range(ny)):
                where = pl.ds(h * half * ny + y, half, stride=ny)
                later = chain[y] + inv[pl.ds(y * nx + h * half, half), :] * later
                ay[c, where, :] = later * w[where, :]

    firsts = [jnp.zeros((n, LANES), jnp.float32) for n in xlay.sizes]
    lasts = list(firsts)
    for x in range(nx):
        here = pl.ds(x * ny, ny)
        near, far = left[here, :], right[here, :]
        for c in range(comps):
            cells = ay[c, here, :]
            firsts[c] = firsts[c] + near * cells
            lasts[c] = lasts[c] + far * cells
        here = pl.ds(x * TILE, TILE)
        cells = ghost[here, :]
        firsts[comps] = firsts[comps] + gleft[here, :] * cells
        lasts[comps] = lasts[comps] + gright[here, :] * cells
    record = {"first": firsts, "last": lasts}
    if xlay.leads:
        pieces = [part[pl.ds(i * ny, ny), :] for i in range(5)]
        record["near"] = [pieces[0], corner * total]
        record["cross"] = [pieces[1], total]
        record["far"] = [pieces[2], end * total]
        record["head"], record["tail"] = pieces[3:4], pieces[4:5]
    write_block(xlay, block, record)
    if xlay.leads:
        slim[pl.ds(0, xlay.couple), :] = block[pl.ds(0, xlay.couple), :]
        slim[pl.ds(xlay.couple, TILE), :] = block[pl.ds(xlay.packed, TILE), :]


def x_kernel(dims, lay, lead, levels, shift, start, me_ref, *refs):
    nx, ny = dims
    count = (2 if lay.leads else 4) * levels
    state, _ = solve_lines(lay, lead, levels, me_ref[0] >> shift, refs[:count])
    xinv, ginv, ay, ghost, w, lower, higher, flows, *rest = refs[count:]
    out_any, out, field, fluxes, sems = rest[-5:]
    rows = nx * ny
    comps = len(lay.sizes) - 1
    tiles = ny // TILE
    starts, nexts, behind, ahead = state
    near, far = behind[0], ahead[0]

    def sweep(x, carry):
        span, above = pl.ds(x * ny, ny), pl.ds((x + 1) * ny, ny)
        factor = xinv[span, :]
        new = []
        for c in range(comps):
            value = (ay[c, span, :] + carry[c]) * factor
            field[c, above, :] = value
            new.append(value)
        here = pl.ds(x * TILE, TILE)
        edge = (ghost[here, :] + carry[comps]) * ginv[here, :]
        fluxes[here, :] = edge
        return tuple(new) + (edge,)

    lax.fori_loop(0, nx, sweep, tuple(starts), unroll=16)

    def back(step, carry):
        x = nx - 1 - step
        span, above = pl.ds(x * ny, ny), pl.ds((x + 1) * ny, ny)
        factor = xinv[span, :]
        weight = w[span, :]
        new = []
        for c in range(comps):
            value = field[c, above, :] + factor * carry[c]
            field[c, above, :] = value * weight
            new.append(value)
        here = pl.ds(x * TILE, TILE)
        edge = fluxes[here, :] + ginv[here, :] * carry[comps]
        fluxes[here, :] = edge * two_sides(lower[pl.ds(nx + x, 1), :], higher[pl.ds(nx + x, 1), :])
        return tuple(new) + (edge,)

    lax.fori_loop(0, nx, back, tuple(nexts), unroll=16)
    blank = jnp.zeros((comps, ny, LANES), jnp.float32)
    field[:, pl.ds(0, ny), :] = blank
    field[:, pl.ds((nx + 1) * ny, ny), :] = blank

    line = lax.broadcasted_iota(jnp.int32, (TILE, LANES), 0)

    def advect(x, carry):
        before = jnp.maximum(x - 1, 0)
        beyond = jnp.minimum(x + 1, nx - 1)

        def flow(kind, plane, t):
            begin = pl.multiple_of(kind * rows + plane * ny + t * TILE, TILE)
            return flows[pl.ds(begin, TILE), :]

        own = [flow(0, x, t) for t in range(tiles)]
        ahead_x = [flow(1, beyond, t) for t in range(tiles)]
        behind_x = [flow(2, before, t) for t in range(tiles)]
        ahead_y = [flow(3, x, t) for t in range(tiles)]
        behind_y = [flow(4, x, t) for t in range(tiles)]
        ahead_z = [flow(5, x, t) for t in range(tiles)]
        behind_z = [flow(6, x, t) for t in range(tiles)]
        for c in range(comps):

            def cells(plane, t):
                begin = pl.multiple_of((plane + 1) * ny + t * TILE, TILE)
                return field[c, pl.ds(begin, TILE), :]

            grad = [cells(x, t) for t in range(tiles)]
            ups = [pltpu.roll(ahead_y[t] * grad[t], TILE - 1, 0) for t in range(tiles)]
            downs = [pltpu.roll(behind_y[t] * grad[t], 1, 0) for t in range(tiles)]
            lowest = fluxes[pl.ds(x * TILE + c, 1), :]
            highest = fluxes[pl.ds(x * TILE + SIDE + c, 1), :]
            for t in range(tiles):
                part = own[t] * grad[t]
                part = part + ahead_x[t] * cells(x + 1, t) - behind_x[t] * cells(x - 1, t)
                enter = ups[t + 1] if t + 1 < tiles else jnp.broadcast_to(highest, (TILE, LANES))
                part = part + jnp.where(line == TILE - 1, enter, ups[t])
                enter = downs[t - 1] if t > 0 else jnp.broadcast_to(lowest, (TILE, LANES))
                part = part - jnp.where(line == 0, enter, downs[t])
                part = part + pltpu.roll(ahead_z[t] * grad[t], LANES - 1, 1)
                part = part - pltpu.roll(behind_z[t] * grad[t], 1, 1)
                out[c, pl.ds(pl.multiple_of(x * ny + t * TILE, TILE), TILE), :] = part
        return carry

    parts = 4
    share = nx // parts

    def copy(part):
        span = pl.ds(part * share * ny, share * ny)
        target = out_any.at[pl.ds(start, comps), span, :]
        return pltpu.make_async_copy(out.at[:, span, :], target, sems.at[part])

    top, bottom = pl.ds(0, ny), pl.ds(rows - ny, ny)
    for part in range(parts):
        lax.fori_loop(part * share, (part + 1) * share, advect, 0, unroll=share)
        for c in range(comps):
            if part == 0:
                out[c, top, :] = out[c, top, :] - near * starts[c]
            if part == parts - 1:
                out[c, bottom, :] = out[c, bottom, :] + far * nexts[c]
        copy(part).start()
    for part in range(parts):
        copy(part).wait()


def call(
    kernel, name, operands, outs, scratch=(), spaces=None, out_spaces=None, mebibytes=4, aliases=None
):
    params = pltpu.CompilerParams(vmem_limit_bytes=mebibytes * 1024 * 1024)
    memory = {"v": pltpu.VMEM, "k": pltpu.VMEM, "h": pltpu.HBM, "s": pltpu.SMEM}
    held = {"h": pltpu.HBM, "k": pltpu.VMEM}
    spaces = spaces or "s" + "v" * (len(operands) - 1)
    out_spaces = out_spaces or "v" * len(outs)
    operands = [
        pltpu.with_memory_space_constraint(o, held[s]) if s in held else o
        for o, s in zip(operands, spaces)
    ]
    return pl.pallas_call(
        kernel,
        name=name,
        out_shape=[
            held[s](shape, jnp.float32) if s in held else jax.ShapeDtypeStruct(shape, jnp.float32)
            for shape, s in zip(outs, out_spaces)
        ],
        in_specs=[pl.BlockSpec(memory_space=memory[s]) for s in spaces],
        out_specs=[pl.BlockSpec(memory_space=memory[s]) for s in out_spaces],
        scratch_shapes=list(scratch),
        input_output_aliases=aliases or {},
        compiler_params=params,
        cost_estimate=pl.CostEstimate(flops=10**9, bytes_accessed=10**7, transcendentals=0),
    )(*operands)


def exchange(rows, axis, bit):
    count = lax.axis_size(axis)
    return lax.ppermute(rows, axis, [(i, i ^ (1 << bit)) for i in range(count)])


class Ladder:
    def __init__(self, lay, axis, shift, me, send, keep, lead=None):
        self.lay, self.axis, self.shift, self.me, self.lead = lay, axis, shift, me, lead
        self.levels = (lax.axis_size(axis) - 1).bit_length()
        self.owns, self.gots, self.outgoing = [keep], [], send

    def send(self):
        self.gots.append(exchange(self.outgoing, self.axis, len(self.gots)))

    def merge(self, beside=(), apart=None):
        level = len(self.owns) - 1
        top = level == self.levels - 2
        leader = self.lead or self
        coupled = () if self.lay.leads else (leader.owns[level], leader.gots[level])
        shapes = [(self.lay.rows, LANES)] + ([(self.lay.side_rows, LANES)] if top else [])
        if apart is not None:
            merged, self.gots[0], *side = call(
                functools.partial(first_merge_kernel, self.lay, self.shift, top),
                "merge_" + self.axis,
                (self.me, self.owns[0], self.gots[0], apart) + tuple(beside),
                shapes[:1] + shapes,
            )
            self.owns.append(merged)
            self.outgoing = side[-1] if top else merged
            return
        merged = call(
            functools.partial(merge_kernel, self.lay, leader.lay, self.shift + level, top),
            "merge_" + self.axis,
            (self.me, self.owns[-1], self.gots[-1]) + coupled + tuple(beside),
            shapes,
        )
        self.owns.append(merged[0])
        self.outgoing = merged[-1]

    def records(self):
        found = (*self.owns, *self.gots)
        return found if self.lay.leads else found + (*self.lead.owns, *self.lead.gots)


def on_device(cotangent, diffusion, phase, courant, upwind):
    comps, nx, ny, nz = cotangent.shape
    shift = (lax.axis_size("gy") - 1).bit_length()
    rows = nx * ny
    half = nx // 2
    size = comps // 2
    starts = (0, size)
    counts = (size, comps - size)
    ylays = [Layout([half] * n, 1, 2, half, g == 0) for g, n in enumerate(counts)]
    xlays = [Layout([ny] * n + [TILE], 2, 1, ny, g == 0) for g, n in enumerate(counts)]
    me = lax.axis_index(("gx", "gy")).astype(jnp.int32).reshape(1)

    def vmem(*shape, dtype=jnp.float32):
        return pltpu.VMEM(shape, dtype)

    flat = (rows, nz)
    cot = cotangent.reshape(comps, rows, nz)
    cour = courant.reshape(3, rows, nz)
    upw = upwind.reshape(3, rows, nz)
    n = counts[0]
    keep, send, az, w, inv, left, right, phi, psi, cot_next = call(
        functools.partial(lead_z_kernel, (nx, ny), ylays[0]),
        "z_solve_lead",
        (me, cot, diffusion.reshape(flat), phase.reshape(flat), cour, upw),
        [(ylays[0].rows, nz)] * 2 + [(n, rows, nz)] + [flat] * 6 + [(counts[1], rows, nz)],
        [
            vmem(n, rows, nz), vmem(*flat), vmem(*flat, dtype=jnp.int32),
            vmem(*flat), vmem(*flat, dtype=jnp.int32),
            vmem(*flat), vmem(*flat), vmem(*flat), vmem(2 * ylays[0].rows, nz),
            pltpu.SemaphoreType.DMA((n,)), pltpu.SemaphoreType.DMA((5,)),
        ],
        spaces="shhhhh",
        mebibytes=12,
    )
    lead = Ladder(ylays[0], "gy", 0, me, send, keep)
    lead.send()
    azs = [az]
    n = counts[1]
    keep, send, az = call(
        functools.partial(next_z_kernel, (nx, ny), ylays[1]),
        "z_solve_next",
        (me, cot_next, phi, psi, w, left, right),
        [(ylays[1].rows, nz)] * 2 + [(n, rows, nz)],
        [vmem(2 * ylays[1].rows, nz)],
        mebibytes=8,
    )
    azs.append(az)
    follow = Ladder(ylays[1], "gy", 0, me, send, keep, lead)
    follow.send()
    beside = (send,)
    for level in range(lead.levels - 1):
        lead.merge(beside)
        lead.send()
        follow.merge()
        follow.send()
        beside = (follow.outgoing,)
        if level == 0:
            part, xinv, xleft, xright, flows = call(
                functools.partial(coef_kernel, (nx, ny)),
                "x_coefficients",
                (w, cour, upw, lead.owns[1]),
                [(5 * ny, nz), flat, flat, flat, (7 * rows, nz)],
                spaces="vvvv",
                mebibytes=8,
            )
            beside = (part, follow.outgoing)
            apart = exchange(part, "gx", 0)
    ladders, mets, answers = (lead, follow), [], []
    for g, ladder in enumerate(ladders):
        answer, passed = call(
            functools.partial(solve_kernel, ylays[g], ylays[0], ladder.levels),
            "y_reduced",
            (me,) + ladder.records() + (beside + (apart,) if g == 0 else ()),
            [(ylays[g].answer_rows, nz)] * 2,
        )
        answers.append(answer)
        mets.append(exchange(passed, "gy", 0))
    ays, ghosts, climbs = [], [], []
    for g in range(2):
        common = (me, azs[g], answers[g], mets[g], w, inv, xleft, xright)
        outs = [(counts[g], rows, nz), (nx * TILE, nz)]
        scratch = [vmem(2 * ylays[g].answer_rows, nz)]
        body = functools.partial(y_kernel, (nx, ny), ylays[g], xlays[g])
        if g == 0:
            block, slim, ay, ghost, ginv, gleft, gright, before, after = call(
                body,
                "y_solve_lead",
                common + (part,),
                [(xlays[0].rows, nz), (xlays[0].couple + TILE, nz)]
                + outs + [(nx * TILE, nz)] * 3 + [(2 * nx, nz)] * 2,
                scratch,
                mebibytes=6,
            )
        else:
            block, ay, ghost = call(
                body,
                "y_solve_next",
                common + (before, after, gleft, gright),
                [(xlays[1].rows, nz)] + outs,
                scratch,
                mebibytes=6,
            )
        ays.append(ay)
        ghosts.append(ghost)
        outgoing, leader = (block, climbs[0]) if g else (slim, None)
        climbs.append(Ladder(xlays[g], "gx", shift, me, outgoing, block, leader))
        climbs[g].send()
    beside = (block,)
    for level in range(climbs[0].levels - 1):
        for ladder in climbs:
            leads = ladder.lay.leads
            ladder.merge(beside if leads else (), apart if leads and level == 0 else None)
            ladder.send()
        beside = (climbs[1].outgoing,)
    grad = None
    for g, ladder in enumerate(climbs):
        operands = (me,) + ladder.records() + (
            xinv, ginv, ays[g], ghosts[g], w, before, after, flows,
        )
        spaces = "s" + "v" * (len(operands) - 1)
        aliases = None
        if g:
            aliases = {len(operands): 0}
            operands, spaces = operands + (grad,), spaces + "h"
        (grad,) = call(
            functools.partial(
                x_kernel, (nx, ny), xlays[g], xlays[0], ladder.levels, shift, starts[g]
            ),
            "x_solve",
            operands,
            [(comps, rows, nz)],
            [
                vmem(counts[g], rows, nz), vmem(counts[g], rows + 2 * ny, nz), vmem(nx * TILE, nz),
                pltpu.SemaphoreType.DMA((4,)),
            ],
            spaces=spaces,
            out_spaces="h",
            mebibytes=8,
            aliases=aliases,
        )
    return grad.reshape(comps, nx, ny, nz)


def solution(mesh):
    placed = (
        P(None, "gx", "gy", None),
        P("gx", "gy", None),
        P("gx", "gy", None),
        P(None, "gx", "gy", None),
        P(None, "gx", "gy", None),
    )
    return jax.shard_map(
        on_device, mesh=mesh, in_specs=placed, out_specs=P(None, "gx", "gy", None), check_vma=False
    )
```

```python
import functools

import jax
import jax.numpy as jnp
from jax import lax
from jax.experimental import pallas as pl
from jax.experimental.pallas import tpu as pltpu
from jax.sharding import PartitionSpec as P

COMPS = 6
LANES = 128
TILE = 8
SIDE = TILE // 2


def weight_of(diffusion, phase):
    return 1.0 / (diffusion * (1.0 + 3.0 * phase.astype(jnp.float32)))


def growing_step(value, slope, weight):
    slope = slope + weight * value
    return value + slope, slope


def split3(cells):
    high = cells.astype(jnp.bfloat16)
    rest = cells - high.astype(jnp.float32)
    middle = rest.astype(jnp.bfloat16)
    low = (rest - middle.astype(jnp.float32)).astype(jnp.bfloat16)
    return high, middle, low


def sum_matrix():
    row = lax.broadcasted_iota(jnp.int32, (2 * LANES, 2 * LANES), 0)
    col = lax.broadcasted_iota(jnp.int32, (2 * LANES, 2 * LANES), 1)
    before = (row < LANES) & (col < LANES) & (row <= col)
    after = (row >= LANES) & (col >= LANES) & (row > col)
    return jnp.where(before | after, 1.0, 0.0).astype(jnp.bfloat16)


class Layout:
    def __init__(self, sizes, groups, edges, lines, leads):
        self.sizes, self.groups, self.edges, self.lines, self.leads = sizes, groups, edges, lines, leads
        self.offsets = [sum(sizes[:i]) for i in range(len(sizes))]
        self.total = sum(sizes)
        packed = TILE if groups > 1 else 0
        self.couple = 2 * self.total
        self.packed = self.couple + 3 * lines
        self.edge = self.packed + packed
        self.side_couple = self.total
        self.side_packed = self.side_couple + lines
        self.side_edge = self.side_packed + packed
        extra = 2 * edges * lines
        self.rows = self.edge + extra if leads else self.couple
        self.side_rows = self.side_edge + extra // 2 if leads else self.total
        self.answer_rows = 2 * self.total + (extra if leads else 0)

    def group(self, piece):
        return 1 if self.groups > 1 and piece == len(self.sizes) - 1 else 0


def read_pieces(lay, ref, base=0):
    return [ref[pl.ds(base + o, n), :] for o, n in zip(lay.offsets, lay.sizes)]


def write_pieces(lay, ref, values, base=0):
    for o, n, value in zip(lay.offsets, lay.sizes, values):
        ref[pl.ds(base + o, n), :] = value


def read_rows(ref, base, count, lines):
    return [ref[pl.ds(base + i * lines, lines), :] for i in range(count)]


def write_rows(ref, base, values, lines):
    for i, value in enumerate(values):
        ref[pl.ds(base + i * lines, lines), :] = value


def two_sides(low, high):
    return jnp.concatenate(
        [jnp.broadcast_to(low, (SIDE, LANES)), jnp.broadcast_to(high, (SIDE, LANES))], axis=0
    )


def read_pair(ref, row):
    return two_sides(ref[pl.ds(row, 1), :], ref[pl.ds(row + 1, 1), :])


def write_pair(ref, row, value):
    ref[pl.ds(row, 1), :] = value[:1]
    ref[pl.ds(row + 1, 1), :] = value[SIDE : SIDE + 1]


def read_block(lay, ref, lead, lead_ref):
    n = lead.lines
    block = {"first": read_pieces(lay, ref), "last": read_pieces(lay, ref, lay.total)}
    for e, name in enumerate(("near", "cross", "far")):
        entry = [lead_ref[pl.ds(lead.couple + e * n, n), :]]
        if lead.groups > 1:
            entry.append(read_pair(lead_ref, lead.packed + 2 * e))
        block[name] = entry
    block["head"] = read_rows(lead_ref, lead.edge, lead.edges, n)
    block["tail"] = read_rows(lead_ref, lead.edge + lead.edges * n, lead.edges, n)
    return block


def write_block(lay, ref, block):
    n = lay.lines
    write_pieces(lay, ref, block["first"])
    write_pieces(lay, ref, block["last"], lay.total)
    if not lay.leads:
        return
    for e, name in enumerate(("near", "cross", "far")):
        ref[pl.ds(lay.couple + e * n, n), :] = block[name][0]
        if lay.groups > 1:
            write_pair(ref, lay.packed + 2 * e, block[name][1])
    if lay.groups > 1:
        ref[pl.ds(lay.packed + 6, 2), :] = jnp.zeros((2, LANES), jnp.float32)
    write_rows(ref, lay.edge, block["head"], n)
    write_rows(ref, lay.edge + lay.edges * n, block["tail"], n)


def pick(upper, low, high):
    if isinstance(low, list):
        return [pick(upper, a, b) for a, b in zip(low, high)]
    return jnp.where(jnp.full(low.shape, upper, jnp.int32) == 1, high, low)


def write_side(lay, ref, block, upper):
    n = lay.lines
    write_pieces(lay, ref, pick(upper, block["last"], block["first"]))
    if not lay.leads:
        return
    pair = pick(upper, block["far"], block["near"])
    ref[pl.ds(lay.side_couple, n), :] = pair[0]
    if lay.groups > 1:
        ref[pl.ds(lay.side_packed, TILE), :] = pair[1]
    write_rows(ref, lay.side_edge, pick(upper, block["tail"], block["head"]), n)


def read_side(lay, ref, lead, lead_ref):
    n = lead.lines
    couple = [lead_ref[pl.ds(lead.side_couple, n), :]]
    if lead.groups > 1:
        couple.append(lead_ref[pl.ds(lead.side_packed, TILE), :])
    return read_pieces(lay, ref), couple, read_rows(lead_ref, lead.side_edge, lead.edges, n)


def ordered(upper, own, other):
    low = {name: pick(upper, own[name], other[name]) for name in own}
    high = {name: pick(upper, other[name], own[name]) for name in own}
    return low, high


def joint(low, high):
    return [1.0 / (1.0 - far * near) for far, near in zip(low["far"], high["near"])]


def merge(lay, low, high):
    shrink = joint(low, high)
    groups = range(len(shrink))
    to_low = [low["cross"][g] * shrink[g] for g in groups]
    to_high = [high["cross"][g] * shrink[g] for g in groups]
    span = range(len(lay.sizes))
    of = lay.group
    block = {
        "first": [
            low["first"][i]
            + to_low[of(i)] * (high["first"][i] + high["near"][of(i)] * low["last"][i])
            for i in span
        ],
        "last": [
            high["last"][i]
            + to_high[of(i)] * (low["last"][i] + low["far"][of(i)] * high["first"][i])
            for i in span
        ],
    }
    block["near"] = [low["near"][g] + to_low[g] * low["cross"][g] * high["near"][g] for g in groups]
    block["cross"] = [to_low[g] * high["cross"][g] for g in groups]
    block["far"] = [high["far"][g] + to_high[g] * high["cross"][g] * low["far"][g] for g in groups]
    block["head"] = low["head"]
    block["tail"] = high["tail"]
    return block


def inner(lay, low, high, before, after):
    shrink = joint(low, high)
    low_last, high_first = [], []
    for i in range(len(lay.sizes)):
        g = lay.group(i)
        left = low["last"][i] + low["cross"][g] * before[i]
        right = high["first"][i] + high["cross"][g] * after[i]
        low_last.append((left + low["far"][g] * right) * shrink[g])
        high_first.append((right + high["near"][g] * left) * shrink[g])
    return low_last, high_first


def merge_kernel(lay, lead, bit, top, me_ref, own, other, *refs):
    out, *side = refs[-2:] if top else refs[-1:]
    lead_own, lead_other = (own, other) if lay.leads else refs[:2]
    upper = (me_ref[0] >> bit) & 1
    low, high = ordered(
        upper, read_block(lay, own, lead, lead_own), read_block(lay, other, lead, lead_other)
    )
    block = merge(lay, low, high)
    write_block(lay, out, block)
    if top:
        write_side(lay, side[0], block, (me_ref[0] >> (bit + 1)) & 1)


def relay_merge_kernel(lay, bit, me_ref, own, other, held, out, passed):
    passed[...] = held[...]
    merge_kernel(lay, lay, bit, False, me_ref, own, other, out)


def joint_merge_kernel(lay, lead, bit, me_ref, own, other, lead_own, lead_other, side, out, joint):
    joint[pl.ds(0, lead.side_rows), :] = side[...]
    rest = joint.at[pl.ds(lead.side_rows, lay.side_rows)]
    merge_kernel(lay, lead, bit, True, me_ref, own, other, lead_own, lead_other, out, rest)


def first_merge_kernel(lay, bit, top, me_ref, own, slim, apart, *refs):
    out, joined, *side = refs[-3:] if top else refs[-2:]
    joined[pl.ds(0, lay.couple), :] = slim[pl.ds(0, lay.couple), :]
    joined[pl.ds(lay.packed, TILE), :] = slim[pl.ds(lay.couple, TILE), :]
    joined[pl.ds(lay.couple, 3 * lay.lines), :] = apart[pl.ds(0, 3 * lay.lines), :]
    edges = 2 * lay.edges * lay.lines
    joined[pl.ds(lay.edge, edges), :] = apart[pl.ds(3 * lay.lines, edges), :]
    merge_kernel(lay, lay, bit, top, me_ref, own, joined, out, *side)


def solve_lines(lay, lead, levels, me, refs):
    owns, gots = refs[:levels], refs[levels : 2 * levels]
    lead_owns, lead_gots = owns, gots
    if not lay.leads:
        lead_owns, lead_gots = refs[2 * levels : 3 * levels], refs[3 * levels : 4 * levels]
    top = levels - 1
    upper = (me >> top) & 1
    own = read_block(lay, owns[top], lead, lead_owns[top])
    met, met_couple, met_edge = read_side(lay, gots[top], lead, lead_gots[top])
    facing = pick(upper, own["last"], own["first"])
    couple = pick(upper, own["far"], own["near"])
    shrink = [1.0 / (1.0 - a * b) for a, b in zip(met_couple, couple)]
    found = []
    for i in range(len(lay.sizes)):
        g = lay.group(i)
        found.append((met[i] + met_couple[g] * facing[i]) * shrink[g])
    zeros = [jnp.zeros_like(v) for v in found]
    blank = [jnp.zeros_like(v) for v in met_edge]
    state = (
        pick(upper, zeros, found), pick(upper, found, zeros),
        pick(upper, blank, met_edge), pick(upper, met_edge, blank),
    )
    partner = None
    for level in reversed(range(top)):
        upper = (me >> level) & 1
        low, high = ordered(
            upper,
            read_block(lay, owns[level], lead, lead_owns[level]),
            read_block(lay, gots[level], lead, lead_gots[level]),
        )
        before, after, behind, ahead = state
        low_last, high_first = inner(lay, low, high, before, after)
        lower = (before, high_first, behind, high["head"])
        higher = (low_last, after, low["tail"], ahead)
        state = tuple(pick(upper, a, b) for a, b in zip(lower, higher))
        partner = tuple(pick(upper, a, b) for a, b in zip(higher, lower))
    return state, partner


def write_answer(lay, ref, state):
    before, after, behind, ahead = state
    write_pieces(lay, ref, before)
    write_pieces(lay, ref, after, lay.total)
    if lay.leads:
        write_rows(ref, 2 * lay.total, behind + ahead, lay.lines)


def solve_kernel(lay, lead, levels, me_ref, *refs):
    state, partner = solve_lines(lay, lead, levels, me_ref[0], refs[:-2])
    write_answer(lay, refs[-2], state)
    write_answer(lay, refs[-1], partner)


def corners(weights):
    one = jnp.ones_like(weights[0])
    value, slope, chain = one, one, [one]
    for weight in weights:
        value, slope = growing_step(value, slope, weight)
        chain.append(value)
    back, fall, backs = one, one, []
    for weight in reversed(weights):
        backs.append(back)
        back, fall = growing_step(back, fall, weight)
    backs.reverse()
    return chain, backs, 1.0 / value


def post(lay, both, row, cells):
    half = cells.shape[0] // 2
    for h in range(2):
        both[pl.ds(h * lay.rows + row, half), :] = cells[h * half : (h + 1) * half]


def z_part(dims, lay, me_ref, cot, phi, psi, w, left, right, arrived, az, both, keep, send):
    nx, ny = dims
    tiles = nx * ny // LANES
    sums = sum_matrix()
    for c in range(len(lay.sizes)):
        arrived(c)
        for t in range(tiles):
            span = pl.ds(t * LANES, LANES)
            cells, up, down = cot[c, span, :], phi[span, :], psi[span, :]
            wide = jnp.concatenate([up * cells, down * cells], axis=1)
            found = jnp.dot(
                jnp.concatenate(split3(wide), axis=0), sums, preferred_element_type=jnp.float32
            )
            found = found[:LANES] + (found[LANES : 2 * LANES] + found[2 * LANES :])
            az[c, span, :] = w[span, :] * (down * found[:, :LANES] + up * found[:, LANES:])
        first = jnp.zeros((nx, LANES), jnp.float32)
        last = jnp.zeros((nx, LANES), jnp.float32)
        for y in range(ny):
            cells = az[c, pl.ds(y, nx, stride=ny), :]
            span = pl.ds(y * nx, nx)
            first = first + left[span, :] * cells
            last = last + right[span, :] * cells
        post(lay, both, lay.offsets[c], first)
        post(lay, both, lay.total + lay.offsets[c], last)
    mine = me_ref[0] & 1
    keep[...] = both[pl.ds(pl.multiple_of(mine * lay.rows, TILE), lay.rows), :]
    send[...] = both[pl.ds(pl.multiple_of((1 - mine) * lay.rows, TILE), lay.rows), :]


def lead_z_kernel(
    dims, lay, me_ref, cot_any, diff_any, phase_any, cour_any, upw_any,
    keep, send, az, w, left, right, phi, psi, later,
    cot, diff, phase, cour, upw, wt, pht, pst, both, in_sems, sems,
):
    nx, ny = dims
    tiles = nx * ny // LANES
    half = nx // 2
    count = len(lay.sizes)
    ahead = pltpu.make_async_copy(cot_any.at[pl.ds(count, later.shape[0])], later, sems.at[4])
    small = [(diff_any, diff), (phase_any, phase), (cour_any.at[1], cour), (upw_any.at[1], upw)]
    for i, (source, target) in enumerate(small):
        pltpu.make_async_copy(source, target, sems.at[i]).start()
    for c in range(count):
        pltpu.make_async_copy(cot_any.at[c], cot.at[c], in_sems.at[c]).start()
    ahead.start()

    for i, (source, target) in enumerate(small[:2]):
        pltpu.make_async_copy(source, target, sems.at[i]).wait()
    w[...] = weight_of(diff[...], phase[...])
    for t in range(tiles):
        span = pl.ds(t * LANES, LANES)
        wt[span, :] = w[span, :].T
    ones = jnp.ones((tiles, LANES), jnp.float32)
    value, slope = ones, ones
    back, fall = ones, ones
    for k in range(LANES):
        here = pl.ds(k, tiles, stride=LANES)
        pht[here, :] = value
        value, slope = growing_step(value, slope, wt[here, :])
        there = pl.ds(LANES - 1 - k, tiles, stride=LANES)
        pst[there, :] = back
        back, fall = growing_step(back, fall, wt[there, :])
    scale = 1.0 / value
    for t in range(tiles):
        span = pl.ds(t * LANES, LANES)
        phi[span, :] = pht[span, :].T
        psi[span, :] = (pst[span, :] * scale[t : t + 1]).T

    chain, backs, total = corners([w[pl.ds(y, nx, stride=ny), :] for y in range(ny)])
    for y in range(ny):
        span = pl.ds(y * nx, nx)
        left[span, :] = backs[y] * total
        right[span, :] = chain[y] * total
    post(lay, both, lay.couple, backs[0] * total)
    post(lay, both, lay.couple + half, total)
    post(lay, both, lay.couple + 2 * half, chain[ny - 1] * total)
    for i, (source, target) in enumerate(small[2:]):
        pltpu.make_async_copy(source, target, sems.at[2 + i]).wait()
    for e, y in enumerate((0, ny - 1)):
        edge = pl.ds(y, nx, stride=ny)
        weight = w[edge, :]
        up = cour[edge, :] * upw[edge, :].astype(jnp.float32)
        flow = up if e == 0 else cour[edge, :] - up
        post(lay, both, lay.edge + 2 * e * half, weight)
        post(lay, both, lay.edge + (2 * e + 1) * half, weight * flow)

    def arrived(c):
        pltpu.make_async_copy(cot_any.at[c], cot.at[c], in_sems.at[c]).wait()

    z_part(dims, lay, me_ref, cot, phi, psi, w, left, right, arrived, az, both, keep, send)
    ahead.wait()


def next_z_kernel(dims, lay, me_ref, cot, phi, psi, w, left, right, keep, send, az, both):
    z_part(
        dims, lay, me_ref, cot, phi, psi, w, left, right, lambda c: None, az, both, keep, send
    )


def coef_kernel(dims, w, courant, upwind, after, block, inv, xinv, left, right, flows):
    del after
    nx, ny = dims
    rows = nx * ny
    one = jnp.ones((ny, LANES), jnp.float32)
    value, slope, back, fall = one, one, one, one
    for k in range(nx):
        low, high = pl.ds(k * ny, ny), pl.ds((nx - 1 - k) * ny, ny)
        right[low, :] = value
        left[high, :] = back
        new_value, slope = growing_step(value, slope, w[low, :])
        xinv[low, :] = value / new_value
        end, value = value, new_value
        corner = back
        back, fall = growing_step(back, fall, w[high, :])
    total = 1.0 / value
    block[pl.ds(0, ny), :] = corner * total
    block[pl.ds(ny, ny), :] = total
    block[pl.ds(2 * ny, ny), :] = end * total
    value = jnp.ones((nx, LANES), jnp.float32)
    slope = value
    for y in range(ny):
        new_value, slope = growing_step(value, slope, w[pl.ds(y, nx, stride=ny), :])
        inv[pl.ds(y * nx, nx), :] = value / new_value
        value = new_value

    lane = lax.broadcasted_iota(jnp.int32, (ny, LANES), 1)

    def plane(x, carry):
        span = pl.ds(x * ny, ny)
        scale = w[span, :] * total
        left[span, :] = left[span, :] * scale
        right[span, :] = right[span, :] * scale
        own = one
        for d in range(3):
            flow = courant[d, span, :]
            up = flow * upwind[d, span, :].astype(jnp.float32)
            down = flow - up
            own = own + (down - up)
            if d == 2:
                up = jnp.where(lane == 0, 0.0, up)
                down = jnp.where(lane == LANES - 1, 0.0, down)
            flows[pl.ds((1 + 2 * d) * rows + x * ny, ny), :] = up
            flows[pl.ds((2 + 2 * d) * rows + x * ny, ny), :] = down
        flows[span, :] = own
        return carry

    lax.fori_loop(0, nx, plane, 0, unroll=4)
    first, last = pl.ds(0, ny), pl.ds(rows - ny, ny)
    block[pl.ds(3 * ny, ny), :] = w[first, :] * flows[pl.ds(rows, ny), :]
    block[pl.ds(4 * ny, ny), :] = w[last, :] * flows[pl.ds(2 * rows + rows - ny, ny), :]


def sides(before, after, x):
    return two_sides(before[pl.ds(x, 1), :], after[pl.ds(x, 1), :])


def y_kernel(dims, ylay, xlay, me_ref, az, own, got, w, inv, xinv, *refs):
    nx, ny = dims
    half = nx // 2
    comps = len(ylay.sizes)
    if xlay.leads:
        part, block, slim, field, ghost, ginv, gleft, gright, before, after, ay, joined = refs
    else:
        before, after, ginv, block, field, ghost, ay, joined = refs
    mine = me_ref[0] & 1
    span = ylay.answer_rows
    joined[pl.ds(pl.multiple_of(mine * span, TILE), span), :] = own[...]
    joined[pl.ds(pl.multiple_of((1 - mine) * span, TILE), span), :] = got[...]
    if xlay.leads:
        for h in range(2):
            for e in range(2):
                where = pl.ds(e * nx + h * half, half)
                row = h * span + 2 * ylay.total + e * half
                before[where, :] = joined[pl.ds(row, half), :]
                after[where, :] = joined[pl.ds(row + 2 * half, half), :]
        one = jnp.ones((TILE, LANES), jnp.float32)
        value, slope, back, fall = one, one, one, one
        for k in range(nx):
            low, high = pl.ds(k * TILE, TILE), pl.ds((nx - 1 - k) * TILE, TILE)
            gright[low, :] = value
            gleft[high, :] = back
            new_value, slope = growing_step(value, slope, sides(before, after, k))
            ginv[low, :] = value / new_value
            end, value = value, new_value
            corner = back
            back, fall = growing_step(back, fall, sides(before, after, nx - 1 - k))
        total = 1.0 / value
        for x in range(nx):
            here = pl.ds(x * TILE, TILE)
            scale = sides(before, after, nx + x) * total
            gleft[here, :] = gleft[here, :] * scale
            gright[here, :] = gright[here, :] * scale

    ghost[...] = jnp.zeros(ghost.shape, jnp.float32)
    for c in range(comps):
        for h in range(2):
            piece = pl.ds(h * half, half)
            fb = joined[pl.ds(h * span + c * half, half), :]
            fa = joined[pl.ds(h * span + ylay.total + c * half, half), :]
            ghost[pl.ds(h * half * TILE + c, half, stride=TILE), :] = before[piece, :] * fb
            ghost[pl.ds(h * half * TILE + SIDE + c, half, stride=TILE), :] = after[piece, :] * fa
            swept, chain = fb, []
            for y in range(ny):
                cells = az[c, pl.ds(h * half * ny + y, half, stride=ny), :]
                swept = (cells + swept) * inv[pl.ds(y * nx + h * half, half), :]
                chain.append(swept)
            later = fa
            for y in reversed(range(ny)):
                where = pl.ds(h * half * ny + y, half, stride=ny)
                later = chain[y] + inv[pl.ds(y * nx + h * half, half), :] * later
                ay[c, where, :] = later * w[where, :]

    swept = [jnp.zeros((n, LANES), jnp.float32) for n in xlay.sizes]
    for x in range(nx):
        here, there = pl.ds(x * ny, ny), pl.ds(x * TILE, TILE)
        for c in range(comps):
            swept[c] = (ay[c, here, :] + swept[c]) * xinv[here, :]
            ay[c, here, :] = swept[c]
        swept[comps] = (ghost[there, :] + swept[comps]) * ginv[there, :]
        ghost[there, :] = swept[comps]
    lasts, solved = list(swept), list(swept)
    for x in reversed(range(nx)):
        here, there = pl.ds(x * ny, ny), pl.ds(x * TILE, TILE)
        for c in range(comps):
            if x + 1 < nx:
                solved[c] = ay[c, here, :] + xinv[here, :] * solved[c]
            field[c, here, :] = solved[c] * w[here, :]
        if x + 1 < nx:
            solved[comps] = ghost[there, :] + ginv[there, :] * solved[comps]
        ghost[there, :] = solved[comps] * sides(before, after, nx + x)
    record = {"first": solved, "last": lasts}
    if xlay.leads:
        pieces = [part[pl.ds(i * ny, ny), :] for i in range(5)]
        record["near"] = [pieces[0], corner * total]
        record["cross"] = [pieces[1], total]
        record["far"] = [pieces[2], end * total]
        record["head"], record["tail"] = pieces[3:4], pieces[4:5]
    write_block(xlay, block, record)
    if xlay.leads:
        slim[pl.ds(0, xlay.couple), :] = block[pl.ds(0, xlay.couple), :]
        slim[pl.ds(xlay.couple, TILE), :] = block[pl.ds(xlay.packed, TILE), :]


def x_kernel(dims, lays, levels, shift, me_ref, *refs):
    nx, ny = dims
    lead, follow = lays
    owns, gots, later_owns, later_gots = (refs[i * levels : (i + 1) * levels] for i in range(4))
    later_gots = later_gots[:-1]
    (left, right, gleft, gright, flows, *rest) = refs[4 * levels - 1 :]
    inputs, ghosts = rest[:2], rest[2:4]
    out_any, out, field, fluxes, sems = rest[4:]
    rows = nx * ny
    tiles = ny // TILE
    me = me_ref[0] >> shift
    joint = gots[-1]
    gots = gots[:-1] + (joint.at[pl.ds(0, lead.side_rows)],)
    later_gots = later_gots + (joint.at[pl.ds(lead.side_rows, follow.side_rows)],)
    first, _ = solve_lines(lead, lead, levels, me, owns + gots)
    second, _ = solve_lines(follow, lead, levels, me, later_owns + later_gots + owns + gots)
    near, far = first[2][0], first[3][0]
    groups = (first, second)
    place = [(g, c) for g, lay in enumerate(lays) for c in range(len(lay.sizes) - 1)]
    starts = [groups[g][0][c] for g, c in place]
    nexts = [groups[g][1][c] for g, c in place]
    comps = len(place)

    def fill(x, carry):
        span, above = pl.ds(x * ny, ny), pl.ds((x + 1) * ny, ny)
        lower, upper = left[span, :], right[span, :]
        for i, (g, c) in enumerate(place):
            field[i, above, :] = inputs[g][c, span, :] + lower * starts[i] + upper * nexts[i]
        here = pl.ds(x * TILE, TILE)
        lower, upper = gleft[here, :], gright[here, :]
        for g in range(2):
            fluxes[g, here, :] = ghosts[g][here, :] + lower * groups[g][0][-1] + upper * groups[g][1][-1]
        return carry

    lax.fori_loop(0, nx, fill, 0, unroll=8)
    blank = jnp.zeros((comps, ny, LANES), jnp.float32)
    field[:, pl.ds(0, ny), :] = blank
    field[:, pl.ds((nx + 1) * ny, ny), :] = blank

    line = lax.broadcasted_iota(jnp.int32, (TILE, LANES), 0)

    def advect(x, carry):
        before = jnp.maximum(x - 1, 0)
        beyond = jnp.minimum(x + 1, nx - 1)

        def flow(kind, plane, t):
            begin = pl.multiple_of(kind * rows + plane * ny + t * TILE, TILE)
            return flows[pl.ds(begin, TILE), :]

        own = [flow(0, x, t) for t in range(tiles)]
        ahead_x = [flow(1, beyond, t) for t in range(tiles)]
        behind_x = [flow(2, before, t) for t in range(tiles)]
        ahead_y = [flow(3, x, t) for t in range(tiles)]
        behind_y = [flow(4, x, t) for t in range(tiles)]
        ahead_z = [flow(5, x, t) for t in range(tiles)]
        behind_z = [flow(6, x, t) for t in range(tiles)]
        for i, (g, c) in enumerate(place):

            def cells(plane, t):
                begin = pl.multiple_of((plane + 1) * ny + t * TILE, TILE)
                return field[i, pl.ds(begin, TILE), :]

            grad = [cells(x, t) for t in range(tiles)]
            ups = [pltpu.roll(ahead_y[t] * grad[t], TILE - 1, 0) for t in range(tiles)]
            downs = [pltpu.roll(behind_y[t] * grad[t], 1, 0) for t in range(tiles)]
            lowest = fluxes[g, pl.ds(x * TILE + c, 1), :]
            highest = fluxes[g, pl.ds(x * TILE + SIDE + c, 1), :]
            for t in range(tiles):
                part = own[t] * grad[t]
                part = part + ahead_x[t] * cells(x + 1, t) - behind_x[t] * cells(x - 1, t)
                enter = ups[t + 1] if t + 1 < tiles else jnp.broadcast_to(highest, (TILE, LANES))
                part = part + jnp.where(line == TILE - 1, enter, ups[t])
                enter = downs[t - 1] if t > 0 else jnp.broadcast_to(lowest, (TILE, LANES))
                part = part - jnp.where(line == 0, enter, downs[t])
                part = part + pltpu.roll(ahead_z[t] * grad[t], LANES - 1, 1)
                part = part - pltpu.roll(behind_z[t] * grad[t], 1, 1)
                out[i, pl.ds(pl.multiple_of(x * ny + t * TILE, TILE), TILE), :] = part
        return carry

    parts = 8
    share = nx // parts

    def copy(part):
        span = pl.ds(part * share * ny, share * ny)
        return pltpu.make_async_copy(out.at[:, span, :], out_any.at[:, span, :], sems.at[part])

    top, bottom = pl.ds(0, ny), pl.ds(rows - ny, ny)
    for part in range(parts):
        lax.fori_loop(part * share, (part + 1) * share, advect, 0, unroll=share)
        for i in range(comps):
            if part == 0:
                out[i, top, :] = out[i, top, :] - near * starts[i]
            if part == parts - 1:
                out[i, bottom, :] = out[i, bottom, :] + far * nexts[i]
        copy(part).start()
    for part in range(parts):
        copy(part).wait()


def call(
    kernel, name, operands, outs, scratch=(), spaces=None, out_spaces=None, mebibytes=4, aliases=None
):
    params = pltpu.CompilerParams(vmem_limit_bytes=mebibytes * 1024 * 1024)
    memory = {"v": pltpu.VMEM, "k": pltpu.VMEM, "h": pltpu.HBM, "s": pltpu.SMEM}
    held = {"h": pltpu.HBM, "k": pltpu.VMEM}
    spaces = spaces or "s" + "v" * (len(operands) - 1)
    out_spaces = out_spaces or "v" * len(outs)
    operands = [
        pltpu.with_memory_space_constraint(o, held[s]) if s in held else o
        for o, s in zip(operands, spaces)
    ]
    return pl.pallas_call(
        kernel,
        name=name,
        out_shape=[
            held[s](shape, jnp.float32) if s in held else jax.ShapeDtypeStruct(shape, jnp.float32)
            for shape, s in zip(outs, out_spaces)
        ],
        in_specs=[pl.BlockSpec(memory_space=memory[s]) for s in spaces],
        out_specs=[pl.BlockSpec(memory_space=memory[s]) for s in out_spaces],
        scratch_shapes=list(scratch),
        input_output_aliases=aliases or {},
        compiler_params=params,
        cost_estimate=pl.CostEstimate(flops=10**9, bytes_accessed=10**7, transcendentals=0),
    )(*operands)


def exchange(rows, axis, bit):
    count = lax.axis_size(axis)
    return lax.ppermute(rows, axis, [(i, i ^ (1 << bit)) for i in range(count)])


class Ladder:
    def __init__(self, lay, axis, shift, me, send, keep, lead=None):
        self.lay, self.axis, self.shift, self.me, self.lead = lay, axis, shift, me, lead
        self.levels = (lax.axis_size(axis) - 1).bit_length()
        self.owns, self.gots, self.outgoing = [keep], [], send

    def send(self):
        self.gots.append(exchange(self.outgoing, self.axis, len(self.gots)))

    def merge(self, beside=(), apart=None, held=None, joint=False):
        level = len(self.owns) - 1
        top = level == self.levels - 2
        lay, bit = self.lay, self.shift + level
        leader = self.lead or self
        operands = (self.me, self.owns[-1], self.gots[-1])
        if not lay.leads:
            operands += (leader.owns[level], leader.gots[level])
        shapes = [(lay.rows, LANES)] + ([(lay.side_rows, LANES)] if top else [])
        kernel = functools.partial(merge_kernel, lay, leader.lay, bit, top)
        if apart is not None:
            kernel = functools.partial(first_merge_kernel, lay, bit, top)
            operands += (apart,)
            shapes = shapes[:1] + shapes
        elif held is not None:
            kernel = functools.partial(relay_merge_kernel, lay, bit)
            operands += (held,)
            shapes.append(held.shape)
        elif joint and top:
            kernel = functools.partial(joint_merge_kernel, lay, leader.lay, bit)
            operands += (leader.outgoing,)
            shapes = [shapes[0], (leader.lay.side_rows + lay.side_rows, LANES)]
        found = call(kernel, "merge_" + self.axis, operands + tuple(beside), shapes)
        self.owns.append(found[0])
        self.outgoing = found[-1] if top else found[0]
        if apart is not None:
            self.gots[0] = found[1]
        return found[-1]

    def records(self):
        found = (*self.owns, *self.gots)
        return found if self.lay.leads else found + (*self.lead.owns, *self.lead.gots)


def on_device(cotangent, diffusion, phase, courant, upwind):
    comps, nx, ny, nz = cotangent.shape
    shift = (lax.axis_size("gy") - 1).bit_length()
    rows = nx * ny
    half = nx // 2
    size = comps // 2
    starts = (0, size)
    counts = (size, comps - size)
    ylays = [Layout([half] * n, 1, 2, half, g == 0) for g, n in enumerate(counts)]
    xlays = [Layout([ny] * n + [TILE], 2, 1, ny, g == 0) for g, n in enumerate(counts)]
    me = lax.axis_index(("gx", "gy")).astype(jnp.int32).reshape(1)

    def vmem(*shape, dtype=jnp.float32):
        return pltpu.VMEM(shape, dtype)

    flat = (rows, nz)
    cot = cotangent.reshape(comps, rows, nz)
    cour = courant.reshape(3, rows, nz)
    upw = upwind.reshape(3, rows, nz)
    n = counts[0]
    keep, send, az, w, left, right, phi, psi, cot_next = call(
        functools.partial(lead_z_kernel, (nx, ny), ylays[0]),
        "z_solve_lead",
        (me, cot, diffusion.reshape(flat), phase.reshape(flat), cour, upw),
        [(ylays[0].rows, nz)] * 2 + [(n, rows, nz)] + [flat] * 5 + [(counts[1], rows, nz)],
        [
            vmem(n, rows, nz), vmem(*flat), vmem(*flat, dtype=jnp.int32),
            vmem(*flat), vmem(*flat, dtype=jnp.int32),
            vmem(*flat), vmem(*flat), vmem(*flat), vmem(2 * ylays[0].rows, nz),
            pltpu.SemaphoreType.DMA((n,)), pltpu.SemaphoreType.DMA((5,)),
        ],
        spaces="shhhhh",
        mebibytes=12,
    )
    lead = Ladder(ylays[0], "gy", 0, me, send, keep)
    lead.send()
    azs = [az]
    n = counts[1]
    keep, send, az = call(
        functools.partial(next_z_kernel, (nx, ny), ylays[1]),
        "z_solve_next",
        (me, cot_next, phi, psi, w, left, right),
        [(ylays[1].rows, nz)] * 2 + [(n, rows, nz)],
        [vmem(2 * ylays[1].rows, nz)],
        mebibytes=8,
    )
    azs.append(az)
    send = lead.merge(held=send)
    lead.send()
    follow = Ladder(ylays[1], "gy", 0, me, send, keep, lead)
    follow.send()
    for level in range(lead.levels - 1):
        if level:
            lead.merge(beside)
            lead.send()
        follow.merge()
        follow.send()
        beside = (follow.outgoing,)
        if level == 0:
            part, inv, xinv, xleft, xright, flows = call(
                functools.partial(coef_kernel, (nx, ny)),
                "x_coefficients",
                (w, cour, upw, lead.owns[1]),
                [(5 * ny, nz), flat, flat, flat, flat, (7 * rows, nz)],
                spaces="vvvv",
                mebibytes=8,
            )
            beside = (part, follow.outgoing)
            apart = exchange(part, "gx", 0)
    ladders, mets, answers = (lead, follow), [], []
    for g, ladder in enumerate(ladders):
        answer, passed = call(
            functools.partial(solve_kernel, ylays[g], ylays[0], ladder.levels),
            "y_reduced",
            (me,) + ladder.records() + (beside + (apart,) if g == 0 else ()),
            [(ylays[g].answer_rows, nz)] * 2,
        )
        answers.append(answer)
        mets.append(exchange(passed, "gy", 0))
    fields, ghosts, climbs = [], [], []
    for g in range(2):
        common = (me, azs[g], answers[g], mets[g], w, inv, xinv)
        edge = (nx * TILE, nz)
        outs = [(counts[g], rows, nz), edge]
        scratch = [vmem(counts[g], rows, nz), vmem(2 * ylays[g].answer_rows, nz)]
        body = functools.partial(y_kernel, (nx, ny), ylays[g], xlays[g])
        if g == 0:
            block, slim, field, ghost, ginv, gleft, gright, before, after = call(
                body,
                "y_solve_lead",
                common + (part,),
                [(xlays[0].rows, nz), (xlays[0].couple + TILE, nz)]
                + outs + [edge] * 3 + [(2 * nx, nz)] * 2,
                scratch,
                mebibytes=6,
            )
            climbs.append(Ladder(xlays[0], "gx", shift, me, slim, block))
        else:
            block, field, ghost = call(
                body,
                "y_solve_next",
                common + (before, after, ginv),
                [(xlays[1].rows, nz)] + outs,
                scratch,
                mebibytes=6,
            )
            climbs.append(Ladder(xlays[1], "gx", shift, me, block, block, climbs[0]))
        fields.append(field)
        ghosts.append(ghost)
        climbs[g].send()
    beside = (block,)
    first, second = climbs
    for level in range(first.levels - 1):
        top = level == first.levels - 2
        first.merge(beside, apart if level == 0 else None)
        if not top:
            first.send()
        second.merge(joint=True)
        second.send()
        beside = (second.outgoing,)
    joint = second.gots.pop()
    (grad,) = call(
        functools.partial(x_kernel, (nx, ny), xlays, first.levels, shift),
        "x_solve",
        (me, *first.owns, *first.gots, joint, *second.owns, *second.gots)
        + (xleft, xright, gleft, gright, flows, *fields, *ghosts),
        [(comps, rows, nz)],
        [
            vmem(comps, rows, nz), vmem(comps, rows + 2 * ny, nz), vmem(2, nx * TILE, nz),
            pltpu.SemaphoreType.DMA((8,)),
        ],
        out_spaces="h",
        mebibytes=12,
    )
    return grad.reshape(comps, nx, ny, nz)


def solution(mesh):
    placed = (
        P(None, "gx", "gy", None),
        P("gx", "gy", None),
        P("gx", "gy", None),
        P(None, "gx", "gy", None),
        P(None, "gx", "gy", None),
    )
    return jax.shard_map(
        on_device, mesh=mesh, in_specs=placed, out_specs=P(None, "gx", "gy", None), check_vma=False
    )
```

```python
import functools

import jax
import jax.numpy as jnp
from jax import lax
from jax.experimental import pallas as pl
from jax.experimental.pallas import tpu as pltpu
from jax.sharding import PartitionSpec as P

COMPS = 6
LANES = 128
TILE = 8
SIDE = TILE // 2


def weight_of(diffusion, phase):
    return 1.0 / (diffusion * (1.0 + 3.0 * phase.astype(jnp.float32)))


def growing_step(value, slope, weight):
    slope = slope + weight * value
    return value + slope, slope


def split3(cells):
    high = cells.astype(jnp.bfloat16)
    rest = cells - high.astype(jnp.float32)
    middle = rest.astype(jnp.bfloat16)
    low = (rest - middle.astype(jnp.float32)).astype(jnp.bfloat16)
    return high, middle, low


def sum_matrix():
    row = lax.broadcasted_iota(jnp.int32, (2 * LANES, 2 * LANES), 0)
    col = lax.broadcasted_iota(jnp.int32, (2 * LANES, 2 * LANES), 1)
    before = (row < LANES) & (col < LANES) & (row <= col)
    after = (row >= LANES) & (col >= LANES) & (row > col)
    return jnp.where(before | after, 1.0, 0.0).astype(jnp.bfloat16)


class Layout:
    def __init__(self, sizes, groups, edges, lines, leads):
        self.sizes, self.groups, self.edges, self.lines, self.leads = sizes, groups, edges, lines, leads
        self.offsets = [sum(sizes[:i]) for i in range(len(sizes))]
        self.total = sum(sizes)
        packed = TILE if groups > 1 else 0
        self.couple = 2 * self.total
        self.packed = self.couple + 3 * lines
        self.edge = self.packed + packed
        self.side_couple = self.total
        self.side_packed = self.side_couple + lines
        self.side_edge = self.side_packed + packed
        extra = 2 * edges * lines
        self.rows = self.edge + extra if leads else self.couple
        self.side_rows = self.side_edge + extra // 2 if leads else self.total
        self.answer_rows = 2 * self.total + (extra if leads else 0)

    def group(self, piece):
        return 1 if self.groups > 1 and piece == len(self.sizes) - 1 else 0


def read_pieces(lay, ref, base=0):
    return [ref[pl.ds(base + o, n), :] for o, n in zip(lay.offsets, lay.sizes)]


def write_pieces(lay, ref, values, base=0):
    for o, n, value in zip(lay.offsets, lay.sizes, values):
        ref[pl.ds(base + o, n), :] = value


def read_rows(ref, base, count, lines):
    return [ref[pl.ds(base + i * lines, lines), :] for i in range(count)]


def write_rows(ref, base, values, lines):
    for i, value in enumerate(values):
        ref[pl.ds(base + i * lines, lines), :] = value


def two_sides(low, high):
    return jnp.concatenate(
        [jnp.broadcast_to(low, (SIDE, LANES)), jnp.broadcast_to(high, (SIDE, LANES))], axis=0
    )


def read_pair(ref, row):
    return two_sides(ref[pl.ds(row, 1), :], ref[pl.ds(row + 1, 1), :])


def write_pair(ref, row, value):
    ref[pl.ds(row, 1), :] = value[:1]
    ref[pl.ds(row + 1, 1), :] = value[SIDE : SIDE + 1]


def read_block(lay, ref, lead, lead_ref):
    n = lead.lines
    block = {"first": read_pieces(lay, ref), "last": read_pieces(lay, ref, lay.total)}
    for e, name in enumerate(("near", "cross", "far")):
        entry = [lead_ref[pl.ds(lead.couple + e * n, n), :]]
        if lead.groups > 1:
            entry.append(read_pair(lead_ref, lead.packed + 2 * e))
        block[name] = entry
    block["head"] = read_rows(lead_ref, lead.edge, lead.edges, n)
    block["tail"] = read_rows(lead_ref, lead.edge + lead.edges * n, lead.edges, n)
    return block


def write_block(lay, ref, block):
    n = lay.lines
    write_pieces(lay, ref, block["first"])
    write_pieces(lay, ref, block["last"], lay.total)
    if not lay.leads:
        return
    for e, name in enumerate(("near", "cross", "far")):
        ref[pl.ds(lay.couple + e * n, n), :] = block[name][0]
        if lay.groups > 1:
            write_pair(ref, lay.packed + 2 * e, block[name][1])
    if lay.groups > 1:
        ref[pl.ds(lay.packed + 6, 2), :] = jnp.zeros((2, LANES), jnp.float32)
    write_rows(ref, lay.edge, block["head"], n)
    write_rows(ref, lay.edge + lay.edges * n, block["tail"], n)


def pick(upper, low, high):
    if isinstance(low, list):
        return [pick(upper, a, b) for a, b in zip(low, high)]
    return jnp.where(jnp.full(low.shape, upper, jnp.int32) == 1, high, low)


def write_side(lay, ref, block, upper):
    n = lay.lines
    write_pieces(lay, ref, pick(upper, block["last"], block["first"]))
    if not lay.leads:
        return
    pair = pick(upper, block["far"], block["near"])
    ref[pl.ds(lay.side_couple, n), :] = pair[0]
    if lay.groups > 1:
        ref[pl.ds(lay.side_packed, TILE), :] = pair[1]
    write_rows(ref, lay.side_edge, pick(upper, block["tail"], block["head"]), n)


def read_side(lay, ref, lead, lead_ref):
    n = lead.lines
    couple = [lead_ref[pl.ds(lead.side_couple, n), :]]
    if lead.groups > 1:
        couple.append(lead_ref[pl.ds(lead.side_packed, TILE), :])
    return read_pieces(lay, ref), couple, read_rows(lead_ref, lead.side_edge, lead.edges, n)


def ordered(upper, own, other):
    low = {name: pick(upper, own[name], other[name]) for name in own}
    high = {name: pick(upper, other[name], own[name]) for name in own}
    return low, high


def joint(low, high):
    return [1.0 / (1.0 - far * near) for far, near in zip(low["far"], high["near"])]


def merge(lay, low, high):
    shrink = joint(low, high)
    groups = range(len(shrink))
    to_low = [low["cross"][g] * shrink[g] for g in groups]
    to_high = [high["cross"][g] * shrink[g] for g in groups]
    span = range(len(lay.sizes))
    of = lay.group
    block = {
        "first": [
            low["first"][i]
            + to_low[of(i)] * (high["first"][i] + high["near"][of(i)] * low["last"][i])
            for i in span
        ],
        "last": [
            high["last"][i]
            + to_high[of(i)] * (low["last"][i] + low["far"][of(i)] * high["first"][i])
            for i in span
        ],
    }
    block["near"] = [low["near"][g] + to_low[g] * low["cross"][g] * high["near"][g] for g in groups]
    block["cross"] = [to_low[g] * high["cross"][g] for g in groups]
    block["far"] = [high["far"][g] + to_high[g] * high["cross"][g] * low["far"][g] for g in groups]
    block["head"] = low["head"]
    block["tail"] = high["tail"]
    return block


def inner(lay, low, high, before, after):
    shrink = joint(low, high)
    low_last, high_first = [], []
    for i in range(len(lay.sizes)):
        g = lay.group(i)
        left = low["last"][i] + low["cross"][g] * before[i]
        right = high["first"][i] + high["cross"][g] * after[i]
        low_last.append((left + low["far"][g] * right) * shrink[g])
        high_first.append((right + high["near"][g] * left) * shrink[g])
    return low_last, high_first


def merge_kernel(lay, lead, bit, top, me_ref, own, other, *refs):
    out, *side = refs[-2:] if top else refs[-1:]
    lead_own, lead_other = (own, other) if lay.leads else refs[:2]
    upper = (me_ref[0] >> bit) & 1
    low, high = ordered(
        upper, read_block(lay, own, lead, lead_own), read_block(lay, other, lead, lead_other)
    )
    block = merge(lay, low, high)
    write_block(lay, out, block)
    if top:
        write_side(lay, side[0], block, (me_ref[0] >> (bit + 1)) & 1)


def first_merge_kernel(lay, bit, top, me_ref, own, slim, apart, *refs):
    out, joined, *side = refs[-3:] if top else refs[-2:]
    joined[pl.ds(0, lay.couple), :] = slim[pl.ds(0, lay.couple), :]
    joined[pl.ds(lay.packed, TILE), :] = slim[pl.ds(lay.couple, TILE), :]
    joined[pl.ds(lay.couple, 3 * lay.lines), :] = apart[pl.ds(0, 3 * lay.lines), :]
    edges = 2 * lay.edges * lay.lines
    joined[pl.ds(lay.edge, edges), :] = apart[pl.ds(3 * lay.lines, edges), :]
    merge_kernel(lay, lay, bit, top, me_ref, own, joined, out, *side)


def solve_lines(lay, lead, levels, me, refs):
    owns, gots = refs[:levels], refs[levels : 2 * levels]
    lead_owns, lead_gots = owns, gots
    if not lay.leads:
        lead_owns, lead_gots = refs[2 * levels : 3 * levels], refs[3 * levels : 4 * levels]
    top = levels - 1
    upper = (me >> top) & 1
    own = read_block(lay, owns[top], lead, lead_owns[top])
    met, met_couple, met_edge = read_side(lay, gots[top], lead, lead_gots[top])
    facing = pick(upper, own["last"], own["first"])
    couple = pick(upper, own["far"], own["near"])
    shrink = [1.0 / (1.0 - a * b) for a, b in zip(met_couple, couple)]
    found = []
    for i in range(len(lay.sizes)):
        g = lay.group(i)
        found.append((met[i] + met_couple[g] * facing[i]) * shrink[g])
    zeros = [jnp.zeros_like(v) for v in found]
    blank = [jnp.zeros_like(v) for v in met_edge]
    state = (
        pick(upper, zeros, found), pick(upper, found, zeros),
        pick(upper, blank, met_edge), pick(upper, met_edge, blank),
    )
    partner = None
    for level in reversed(range(top)):
        upper = (me >> level) & 1
        low, high = ordered(
            upper,
            read_block(lay, owns[level], lead, lead_owns[level]),
            read_block(lay, gots[level], lead, lead_gots[level]),
        )
        before, after, behind, ahead = state
        low_last, high_first = inner(lay, low, high, before, after)
        lower = (before, high_first, behind, high["head"])
        higher = (low_last, after, low["tail"], ahead)
        state = tuple(pick(upper, a, b) for a, b in zip(lower, higher))
        partner = tuple(pick(upper, a, b) for a, b in zip(higher, lower))
    return state, partner


def write_answer(lay, ref, state):
    before, after, behind, ahead = state
    write_pieces(lay, ref, before)
    write_pieces(lay, ref, after, lay.total)
    if lay.leads:
        write_rows(ref, 2 * lay.total, behind + ahead, lay.lines)


def solve_kernel(lay, lead, levels, me_ref, *refs):
    state, partner = solve_lines(lay, lead, levels, me_ref[0], refs[:-2])
    write_answer(lay, refs[-2], state)
    write_answer(lay, refs[-1], partner)


def corners(weights):
    one = jnp.ones_like(weights[0])
    value, slope, chain = one, one, [one]
    for weight in weights:
        value, slope = growing_step(value, slope, weight)
        chain.append(value)
    back, fall, backs = one, one, []
    for weight in reversed(weights):
        backs.append(back)
        back, fall = growing_step(back, fall, weight)
    backs.reverse()
    return chain, backs, 1.0 / value


def post(lay, both, row, cells):
    half = cells.shape[0] // 2
    for h in range(2):
        both[pl.ds(h * lay.rows + row, half), :] = cells[h * half : (h + 1) * half]


def z_part(dims, lay, me_ref, cot, phi, psi, w, left, right, arrived, az, both, keep, send):
    nx, ny = dims
    tiles = nx * ny // LANES
    sums = sum_matrix()
    for c in range(len(lay.sizes)):
        arrived(c)
        for t in range(tiles):
            span = pl.ds(t * LANES, LANES)
            cells, up, down = cot[c, span, :], phi[span, :], psi[span, :]
            wide = jnp.concatenate([up * cells, down * cells], axis=1)
            found = jnp.dot(
                jnp.concatenate(split3(wide), axis=0), sums, preferred_element_type=jnp.float32
            )
            found = found[:LANES] + (found[LANES : 2 * LANES] + found[2 * LANES :])
            az[c, span, :] = w[span, :] * (down * found[:, :LANES] + up * found[:, LANES:])
        first = jnp.zeros((nx, LANES), jnp.float32)
        last = jnp.zeros((nx, LANES), jnp.float32)
        for y in range(ny):
            cells = az[c, pl.ds(y, nx, stride=ny), :]
            span = pl.ds(y * nx, nx)
            first = first + left[span, :] * cells
            last = last + right[span, :] * cells
        post(lay, both, lay.offsets[c], first)
        post(lay, both, lay.total + lay.offsets[c], last)
    mine = me_ref[0] & 1
    keep[...] = both[pl.ds(pl.multiple_of(mine * lay.rows, TILE), lay.rows), :]
    send[...] = both[pl.ds(pl.multiple_of((1 - mine) * lay.rows, TILE), lay.rows), :]


def lead_z_kernel(
    dims, lay, me_ref, cot_any, diff_any, phase_any, cour_any, upw_any,
    keep, send, az, w, left, right, phi, psi, later,
    cot, diff, phase, cour, upw, wt, pht, pst, both, in_sems, sems,
):
    nx, ny = dims
    tiles = nx * ny // LANES
    half = nx // 2
    count = len(lay.sizes)
    ahead = pltpu.make_async_copy(cot_any.at[pl.ds(count, later.shape[0])], later, sems.at[4])
    small = [(diff_any, diff), (phase_any, phase), (cour_any.at[1], cour), (upw_any.at[1], upw)]
    for i, (source, target) in enumerate(small[:2]):
        pltpu.make_async_copy(source, target, sems.at[i]).start()
    for i, (source, target) in enumerate(small[:2]):
        pltpu.make_async_copy(source, target, sems.at[i]).wait()
    for c in range(count):
        pltpu.make_async_copy(cot_any.at[c], cot.at[c], in_sems.at[c]).start()
    for i, (source, target) in enumerate(small[2:]):
        pltpu.make_async_copy(source, target, sems.at[2 + i]).start()
    ahead.start()
    w[...] = weight_of(diff[...], phase[...])
    for t in range(tiles):
        span = pl.ds(t * LANES, LANES)
        wt[span, :] = w[span, :].T
    ones = jnp.ones((tiles, LANES), jnp.float32)
    value, slope = ones, ones
    back, fall = ones, ones
    for k in range(LANES):
        here = pl.ds(k, tiles, stride=LANES)
        pht[here, :] = value
        value, slope = growing_step(value, slope, wt[here, :])
        there = pl.ds(LANES - 1 - k, tiles, stride=LANES)
        pst[there, :] = back
        back, fall = growing_step(back, fall, wt[there, :])
    scale = 1.0 / value
    for t in range(tiles):
        span = pl.ds(t * LANES, LANES)
        phi[span, :] = pht[span, :].T
        psi[span, :] = (pst[span, :] * scale[t : t + 1]).T

    chain, backs, total = corners([w[pl.ds(y, nx, stride=ny), :] for y in range(ny)])
    for y in range(ny):
        span = pl.ds(y * nx, nx)
        left[span, :] = backs[y] * total
        right[span, :] = chain[y] * total
    post(lay, both, lay.couple, backs[0] * total)
    post(lay, both, lay.couple + half, total)
    post(lay, both, lay.couple + 2 * half, chain[ny - 1] * total)
    for i, (source, target) in enumerate(small[2:]):
        pltpu.make_async_copy(source, target, sems.at[2 + i]).wait()
    for e, y in enumerate((0, ny - 1)):
        edge = pl.ds(y, nx, stride=ny)
        weight = w[edge, :]
        up = cour[edge, :] * upw[edge, :].astype(jnp.float32)
        flow = up if e == 0 else cour[edge, :] - up
        post(lay, both, lay.edge + 2 * e * half, weight)
        post(lay, both, lay.edge + (2 * e + 1) * half, weight * flow)

    def arrived(c):
        pltpu.make_async_copy(cot_any.at[c], cot.at[c], in_sems.at[c]).wait()

    z_part(dims, lay, me_ref, cot, phi, psi, w, left, right, arrived, az, both, keep, send)
    ahead.wait()


def next_z_kernel(dims, lay, me_ref, cot, phi, psi, w, left, right, keep, send, az, both):
    z_part(
        dims, lay, me_ref, cot, phi, psi, w, left, right, lambda c: None, az, both, keep, send
    )


def coef_kernel(dims, w, courant, upwind, after, block, inv, xinv, left, right, flows):
    del after
    nx, ny = dims
    rows = nx * ny
    one = jnp.ones((ny, LANES), jnp.float32)
    value, slope, back, fall = one, one, one, one
    for k in range(nx):
        low, high = pl.ds(k * ny, ny), pl.ds((nx - 1 - k) * ny, ny)
        right[low, :] = value
        left[high, :] = back
        new_value, slope = growing_step(value, slope, w[low, :])
        xinv[low, :] = value / new_value
        end, value = value, new_value
        corner = back
        back, fall = growing_step(back, fall, w[high, :])
    total = 1.0 / value
    block[pl.ds(0, ny), :] = corner * total
    block[pl.ds(ny, ny), :] = total
    block[pl.ds(2 * ny, ny), :] = end * total
    value = jnp.ones((nx, LANES), jnp.float32)
    slope = value
    for y in range(ny):
        new_value, slope = growing_step(value, slope, w[pl.ds(y, nx, stride=ny), :])
        inv[pl.ds(y * nx, nx), :] = value / new_value
        value = new_value

    lane = lax.broadcasted_iota(jnp.int32, (ny, LANES), 1)

    def plane(x, carry):
        span = pl.ds(x * ny, ny)
        scale = w[span, :] * total
        left[span, :] = left[span, :] * scale
        right[span, :] = right[span, :] * scale
        own = one
        for d in range(3):
            flow = courant[d, span, :]
            up = flow * upwind[d, span, :].astype(jnp.float32)
            down = flow - up
            own = own + (down - up)
            if d == 2:
                up = jnp.where(lane == 0, 0.0, up)
                down = jnp.where(lane == LANES - 1, 0.0, down)
            flows[pl.ds((1 + 2 * d) * rows + x * ny, ny), :] = up
            flows[pl.ds((2 + 2 * d) * rows + x * ny, ny), :] = down
        flows[span, :] = own
        return carry

    lax.fori_loop(0, nx, plane, 0, unroll=4)
    first, last = pl.ds(0, ny), pl.ds(rows - ny, ny)
    block[pl.ds(3 * ny, ny), :] = w[first, :] * flows[pl.ds(rows, ny), :]
    block[pl.ds(4 * ny, ny), :] = w[last, :] * flows[pl.ds(2 * rows + rows - ny, ny), :]


def sides(before, after, x):
    return two_sides(before[pl.ds(x, 1), :], after[pl.ds(x, 1), :])


def y_kernel(dims, ylay, xlay, me_ref, az, own, got, w, inv, xinv, *refs):
    nx, ny = dims
    half = nx // 2
    comps = len(ylay.sizes)
    if xlay.leads:
        part, block, slim, field, ghost, ginv, gleft, gright, before, after, ay, joined = refs
    else:
        before, after, ginv, block, field, ghost, ay, joined = refs
    mine = me_ref[0] & 1
    span = ylay.answer_rows
    joined[pl.ds(pl.multiple_of(mine * span, TILE), span), :] = own[...]
    joined[pl.ds(pl.multiple_of((1 - mine) * span, TILE), span), :] = got[...]
    if xlay.leads:
        for h in range(2):
            for e in range(2):
                where = pl.ds(e * nx + h * half, half)
                row = h * span + 2 * ylay.total + e * half
                before[where, :] = joined[pl.ds(row, half), :]
                after[where, :] = joined[pl.ds(row + 2 * half, half), :]
        one = jnp.ones((TILE, LANES), jnp.float32)
        value, slope, back, fall = one, one, one, one
        for k in range(nx):
            low, high = pl.ds(k * TILE, TILE), pl.ds((nx - 1 - k) * TILE, TILE)
            gright[low, :] = value
            gleft[high, :] = back
            new_value, slope = growing_step(value, slope, sides(before, after, k))
            ginv[low, :] = value / new_value
            end, value = value, new_value
            corner = back
            back, fall = growing_step(back, fall, sides(before, after, nx - 1 - k))
        total = 1.0 / value
        for x in range(nx):
            here = pl.ds(x * TILE, TILE)
            scale = sides(before, after, nx + x) * total
            gleft[here, :] = gleft[here, :] * scale
            gright[here, :] = gright[here, :] * scale

    ghost[...] = jnp.zeros(ghost.shape, jnp.float32)
    for c in range(comps):
        for h in range(2):
            piece = pl.ds(h * half, half)
            fb = joined[pl.ds(h * span + c * half, half), :]
            fa = joined[pl.ds(h * span + ylay.total + c * half, half), :]
            ghost[pl.ds(h * half * TILE + c, half, stride=TILE), :] = before[piece, :] * fb
            ghost[pl.ds(h * half * TILE + SIDE + c, half, stride=TILE), :] = after[piece, :] * fa
            swept, chain = fb, []
            for y in range(ny):
                cells = az[c, pl.ds(h * half * ny + y, half, stride=ny), :]
                swept = (cells + swept) * inv[pl.ds(y * nx + h * half, half), :]
                chain.append(swept)
            later = fa
            for y in reversed(range(ny)):
                where = pl.ds(h * half * ny + y, half, stride=ny)
                later = chain[y] + inv[pl.ds(y * nx + h * half, half), :] * later
                ay[c, where, :] = later * w[where, :]

    swept = [jnp.zeros((n, LANES), jnp.float32) for n in xlay.sizes]
    for x in range(nx):
        here, there = pl.ds(x * ny, ny), pl.ds(x * TILE, TILE)
        for c in range(comps):
            swept[c] = (ay[c, here, :] + swept[c]) * xinv[here, :]
            ay[c, here, :] = swept[c]
        swept[comps] = (ghost[there, :] + swept[comps]) * ginv[there, :]
        ghost[there, :] = swept[comps]
    lasts, solved = list(swept), list(swept)
    for x in reversed(range(nx)):
        here, there = pl.ds(x * ny, ny), pl.ds(x * TILE, TILE)
        for c in range(comps):
            if x + 1 < nx:
                solved[c] = ay[c, here, :] + xinv[here, :] * solved[c]
            field[c, here, :] = solved[c] * w[here, :]
        if x + 1 < nx:
            solved[comps] = ghost[there, :] + ginv[there, :] * solved[comps]
        ghost[there, :] = solved[comps] * sides(before, after, nx + x)
    record = {"first": solved, "last": lasts}
    if xlay.leads:
        pieces = [part[pl.ds(i * ny, ny), :] for i in range(5)]
        record["near"] = [pieces[0], corner * total]
        record["cross"] = [pieces[1], total]
        record["far"] = [pieces[2], end * total]
        record["head"], record["tail"] = pieces[3:4], pieces[4:5]
    write_block(xlay, block, record)
    if xlay.leads:
        slim[pl.ds(0, xlay.couple), :] = block[pl.ds(0, xlay.couple), :]
        slim[pl.ds(xlay.couple, TILE), :] = block[pl.ds(xlay.packed, TILE), :]


def x_kernel(dims, lay, lead, levels, shift, start, me_ref, *refs):
    nx, ny = dims
    count = (2 if lay.leads else 4) * levels
    state, _ = solve_lines(lay, lead, levels, me_ref[0] >> shift, refs[:count])
    left, right, gleft, gright, flows, inputs, ghost, *rest = refs[count:]
    out_any, out, field, fluxes, sems = rest[-5:]
    rows = nx * ny
    tiles = ny // TILE
    comps = len(lay.sizes) - 1
    starts, nexts, (near,), (far,) = state

    def fill(x, carry):
        span, above = pl.ds(x * ny, ny), pl.ds((x + 1) * ny, ny)
        lower, upper = left[span, :], right[span, :]
        for c in range(comps):
            field[c, above, :] = inputs[c, span, :] + lower * starts[c] + upper * nexts[c]
        here = pl.ds(x * TILE, TILE)
        fluxes[here, :] = ghost[here, :] + gleft[here, :] * starts[comps] + gright[here, :] * nexts[comps]
        return carry

    lax.fori_loop(0, nx, fill, 0, unroll=8)
    blank = jnp.zeros((comps, ny, LANES), jnp.float32)
    field[:, pl.ds(0, ny), :] = blank
    field[:, pl.ds((nx + 1) * ny, ny), :] = blank

    line = lax.broadcasted_iota(jnp.int32, (TILE, LANES), 0)

    def advect(x, carry):
        before = jnp.maximum(x - 1, 0)
        beyond = jnp.minimum(x + 1, nx - 1)

        def flow(kind, plane, t):
            begin = pl.multiple_of(kind * rows + plane * ny + t * TILE, TILE)
            return flows[pl.ds(begin, TILE), :]

        own = [flow(0, x, t) for t in range(tiles)]
        ahead_x = [flow(1, beyond, t) for t in range(tiles)]
        behind_x = [flow(2, before, t) for t in range(tiles)]
        ahead_y = [flow(3, x, t) for t in range(tiles)]
        behind_y = [flow(4, x, t) for t in range(tiles)]
        ahead_z = [flow(5, x, t) for t in range(tiles)]
        behind_z = [flow(6, x, t) for t in range(tiles)]
        for c in range(comps):

            def cells(plane, t):
                begin = pl.multiple_of((plane + 1) * ny + t * TILE, TILE)
                return field[c, pl.ds(begin, TILE), :]

            grad = [cells(x, t) for t in range(tiles)]
            ups = [pltpu.roll(ahead_y[t] * grad[t], TILE - 1, 0) for t in range(tiles)]
            downs = [pltpu.roll(behind_y[t] * grad[t], 1, 0) for t in range(tiles)]
            lowest = fluxes[pl.ds(x * TILE + c, 1), :]
            highest = fluxes[pl.ds(x * TILE + SIDE + c, 1), :]
            for t in range(tiles):
                part = own[t] * grad[t]
                part = part + ahead_x[t] * cells(x + 1, t) - behind_x[t] * cells(x - 1, t)
                enter = ups[t + 1] if t + 1 < tiles else jnp.broadcast_to(highest, (TILE, LANES))
                part = part + jnp.where(line == TILE - 1, enter, ups[t])
                enter = downs[t - 1] if t > 0 else jnp.broadcast_to(lowest, (TILE, LANES))
                part = part - jnp.where(line == 0, enter, downs[t])
                part = part + pltpu.roll(ahead_z[t] * grad[t], LANES - 1, 1)
                part = part - pltpu.roll(behind_z[t] * grad[t], 1, 1)
                out[c, pl.ds(pl.multiple_of(x * ny + t * TILE, TILE), TILE), :] = part
        return carry

    parts = 8
    share = nx // parts

    def copy(part):
        span = pl.ds(part * share * ny, share * ny)
        target = out_any.at[pl.ds(start, comps), span, :]
        return pltpu.make_async_copy(out.at[:, span, :], target, sems.at[part])

    top, bottom = pl.ds(0, ny), pl.ds(rows - ny, ny)
    for part in range(parts):
        lax.fori_loop(part * share, (part + 1) * share, advect, 0, unroll=share)
        for c in range(comps):
            if part == 0:
                out[c, top, :] = out[c, top, :] - near * starts[c]
            if part == parts - 1:
                out[c, bottom, :] = out[c, bottom, :] + far * nexts[c]
        copy(part).start()
    for part in range(parts):
        copy(part).wait()


def call(
    kernel, name, operands, outs, scratch=(), spaces=None, out_spaces=None, mebibytes=4, aliases=None
):
    params = pltpu.CompilerParams(vmem_limit_bytes=mebibytes * 1024 * 1024)
    memory = {"v": pltpu.VMEM, "k": pltpu.VMEM, "h": pltpu.HBM, "s": pltpu.SMEM}
    held = {"h": pltpu.HBM, "k": pltpu.VMEM}
    spaces = spaces or "s" + "v" * (len(operands) - 1)
    out_spaces = out_spaces or "v" * len(outs)
    operands = [
        pltpu.with_memory_space_constraint(o, held[s]) if s in held else o
        for o, s in zip(operands, spaces)
    ]
    return pl.pallas_call(
        kernel,
        name=name,
        out_shape=[
            held[s](shape, jnp.float32) if s in held else jax.ShapeDtypeStruct(shape, jnp.float32)
            for shape, s in zip(outs, out_spaces)
        ],
        in_specs=[pl.BlockSpec(memory_space=memory[s]) for s in spaces],
        out_specs=[pl.BlockSpec(memory_space=memory[s]) for s in out_spaces],
        scratch_shapes=list(scratch),
        input_output_aliases=aliases or {},
        compiler_params=params,
        cost_estimate=pl.CostEstimate(flops=10**9, bytes_accessed=10**7, transcendentals=0),
    )(*operands)


def exchange(rows, axis, bit):
    count = lax.axis_size(axis)
    return lax.ppermute(rows, axis, [(i, i ^ (1 << bit)) for i in range(count)])


class Ladder:
    def __init__(self, lay, axis, shift, me, send, keep, lead=None):
        self.lay, self.axis, self.shift, self.me, self.lead = lay, axis, shift, me, lead
        self.levels = (lax.axis_size(axis) - 1).bit_length()
        self.owns, self.gots, self.outgoing = [keep], [], send

    def send(self):
        self.gots.append(exchange(self.outgoing, self.axis, len(self.gots)))

    def merge(self, beside=(), apart=None):
        level = len(self.owns) - 1
        top = level == self.levels - 2
        lay, bit = self.lay, self.shift + level
        leader = self.lead or self
        operands = (self.me, self.owns[-1], self.gots[-1])
        if not lay.leads:
            operands += (leader.owns[level], leader.gots[level])
        shapes = [(lay.rows, LANES)] + ([(lay.side_rows, LANES)] if top else [])
        kernel = functools.partial(merge_kernel, lay, leader.lay, bit, top)
        if apart is not None:
            kernel = functools.partial(first_merge_kernel, lay, bit, top)
            operands += (apart,)
            shapes = shapes[:1] + shapes
        found = call(kernel, "merge_" + self.axis, operands + tuple(beside), shapes)
        self.owns.append(found[0])
        self.outgoing = found[-1] if top else found[0]
        if apart is not None:
            self.gots[0] = found[1]

    def records(self):
        found = (*self.owns, *self.gots)
        return found if self.lay.leads else found + (*self.lead.owns, *self.lead.gots)


def on_device(cotangent, diffusion, phase, courant, upwind):
    comps, nx, ny, nz = cotangent.shape
    shift = (lax.axis_size("gy") - 1).bit_length()
    rows = nx * ny
    half = nx // 2
    size = comps // 2
    starts = (0, size)
    counts = (size, comps - size)
    ylays = [Layout([half] * n, 1, 2, half, g == 0) for g, n in enumerate(counts)]
    xlays = [Layout([ny] * n + [TILE], 2, 1, ny, g == 0) for g, n in enumerate(counts)]
    me = lax.axis_index(("gx", "gy")).astype(jnp.int32).reshape(1)

    def vmem(*shape, dtype=jnp.float32):
        return pltpu.VMEM(shape, dtype)

    flat = (rows, nz)
    cot = cotangent.reshape(comps, rows, nz)
    cour = courant.reshape(3, rows, nz)
    upw = upwind.reshape(3, rows, nz)
    n = counts[0]
    keep, send, az, w, left, right, phi, psi, cot_next = call(
        functools.partial(lead_z_kernel, (nx, ny), ylays[0]),
        "z_solve_lead",
        (me, cot, diffusion.reshape(flat), phase.reshape(flat), cour, upw),
        [(ylays[0].rows, nz)] * 2 + [(n, rows, nz)] + [flat] * 5 + [(counts[1], rows, nz)],
        [
            vmem(n, rows, nz), vmem(*flat), vmem(*flat, dtype=jnp.int32),
            vmem(*flat), vmem(*flat, dtype=jnp.int32),
            vmem(*flat), vmem(*flat), vmem(*flat), vmem(2 * ylays[0].rows, nz),
            pltpu.SemaphoreType.DMA((n,)), pltpu.SemaphoreType.DMA((5,)),
        ],
        spaces="shhhhh",
        mebibytes=12,
    )
    lead = Ladder(ylays[0], "gy", 0, me, send, keep)
    lead.send()
    azs = [az]
    n = counts[1]
    keep, send, az = call(
        functools.partial(next_z_kernel, (nx, ny), ylays[1]),
        "z_solve_next",
        (me, cot_next, phi, psi, w, left, right),
        [(ylays[1].rows, nz)] * 2 + [(n, rows, nz)],
        [vmem(2 * ylays[1].rows, nz)],
        mebibytes=8,
    )
    azs.append(az)
    follow = Ladder(ylays[1], "gy", 0, me, send, keep, lead)
    follow.send()
    beside = (send,)
    for level in range(lead.levels - 1):
        lead.merge(beside)
        lead.send()
        follow.merge()
        follow.send()
        beside = (follow.outgoing,)
        if level == 0:
            part, inv, xinv, xleft, xright, flows = call(
                functools.partial(coef_kernel, (nx, ny)),
                "x_coefficients",
                (w, cour, upw, lead.owns[1]),
                [(5 * ny, nz), flat, flat, flat, flat, (7 * rows, nz)],
                spaces="vvvv",
                mebibytes=8,
            )
            beside = (part, follow.outgoing)
            apart = exchange(part, "gx", 0)
    ladders, mets, answers = (lead, follow), [], []
    for g, ladder in enumerate(ladders):
        answer, passed = call(
            functools.partial(solve_kernel, ylays[g], ylays[0], ladder.levels),
            "y_reduced",
            (me,) + ladder.records() + (beside + (apart,) if g == 0 else ()),
            [(ylays[g].answer_rows, nz)] * 2,
        )
        answers.append(answer)
        mets.append(exchange(passed, "gy", 0))
    fields, ghosts, climbs = [], [], []
    for g in range(2):
        common = (me, azs[g], answers[g], mets[g], w, inv, xinv)
        edge = (nx * TILE, nz)
        outs = [(counts[g], rows, nz), edge]
        scratch = [vmem(counts[g], rows, nz), vmem(2 * ylays[g].answer_rows, nz)]
        body = functools.partial(y_kernel, (nx, ny), ylays[g], xlays[g])
        if g == 0:
            block, slim, field, ghost, ginv, gleft, gright, before, after = call(
                body,
                "y_solve_lead",
                common + (part,),
                [(xlays[0].rows, nz), (xlays[0].couple + TILE, nz)]
                + outs + [edge] * 3 + [(2 * nx, nz)] * 2,
                scratch,
                mebibytes=6,
            )
            climbs.append(Ladder(xlays[0], "gx", shift, me, slim, block))
        else:
            block, field, ghost = call(
                body,
                "y_solve_next",
                common + (before, after, ginv),
                [(xlays[1].rows, nz)] + outs,
                scratch,
                mebibytes=6,
            )
            climbs.append(Ladder(xlays[1], "gx", shift, me, block, block, climbs[0]))
        fields.append(field)
        ghosts.append(ghost)
        climbs[g].send()
    beside = (block,)
    for level in range(climbs[0].levels - 1):
        for ladder in climbs:
            leads = ladder.lay.leads
            ladder.merge(beside if leads else (), apart if leads and level == 0 else None)
            ladder.send()
        beside = (climbs[1].outgoing,)
    grad = None
    for g, ladder in enumerate(climbs):
        operands = (me, *ladder.records(), xleft, xright, gleft, gright, flows, fields[g], ghosts[g])
        spaces = "s" + "v" * (len(operands) - 1)
        aliases = None
        if g:
            aliases = {len(operands): 0}
            operands, spaces = operands + (grad,), spaces + "h"
        (grad,) = call(
            functools.partial(
                x_kernel, (nx, ny), xlays[g], xlays[0], ladder.levels, shift, starts[g]
            ),
            "x_solve",
            operands,
            [(comps, rows, nz)],
            [
                vmem(counts[g], rows, nz), vmem(counts[g], rows + 2 * ny, nz), vmem(nx * TILE, nz),
                pltpu.SemaphoreType.DMA((8,)),
            ],
            spaces=spaces,
            out_spaces="h",
            mebibytes=8,
            aliases=aliases,
        )
    return grad.reshape(comps, nx, ny, nz)


def solution(mesh):
    placed = (
        P(None, "gx", "gy", None),
        P("gx", "gy", None),
        P("gx", "gy", None),
        P(None, "gx", "gy", None),
        P(None, "gx", "gy", None),
    )
    return jax.shard_map(
        on_device, mesh=mesh, in_specs=placed, out_specs=P(None, "gx", "gy", None), check_vma=False
    )
```

```python
import functools

import jax
import jax.numpy as jnp
from jax import lax
from jax.experimental import pallas as pl
from jax.experimental.pallas import tpu as pltpu
from jax.sharding import PartitionSpec as P

COMPS = 6
LANES = 128
TILE = 8
SIDE = TILE // 2


def weight_of(diffusion, phase):
    return 1.0 / (diffusion * (1.0 + 3.0 * phase.astype(jnp.float32)))


def growing_step(value, slope, weight):
    slope = slope + weight * value
    return value + slope, slope


def split3(cells):
    high = cells.astype(jnp.bfloat16)
    rest = cells - high.astype(jnp.float32)
    middle = rest.astype(jnp.bfloat16)
    low = (rest - middle.astype(jnp.float32)).astype(jnp.bfloat16)
    return high, middle, low


def sum_matrix():
    row = lax.broadcasted_iota(jnp.int32, (2 * LANES, 2 * LANES), 0)
    col = lax.broadcasted_iota(jnp.int32, (2 * LANES, 2 * LANES), 1)
    before = (row < LANES) & (col < LANES) & (row <= col)
    after = (row >= LANES) & (col >= LANES) & (row > col)
    return jnp.where(before | after, 1.0, 0.0).astype(jnp.bfloat16)


class Layout:
    def __init__(self, sizes, groups, edges, lines, leads):
        self.sizes, self.groups, self.edges, self.lines, self.leads = sizes, groups, edges, lines, leads
        self.offsets = [sum(sizes[:i]) for i in range(len(sizes))]
        self.total = sum(sizes)
        packed = TILE if groups > 1 else 0
        self.couple = 2 * self.total
        self.packed = self.couple + 3 * lines
        self.edge = self.packed + packed
        self.side_couple = self.total
        self.side_packed = self.side_couple + lines
        self.side_edge = self.side_packed + packed
        extra = 2 * edges * lines
        self.rows = self.edge + extra if leads else self.couple
        self.side_rows = self.side_edge + extra // 2 if leads else self.total
        self.answer_rows = 2 * self.total + (extra if leads else 0)

    def group(self, piece):
        return 1 if self.groups > 1 and piece == len(self.sizes) - 1 else 0


def read_pieces(lay, ref, base=0):
    return [ref[pl.ds(base + o, n), :] for o, n in zip(lay.offsets, lay.sizes)]


def write_pieces(lay, ref, values, base=0):
    for o, n, value in zip(lay.offsets, lay.sizes, values):
        ref[pl.ds(base + o, n), :] = value


def read_rows(ref, base, count, lines):
    return [ref[pl.ds(base + i * lines, lines), :] for i in range(count)]


def write_rows(ref, base, values, lines):
    for i, value in enumerate(values):
        ref[pl.ds(base + i * lines, lines), :] = value


def two_sides(low, high):
    return jnp.concatenate(
        [jnp.broadcast_to(low, (SIDE, LANES)), jnp.broadcast_to(high, (SIDE, LANES))], axis=0
    )


def read_pair(ref, row):
    return two_sides(ref[pl.ds(row, 1), :], ref[pl.ds(row + 1, 1), :])


def write_pair(ref, row, value):
    ref[pl.ds(row, 1), :] = value[:1]
    ref[pl.ds(row + 1, 1), :] = value[SIDE : SIDE + 1]


def read_block(lay, ref, lead, lead_ref):
    n = lead.lines
    block = {"first": read_pieces(lay, ref), "last": read_pieces(lay, ref, lay.total)}
    for e, name in enumerate(("near", "cross", "far")):
        entry = [lead_ref[pl.ds(lead.couple + e * n, n), :]]
        if lead.groups > 1:
            entry.append(read_pair(lead_ref, lead.packed + 2 * e))
        block[name] = entry
    block["head"] = read_rows(lead_ref, lead.edge, lead.edges, n)
    block["tail"] = read_rows(lead_ref, lead.edge + lead.edges * n, lead.edges, n)
    return block


def write_block(lay, ref, block):
    n = lay.lines
    write_pieces(lay, ref, block["first"])
    write_pieces(lay, ref, block["last"], lay.total)
    if not lay.leads:
        return
    for e, name in enumerate(("near", "cross", "far")):
        ref[pl.ds(lay.couple + e * n, n), :] = block[name][0]
        if lay.groups > 1:
            write_pair(ref, lay.packed + 2 * e, block[name][1])
    if lay.groups > 1:
        ref[pl.ds(lay.packed + 6, 2), :] = jnp.zeros((2, LANES), jnp.float32)
    write_rows(ref, lay.edge, block["head"], n)
    write_rows(ref, lay.edge + lay.edges * n, block["tail"], n)


def pick(upper, low, high):
    if isinstance(low, list):
        return [pick(upper, a, b) for a, b in zip(low, high)]
    return jnp.where(jnp.full(low.shape, upper, jnp.int32) == 1, high, low)


def write_side(lay, ref, block, upper):
    n = lay.lines
    write_pieces(lay, ref, pick(upper, block["last"], block["first"]))
    if not lay.leads:
        return
    pair = pick(upper, block["far"], block["near"])
    ref[pl.ds(lay.side_couple, n), :] = pair[0]
    if lay.groups > 1:
        ref[pl.ds(lay.side_packed, TILE), :] = pair[1]
    write_rows(ref, lay.side_edge, pick(upper, block["tail"], block["head"]), n)


def read_side(lay, ref, lead, lead_ref):
    n = lead.lines
    couple = [lead_ref[pl.ds(lead.side_couple, n), :]]
    if lead.groups > 1:
        couple.append(lead_ref[pl.ds(lead.side_packed, TILE), :])
    return read_pieces(lay, ref), couple, read_rows(lead_ref, lead.side_edge, lead.edges, n)


def ordered(upper, own, other):
    low = {name: pick(upper, own[name], other[name]) for name in own}
    high = {name: pick(upper, other[name], own[name]) for name in own}
    return low, high


def joint(low, high):
    return [1.0 / (1.0 - far * near) for far, near in zip(low["far"], high["near"])]


def merge(lay, low, high):
    shrink = joint(low, high)
    groups = range(len(shrink))
    to_low = [low["cross"][g] * shrink[g] for g in groups]
    to_high = [high["cross"][g] * shrink[g] for g in groups]
    span = range(len(lay.sizes))
    of = lay.group
    block = {
        "first": [
            low["first"][i]
            + to_low[of(i)] * (high["first"][i] + high["near"][of(i)] * low["last"][i])
            for i in span
        ],
        "last": [
            high["last"][i]
            + to_high[of(i)] * (low["last"][i] + low["far"][of(i)] * high["first"][i])
            for i in span
        ],
    }
    block["near"] = [low["near"][g] + to_low[g] * low["cross"][g] * high["near"][g] for g in groups]
    block["cross"] = [to_low[g] * high["cross"][g] for g in groups]
    block["far"] = [high["far"][g] + to_high[g] * high["cross"][g] * low["far"][g] for g in groups]
    block["head"] = low["head"]
    block["tail"] = high["tail"]
    return block


def inner(lay, low, high, before, after):
    shrink = joint(low, high)
    low_last, high_first = [], []
    for i in range(len(lay.sizes)):
        g = lay.group(i)
        left = low["last"][i] + low["cross"][g] * before[i]
        right = high["first"][i] + high["cross"][g] * after[i]
        low_last.append((left + low["far"][g] * right) * shrink[g])
        high_first.append((right + high["near"][g] * left) * shrink[g])
    return low_last, high_first


def merge_kernel(lay, lead, bit, top, me_ref, own, other, *refs):
    out, *side = refs[-2:] if top else refs[-1:]
    lead_own, lead_other = (own, other) if lay.leads else refs[:2]
    upper = (me_ref[0] >> bit) & 1
    low, high = ordered(
        upper, read_block(lay, own, lead, lead_own), read_block(lay, other, lead, lead_other)
    )
    block = merge(lay, low, high)
    write_block(lay, out, block)
    if top:
        write_side(lay, side[0], block, (me_ref[0] >> (bit + 1)) & 1)


def first_merge_kernel(lay, bit, top, me_ref, own, slim, apart, *refs):
    out, joined, *side = refs[-3:] if top else refs[-2:]
    joined[pl.ds(0, lay.couple), :] = slim[pl.ds(0, lay.couple), :]
    joined[pl.ds(lay.packed, TILE), :] = slim[pl.ds(lay.couple, TILE), :]
    joined[pl.ds(lay.couple, 3 * lay.lines), :] = apart[pl.ds(0, 3 * lay.lines), :]
    edges = 2 * lay.edges * lay.lines
    joined[pl.ds(lay.edge, edges), :] = apart[pl.ds(3 * lay.lines, edges), :]
    merge_kernel(lay, lay, bit, top, me_ref, own, joined, out, *side)


def solve_lines(lay, lead, levels, me, refs):
    owns, gots = refs[:levels], refs[levels : 2 * levels]
    lead_owns, lead_gots = owns, gots
    if not lay.leads:
        lead_owns, lead_gots = refs[2 * levels : 3 * levels], refs[3 * levels : 4 * levels]
    top = levels - 1
    upper = (me >> top) & 1
    own = read_block(lay, owns[top], lead, lead_owns[top])
    met, met_couple, met_edge = read_side(lay, gots[top], lead, lead_gots[top])
    facing = pick(upper, own["last"], own["first"])
    couple = pick(upper, own["far"], own["near"])
    shrink = [1.0 / (1.0 - a * b) for a, b in zip(met_couple, couple)]
    found = []
    for i in range(len(lay.sizes)):
        g = lay.group(i)
        found.append((met[i] + met_couple[g] * facing[i]) * shrink[g])
    zeros = [jnp.zeros_like(v) for v in found]
    blank = [jnp.zeros_like(v) for v in met_edge]
    state = (
        pick(upper, zeros, found), pick(upper, found, zeros),
        pick(upper, blank, met_edge), pick(upper, met_edge, blank),
    )
    partner = None
    for level in reversed(range(top)):
        upper = (me >> level) & 1
        low, high = ordered(
            upper,
            read_block(lay, owns[level], lead, lead_owns[level]),
            read_block(lay, gots[level], lead, lead_gots[level]),
        )
        before, after, behind, ahead = state
        low_last, high_first = inner(lay, low, high, before, after)
        lower = (before, high_first, behind, high["head"])
        higher = (low_last, after, low["tail"], ahead)
        state = tuple(pick(upper, a, b) for a, b in zip(lower, higher))
        partner = tuple(pick(upper, a, b) for a, b in zip(higher, lower))
    return state, partner


def write_answer(lay, ref, state):
    before, after, behind, ahead = state
    write_pieces(lay, ref, before)
    write_pieces(lay, ref, after, lay.total)
    if lay.leads:
        write_rows(ref, 2 * lay.total, behind + ahead, lay.lines)


def solve_kernel(lay, lead, levels, me_ref, *refs):
    state, partner = solve_lines(lay, lead, levels, me_ref[0], refs[:-2])
    write_answer(lay, refs[-2], state)
    write_answer(lay, refs[-1], partner)


def corners(weights):
    one = jnp.ones_like(weights[0])
    value, slope, chain = one, one, [one]
    for weight in weights:
        value, slope = growing_step(value, slope, weight)
        chain.append(value)
    back, fall, backs = one, one, []
    for weight in reversed(weights):
        backs.append(back)
        back, fall = growing_step(back, fall, weight)
    backs.reverse()
    return chain, backs, 1.0 / value


def post(lay, both, row, cells):
    half = cells.shape[0] // 2
    for h in range(2):
        both[pl.ds(h * lay.rows + row, half), :] = cells[h * half : (h + 1) * half]


def z_part(dims, lay, me_ref, cot, phi, psi, w, left, right, arrived, az, both, keep, send):
    nx, ny = dims
    tiles = nx * ny // LANES
    sums = sum_matrix()
    for c in range(len(lay.sizes)):
        arrived(c)
        for t in range(tiles):
            span = pl.ds(t * LANES, LANES)
            cells, up, down = cot[c, span, :], phi[span, :], psi[span, :]
            wide = jnp.concatenate([up * cells, down * cells], axis=1)
            found = jnp.dot(
                jnp.concatenate(split3(wide), axis=0), sums, preferred_element_type=jnp.float32
            )
            found = found[:LANES] + (found[LANES : 2 * LANES] + found[2 * LANES :])
            az[c, span, :] = w[span, :] * (down * found[:, :LANES] + up * found[:, LANES:])
        first = jnp.zeros((nx, LANES), jnp.float32)
        last = jnp.zeros((nx, LANES), jnp.float32)
        for y in range(ny):
            cells = az[c, pl.ds(y, nx, stride=ny), :]
            span = pl.ds(y * nx, nx)
            first = first + left[span, :] * cells
            last = last + right[span, :] * cells
        post(lay, both, lay.offsets[c], first)
        post(lay, both, lay.total + lay.offsets[c], last)
    mine = me_ref[0] & 1
    keep[...] = both[pl.ds(pl.multiple_of(mine * lay.rows, TILE), lay.rows), :]
    send[...] = both[pl.ds(pl.multiple_of((1 - mine) * lay.rows, TILE), lay.rows), :]


def carried(maps, state):
    return maps[0] * state[0] + maps[1] * state[1], maps[2] * state[0] + maps[3] * state[1]


def z_continuants(tiles, wt, pht, pst, maps, ends):
    deep = LANES // TILE
    lines = tiles * TILE
    one = jnp.ones((lines, LANES), jnp.float32)
    zero = jnp.zeros((lines, LANES), jnp.float32)

    def at(k, t):
        return pl.ds(t * LANES + k, TILE, stride=deep)

    weights = [
        jnp.concatenate([wt[at(k, t), :] for t in range(tiles)], axis=0) for k in range(deep)
    ]
    found = []
    for order in (range(deep), reversed(range(deep))):
        pair = [(one, zero), (zero, one)]
        values = {}
        for k in order:
            values[k] = (pair[0][0], pair[1][0])
            pair = [growing_step(*state, weights[k]) for state in pair]
        base = len(found) * 4 * lines
        found.append(values)
        for i, entry in enumerate((pair[0][0], pair[1][0], pair[0][1], pair[1][1])):
            maps[pl.ds(base + i * lines, lines), :] = entry
    state = (jnp.ones((tiles, LANES), jnp.float32),) * 2
    for side, order in enumerate((range(TILE), reversed(range(TILE)))):
        for s in order:
            for i in range(2):
                ends[pl.ds((2 * side + i) * lines + s, tiles, stride=TILE), :] = state[i]
            rows = [pl.ds((4 * side + i) * lines + s, tiles, stride=TILE) for i in range(4)]
            state = carried([maps[row, :] for row in rows], state)
        state = (1.0 / state[0],) * 2
    for values, target, side in ((found[0], pht, 0), (found[1], pst, 1)):
        first, second = (ends[pl.ds((2 * side + i) * lines, lines), :] for i in range(2))
        for k in range(deep):
            cells = values[k][0] * first + values[k][1] * second
            for t in range(tiles):
                target[at(k, t), :] = cells[t * TILE : (t + 1) * TILE]


def lead_z_kernel(
    dims, lay, me_ref, cot_any, diff_any, phase_any, cour_any, upw_any,
    keep, send, az, w, left, right, phi, psi, later,
    cot, diff, phase, cour, upw, wt, pht, pst, maps, ends, both, in_sems, sems,
):
    nx, ny = dims
    tiles = nx * ny // LANES
    half = nx // 2
    count = len(lay.sizes)
    ahead = pltpu.make_async_copy(cot_any.at[pl.ds(count, later.shape[0])], later, sems.at[4])
    small = [(diff_any, diff), (phase_any, phase), (cour_any.at[1], cour), (upw_any.at[1], upw)]
    for i, (source, target) in enumerate(small):
        pltpu.make_async_copy(source, target, sems.at[i]).start()
    for c in range(count):
        pltpu.make_async_copy(cot_any.at[c], cot.at[c], in_sems.at[c]).start()
    ahead.start()

    for i, (source, target) in enumerate(small[:2]):
        pltpu.make_async_copy(source, target, sems.at[i]).wait()
    w[...] = weight_of(diff[...], phase[...])
    for t in range(tiles):
        span = pl.ds(t * LANES, LANES)
        wt[span, :] = w[span, :].T
    z_continuants(tiles, wt, pht, pst, maps, ends)
    for t in range(tiles):
        span = pl.ds(t * LANES, LANES)
        phi[span, :] = pht[span, :].T
        psi[span, :] = pst[span, :].T

    chain, backs, total = corners([w[pl.ds(y, nx, stride=ny), :] for y in range(ny)])
    for y in range(ny):
        span = pl.ds(y * nx, nx)
        left[span, :] = backs[y] * total
        right[span, :] = chain[y] * total
    post(lay, both, lay.couple, backs[0] * total)
    post(lay, both, lay.couple + half, total)
    post(lay, both, lay.couple + 2 * half, chain[ny - 1] * total)
    for i, (source, target) in enumerate(small[2:]):
        pltpu.make_async_copy(source, target, sems.at[2 + i]).wait()
    for e, y in enumerate((0, ny - 1)):
        edge = pl.ds(y, nx, stride=ny)
        weight = w[edge, :]
        up = cour[edge, :] * upw[edge, :].astype(jnp.float32)
        flow = up if e == 0 else cour[edge, :] - up
        post(lay, both, lay.edge + 2 * e * half, weight)
        post(lay, both, lay.edge + (2 * e + 1) * half, weight * flow)

    def arrived(c):
        pltpu.make_async_copy(cot_any.at[c], cot.at[c], in_sems.at[c]).wait()

    z_part(dims, lay, me_ref, cot, phi, psi, w, left, right, arrived, az, both, keep, send)
    ahead.wait()


def next_z_kernel(dims, lay, me_ref, cot, phi, psi, w, left, right, keep, send, az, both):
    z_part(
        dims, lay, me_ref, cot, phi, psi, w, left, right, lambda c: None, az, both, keep, send
    )


def coef_kernel(dims, w, courant, upwind, after, block, inv, xinv, left, right, flows):
    del after
    nx, ny = dims
    rows = nx * ny
    one = jnp.ones((ny, LANES), jnp.float32)
    value, slope, back, fall = one, one, one, one
    for k in range(nx):
        low, high = pl.ds(k * ny, ny), pl.ds((nx - 1 - k) * ny, ny)
        right[low, :] = value
        left[high, :] = back
        new_value, slope = growing_step(value, slope, w[low, :])
        xinv[low, :] = value / new_value
        end, value = value, new_value
        corner = back
        back, fall = growing_step(back, fall, w[high, :])
    total = 1.0 / value
    block[pl.ds(0, ny), :] = corner * total
    block[pl.ds(ny, ny), :] = total
    block[pl.ds(2 * ny, ny), :] = end * total
    value = jnp.ones((nx, LANES), jnp.float32)
    slope = value
    for y in range(ny):
        new_value, slope = growing_step(value, slope, w[pl.ds(y, nx, stride=ny), :])
        inv[pl.ds(y * nx, nx), :] = value / new_value
        value = new_value

    lane = lax.broadcasted_iota(jnp.int32, (ny, LANES), 1)

    def plane(x, carry):
        span = pl.ds(x * ny, ny)
        scale = w[span, :] * total
        left[span, :] = left[span, :] * scale
        right[span, :] = right[span, :] * scale
        own = one
        for d in range(3):
            flow = courant[d, span, :]
            up = flow * upwind[d, span, :].astype(jnp.float32)
            down = flow - up
            own = own + (down - up)
            if d == 2:
                up = jnp.where(lane == 0, 0.0, up)
                down = jnp.where(lane == LANES - 1, 0.0, down)
            flows[pl.ds((1 + 2 * d) * rows + x * ny, ny), :] = up
            flows[pl.ds((2 + 2 * d) * rows + x * ny, ny), :] = down
        flows[span, :] = own
        return carry

    lax.fori_loop(0, nx, plane, 0, unroll=4)
    first, last = pl.ds(0, ny), pl.ds(rows - ny, ny)
    block[pl.ds(3 * ny, ny), :] = w[first, :] * flows[pl.ds(rows, ny), :]
    block[pl.ds(4 * ny, ny), :] = w[last, :] * flows[pl.ds(2 * rows + rows - ny, ny), :]


def sides(before, after, x):
    return two_sides(before[pl.ds(x, 1), :], after[pl.ds(x, 1), :])


def y_kernel(dims, ylay, xlay, me_ref, az, own, got, w, inv, xinv, *refs):
    nx, ny = dims
    half = nx // 2
    comps = len(ylay.sizes)
    if xlay.leads:
        part, block, slim, field, ghost, ginv, gleft, gright, before, after, ay, joined = refs
    else:
        before, after, ginv, gleft, gright, block, field, ghost, fleft, fright, ay, joined = refs
        for x in range(nx):
            here = pl.ds(x * TILE, TILE)
            scale = sides(before, after, nx + x)
            fleft[here, :] = gleft[here, :] * scale
            fright[here, :] = gright[here, :] * scale
    mine = me_ref[0] & 1
    span = ylay.answer_rows
    joined[pl.ds(pl.multiple_of(mine * span, TILE), span), :] = own[...]
    joined[pl.ds(pl.multiple_of((1 - mine) * span, TILE), span), :] = got[...]
    if xlay.leads:
        for h in range(2):
            for e in range(2):
                where = pl.ds(e * nx + h * half, half)
                row = h * span + 2 * ylay.total + e * half
                before[where, :] = joined[pl.ds(row, half), :]
                after[where, :] = joined[pl.ds(row + 2 * half, half), :]
        one = jnp.ones((TILE, LANES), jnp.float32)
        value, slope, back, fall = one, one, one, one
        for k in range(nx):
            low, high = pl.ds(k * TILE, TILE), pl.ds((nx - 1 - k) * TILE, TILE)
            gright[low, :] = value
            gleft[high, :] = back
            new_value, slope = growing_step(value, slope, sides(before, after, k))
            ginv[low, :] = value / new_value
            end, value = value, new_value
            corner = back
            back, fall = growing_step(back, fall, sides(before, after, nx - 1 - k))
        total = 1.0 / value
        for x in range(nx):
            here = pl.ds(x * TILE, TILE)
            gleft[here, :] = gleft[here, :] * total
            gright[here, :] = gright[here, :] * total

    ghost[...] = jnp.zeros(ghost.shape, jnp.float32)
    for c in range(comps):
        for h in range(2):
            piece = pl.ds(h * half, half)
            fb = joined[pl.ds(h * span + c * half, half), :]
            fa = joined[pl.ds(h * span + ylay.total + c * half, half), :]
            ghost[pl.ds(h * half * TILE + c, half, stride=TILE), :] = before[piece, :] * fb
            ghost[pl.ds(h * half * TILE + SIDE + c, half, stride=TILE), :] = after[piece, :] * fa
            swept, chain = fb, []
            for y in range(ny):
                cells = az[c, pl.ds(h * half * ny + y, half, stride=ny), :]
                swept = (cells + swept) * inv[pl.ds(y * nx + h * half, half), :]
                chain.append(swept)
            later = fa
            for y in reversed(range(ny)):
                where = pl.ds(h * half * ny + y, half, stride=ny)
                later = chain[y] + inv[pl.ds(y * nx + h * half, half), :] * later
                ay[c, where, :] = later * w[where, :]

    swept = [jnp.zeros((n, LANES), jnp.float32) for n in xlay.sizes]
    for x in range(nx):
        here, there = pl.ds(x * ny, ny), pl.ds(x * TILE, TILE)
        for c in range(comps):
            swept[c] = (ay[c, here, :] + swept[c]) * xinv[here, :]
            ay[c, here, :] = swept[c]
        swept[comps] = (ghost[there, :] + swept[comps]) * ginv[there, :]
        ghost[there, :] = swept[comps]
    lasts, solved = list(swept), list(swept)
    for x in reversed(range(nx)):
        here, there = pl.ds(x * ny, ny), pl.ds(x * TILE, TILE)
        for c in range(comps):
            if x + 1 < nx:
                solved[c] = ay[c, here, :] + xinv[here, :] * solved[c]
            field[c, here, :] = solved[c] * w[here, :]
        if x + 1 < nx:
            solved[comps] = ghost[there, :] + ginv[there, :] * solved[comps]
        ghost[there, :] = solved[comps] * sides(before, after, nx + x)
    record = {"first": solved, "last": lasts}
    if xlay.leads:
        pieces = [part[pl.ds(i * ny, ny), :] for i in range(5)]
        record["near"] = [pieces[0], corner * total]
        record["cross"] = [pieces[1], total]
        record["far"] = [pieces[2], end * total]
        record["head"], record["tail"] = pieces[3:4], pieces[4:5]
    write_block(xlay, block, record)
    if xlay.leads:
        slim[pl.ds(0, xlay.couple), :] = block[pl.ds(0, xlay.couple), :]
        slim[pl.ds(xlay.couple, TILE), :] = block[pl.ds(xlay.packed, TILE), :]


def x_kernel(dims, lay, lead, levels, shift, start, me_ref, *refs):
    nx, ny = dims
    count = (2 if lay.leads else 4) * levels
    state, _ = solve_lines(lay, lead, levels, me_ref[0] >> shift, refs[:count])
    left, right, gleft, gright, flows, inputs, ghost, *rest = refs[count:]
    out_any, out, field, fluxes, sems = rest[-5:]
    rows = nx * ny
    tiles = ny // TILE
    comps = len(lay.sizes) - 1
    starts, nexts, (near,), (far,) = state

    def fill(x, carry):
        span, above = pl.ds(x * ny, ny), pl.ds((x + 1) * ny, ny)
        lower, upper = left[span, :], right[span, :]
        for c in range(comps):
            field[c, above, :] = inputs[c, span, :] + lower * starts[c] + upper * nexts[c]
        here = pl.ds(x * TILE, TILE)
        fluxes[here, :] = ghost[here, :] + gleft[here, :] * starts[comps] + gright[here, :] * nexts[comps]
        return carry

    lax.fori_loop(0, nx, fill, 0, unroll=8)
    blank = jnp.zeros((comps, ny, LANES), jnp.float32)
    field[:, pl.ds(0, ny), :] = blank
    field[:, pl.ds((nx + 1) * ny, ny), :] = blank

    line = lax.broadcasted_iota(jnp.int32, (TILE, LANES), 0)

    def advect(x, carry):
        before = jnp.maximum(x - 1, 0)
        beyond = jnp.minimum(x + 1, nx - 1)

        def flow(kind, plane, t):
            begin = pl.multiple_of(kind * rows + plane * ny + t * TILE, TILE)
            return flows[pl.ds(begin, TILE), :]

        own = [flow(0, x, t) for t in range(tiles)]
        ahead_x = [flow(1, beyond, t) for t in range(tiles)]
        behind_x = [flow(2, before, t) for t in range(tiles)]
        ahead_y = [flow(3, x, t) for t in range(tiles)]
        behind_y = [flow(4, x, t) for t in range(tiles)]
        ahead_z = [flow(5, x, t) for t in range(tiles)]
        behind_z = [flow(6, x, t) for t in range(tiles)]
        for c in range(comps):

            def cells(plane, t):
                begin = pl.multiple_of((plane + 1) * ny + t * TILE, TILE)
                return field[c, pl.ds(begin, TILE), :]

            grad = [cells(x, t) for t in range(tiles)]
            ups = [pltpu.roll(ahead_y[t] * grad[t], TILE - 1, 0) for t in range(tiles)]
            downs = [pltpu.roll(behind_y[t] * grad[t], 1, 0) for t in range(tiles)]
            lowest = fluxes[pl.ds(x * TILE + c, 1), :]
            highest = fluxes[pl.ds(x * TILE + SIDE + c, 1), :]
            for t in range(tiles):
                part = own[t] * grad[t]
                part = part + ahead_x[t] * cells(x + 1, t) - behind_x[t] * cells(x - 1, t)
                enter = ups[t + 1] if t + 1 < tiles else jnp.broadcast_to(highest, (TILE, LANES))
                part = part + jnp.where(line == TILE - 1, enter, ups[t])
                enter = downs[t - 1] if t > 0 else jnp.broadcast_to(lowest, (TILE, LANES))
                part = part - jnp.where(line == 0, enter, downs[t])
                part = part + pltpu.roll(ahead_z[t] * grad[t], LANES - 1, 1)
                part = part - pltpu.roll(behind_z[t] * grad[t], 1, 1)
                out[c, pl.ds(pl.multiple_of(x * ny + t * TILE, TILE), TILE), :] = part
        return carry

    parts = 8
    share = nx // parts

    def copy(part):
        span = pl.ds(part * share * ny, share * ny)
        target = out_any.at[pl.ds(start, comps), span, :]
        return pltpu.make_async_copy(out.at[:, span, :], target, sems.at[part])

    top, bottom = pl.ds(0, ny), pl.ds(rows - ny, ny)
    for part in range(parts):
        lax.fori_loop(part * share, (part + 1) * share, advect, 0, unroll=share)
        for c in range(comps):
            if part == 0:
                out[c, top, :] = out[c, top, :] - near * starts[c]
            if part == parts - 1:
                out[c, bottom, :] = out[c, bottom, :] + far * nexts[c]
        copy(part).start()
    for part in range(parts):
        copy(part).wait()


def call(
    kernel, name, operands, outs, scratch=(), spaces=None, out_spaces=None, mebibytes=4, aliases=None
):
    params = pltpu.CompilerParams(vmem_limit_bytes=mebibytes * 1024 * 1024)
    memory = {"v": pltpu.VMEM, "k": pltpu.VMEM, "h": pltpu.HBM, "s": pltpu.SMEM}
    held = {"h": pltpu.HBM, "k": pltpu.VMEM}
    spaces = spaces or "s" + "v" * (len(operands) - 1)
    out_spaces = out_spaces or "v" * len(outs)
    operands = [
        pltpu.with_memory_space_constraint(o, held[s]) if s in held else o
        for o, s in zip(operands, spaces)
    ]
    return pl.pallas_call(
        kernel,
        name=name,
        out_shape=[
            held[s](shape, jnp.float32) if s in held else jax.ShapeDtypeStruct(shape, jnp.float32)
            for shape, s in zip(outs, out_spaces)
        ],
        in_specs=[pl.BlockSpec(memory_space=memory[s]) for s in spaces],
        out_specs=[pl.BlockSpec(memory_space=memory[s]) for s in out_spaces],
        scratch_shapes=list(scratch),
        input_output_aliases=aliases or {},
        compiler_params=params,
        cost_estimate=pl.CostEstimate(flops=10**9, bytes_accessed=10**7, transcendentals=0),
    )(*operands)


def exchange(rows, axis, bit):
    count = lax.axis_size(axis)
    return lax.ppermute(rows, axis, [(i, i ^ (1 << bit)) for i in range(count)])


class Ladder:
    def __init__(self, lay, axis, shift, me, send, keep, lead=None):
        self.lay, self.axis, self.shift, self.me, self.lead = lay, axis, shift, me, lead
        self.levels = (lax.axis_size(axis) - 1).bit_length()
        self.owns, self.gots, self.outgoing = [keep], [], send

    def send(self):
        self.gots.append(exchange(self.outgoing, self.axis, len(self.gots)))

    def merge(self, beside=(), apart=None):
        level = len(self.owns) - 1
        top = level == self.levels - 2
        lay, bit = self.lay, self.shift + level
        leader = self.lead or self
        operands = (self.me, self.owns[-1], self.gots[-1])
        if not lay.leads:
            operands += (leader.owns[level], leader.gots[level])
        shapes = [(lay.rows, LANES)] + ([(lay.side_rows, LANES)] if top else [])
        kernel = functools.partial(merge_kernel, lay, leader.lay, bit, top)
        if apart is not None:
            kernel = functools.partial(first_merge_kernel, lay, bit, top)
            operands += (apart,)
            shapes = shapes[:1] + shapes
        found = call(kernel, "merge_" + self.axis, operands + tuple(beside), shapes)
        self.owns.append(found[0])
        self.outgoing = found[-1] if top else found[0]
        if apart is not None:
            self.gots[0] = found[1]

    def records(self):
        found = (*self.owns, *self.gots)
        return found if self.lay.leads else found + (*self.lead.owns, *self.lead.gots)


def on_device(cotangent, diffusion, phase, courant, upwind):
    comps, nx, ny, nz = cotangent.shape
    shift = (lax.axis_size("gy") - 1).bit_length()
    rows = nx * ny
    half = nx // 2
    size = comps // 2
    starts = (0, size)
    counts = (size, comps - size)
    ylays = [Layout([half] * n, 1, 2, half, g == 0) for g, n in enumerate(counts)]
    xlays = [Layout([ny] * n + [TILE], 2, 1, ny, g == 0) for g, n in enumerate(counts)]
    me = lax.axis_index(("gx", "gy")).astype(jnp.int32).reshape(1)

    def vmem(*shape, dtype=jnp.float32):
        return pltpu.VMEM(shape, dtype)

    flat = (rows, nz)
    cot = cotangent.reshape(comps, rows, nz)
    cour = courant.reshape(3, rows, nz)
    upw = upwind.reshape(3, rows, nz)
    n = counts[0]
    keep, send, az, w, left, right, phi, psi, cot_next = call(
        functools.partial(lead_z_kernel, (nx, ny), ylays[0]),
        "z_solve_lead",
        (me, cot, diffusion.reshape(flat), phase.reshape(flat), cour, upw),
        [(ylays[0].rows, nz)] * 2 + [(n, rows, nz)] + [flat] * 5 + [(counts[1], rows, nz)],
        [
            vmem(n, rows, nz), vmem(*flat), vmem(*flat, dtype=jnp.int32),
            vmem(*flat), vmem(*flat, dtype=jnp.int32),
            vmem(*flat), vmem(*flat), vmem(*flat),
            vmem(rows // LANES * 8 * TILE, nz), vmem(rows // LANES * 4 * TILE, nz),
            vmem(2 * ylays[0].rows, nz),
            pltpu.SemaphoreType.DMA((n,)), pltpu.SemaphoreType.DMA((5,)),
        ],
        spaces="shhhhh",
        mebibytes=12,
    )
    lead = Ladder(ylays[0], "gy", 0, me, send, keep)
    lead.send()
    azs = [az]
    n = counts[1]
    keep, send, az = call(
        functools.partial(next_z_kernel, (nx, ny), ylays[1]),
        "z_solve_next",
        (me, cot_next, phi, psi, w, left, right),
        [(ylays[1].rows, nz)] * 2 + [(n, rows, nz)],
        [vmem(2 * ylays[1].rows, nz)],
        mebibytes=8,
    )
    azs.append(az)
    follow = Ladder(ylays[1], "gy", 0, me, send, keep, lead)
    follow.send()
    beside = (send,)
    for level in range(lead.levels - 1):
        lead.merge(beside)
        lead.send()
        follow.merge()
        follow.send()
        beside = (follow.outgoing,)
        if level == 0:
            part, inv, xinv, xleft, xright, flows = call(
                functools.partial(coef_kernel, (nx, ny)),
                "x_coefficients",
                (w, cour, upw, lead.owns[1]),
                [(5 * ny, nz), flat, flat, flat, flat, (7 * rows, nz)],
                spaces="vvvv",
                mebibytes=8,
            )
            beside = (part, follow.outgoing)
            apart = exchange(part, "gx", 0)
    ladders, mets, answers = (lead, follow), [], []
    for g, ladder in enumerate(ladders):
        answer, passed = call(
            functools.partial(solve_kernel, ylays[g], ylays[0], ladder.levels),
            "y_reduced",
            (me,) + ladder.records() + (beside + (apart,) if g == 0 else ()),
            [(ylays[g].answer_rows, nz)] * 2,
        )
        answers.append(answer)
        mets.append(exchange(passed, "gy", 0))
    fields, ghosts, climbs = [], [], []
    for g in range(2):
        common = (me, azs[g], answers[g], mets[g], w, inv, xinv)
        edge = (nx * TILE, nz)
        outs = [(counts[g], rows, nz), edge]
        scratch = [vmem(counts[g], rows, nz), vmem(2 * ylays[g].answer_rows, nz)]
        body = functools.partial(y_kernel, (nx, ny), ylays[g], xlays[g])
        if g == 0:
            block, slim, field, ghost, ginv, gleft, gright, before, after = call(
                body,
                "y_solve_lead",
                common + (part,),
                [(xlays[0].rows, nz), (xlays[0].couple + TILE, nz)]
                + outs + [edge] * 3 + [(2 * nx, nz)] * 2,
                scratch,
                mebibytes=6,
            )
            climbs.append(Ladder(xlays[0], "gx", shift, me, slim, block))
        else:
            block, field, ghost, gleft, gright = call(
                body,
                "y_solve_next",
                common + (before, after, ginv, gleft, gright),
                [(xlays[1].rows, nz)] + outs + [edge] * 2,
                scratch,
                mebibytes=6,
            )
            climbs.append(Ladder(xlays[1], "gx", shift, me, block, block, climbs[0]))
        fields.append(field)
        ghosts.append(ghost)
        climbs[g].send()
    beside = (block,)
    for level in range(climbs[0].levels - 1):
        for ladder in climbs:
            leads = ladder.lay.leads
            ladder.merge(beside if leads else (), apart if leads and level == 0 else None)
            ladder.send()
        beside = (climbs[1].outgoing,)
    grad = None
    for g, ladder in enumerate(climbs):
        operands = (me, *ladder.records(), xleft, xright, gleft, gright, flows, fields[g], ghosts[g])
        spaces = "s" + "v" * (len(operands) - 1)
        aliases = None
        if g:
            aliases = {len(operands): 0}
            operands, spaces = operands + (grad,), spaces + "h"
        (grad,) = call(
            functools.partial(
                x_kernel, (nx, ny), xlays[g], xlays[0], ladder.levels, shift, starts[g]
            ),
            "x_solve",
            operands,
            [(comps, rows, nz)],
            [
                vmem(counts[g], rows, nz), vmem(counts[g], rows + 2 * ny, nz), vmem(nx * TILE, nz),
                pltpu.SemaphoreType.DMA((8,)),
            ],
            spaces=spaces,
            out_spaces="h",
            mebibytes=8,
            aliases=aliases,
        )
    return grad.reshape(comps, nx, ny, nz)


def solution(mesh):
    placed = (
        P(None, "gx", "gy", None),
        P("gx", "gy", None),
        P("gx", "gy", None),
        P(None, "gx", "gy", None),
        P(None, "gx", "gy", None),
    )
    return jax.shard_map(
        on_device, mesh=mesh, in_specs=placed, out_specs=P(None, "gx", "gy", None), check_vma=False
    )
```

```python
import functools

import jax
import jax.numpy as jnp
from jax import lax
from jax.experimental import pallas as pl
from jax.experimental.pallas import tpu as pltpu
from jax.sharding import PartitionSpec as P

COMPS = 6
LANES = 128
TILE = 8
SIDE = TILE // 2


def weight_of(diffusion, phase):
    return 1.0 / (diffusion * (1.0 + 3.0 * phase.astype(jnp.float32)))


def growing_step(value, slope, weight):
    slope = slope + weight * value
    return value + slope, slope


def split3(cells):
    high = cells.astype(jnp.bfloat16)
    rest = cells - high.astype(jnp.float32)
    middle = rest.astype(jnp.bfloat16)
    low = (rest - middle.astype(jnp.float32)).astype(jnp.bfloat16)
    return high, middle, low


def sum_matrix():
    row = lax.broadcasted_iota(jnp.int32, (2 * LANES, 2 * LANES), 0)
    col = lax.broadcasted_iota(jnp.int32, (2 * LANES, 2 * LANES), 1)
    before = (row < LANES) & (col < LANES) & (row <= col)
    after = (row >= LANES) & (col >= LANES) & (row > col)
    return jnp.where(before | after, 1.0, 0.0).astype(jnp.bfloat16)


class Layout:
    def __init__(self, sizes, groups, edges, lines, leads):
        self.sizes, self.groups, self.edges, self.lines, self.leads = sizes, groups, edges, lines, leads
        self.offsets = [sum(sizes[:i]) for i in range(len(sizes))]
        self.total = sum(sizes)
        packed = TILE if groups > 1 else 0
        self.couple = 2 * self.total
        self.packed = self.couple + 3 * lines
        self.edge = self.packed + packed
        self.side_couple = self.total
        self.side_packed = self.side_couple + lines
        self.side_edge = self.side_packed + packed
        extra = 2 * edges * lines
        self.rows = self.edge + extra if leads else self.couple
        self.side_rows = self.side_edge + extra // 2 if leads else self.total
        self.answer_rows = 2 * self.total + (extra if leads else 0)

    def group(self, piece):
        return 1 if self.groups > 1 and piece == len(self.sizes) - 1 else 0


def read_pieces(lay, ref, base=0):
    return [ref[pl.ds(base + o, n), :] for o, n in zip(lay.offsets, lay.sizes)]


def write_pieces(lay, ref, values, base=0):
    for o, n, value in zip(lay.offsets, lay.sizes, values):
        ref[pl.ds(base + o, n), :] = value


def read_rows(ref, base, count, lines):
    return [ref[pl.ds(base + i * lines, lines), :] for i in range(count)]


def write_rows(ref, base, values, lines):
    for i, value in enumerate(values):
        ref[pl.ds(base + i * lines, lines), :] = value


def two_sides(low, high):
    return jnp.concatenate(
        [jnp.broadcast_to(low, (SIDE, LANES)), jnp.broadcast_to(high, (SIDE, LANES))], axis=0
    )


def read_pair(ref, row):
    return two_sides(ref[pl.ds(row, 1), :], ref[pl.ds(row + 1, 1), :])


def write_pair(ref, row, value):
    ref[pl.ds(row, 1), :] = value[:1]
    ref[pl.ds(row + 1, 1), :] = value[SIDE : SIDE + 1]


def read_block(lay, ref, lead, lead_ref):
    n = lead.lines
    block = {"first": read_pieces(lay, ref), "last": read_pieces(lay, ref, lay.total)}
    for e, name in enumerate(("near", "cross", "far")):
        entry = [lead_ref[pl.ds(lead.couple + e * n, n), :]]
        if lead.groups > 1:
            entry.append(read_pair(lead_ref, lead.packed + 2 * e))
        block[name] = entry
    block["head"] = read_rows(lead_ref, lead.edge, lead.edges, n)
    block["tail"] = read_rows(lead_ref, lead.edge + lead.edges * n, lead.edges, n)
    return block


def write_block(lay, ref, block):
    n = lay.lines
    write_pieces(lay, ref, block["first"])
    write_pieces(lay, ref, block["last"], lay.total)
    if not lay.leads:
        return
    for e, name in enumerate(("near", "cross", "far")):
        ref[pl.ds(lay.couple + e * n, n), :] = block[name][0]
        if lay.groups > 1:
            write_pair(ref, lay.packed + 2 * e, block[name][1])
    if lay.groups > 1:
        ref[pl.ds(lay.packed + 6, 2), :] = jnp.zeros((2, LANES), jnp.float32)
    write_rows(ref, lay.edge, block["head"], n)
    write_rows(ref, lay.edge + lay.edges * n, block["tail"], n)


def pick(upper, low, high):
    if isinstance(low, list):
        return [pick(upper, a, b) for a, b in zip(low, high)]
    return jnp.where(jnp.full(low.shape, upper, jnp.int32) == 1, high, low)


def write_side(lay, ref, block, upper):
    n = lay.lines
    write_pieces(lay, ref, pick(upper, block["last"], block["first"]))
    if not lay.leads:
        return
    pair = pick(upper, block["far"], block["near"])
    ref[pl.ds(lay.side_couple, n), :] = pair[0]
    if lay.groups > 1:
        ref[pl.ds(lay.side_packed, TILE), :] = pair[1]
    write_rows(ref, lay.side_edge, pick(upper, block["tail"], block["head"]), n)


def read_side(lay, ref, lead, lead_ref):
    n = lead.lines
    couple = [lead_ref[pl.ds(lead.side_couple, n), :]]
    if lead.groups > 1:
        couple.append(lead_ref[pl.ds(lead.side_packed, TILE), :])
    return read_pieces(lay, ref), couple, read_rows(lead_ref, lead.side_edge, lead.edges, n)


def ordered(upper, own, other):
    low = {name: pick(upper, own[name], other[name]) for name in own}
    high = {name: pick(upper, other[name], own[name]) for name in own}
    return low, high


def joint(low, high):
    return [1.0 / (1.0 - far * near) for far, near in zip(low["far"], high["near"])]


def merge(lay, low, high):
    shrink = joint(low, high)
    groups = range(len(shrink))
    to_low = [low["cross"][g] * shrink[g] for g in groups]
    to_high = [high["cross"][g] * shrink[g] for g in groups]
    span = range(len(lay.sizes))
    of = lay.group
    block = {
        "first": [
            low["first"][i]
            + to_low[of(i)] * (high["first"][i] + high["near"][of(i)] * low["last"][i])
            for i in span
        ],
        "last": [
            high["last"][i]
            + to_high[of(i)] * (low["last"][i] + low["far"][of(i)] * high["first"][i])
            for i in span
        ],
    }
    block["near"] = [low["near"][g] + to_low[g] * low["cross"][g] * high["near"][g] for g in groups]
    block["cross"] = [to_low[g] * high["cross"][g] for g in groups]
    block["far"] = [high["far"][g] + to_high[g] * high["cross"][g] * low["far"][g] for g in groups]
    block["head"] = low["head"]
    block["tail"] = high["tail"]
    return block


def inner(lay, low, high, before, after):
    shrink = joint(low, high)
    low_last, high_first = [], []
    for i in range(len(lay.sizes)):
        g = lay.group(i)
        left = low["last"][i] + low["cross"][g] * before[i]
        right = high["first"][i] + high["cross"][g] * after[i]
        low_last.append((left + low["far"][g] * right) * shrink[g])
        high_first.append((right + high["near"][g] * left) * shrink[g])
    return low_last, high_first


def merge_kernel(lay, lead, bit, top, me_ref, own, other, *refs):
    out, *side = refs[-2:] if top else refs[-1:]
    lead_own, lead_other = (own, other) if lay.leads else refs[:2]
    upper = (me_ref[0] >> bit) & 1
    low, high = ordered(
        upper, read_block(lay, own, lead, lead_own), read_block(lay, other, lead, lead_other)
    )
    block = merge(lay, low, high)
    write_block(lay, out, block)
    if top:
        write_side(lay, side[0], block, (me_ref[0] >> (bit + 1)) & 1)


def first_merge_kernel(lay, bit, top, me_ref, own, slim, apart, *refs):
    out, joined, *side = refs[-3:] if top else refs[-2:]
    joined[pl.ds(0, lay.couple), :] = slim[pl.ds(0, lay.couple), :]
    joined[pl.ds(lay.packed, TILE), :] = slim[pl.ds(lay.couple, TILE), :]
    joined[pl.ds(lay.couple, 3 * lay.lines), :] = apart[pl.ds(0, 3 * lay.lines), :]
    edges = 2 * lay.edges * lay.lines
    joined[pl.ds(lay.edge, edges), :] = apart[pl.ds(3 * lay.lines, edges), :]
    merge_kernel(lay, lay, bit, top, me_ref, own, joined, out, *side)


def solve_lines(lay, lead, levels, me, refs):
    owns, gots = refs[:levels], refs[levels : 2 * levels]
    lead_owns, lead_gots = owns, gots
    if not lay.leads:
        lead_owns, lead_gots = refs[2 * levels : 3 * levels], refs[3 * levels : 4 * levels]
    top = levels - 1
    upper = (me >> top) & 1
    own = read_block(lay, owns[top], lead, lead_owns[top])
    met, met_couple, met_edge = read_side(lay, gots[top], lead, lead_gots[top])
    facing = pick(upper, own["last"], own["first"])
    couple = pick(upper, own["far"], own["near"])
    shrink = [1.0 / (1.0 - a * b) for a, b in zip(met_couple, couple)]
    found = []
    for i in range(len(lay.sizes)):
        g = lay.group(i)
        found.append((met[i] + met_couple[g] * facing[i]) * shrink[g])
    zeros = [jnp.zeros_like(v) for v in found]
    blank = [jnp.zeros_like(v) for v in met_edge]
    state = (
        pick(upper, zeros, found), pick(upper, found, zeros),
        pick(upper, blank, met_edge), pick(upper, met_edge, blank),
    )
    partner = None
    for level in reversed(range(top)):
        upper = (me >> level) & 1
        low, high = ordered(
            upper,
            read_block(lay, owns[level], lead, lead_owns[level]),
            read_block(lay, gots[level], lead, lead_gots[level]),
        )
        before, after, behind, ahead = state
        low_last, high_first = inner(lay, low, high, before, after)
        lower = (before, high_first, behind, high["head"])
        higher = (low_last, after, low["tail"], ahead)
        state = tuple(pick(upper, a, b) for a, b in zip(lower, higher))
        partner = tuple(pick(upper, a, b) for a, b in zip(higher, lower))
    return state, partner


def write_answer(lay, ref, state):
    before, after, behind, ahead = state
    write_pieces(lay, ref, before)
    write_pieces(lay, ref, after, lay.total)
    if lay.leads:
        write_rows(ref, 2 * lay.total, behind + ahead, lay.lines)


def solve_kernel(lay, lead, levels, me_ref, *refs):
    state, partner = solve_lines(lay, lead, levels, me_ref[0], refs[:-2])
    write_answer(lay, refs[-2], state)
    write_answer(lay, refs[-1], partner)


def corners(weights):
    one = jnp.ones_like(weights[0])
    value, slope, chain = one, one, [one]
    for weight in weights:
        value, slope = growing_step(value, slope, weight)
        chain.append(value)
    back, fall, backs = one, one, []
    for weight in reversed(weights):
        backs.append(back)
        back, fall = growing_step(back, fall, weight)
    backs.reverse()
    return chain, backs, 1.0 / value


def post(lay, both, row, cells):
    half = cells.shape[0] // 2
    for h in range(2):
        both[pl.ds(h * lay.rows + row, half), :] = cells[h * half : (h + 1) * half]


def z_part(dims, lay, me_ref, cot, phi, psi, w, left, right, arrived, turned, az, both, keep, send):
    nx, ny = dims
    tiles = nx * ny // LANES
    sums = sum_matrix()
    for c in range(len(lay.sizes)):
        arrived(c)
        for t in range(tiles):
            span = pl.ds(t * LANES, LANES)
            cells, up, down = cot[c, span, :], phi[span, :], psi[span, :]
            wide = jnp.concatenate([up * cells, down * cells], axis=1)
            found = jnp.dot(
                jnp.concatenate(split3(wide), axis=0), sums, preferred_element_type=jnp.float32
            )
            found = found[:LANES] + (found[LANES : 2 * LANES] + found[2 * LANES :])
            az[c, span, :] = w[span, :] * (down * found[:, :LANES] + up * found[:, LANES:])
        first = jnp.zeros((nx, LANES), jnp.float32)
        last = jnp.zeros((nx, LANES), jnp.float32)
        for y in range(ny):
            cells = az[c, pl.ds(y, nx, stride=ny), :]
            span = pl.ds(y * nx, nx)
            turned[c, span, :] = cells
            first = first + left[span, :] * cells
            last = last + right[span, :] * cells
        post(lay, both, lay.offsets[c], first)
        post(lay, both, lay.total + lay.offsets[c], last)
    mine = me_ref[0] & 1
    keep[...] = both[pl.ds(pl.multiple_of(mine * lay.rows, TILE), lay.rows), :]
    send[...] = both[pl.ds(pl.multiple_of((1 - mine) * lay.rows, TILE), lay.rows), :]


def carried(maps, state):
    return maps[0] * state[0] + maps[1] * state[1], maps[2] * state[0] + maps[3] * state[1]


def z_continuants(tiles, wt, pht, pst, maps, ends):
    deep = LANES // TILE
    lines = tiles * TILE
    one = jnp.ones((lines, LANES), jnp.float32)
    zero = jnp.zeros((lines, LANES), jnp.float32)

    def at(k, t):
        return pl.ds(t * LANES + k, TILE, stride=deep)

    weights = [
        jnp.concatenate([wt[at(k, t), :] for t in range(tiles)], axis=0) for k in range(deep)
    ]
    found = []
    for order in (range(deep), reversed(range(deep))):
        pair = [(one, zero), (zero, one)]
        values = {}
        for k in order:
            values[k] = (pair[0][0], pair[1][0])
            pair = [growing_step(*state, weights[k]) for state in pair]
        base = len(found) * 4 * lines
        found.append(values)
        for i, entry in enumerate((pair[0][0], pair[1][0], pair[0][1], pair[1][1])):
            maps[pl.ds(base + i * lines, lines), :] = entry
    state = (jnp.ones((tiles, LANES), jnp.float32),) * 2
    for side, order in enumerate((range(TILE), reversed(range(TILE)))):
        for s in order:
            for i in range(2):
                ends[pl.ds((2 * side + i) * lines + s, tiles, stride=TILE), :] = state[i]
            rows = [pl.ds((4 * side + i) * lines + s, tiles, stride=TILE) for i in range(4)]
            state = carried([maps[row, :] for row in rows], state)
        state = (1.0 / state[0],) * 2
    for values, target, side in ((found[0], pht, 0), (found[1], pst, 1)):
        first, second = (ends[pl.ds((2 * side + i) * lines, lines), :] for i in range(2))
        for k in range(deep):
            cells = values[k][0] * first + values[k][1] * second
            for t in range(tiles):
                target[at(k, t), :] = cells[t * TILE : (t + 1) * TILE]


def lead_z_kernel(
    dims, lay, me_ref, cot_any, diff_any, phase_any, cour_any, upw_any,
    keep, send, turned, w, left, right, phi, psi, later,
    az, cot, diff, phase, cour, upw, wt, pht, pst, maps, ends, both, in_sems, sems,
):
    nx, ny = dims
    tiles = nx * ny // LANES
    half = nx // 2
    count = len(lay.sizes)
    ahead = pltpu.make_async_copy(cot_any.at[pl.ds(count, later.shape[0])], later, sems.at[4])
    small = [(diff_any, diff), (phase_any, phase), (cour_any.at[1], cour), (upw_any.at[1], upw)]
    for i, (source, target) in enumerate(small):
        pltpu.make_async_copy(source, target, sems.at[i]).start()
    for c in range(count):
        pltpu.make_async_copy(cot_any.at[c], cot.at[c], in_sems.at[c]).start()
    ahead.start()

    for i, (source, target) in enumerate(small[:2]):
        pltpu.make_async_copy(source, target, sems.at[i]).wait()
    w[...] = weight_of(diff[...], phase[...])
    for t in range(tiles):
        span = pl.ds(t * LANES, LANES)
        wt[span, :] = w[span, :].T
    z_continuants(tiles, wt, pht, pst, maps, ends)
    for t in range(tiles):
        span = pl.ds(t * LANES, LANES)
        phi[span, :] = pht[span, :].T
        psi[span, :] = pst[span, :].T

    chain, backs, total = corners([w[pl.ds(y, nx, stride=ny), :] for y in range(ny)])
    for y in range(ny):
        span = pl.ds(y * nx, nx)
        left[span, :] = backs[y] * total
        right[span, :] = chain[y] * total
    post(lay, both, lay.couple, backs[0] * total)
    post(lay, both, lay.couple + half, total)
    post(lay, both, lay.couple + 2 * half, chain[ny - 1] * total)
    for i, (source, target) in enumerate(small[2:]):
        pltpu.make_async_copy(source, target, sems.at[2 + i]).wait()
    for e, y in enumerate((0, ny - 1)):
        edge = pl.ds(y, nx, stride=ny)
        weight = w[edge, :]
        up = cour[edge, :] * upw[edge, :].astype(jnp.float32)
        flow = up if e == 0 else cour[edge, :] - up
        post(lay, both, lay.edge + 2 * e * half, weight)
        post(lay, both, lay.edge + (2 * e + 1) * half, weight * flow)

    def arrived(c):
        pltpu.make_async_copy(cot_any.at[c], cot.at[c], in_sems.at[c]).wait()

    z_part(dims, lay, me_ref, cot, phi, psi, w, left, right, arrived, turned, az, both, keep, send)
    ahead.wait()


def next_z_kernel(dims, lay, me_ref, cot, phi, psi, w, left, right, keep, send, turned, az, both):
    z_part(
        dims, lay, me_ref, cot, phi, psi, w, left, right, lambda c: None, turned, az, both, keep, send
    )


def coef_kernel(dims, w, courant, upwind, after, block, inv, wy, xinv, seam, left, right, flows):
    del after
    nx, ny = dims
    rows = nx * ny
    one = jnp.ones((ny, LANES), jnp.float32)
    value, slope, back, fall = one, one, one, one
    for k in range(nx):
        low, high = pl.ds(k * ny, ny), pl.ds((nx - 1 - k) * ny, ny)
        right[low, :] = value
        left[high, :] = back
        new_value, slope = growing_step(value, slope, w[low, :])
        new_back, fall = growing_step(back, fall, w[high, :])
        if k < nx // 2:
            up, down = value / new_value, back / new_back
            xinv[low, :] = up
            xinv[high, :] = down
        end, value = value, new_value
        corner, back = back, new_back
    seam[...] = 1.0 / (1.0 - up * down)
    total = 1.0 / value
    block[pl.ds(0, ny), :] = corner * total
    block[pl.ds(ny, ny), :] = total
    block[pl.ds(2 * ny, ny), :] = end * total
    value = jnp.ones((nx, LANES), jnp.float32)
    slope = value
    for y in range(ny):
        weight = w[pl.ds(y, nx, stride=ny), :]
        wy[pl.ds(y * nx, nx), :] = weight
        new_value, slope = growing_step(value, slope, weight)
        inv[pl.ds(y * nx, nx), :] = value / new_value
        value = new_value

    lane = lax.broadcasted_iota(jnp.int32, (ny, LANES), 1)

    def plane(x, carry):
        span = pl.ds(x * ny, ny)
        scale = w[span, :] * total
        left[span, :] = left[span, :] * scale
        right[span, :] = right[span, :] * scale
        own = one
        for d in range(3):
            flow = courant[d, span, :]
            up = flow * upwind[d, span, :].astype(jnp.float32)
            down = flow - up
            own = own + (down - up)
            if d == 2:
                up = jnp.where(lane == 0, 0.0, up)
                down = jnp.where(lane == LANES - 1, 0.0, down)
            flows[pl.ds((1 + 2 * d) * rows + x * ny, ny), :] = up
            flows[pl.ds((2 + 2 * d) * rows + x * ny, ny), :] = down
        flows[span, :] = own
        return carry

    lax.fori_loop(0, nx, plane, 0, unroll=4)
    first, last = pl.ds(0, ny), pl.ds(rows - ny, ny)
    block[pl.ds(3 * ny, ny), :] = w[first, :] * flows[pl.ds(rows, ny), :]
    block[pl.ds(4 * ny, ny), :] = w[last, :] * flows[pl.ds(2 * rows + rows - ny, ny), :]


def sides(before, after, x):
    return two_sides(before[pl.ds(x, 1), :], after[pl.ds(x, 1), :])


def y_kernel(dims, ylay, xlay, me_ref, az, own, got, w, wy, inv, xinv, seam, *refs):
    nx, ny = dims
    half = nx // 2
    comps = len(ylay.sizes)
    if xlay.leads:
        part, block, slim, field, ghost, ginv, gseam, gleft, gright, before, after, ay, joined = refs
    else:
        before, after, ginv, gseam, gleft, gright, block, field, ghost, fleft, fright, ay, joined = refs
        for x in range(nx):
            here = pl.ds(x * TILE, TILE)
            scale = sides(before, after, nx + x)
            fleft[here, :] = gleft[here, :] * scale
            fright[here, :] = gright[here, :] * scale
    mine = me_ref[0] & 1
    span = ylay.answer_rows
    joined[pl.ds(pl.multiple_of(mine * span, TILE), span), :] = own[...]
    joined[pl.ds(pl.multiple_of((1 - mine) * span, TILE), span), :] = got[...]
    if xlay.leads:
        for h in range(2):
            for e in range(2):
                where = pl.ds(e * nx + h * half, half)
                row = h * span + 2 * ylay.total + e * half
                before[where, :] = joined[pl.ds(row, half), :]
                after[where, :] = joined[pl.ds(row + 2 * half, half), :]
        one = jnp.ones((TILE, LANES), jnp.float32)
        value, slope, back, fall = one, one, one, one
        for k in range(nx):
            low, high = pl.ds(k * TILE, TILE), pl.ds((nx - 1 - k) * TILE, TILE)
            gright[low, :] = value
            gleft[high, :] = back
            new_value, slope = growing_step(value, slope, sides(before, after, k))
            new_back, fall = growing_step(back, fall, sides(before, after, nx - 1 - k))
            if k < nx // 2:
                up, down = value / new_value, back / new_back
                ginv[low, :] = up
                ginv[high, :] = down
            end, value = value, new_value
            corner, back = back, new_back
        gseam[...] = 1.0 / (1.0 - up * down)
        total = 1.0 / value
        for x in range(nx):
            here = pl.ds(x * TILE, TILE)
            gleft[here, :] = gleft[here, :] * total
            gright[here, :] = gright[here, :] * total

    ghost[...] = jnp.zeros(ghost.shape, jnp.float32)
    for c in range(comps):
        for h in range(2):
            piece = pl.ds(h * half, half)
            fb = joined[pl.ds(h * span + c * half, half), :]
            fa = joined[pl.ds(h * span + ylay.total + c * half, half), :]
            ghost[pl.ds(h * half * TILE + c, half, stride=TILE), :] = before[piece, :] * fb
            ghost[pl.ds(h * half * TILE + SIDE + c, half, stride=TILE), :] = after[piece, :] * fa
            swept, chain = fb, []
            for y in range(ny):
                cells = az[c, pl.ds(y * nx + h * half, half), :]
                swept = (cells + swept) * inv[pl.ds(y * nx + h * half, half), :]
                chain.append(swept)
            later = fa
            for y in reversed(range(ny)):
                row = pl.ds(y * nx + h * half, half)
                later = chain[y] + inv[row, :] * later
                ay[c, pl.ds(h * half * ny + y, half, stride=ny), :] = later * wy[row, :]

    def load(i, x):
        return ghost[pl.ds(x * TILE, TILE), :] if i == comps else ay[i, pl.ds(x * ny, ny), :]

    def keep(i, x, cells):
        if i == comps:
            ghost[pl.ds(x * TILE, TILE), :] = cells
        else:
            ay[i, pl.ds(x * ny, ny), :] = cells

    def pivot(i, x):
        return ginv[pl.ds(x * TILE, TILE), :] if i == comps else xinv[pl.ds(x * ny, ny), :]

    def finish(i, x, cells):
        if i == comps:
            ghost[pl.ds(x * TILE, TILE), :] = cells * sides(before, after, nx + x)
        else:
            here = pl.ds(x * ny, ny)
            field[i, here, :] = cells * w[here, :]

    pieces = range(comps + 1)
    middle = nx // 2
    lows = [jnp.zeros((n, LANES), jnp.float32) for n in xlay.sizes]
    highs = list(lows)
    for k in range(middle):
        x, mirror = k, nx - 1 - k
        for i in pieces:
            lows[i] = (load(i, x) + lows[i]) * pivot(i, x)
            highs[i] = (load(i, mirror) + highs[i]) * pivot(i, mirror)
            if k + 1 < middle:
                keep(i, x, lows[i])
                keep(i, mirror, highs[i])
    for i in pieces:
        joint_scale = gseam[...] if i == comps else seam[...]
        highs[i] = (highs[i] + pivot(i, middle) * lows[i]) * joint_scale
        lows[i] = lows[i] + pivot(i, middle - 1) * highs[i]
        finish(i, middle - 1, lows[i])
        finish(i, middle, highs[i])
    for k in range(1, middle):
        x, mirror = middle - 1 - k, middle + k
        for i in pieces:
            lows[i] = load(i, x) + pivot(i, x) * lows[i]
            highs[i] = load(i, mirror) + pivot(i, mirror) * highs[i]
            finish(i, x, lows[i])
            finish(i, mirror, highs[i])
    solved, lasts = lows, highs
    record = {"first": solved, "last": lasts}
    if xlay.leads:
        pieces = [part[pl.ds(i * ny, ny), :] for i in range(5)]
        record["near"] = [pieces[0], corner * total]
        record["cross"] = [pieces[1], total]
        record["far"] = [pieces[2], end * total]
        record["head"], record["tail"] = pieces[3:4], pieces[4:5]
    write_block(xlay, block, record)
    if xlay.leads:
        slim[pl.ds(0, xlay.couple), :] = block[pl.ds(0, xlay.couple), :]
        slim[pl.ds(xlay.couple, TILE), :] = block[pl.ds(xlay.packed, TILE), :]


def x_kernel(dims, lay, lead, levels, shift, start, me_ref, *refs):
    nx, ny = dims
    count = (2 if lay.leads else 4) * levels
    state, _ = solve_lines(lay, lead, levels, me_ref[0] >> shift, refs[:count])
    left, right, gleft, gright, flows, inputs, ghost, *rest = refs[count:]
    out_any, out, field, fluxes, sems = rest[-5:]
    rows = nx * ny
    tiles = ny // TILE
    comps = len(lay.sizes) - 1
    starts, nexts, (near,), (far,) = state

    def fill(x, carry):
        span, above = pl.ds(x * ny, ny), pl.ds((x + 1) * ny, ny)
        lower, upper = left[span, :], right[span, :]
        for c in range(comps):
            field[c, above, :] = inputs[c, span, :] + lower * starts[c] + upper * nexts[c]
        here = pl.ds(x * TILE, TILE)
        fluxes[here, :] = ghost[here, :] + gleft[here, :] * starts[comps] + gright[here, :] * nexts[comps]
        return carry

    lax.fori_loop(0, nx, fill, 0, unroll=8)
    blank = jnp.zeros((comps, ny, LANES), jnp.float32)
    field[:, pl.ds(0, ny), :] = blank
    field[:, pl.ds((nx + 1) * ny, ny), :] = blank

    line = lax.broadcasted_iota(jnp.int32, (TILE, LANES), 0)

    def advect(x, carry):
        before = jnp.maximum(x - 1, 0)
        beyond = jnp.minimum(x + 1, nx - 1)

        def flow(kind, plane, t):
            begin = pl.multiple_of(kind * rows + plane * ny + t * TILE, TILE)
            return flows[pl.ds(begin, TILE), :]

        own = [flow(0, x, t) for t in range(tiles)]
        ahead_x = [flow(1, beyond, t) for t in range(tiles)]
        behind_x = [flow(2, before, t) for t in range(tiles)]
        ahead_y = [flow(3, x, t) for t in range(tiles)]
        behind_y = [flow(4, x, t) for t in range(tiles)]
        ahead_z = [flow(5, x, t) for t in range(tiles)]
        behind_z = [flow(6, x, t) for t in range(tiles)]
        for c in range(comps):

            def cells(plane, t):
                begin = pl.multiple_of((plane + 1) * ny + t * TILE, TILE)
                return field[c, pl.ds(begin, TILE), :]

            grad = [cells(x, t) for t in range(tiles)]
            ups = [pltpu.roll(ahead_y[t] * grad[t], TILE - 1, 0) for t in range(tiles)]
            downs = [pltpu.roll(behind_y[t] * grad[t], 1, 0) for t in range(tiles)]
            lowest = fluxes[pl.ds(x * TILE + c, 1), :]
            highest = fluxes[pl.ds(x * TILE + SIDE + c, 1), :]
            for t in range(tiles):
                part = own[t] * grad[t]
                part = part + ahead_x[t] * cells(x + 1, t) - behind_x[t] * cells(x - 1, t)
                enter = ups[t + 1] if t + 1 < tiles else jnp.broadcast_to(highest, (TILE, LANES))
                part = part + jnp.where(line == TILE - 1, enter, ups[t])
                enter = downs[t - 1] if t > 0 else jnp.broadcast_to(lowest, (TILE, LANES))
                part = part - jnp.where(line == 0, enter, downs[t])
                part = part + pltpu.roll(ahead_z[t] * grad[t], LANES - 1, 1)
                part = part - pltpu.roll(behind_z[t] * grad[t], 1, 1)
                out[c, pl.ds(pl.multiple_of(x * ny + t * TILE, TILE), TILE), :] = part
        return carry

    parts = 8
    share = nx // parts

    def copy(part):
        span = pl.ds(part * share * ny, share * ny)
        target = out_any.at[pl.ds(start, comps), span, :]
        return pltpu.make_async_copy(out.at[:, span, :], target, sems.at[part])

    top, bottom = pl.ds(0, ny), pl.ds(rows - ny, ny)
    for part in range(parts):
        lax.fori_loop(part * share, (part + 1) * share, advect, 0, unroll=share)
        for c in range(comps):
            if part == 0:
                out[c, top, :] = out[c, top, :] - near * starts[c]
            if part == parts - 1:
                out[c, bottom, :] = out[c, bottom, :] + far * nexts[c]
        copy(part).start()
    for part in range(parts):
        copy(part).wait()


def call(
    kernel, name, operands, outs, scratch=(), spaces=None, out_spaces=None, mebibytes=4, aliases=None
):
    params = pltpu.CompilerParams(vmem_limit_bytes=mebibytes * 1024 * 1024)
    memory = {"v": pltpu.VMEM, "k": pltpu.VMEM, "h": pltpu.HBM, "s": pltpu.SMEM}
    held = {"h": pltpu.HBM, "k": pltpu.VMEM}
    spaces = spaces or "s" + "v" * (len(operands) - 1)
    out_spaces = out_spaces or "v" * len(outs)
    operands = [
        pltpu.with_memory_space_constraint(o, held[s]) if s in held else o
        for o, s in zip(operands, spaces)
    ]
    return pl.pallas_call(
        kernel,
        name=name,
        out_shape=[
            held[s](shape, jnp.float32) if s in held else jax.ShapeDtypeStruct(shape, jnp.float32)
            for shape, s in zip(outs, out_spaces)
        ],
        in_specs=[pl.BlockSpec(memory_space=memory[s]) for s in spaces],
        out_specs=[pl.BlockSpec(memory_space=memory[s]) for s in out_spaces],
        scratch_shapes=list(scratch),
        input_output_aliases=aliases or {},
        compiler_params=params,
        cost_estimate=pl.CostEstimate(flops=10**9, bytes_accessed=10**7, transcendentals=0),
    )(*operands)


def exchange(rows, axis, bit):
    count = lax.axis_size(axis)
    return lax.ppermute(rows, axis, [(i, i ^ (1 << bit)) for i in range(count)])


class Ladder:
    def __init__(self, lay, axis, shift, me, send, keep, lead=None):
        self.lay, self.axis, self.shift, self.me, self.lead = lay, axis, shift, me, lead
        self.levels = (lax.axis_size(axis) - 1).bit_length()
        self.owns, self.gots, self.outgoing = [keep], [], send

    def send(self):
        self.gots.append(exchange(self.outgoing, self.axis, len(self.gots)))

    def merge(self, beside=(), apart=None):
        level = len(self.owns) - 1
        top = level == self.levels - 2
        lay, bit = self.lay, self.shift + level
        leader = self.lead or self
        operands = (self.me, self.owns[-1], self.gots[-1])
        if not lay.leads:
            operands += (leader.owns[level], leader.gots[level])
        shapes = [(lay.rows, LANES)] + ([(lay.side_rows, LANES)] if top else [])
        kernel = functools.partial(merge_kernel, lay, leader.lay, bit, top)
        if apart is not None:
            kernel = functools.partial(first_merge_kernel, lay, bit, top)
            operands += (apart,)
            shapes = shapes[:1] + shapes
        found = call(kernel, "merge_" + self.axis, operands + tuple(beside), shapes)
        self.owns.append(found[0])
        self.outgoing = found[-1] if top else found[0]
        if apart is not None:
            self.gots[0] = found[1]

    def records(self):
        found = (*self.owns, *self.gots)
        return found if self.lay.leads else found + (*self.lead.owns, *self.lead.gots)


def on_device(cotangent, diffusion, phase, courant, upwind):
    comps, nx, ny, nz = cotangent.shape
    shift = (lax.axis_size("gy") - 1).bit_length()
    rows = nx * ny
    half = nx // 2
    size = comps // 2
    starts = (0, size)
    counts = (size, comps - size)
    ylays = [Layout([half] * n, 1, 2, half, g == 0) for g, n in enumerate(counts)]
    xlays = [Layout([ny] * n + [TILE], 2, 1, ny, g == 0) for g, n in enumerate(counts)]
    me = lax.axis_index(("gx", "gy")).astype(jnp.int32).reshape(1)

    def vmem(*shape, dtype=jnp.float32):
        return pltpu.VMEM(shape, dtype)

    flat = (rows, nz)
    cot = cotangent.reshape(comps, rows, nz)
    cour = courant.reshape(3, rows, nz)
    upw = upwind.reshape(3, rows, nz)
    n = counts[0]
    keep, send, az, w, left, right, phi, psi, cot_next = call(
        functools.partial(lead_z_kernel, (nx, ny), ylays[0]),
        "z_solve_lead",
        (me, cot, diffusion.reshape(flat), phase.reshape(flat), cour, upw),
        [(ylays[0].rows, nz)] * 2 + [(n, rows, nz)] + [flat] * 5 + [(counts[1], rows, nz)],
        [
            vmem(n, rows, nz), vmem(n, rows, nz), vmem(*flat), vmem(*flat, dtype=jnp.int32),
            vmem(*flat), vmem(*flat, dtype=jnp.int32),
            vmem(*flat), vmem(*flat), vmem(*flat),
            vmem(rows // LANES * 8 * TILE, nz), vmem(rows // LANES * 4 * TILE, nz),
            vmem(2 * ylays[0].rows, nz),
            pltpu.SemaphoreType.DMA((n,)), pltpu.SemaphoreType.DMA((5,)),
        ],
        spaces="shhhhh",
        mebibytes=12,
    )
    lead = Ladder(ylays[0], "gy", 0, me, send, keep)
    lead.send()
    azs = [az]
    n = counts[1]
    keep, send, az = call(
        functools.partial(next_z_kernel, (nx, ny), ylays[1]),
        "z_solve_next",
        (me, cot_next, phi, psi, w, left, right),
        [(ylays[1].rows, nz)] * 2 + [(n, rows, nz)],
        [vmem(n, rows, nz), vmem(2 * ylays[1].rows, nz)],
        mebibytes=8,
    )
    azs.append(az)
    follow = Ladder(ylays[1], "gy", 0, me, send, keep, lead)
    follow.send()
    beside = (send,)
    for level in range(lead.levels - 1):
        lead.merge(beside)
        lead.send()
        follow.merge()
        follow.send()
        beside = (follow.outgoing,)
        if level == 0:
            part, inv, wy, xinv, seam, xleft, xright, flows = call(
                functools.partial(coef_kernel, (nx, ny)),
                "x_coefficients",
                (w, cour, upw, lead.owns[1]),
                [(5 * ny, nz), flat, flat, flat, (ny, nz), flat, flat, (7 * rows, nz)],
                spaces="vvvv",
                mebibytes=8,
            )
            beside = (part, follow.outgoing)
            apart = exchange(part, "gx", 0)
    ladders, mets, answers = (lead, follow), [], []
    for g, ladder in enumerate(ladders):
        answer, passed = call(
            functools.partial(solve_kernel, ylays[g], ylays[0], ladder.levels),
            "y_reduced",
            (me,) + ladder.records() + (beside + (apart,) if g == 0 else ()),
            [(ylays[g].answer_rows, nz)] * 2,
        )
        answers.append(answer)
        mets.append(exchange(passed, "gy", 0))
    fields, ghosts, climbs = [], [], []
    for g in range(2):
        common = (me, azs[g], answers[g], mets[g], w, wy, inv, xinv, seam)
        edge = (nx * TILE, nz)
        outs = [(counts[g], rows, nz), edge]
        scratch = [vmem(counts[g], rows, nz), vmem(2 * ylays[g].answer_rows, nz)]
        body = functools.partial(y_kernel, (nx, ny), ylays[g], xlays[g])
        if g == 0:
            block, slim, field, ghost, ginv, gseam, gleft, gright, before, after = call(
                body,
                "y_solve_lead",
                common + (part,),
                [(xlays[0].rows, nz), (xlays[0].couple + TILE, nz)]
                + outs + [edge, (TILE, nz), edge, edge] + [(2 * nx, nz)] * 2,
                scratch,
                mebibytes=6,
            )
            climbs.append(Ladder(xlays[0], "gx", shift, me, slim, block))
        else:
            block, field, ghost, gleft, gright = call(
                body,
                "y_solve_next",
                common + (before, after, ginv, gseam, gleft, gright),
                [(xlays[1].rows, nz)] + outs + [edge] * 2,
                scratch,
                mebibytes=6,
            )
            climbs.append(Ladder(xlays[1], "gx", shift, me, block, block, climbs[0]))
        fields.append(field)
        ghosts.append(ghost)
        climbs[g].send()
    beside = (block,)
    for level in range(climbs[0].levels - 1):
        for ladder in climbs:
            leads = ladder.lay.leads
            ladder.merge(beside if leads else (), apart if leads and level == 0 else None)
            ladder.send()
        beside = (climbs[1].outgoing,)
    grad = None
    for g, ladder in enumerate(climbs):
        operands = (me, *ladder.records(), xleft, xright, gleft, gright, flows, fields[g], ghosts[g])
        spaces = "s" + "v" * (len(operands) - 1)
        aliases = None
        if g:
            aliases = {len(operands): 0}
            operands, spaces = operands + (grad,), spaces + "h"
        (grad,) = call(
            functools.partial(
                x_kernel, (nx, ny), xlays[g], xlays[0], ladder.levels, shift, starts[g]
            ),
            "x_solve",
            operands,
            [(comps, rows, nz)],
            [
                vmem(counts[g], rows, nz), vmem(counts[g], rows + 2 * ny, nz), vmem(nx * TILE, nz),
                pltpu.SemaphoreType.DMA((8,)),
            ],
            spaces=spaces,
            out_spaces="h",
            mebibytes=8,
            aliases=aliases,
        )
    return grad.reshape(comps, nx, ny, nz)


def solution(mesh):
    placed = (
        P(None, "gx", "gy", None),
        P("gx", "gy", None),
        P("gx", "gy", None),
        P(None, "gx", "gy", None),
        P(None, "gx", "gy", None),
    )
    return jax.shard_map(
        on_device, mesh=mesh, in_specs=placed, out_specs=P(None, "gx", "gy", None), check_vma=False
    )
```

```python
import functools

import jax
import jax.numpy as jnp
from jax import lax
from jax.experimental import pallas as pl
from jax.experimental.pallas import tpu as pltpu
from jax.sharding import PartitionSpec as P

COMPS = 6
LANES = 128
TILE = 8
SIDE = TILE // 2


def weight_of(diffusion, phase):
    return 1.0 / (diffusion * (1.0 + 3.0 * phase.astype(jnp.float32)))


def growing_step(value, slope, weight):
    slope = slope + weight * value
    return value + slope, slope


def split3(cells):
    high = cells.astype(jnp.bfloat16)
    rest = cells - high.astype(jnp.float32)
    middle = rest.astype(jnp.bfloat16)
    low = (rest - middle.astype(jnp.float32)).astype(jnp.bfloat16)
    return high, middle, low


def sum_matrix():
    row = lax.broadcasted_iota(jnp.int32, (2 * LANES, 2 * LANES), 0)
    col = lax.broadcasted_iota(jnp.int32, (2 * LANES, 2 * LANES), 1)
    before = (row < LANES) & (col < LANES) & (row <= col)
    after = (row >= LANES) & (col >= LANES) & (row > col)
    return jnp.where(before | after, 1.0, 0.0).astype(jnp.bfloat16)


class Layout:
    def __init__(self, sizes, groups, edges, lines, leads):
        self.sizes, self.groups, self.edges, self.lines, self.leads = sizes, groups, edges, lines, leads
        self.offsets = [sum(sizes[:i]) for i in range(len(sizes))]
        self.total = sum(sizes)
        packed = TILE if groups > 1 else 0
        self.couple = 2 * self.total
        self.packed = self.couple + 3 * lines
        self.edge = self.packed + packed
        self.side_couple = self.total
        self.side_packed = self.side_couple + lines
        self.side_edge = self.side_packed + packed
        extra = 2 * edges * lines
        self.rows = self.edge + extra if leads else self.couple
        self.side_rows = self.side_edge + extra // 2 if leads else self.total
        self.answer_rows = 2 * self.total + (extra if leads else 0)

    def group(self, piece):
        return 1 if self.groups > 1 and piece == len(self.sizes) - 1 else 0


def read_pieces(lay, ref, base=0):
    return [ref[pl.ds(base + o, n), :] for o, n in zip(lay.offsets, lay.sizes)]


def write_pieces(lay, ref, values, base=0):
    for o, n, value in zip(lay.offsets, lay.sizes, values):
        ref[pl.ds(base + o, n), :] = value


def read_rows(ref, base, count, lines):
    return [ref[pl.ds(base + i * lines, lines), :] for i in range(count)]


def write_rows(ref, base, values, lines):
    for i, value in enumerate(values):
        ref[pl.ds(base + i * lines, lines), :] = value


def two_sides(low, high):
    return jnp.concatenate(
        [jnp.broadcast_to(low, (SIDE, LANES)), jnp.broadcast_to(high, (SIDE, LANES))], axis=0
    )


def read_pair(ref, row):
    return two_sides(ref[pl.ds(row, 1), :], ref[pl.ds(row + 1, 1), :])


def write_pair(ref, row, value):
    ref[pl.ds(row, 1), :] = value[:1]
    ref[pl.ds(row + 1, 1), :] = value[SIDE : SIDE + 1]


def read_block(lay, ref, lead, lead_ref):
    n = lead.lines
    block = {"first": read_pieces(lay, ref), "last": read_pieces(lay, ref, lay.total)}
    for e, name in enumerate(("near", "cross", "far")):
        entry = [lead_ref[pl.ds(lead.couple + e * n, n), :]]
        if lead.groups > 1:
            entry.append(read_pair(lead_ref, lead.packed + 2 * e))
        block[name] = entry
    block["head"] = read_rows(lead_ref, lead.edge, lead.edges, n)
    block["tail"] = read_rows(lead_ref, lead.edge + lead.edges * n, lead.edges, n)
    return block


def write_block(lay, ref, block):
    n = lay.lines
    write_pieces(lay, ref, block["first"])
    write_pieces(lay, ref, block["last"], lay.total)
    if not lay.leads:
        return
    for e, name in enumerate(("near", "cross", "far")):
        ref[pl.ds(lay.couple + e * n, n), :] = block[name][0]
        if lay.groups > 1:
            write_pair(ref, lay.packed + 2 * e, block[name][1])
    if lay.groups > 1:
        ref[pl.ds(lay.packed + 6, 2), :] = jnp.zeros((2, LANES), jnp.float32)
    write_rows(ref, lay.edge, block["head"], n)
    write_rows(ref, lay.edge + lay.edges * n, block["tail"], n)


def pick(upper, low, high):
    if isinstance(low, list):
        return [pick(upper, a, b) for a, b in zip(low, high)]
    return jnp.where(jnp.full(low.shape, upper, jnp.int32) == 1, high, low)


def write_side(lay, ref, block, upper):
    n = lay.lines
    write_pieces(lay, ref, pick(upper, block["last"], block["first"]))
    if not lay.leads:
        return
    pair = pick(upper, block["far"], block["near"])
    ref[pl.ds(lay.side_couple, n), :] = pair[0]
    if lay.groups > 1:
        ref[pl.ds(lay.side_packed, TILE), :] = pair[1]
    write_rows(ref, lay.side_edge, pick(upper, block["tail"], block["head"]), n)


def read_side(lay, ref, lead, lead_ref):
    n = lead.lines
    couple = [lead_ref[pl.ds(lead.side_couple, n), :]]
    if lead.groups > 1:
        couple.append(lead_ref[pl.ds(lead.side_packed, TILE), :])
    return read_pieces(lay, ref), couple, read_rows(lead_ref, lead.side_edge, lead.edges, n)


def ordered(upper, own, other):
    low = {name: pick(upper, own[name], other[name]) for name in own}
    high = {name: pick(upper, other[name], own[name]) for name in own}
    return low, high


def joint(low, high):
    return [1.0 / (1.0 - far * near) for far, near in zip(low["far"], high["near"])]


def merge(lay, low, high):
    shrink = joint(low, high)
    groups = range(len(shrink))
    to_low = [low["cross"][g] * shrink[g] for g in groups]
    to_high = [high["cross"][g] * shrink[g] for g in groups]
    span = range(len(lay.sizes))
    of = lay.group
    block = {
        "first": [
            low["first"][i]
            + to_low[of(i)] * (high["first"][i] + high["near"][of(i)] * low["last"][i])
            for i in span
        ],
        "last": [
            high["last"][i]
            + to_high[of(i)] * (low["last"][i] + low["far"][of(i)] * high["first"][i])
            for i in span
        ],
    }
    block["near"] = [low["near"][g] + to_low[g] * low["cross"][g] * high["near"][g] for g in groups]
    block["cross"] = [to_low[g] * high["cross"][g] for g in groups]
    block["far"] = [high["far"][g] + to_high[g] * high["cross"][g] * low["far"][g] for g in groups]
    block["head"] = low["head"]
    block["tail"] = high["tail"]
    return block


def inner(lay, low, high, before, after):
    shrink = joint(low, high)
    low_last, high_first = [], []
    for i in range(len(lay.sizes)):
        g = lay.group(i)
        left = low["last"][i] + low["cross"][g] * before[i]
        right = high["first"][i] + high["cross"][g] * after[i]
        low_last.append((left + low["far"][g] * right) * shrink[g])
        high_first.append((right + high["near"][g] * left) * shrink[g])
    return low_last, high_first


def merge_kernel(lay, lead, bit, top, me_ref, own, other, *refs):
    out, *side = refs[-2:] if top else refs[-1:]
    lead_own, lead_other = (own, other) if lay.leads else refs[:2]
    upper = (me_ref[0] >> bit) & 1
    low, high = ordered(
        upper, read_block(lay, own, lead, lead_own), read_block(lay, other, lead, lead_other)
    )
    block = merge(lay, low, high)
    write_block(lay, out, block)
    if top:
        write_side(lay, side[0], block, (me_ref[0] >> (bit + 1)) & 1)


def first_merge_kernel(lay, bit, top, me_ref, own, slim, apart, *refs):
    out, joined, *side = refs[-3:] if top else refs[-2:]
    joined[pl.ds(0, lay.couple), :] = slim[pl.ds(0, lay.couple), :]
    joined[pl.ds(lay.packed, TILE), :] = slim[pl.ds(lay.couple, TILE), :]
    joined[pl.ds(lay.couple, 3 * lay.lines), :] = apart[pl.ds(0, 3 * lay.lines), :]
    edges = 2 * lay.edges * lay.lines
    joined[pl.ds(lay.edge, edges), :] = apart[pl.ds(3 * lay.lines, edges), :]
    merge_kernel(lay, lay, bit, top, me_ref, own, joined, out, *side)


def solve_lines(lay, lead, levels, me, refs):
    owns, gots = refs[:levels], refs[levels : 2 * levels]
    lead_owns, lead_gots = owns, gots
    if not lay.leads:
        lead_owns, lead_gots = refs[2 * levels : 3 * levels], refs[3 * levels : 4 * levels]
    top = levels - 1
    upper = (me >> top) & 1
    own = read_block(lay, owns[top], lead, lead_owns[top])
    met, met_couple, met_edge = read_side(lay, gots[top], lead, lead_gots[top])
    facing = pick(upper, own["last"], own["first"])
    couple = pick(upper, own["far"], own["near"])
    shrink = [1.0 / (1.0 - a * b) for a, b in zip(met_couple, couple)]
    found = []
    for i in range(len(lay.sizes)):
        g = lay.group(i)
        found.append((met[i] + met_couple[g] * facing[i]) * shrink[g])
    zeros = [jnp.zeros_like(v) for v in found]
    blank = [jnp.zeros_like(v) for v in met_edge]
    state = (
        pick(upper, zeros, found), pick(upper, found, zeros),
        pick(upper, blank, met_edge), pick(upper, met_edge, blank),
    )
    partner = None
    for level in reversed(range(top)):
        upper = (me >> level) & 1
        low, high = ordered(
            upper,
            read_block(lay, owns[level], lead, lead_owns[level]),
            read_block(lay, gots[level], lead, lead_gots[level]),
        )
        before, after, behind, ahead = state
        low_last, high_first = inner(lay, low, high, before, after)
        lower = (before, high_first, behind, high["head"])
        higher = (low_last, after, low["tail"], ahead)
        state = tuple(pick(upper, a, b) for a, b in zip(lower, higher))
        partner = tuple(pick(upper, a, b) for a, b in zip(higher, lower))
    return state, partner


def write_answer(lay, ref, state):
    before, after, behind, ahead = state
    write_pieces(lay, ref, before)
    write_pieces(lay, ref, after, lay.total)
    if lay.leads:
        write_rows(ref, 2 * lay.total, behind + ahead, lay.lines)


def solve_kernel(lay, lead, levels, me_ref, *refs):
    state, partner = solve_lines(lay, lead, levels, me_ref[0], refs[:-2])
    write_answer(lay, refs[-2], state)
    write_answer(lay, refs[-1], partner)


def corners(weights):
    one = jnp.ones_like(weights[0])
    value, slope, chain = one, one, [one]
    for weight in weights:
        value, slope = growing_step(value, slope, weight)
        chain.append(value)
    back, fall, backs = one, one, []
    for weight in reversed(weights):
        backs.append(back)
        back, fall = growing_step(back, fall, weight)
    backs.reverse()
    return chain, backs, 1.0 / value


def z_part(dims, lay, cot, phi, psi, w, left, right, arrived, record, turned, az):
    nx, ny = dims
    tiles = nx * ny // LANES
    sums = sum_matrix()
    for c in range(len(lay.sizes)):
        arrived(c)
        for t in range(tiles):
            span = pl.ds(t * LANES, LANES)
            cells, up, down = cot[c, span, :], phi[span, :], psi[span, :]
            wide = jnp.concatenate([up * cells, down * cells], axis=1)
            found = jnp.dot(
                jnp.concatenate(split3(wide), axis=0), sums, preferred_element_type=jnp.float32
            )
            found = found[:LANES] + (found[LANES : 2 * LANES] + found[2 * LANES :])
            az[c, span, :] = w[span, :] * (down * found[:, :LANES] + up * found[:, LANES:])
        first = jnp.zeros((nx, LANES), jnp.float32)
        last = jnp.zeros((nx, LANES), jnp.float32)
        for y in range(ny):
            cells = az[c, pl.ds(y, nx, stride=ny), :]
            span = pl.ds(y * nx, nx)
            turned[c, span, :] = cells
            first = first + left[span, :] * cells
            last = last + right[span, :] * cells
        record[pl.ds(lay.offsets[c], nx), :] = first
        record[pl.ds(lay.total + lay.offsets[c], nx), :] = last


def carried(maps, state):
    return maps[0] * state[0] + maps[1] * state[1], maps[2] * state[0] + maps[3] * state[1]


def z_continuants(tiles, wt, pht, pst, maps, ends):
    deep = LANES // TILE
    lines = tiles * TILE
    one = jnp.ones((lines, LANES), jnp.float32)
    zero = jnp.zeros((lines, LANES), jnp.float32)

    def at(k, t):
        return pl.ds(t * LANES + k, TILE, stride=deep)

    weights = [
        jnp.concatenate([wt[at(k, t), :] for t in range(tiles)], axis=0) for k in range(deep)
    ]
    found = []
    for order in (range(deep), reversed(range(deep))):
        pair = [(one, zero), (zero, one)]
        values = {}
        for k in order:
            values[k] = (pair[0][0], pair[1][0])
            pair = [growing_step(*state, weights[k]) for state in pair]
        base = len(found) * 4 * lines
        found.append(values)
        for i, entry in enumerate((pair[0][0], pair[1][0], pair[0][1], pair[1][1])):
            maps[pl.ds(base + i * lines, lines), :] = entry
    state = (jnp.ones((tiles, LANES), jnp.float32),) * 2
    for side, order in enumerate((range(TILE), reversed(range(TILE)))):
        for s in order:
            for i in range(2):
                ends[pl.ds((2 * side + i) * lines + s, tiles, stride=TILE), :] = state[i]
            rows = [pl.ds((4 * side + i) * lines + s, tiles, stride=TILE) for i in range(4)]
            state = carried([maps[row, :] for row in rows], state)
        state = (1.0 / state[0],) * 2
    for values, target, side in ((found[0], pht, 0), (found[1], pst, 1)):
        first, second = (ends[pl.ds((2 * side + i) * lines, lines), :] for i in range(2))
        for k in range(deep):
            cells = values[k][0] * first + values[k][1] * second
            for t in range(tiles):
                target[at(k, t), :] = cells[t * TILE : (t + 1) * TILE]


def lead_z_kernel(
    dims, lay, cot_any, diff_any, phase_any, cour_any, upw_any,
    record, turned, w, left, right, phi, psi, later,
    az, cot, diff, phase, cour, upw, wt, pht, pst, maps, ends, in_sems, sems,
):
    nx, ny = dims
    tiles = nx * ny // LANES
    count = len(lay.sizes)
    ahead = pltpu.make_async_copy(cot_any.at[pl.ds(count, later.shape[0])], later, sems.at[4])
    small = [(diff_any, diff), (phase_any, phase), (cour_any.at[1], cour), (upw_any.at[1], upw)]
    for i, (source, target) in enumerate(small):
        pltpu.make_async_copy(source, target, sems.at[i]).start()
    for c in range(count):
        pltpu.make_async_copy(cot_any.at[c], cot.at[c], in_sems.at[c]).start()
    ahead.start()

    for i, (source, target) in enumerate(small[:2]):
        pltpu.make_async_copy(source, target, sems.at[i]).wait()
    w[...] = weight_of(diff[...], phase[...])
    for t in range(tiles):
        span = pl.ds(t * LANES, LANES)
        wt[span, :] = w[span, :].T
    z_continuants(tiles, wt, pht, pst, maps, ends)
    for t in range(tiles):
        span = pl.ds(t * LANES, LANES)
        phi[span, :] = pht[span, :].T
        psi[span, :] = pst[span, :].T

    chain, backs, total = corners([w[pl.ds(y, nx, stride=ny), :] for y in range(ny)])
    for y in range(ny):
        span = pl.ds(y * nx, nx)
        left[span, :] = backs[y] * total
        right[span, :] = chain[y] * total
    write_rows(record, lay.couple, [backs[0] * total, total, chain[ny - 1] * total], nx)
    for i, (source, target) in enumerate(small[2:]):
        pltpu.make_async_copy(source, target, sems.at[2 + i]).wait()
    for e, y in enumerate((0, ny - 1)):
        edge = pl.ds(y, nx, stride=ny)
        weight = w[edge, :]
        up = cour[edge, :] * upw[edge, :].astype(jnp.float32)
        flow = up if e == 0 else cour[edge, :] - up
        write_rows(record, lay.edge + 2 * e * nx, [weight, weight * flow], nx)

    def arrived(c):
        pltpu.make_async_copy(cot_any.at[c], cot.at[c], in_sems.at[c]).wait()

    z_part(dims, lay, cot, phi, psi, w, left, right, arrived, record, turned, az)
    ahead.wait()


def next_z_kernel(dims, lay, cot, phi, psi, w, left, right, record, turned, az):
    z_part(dims, lay, cot, phi, psi, w, left, right, lambda c: None, record, turned, az)


def coef_kernel(dims, w, courant, upwind, after, block, inv, wy, xinv, seam, left, right, flows):
    del after
    nx, ny = dims
    rows = nx * ny
    one = jnp.ones((ny, LANES), jnp.float32)
    value, slope, back, fall = one, one, one, one
    for k in range(nx):
        low, high = pl.ds(k * ny, ny), pl.ds((nx - 1 - k) * ny, ny)
        right[low, :] = value
        left[high, :] = back
        new_value, slope = growing_step(value, slope, w[low, :])
        new_back, fall = growing_step(back, fall, w[high, :])
        if k < nx // 2:
            up, down = value / new_value, back / new_back
            xinv[low, :] = up
            xinv[high, :] = down
        end, value = value, new_value
        corner, back = back, new_back
    seam[...] = 1.0 / (1.0 - up * down)
    total = 1.0 / value
    block[pl.ds(0, ny), :] = corner * total
    block[pl.ds(ny, ny), :] = total
    block[pl.ds(2 * ny, ny), :] = end * total
    value = jnp.ones((nx, LANES), jnp.float32)
    slope = value
    for y in range(ny):
        weight = w[pl.ds(y, nx, stride=ny), :]
        wy[pl.ds(y * nx, nx), :] = weight
        new_value, slope = growing_step(value, slope, weight)
        inv[pl.ds(y * nx, nx), :] = value / new_value
        value = new_value

    lane = lax.broadcasted_iota(jnp.int32, (ny, LANES), 1)

    def plane(x, carry):
        span = pl.ds(x * ny, ny)
        scale = w[span, :] * total
        left[span, :] = left[span, :] * scale
        right[span, :] = right[span, :] * scale
        own = one
        for d in range(3):
            flow = courant[d, span, :]
            up = flow * upwind[d, span, :].astype(jnp.float32)
            down = flow - up
            own = own + (down - up)
            if d == 2:
                up = jnp.where(lane == 0, 0.0, up)
                down = jnp.where(lane == LANES - 1, 0.0, down)
            flows[pl.ds((1 + 2 * d) * rows + x * ny, ny), :] = up
            flows[pl.ds((2 + 2 * d) * rows + x * ny, ny), :] = down
        flows[span, :] = own
        return carry

    lax.fori_loop(0, nx, plane, 0, unroll=4)
    first, last = pl.ds(0, ny), pl.ds(rows - ny, ny)
    block[pl.ds(3 * ny, ny), :] = w[first, :] * flows[pl.ds(rows, ny), :]
    block[pl.ds(4 * ny, ny), :] = w[last, :] * flows[pl.ds(2 * rows + rows - ny, ny), :]


def sides(before, after, x):
    return two_sides(before[pl.ds(x, 1), :], after[pl.ds(x, 1), :])


def y_kernel(dims, ylay, xlay, me_ref, az, own, got, w, wy, inv, xinv, seam, *refs):
    nx, ny = dims
    comps = len(ylay.sizes)
    if xlay.leads:
        part, block, slim, field, ghost, ginv, gseam, gleft, gright, before, after, ay, joined = refs
    else:
        before, after, ginv, gseam, gleft, gright, block, field, ghost, fleft, fright, ay, joined = refs
        for x in range(nx):
            here = pl.ds(x * TILE, TILE)
            scale = sides(before, after, nx + x)
            fleft[here, :] = gleft[here, :] * scale
            fright[here, :] = gright[here, :] * scale
    joined[...] = pick(me_ref[0] & 1, got[...], own[...])
    if xlay.leads:
        before[...] = joined[pl.ds(2 * ylay.total, 2 * nx), :]
        after[...] = joined[pl.ds(2 * ylay.total + 2 * nx, 2 * nx), :]
        one = jnp.ones((TILE, LANES), jnp.float32)
        value, slope, back, fall = one, one, one, one
        for k in range(nx):
            low, high = pl.ds(k * TILE, TILE), pl.ds((nx - 1 - k) * TILE, TILE)
            gright[low, :] = value
            gleft[high, :] = back
            new_value, slope = growing_step(value, slope, sides(before, after, k))
            new_back, fall = growing_step(back, fall, sides(before, after, nx - 1 - k))
            if k < nx // 2:
                up, down = value / new_value, back / new_back
                ginv[low, :] = up
                ginv[high, :] = down
            end, value = value, new_value
            corner, back = back, new_back
        gseam[...] = 1.0 / (1.0 - up * down)
        total = 1.0 / value
        for x in range(nx):
            here = pl.ds(x * TILE, TILE)
            gleft[here, :] = gleft[here, :] * total
            gright[here, :] = gright[here, :] * total

    ghost[...] = jnp.zeros(ghost.shape, jnp.float32)
    for c in range(comps):
        fb = joined[pl.ds(c * nx, nx), :]
        fa = joined[pl.ds(ylay.total + c * nx, nx), :]
        ghost[pl.ds(c, nx, stride=TILE), :] = before[pl.ds(0, nx), :] * fb
        ghost[pl.ds(SIDE + c, nx, stride=TILE), :] = after[pl.ds(0, nx), :] * fa
        swept, chain = fb, []
        for y in range(ny):
            row = pl.ds(y * nx, nx)
            swept = (az[c, row, :] + swept) * inv[row, :]
            chain.append(swept)
        later = fa
        for y in reversed(range(ny)):
            row = pl.ds(y * nx, nx)
            later = chain[y] + inv[row, :] * later
            ay[c, pl.ds(y, nx, stride=ny), :] = later * wy[row, :]

    def load(i, x):
        return ghost[pl.ds(x * TILE, TILE), :] if i == comps else ay[i, pl.ds(x * ny, ny), :]

    def keep(i, x, cells):
        if i == comps:
            ghost[pl.ds(x * TILE, TILE), :] = cells
        else:
            ay[i, pl.ds(x * ny, ny), :] = cells

    def pivot(i, x):
        return ginv[pl.ds(x * TILE, TILE), :] if i == comps else xinv[pl.ds(x * ny, ny), :]

    def finish(i, x, cells):
        if i == comps:
            ghost[pl.ds(x * TILE, TILE), :] = cells * sides(before, after, nx + x)
        else:
            here = pl.ds(x * ny, ny)
            field[i, here, :] = cells * w[here, :]

    pieces = range(comps + 1)
    middle = nx // 2
    lows = [jnp.zeros((n, LANES), jnp.float32) for n in xlay.sizes]
    highs = list(lows)
    for k in range(middle):
        x, mirror = k, nx - 1 - k
        for i in pieces:
            lows[i] = (load(i, x) + lows[i]) * pivot(i, x)
            highs[i] = (load(i, mirror) + highs[i]) * pivot(i, mirror)
            if k + 1 < middle:
                keep(i, x, lows[i])
                keep(i, mirror, highs[i])
    for i in pieces:
        joint_scale = gseam[...] if i == comps else seam[...]
        highs[i] = (highs[i] + pivot(i, middle) * lows[i]) * joint_scale
        lows[i] = lows[i] + pivot(i, middle - 1) * highs[i]
        finish(i, middle - 1, lows[i])
        finish(i, middle, highs[i])
    for k in range(1, middle):
        x, mirror = middle - 1 - k, middle + k
        for i in pieces:
            lows[i] = load(i, x) + pivot(i, x) * lows[i]
            highs[i] = load(i, mirror) + pivot(i, mirror) * highs[i]
            finish(i, x, lows[i])
            finish(i, mirror, highs[i])
    solved, lasts = lows, highs
    record = {"first": solved, "last": lasts}
    if xlay.leads:
        pieces = [part[pl.ds(i * ny, ny), :] for i in range(5)]
        record["near"] = [pieces[0], corner * total]
        record["cross"] = [pieces[1], total]
        record["far"] = [pieces[2], end * total]
        record["head"], record["tail"] = pieces[3:4], pieces[4:5]
    write_block(xlay, block, record)
    if xlay.leads:
        slim[pl.ds(0, xlay.couple), :] = block[pl.ds(0, xlay.couple), :]
        slim[pl.ds(xlay.couple, TILE), :] = block[pl.ds(xlay.packed, TILE), :]


def x_kernel(dims, lay, lead, levels, shift, start, me_ref, *refs):
    nx, ny = dims
    count = (2 if lay.leads else 4) * levels
    state, _ = solve_lines(lay, lead, levels, me_ref[0] >> shift, refs[:count])
    left, right, gleft, gright, flows, inputs, ghost, *rest = refs[count:]
    out_any, out, field, fluxes, sems = rest[-5:]
    rows = nx * ny
    tiles = ny // TILE
    comps = len(lay.sizes) - 1
    starts, nexts, (near,), (far,) = state

    def fill(x, carry):
        span, above = pl.ds(x * ny, ny), pl.ds((x + 1) * ny, ny)
        lower, upper = left[span, :], right[span, :]
        for c in range(comps):
            field[c, above, :] = inputs[c, span, :] + lower * starts[c] + upper * nexts[c]
        here = pl.ds(x * TILE, TILE)
        fluxes[here, :] = ghost[here, :] + gleft[here, :] * starts[comps] + gright[here, :] * nexts[comps]
        return carry

    lax.fori_loop(0, nx, fill, 0, unroll=8)
    blank = jnp.zeros((comps, ny, LANES), jnp.float32)
    field[:, pl.ds(0, ny), :] = blank
    field[:, pl.ds((nx + 1) * ny, ny), :] = blank

    line = lax.broadcasted_iota(jnp.int32, (TILE, LANES), 0)

    def advect(x, carry):
        before = jnp.maximum(x - 1, 0)
        beyond = jnp.minimum(x + 1, nx - 1)

        def flow(kind, plane, t):
            begin = pl.multiple_of(kind * rows + plane * ny + t * TILE, TILE)
            return flows[pl.ds(begin, TILE), :]

        own = [flow(0, x, t) for t in range(tiles)]
        ahead_x = [flow(1, beyond, t) for t in range(tiles)]
        behind_x = [flow(2, before, t) for t in range(tiles)]
        ahead_y = [flow(3, x, t) for t in range(tiles)]
        behind_y = [flow(4, x, t) for t in range(tiles)]
        ahead_z = [flow(5, x, t) for t in range(tiles)]
        behind_z = [flow(6, x, t) for t in range(tiles)]
        for c in range(comps):

            def cells(plane, t):
                begin = pl.multiple_of((plane + 1) * ny + t * TILE, TILE)
                return field[c, pl.ds(begin, TILE), :]

            grad = [cells(x, t) for t in range(tiles)]
            ups = [pltpu.roll(ahead_y[t] * grad[t], TILE - 1, 0) for t in range(tiles)]
            downs = [pltpu.roll(behind_y[t] * grad[t], 1, 0) for t in range(tiles)]
            lowest = fluxes[pl.ds(x * TILE + c, 1), :]
            highest = fluxes[pl.ds(x * TILE + SIDE + c, 1), :]
            for t in range(tiles):
                part = own[t] * grad[t]
                part = part + ahead_x[t] * cells(x + 1, t) - behind_x[t] * cells(x - 1, t)
                enter = ups[t + 1] if t + 1 < tiles else jnp.broadcast_to(highest, (TILE, LANES))
                part = part + jnp.where(line == TILE - 1, enter, ups[t])
                enter = downs[t - 1] if t > 0 else jnp.broadcast_to(lowest, (TILE, LANES))
                part = part - jnp.where(line == 0, enter, downs[t])
                part = part + pltpu.roll(ahead_z[t] * grad[t], LANES - 1, 1)
                part = part - pltpu.roll(behind_z[t] * grad[t], 1, 1)
                out[c, pl.ds(pl.multiple_of(x * ny + t * TILE, TILE), TILE), :] = part
        return carry

    parts = 8
    share = nx // parts

    def copy(part):
        span = pl.ds(part * share * ny, share * ny)
        target = out_any.at[pl.ds(start, comps), span, :]
        return pltpu.make_async_copy(out.at[:, span, :], target, sems.at[part])

    top, bottom = pl.ds(0, ny), pl.ds(rows - ny, ny)
    for part in range(parts):
        lax.fori_loop(part * share, (part + 1) * share, advect, 0, unroll=share)
        for c in range(comps):
            if part == 0:
                out[c, top, :] = out[c, top, :] - near * starts[c]
            if part == parts - 1:
                out[c, bottom, :] = out[c, bottom, :] + far * nexts[c]
        copy(part).start()
    for part in range(parts):
        copy(part).wait()


def call(
    kernel, name, operands, outs, scratch=(), spaces=None, out_spaces=None, mebibytes=4, aliases=None
):
    params = pltpu.CompilerParams(vmem_limit_bytes=mebibytes * 1024 * 1024)
    memory = {"v": pltpu.VMEM, "k": pltpu.VMEM, "h": pltpu.HBM, "s": pltpu.SMEM}
    held = {"h": pltpu.HBM, "k": pltpu.VMEM}
    spaces = spaces or "s" + "v" * (len(operands) - 1)
    out_spaces = out_spaces or "v" * len(outs)
    operands = [
        pltpu.with_memory_space_constraint(o, held[s]) if s in held else o
        for o, s in zip(operands, spaces)
    ]
    return pl.pallas_call(
        kernel,
        name=name,
        out_shape=[
            held[s](shape, jnp.float32) if s in held else jax.ShapeDtypeStruct(shape, jnp.float32)
            for shape, s in zip(outs, out_spaces)
        ],
        in_specs=[pl.BlockSpec(memory_space=memory[s]) for s in spaces],
        out_specs=[pl.BlockSpec(memory_space=memory[s]) for s in out_spaces],
        scratch_shapes=list(scratch),
        input_output_aliases=aliases or {},
        compiler_params=params,
        cost_estimate=pl.CostEstimate(flops=10**9, bytes_accessed=10**7, transcendentals=0),
    )(*operands)


def exchange(rows, axis, bit, odd=False):
    count = lax.axis_size(axis)
    pairs = [(i, i ^ (1 << bit)) for i in range(count)]
    if odd:
        pairs = [(i, j) for i, j in pairs if (j if bit == 0 else i) % 2]
    return lax.ppermute(rows, axis, pairs)


class Ladder:
    def __init__(self, lay, axis, shift, me, send, keep, lead=None, odd=False):
        self.odd = odd
        self.lay, self.axis, self.shift, self.me, self.lead = lay, axis, shift, me, lead
        self.levels = (lax.axis_size(axis) - 1).bit_length()
        self.owns, self.gots, self.outgoing = [keep], [], send

    def send(self):
        self.gots.append(exchange(self.outgoing, self.axis, len(self.gots), self.odd))

    def merge(self, beside=(), apart=None):
        level = len(self.owns) - 1
        top = level == self.levels - 2
        lay, bit = self.lay, self.shift + level
        leader = self.lead or self
        operands = (self.me, self.owns[-1], self.gots[-1])
        if not lay.leads:
            operands += (leader.owns[level], leader.gots[level])
        shapes = [(lay.rows, LANES)] + ([(lay.side_rows, LANES)] if top else [])
        kernel = functools.partial(merge_kernel, lay, leader.lay, bit, top)
        if apart is not None:
            kernel = functools.partial(first_merge_kernel, lay, bit, top)
            operands += (apart,)
            shapes = shapes[:1] + shapes
        found = call(kernel, "merge_" + self.axis, operands + tuple(beside), shapes)
        self.owns.append(found[0])
        self.outgoing = found[-1] if top else found[0]
        if apart is not None:
            self.gots[0] = found[1]

    def records(self):
        found = (*self.owns, *self.gots)
        return found if self.lay.leads else found + (*self.lead.owns, *self.lead.gots)


def on_device(cotangent, diffusion, phase, courant, upwind):
    comps, nx, ny, nz = cotangent.shape
    shift = (lax.axis_size("gy") - 1).bit_length()
    rows = nx * ny
    size = comps // 2
    starts = (0, size)
    counts = (size, comps - size)
    ylays = [Layout([nx] * n, 1, 2, nx, g == 0) for g, n in enumerate(counts)]
    xlays = [Layout([ny] * n + [TILE], 2, 1, ny, g == 0) for g, n in enumerate(counts)]
    me = lax.axis_index(("gx", "gy")).astype(jnp.int32).reshape(1)

    def vmem(*shape, dtype=jnp.float32):
        return pltpu.VMEM(shape, dtype)

    flat = (rows, nz)
    cot = cotangent.reshape(comps, rows, nz)
    cour = courant.reshape(3, rows, nz)
    upw = upwind.reshape(3, rows, nz)
    n = counts[0]
    record, az, w, left, right, phi, psi, cot_next = call(
        functools.partial(lead_z_kernel, (nx, ny), ylays[0]),
        "z_solve_lead",
        (cot, diffusion.reshape(flat), phase.reshape(flat), cour, upw),
        [(ylays[0].rows, nz), (n, rows, nz)] + [flat] * 5 + [(counts[1], rows, nz)],
        [
            vmem(n, rows, nz), vmem(n, rows, nz), vmem(*flat), vmem(*flat, dtype=jnp.int32),
            vmem(*flat), vmem(*flat, dtype=jnp.int32),
            vmem(*flat), vmem(*flat), vmem(*flat),
            vmem(rows // LANES * 8 * TILE, nz), vmem(rows // LANES * 4 * TILE, nz),
            pltpu.SemaphoreType.DMA((n,)), pltpu.SemaphoreType.DMA((5,)),
        ],
        spaces="hhhhh",
        mebibytes=12,
    )
    lead = Ladder(ylays[0], "gy", 0, me, record, record, odd=True)
    lead.send()
    azs = [az]
    n = counts[1]
    record, az = call(
        functools.partial(next_z_kernel, (nx, ny), ylays[1]),
        "z_solve_next",
        (cot_next, phi, psi, w, left, right),
        [(ylays[1].rows, nz), (n, rows, nz)],
        [vmem(n, rows, nz)],
        spaces="vvvvvv",
        mebibytes=8,
    )
    azs.append(az)
    follow = Ladder(ylays[1], "gy", 0, me, record, record, lead, odd=True)
    follow.send()
    beside = (record,)
    for level in range(lead.levels - 1):
        lead.merge(beside)
        lead.send()
        follow.merge((apart,) if level == 1 else ())
        follow.send()
        beside = (follow.outgoing,)
        if level == 0:
            part, inv, wy, xinv, seam, xleft, xright, flows = call(
                functools.partial(coef_kernel, (nx, ny)),
                "x_coefficients",
                (w, cour, upw, lead.owns[1]),
                [(5 * ny, nz), flat, flat, flat, (ny, nz), flat, flat, (7 * rows, nz)],
                spaces="vvvv",
                mebibytes=8,
            )
            beside = (part, follow.outgoing)
            apart = exchange(part, "gx", 0)
    ladders, mets, answers = (lead, follow), [], []
    for g, ladder in enumerate(ladders):
        answer, passed = call(
            functools.partial(solve_kernel, ylays[g], ylays[0], ladder.levels),
            "y_reduced",
            (me,) + ladder.records() + ((follow.gots[-1],) if g == 0 else ()),
            [(ylays[g].answer_rows, nz)] * 2,
        )
        answers.append(answer)
        count = lax.axis_size("gy")
        mets.append(lax.ppermute(passed, "gy", [(i, i - 1) for i in range(1, count, 2)]))
    fields, ghosts, climbs = [], [], []
    for g in range(2):
        common = (me, azs[g], answers[g], mets[g], w, wy, inv, xinv, seam)
        edge = (nx * TILE, nz)
        outs = [(counts[g], rows, nz), edge]
        scratch = [vmem(counts[g], rows, nz), vmem(ylays[g].answer_rows, nz)]
        body = functools.partial(y_kernel, (nx, ny), ylays[g], xlays[g])
        if g == 0:
            block, slim, field, ghost, ginv, gseam, gleft, gright, before, after = call(
                body,
                "y_solve_lead",
                common + (part,),
                [(xlays[0].rows, nz), (xlays[0].couple + TILE, nz)]
                + outs + [edge, (TILE, nz), edge, edge] + [(2 * nx, nz)] * 2,
                scratch,
                mebibytes=6,
            )
            climbs.append(Ladder(xlays[0], "gx", shift, me, slim, block))
        else:
            block, field, ghost, gleft, gright = call(
                body,
                "y_solve_next",
                common + (before, after, ginv, gseam, gleft, gright),
                [(xlays[1].rows, nz)] + outs + [edge] * 2,
                scratch,
                mebibytes=6,
            )
            climbs.append(Ladder(xlays[1], "gx", shift, me, block, block, climbs[0]))
        fields.append(field)
        ghosts.append(ghost)
        climbs[g].send()
    beside = (block,)
    for level in range(climbs[0].levels - 1):
        for ladder in climbs:
            leads = ladder.lay.leads
            ladder.merge(beside if leads else (), apart if leads and level == 0 else None)
            ladder.send()
        beside = (climbs[1].outgoing,)
    grad = None
    for g, ladder in enumerate(climbs):
        operands = (me, *ladder.records(), xleft, xright, gleft, gright, flows, fields[g], ghosts[g])
        spaces = "s" + "v" * (len(operands) - 1)
        aliases = None
        if g:
            aliases = {len(operands): 0}
            operands, spaces = operands + (grad,), spaces + "h"
        (grad,) = call(
            functools.partial(
                x_kernel, (nx, ny), xlays[g], xlays[0], ladder.levels, shift, starts[g]
            ),
            "x_solve",
            operands,
            [(comps, rows, nz)],
            [
                vmem(counts[g], rows, nz), vmem(counts[g], rows + 2 * ny, nz), vmem(nx * TILE, nz),
                pltpu.SemaphoreType.DMA((8,)),
            ],
            spaces=spaces,
            out_spaces="h",
            mebibytes=8,
            aliases=aliases,
        )
    return grad.reshape(comps, nx, ny, nz)


def solution(mesh):
    placed = (
        P(None, "gx", "gy", None),
        P("gx", "gy", None),
        P("gx", "gy", None),
        P(None, "gx", "gy", None),
        P(None, "gx", "gy", None),
    )
    return jax.shard_map(
        on_device, mesh=mesh, in_specs=placed, out_specs=P(None, "gx", "gy", None), check_vma=False
    )
```

```python
import functools

import jax
import jax.numpy as jnp
from jax import lax
from jax.experimental import pallas as pl
from jax.experimental.pallas import tpu as pltpu
from jax.sharding import PartitionSpec as P

COMPS = 6
LANES = 128
TILE = 8
SIDE = TILE // 2


def weight_of(diffusion, phase):
    return 1.0 / (diffusion * (1.0 + 3.0 * phase.astype(jnp.float32)))


def growing_step(value, slope, weight):
    slope = slope + weight * value
    return value + slope, slope


def split3(cells):
    high = cells.astype(jnp.bfloat16)
    rest = cells - high.astype(jnp.float32)
    middle = rest.astype(jnp.bfloat16)
    low = (rest - middle.astype(jnp.float32)).astype(jnp.bfloat16)
    return high, middle, low


def sum_matrix():
    row = lax.broadcasted_iota(jnp.int32, (2 * LANES, 2 * LANES), 0)
    col = lax.broadcasted_iota(jnp.int32, (2 * LANES, 2 * LANES), 1)
    before = (row < LANES) & (col < LANES) & (row <= col)
    after = (row >= LANES) & (col >= LANES) & (row > col)
    return jnp.where(before | after, 1.0, 0.0).astype(jnp.bfloat16)


class Layout:
    def __init__(self, sizes, groups, edges, lines, leads):
        self.sizes, self.groups, self.edges, self.lines, self.leads = sizes, groups, edges, lines, leads
        self.offsets = [sum(sizes[:i]) for i in range(len(sizes))]
        self.total = sum(sizes)
        packed = TILE if groups > 1 else 0
        self.couple = 2 * self.total
        self.packed = self.couple + 3 * lines
        self.edge = self.packed + packed
        self.side_couple = self.total
        self.side_packed = self.side_couple + lines
        self.side_edge = self.side_packed + packed
        extra = 2 * edges * lines
        self.rows = self.edge + extra if leads else self.couple
        self.side_rows = self.side_edge + extra // 2 if leads else self.total
        self.answer_rows = 2 * self.total + (extra if leads else 0)

    def group(self, piece):
        return 1 if self.groups > 1 and piece == len(self.sizes) - 1 else 0


def read_pieces(lay, ref, base=0):
    return [ref[pl.ds(base + o, n), :] for o, n in zip(lay.offsets, lay.sizes)]


def write_pieces(lay, ref, values, base=0):
    for o, n, value in zip(lay.offsets, lay.sizes, values):
        ref[pl.ds(base + o, n), :] = value


def read_rows(ref, base, count, lines):
    return [ref[pl.ds(base + i * lines, lines), :] for i in range(count)]


def write_rows(ref, base, values, lines):
    for i, value in enumerate(values):
        ref[pl.ds(base + i * lines, lines), :] = value


def two_sides(low, high):
    return jnp.concatenate(
        [jnp.broadcast_to(low, (SIDE, LANES)), jnp.broadcast_to(high, (SIDE, LANES))], axis=0
    )


def read_pair(ref, row):
    return two_sides(ref[pl.ds(row, 1), :], ref[pl.ds(row + 1, 1), :])


def write_pair(ref, row, value):
    ref[pl.ds(row, 1), :] = value[:1]
    ref[pl.ds(row + 1, 1), :] = value[SIDE : SIDE + 1]


def read_block(lay, ref, lead, lead_ref):
    n = lead.lines
    block = {"first": read_pieces(lay, ref), "last": read_pieces(lay, ref, lay.total)}
    for e, name in enumerate(("near", "cross", "far")):
        entry = [lead_ref[pl.ds(lead.couple + e * n, n), :]]
        if lead.groups > 1:
            entry.append(read_pair(lead_ref, lead.packed + 2 * e))
        block[name] = entry
    block["head"] = read_rows(lead_ref, lead.edge, lead.edges, n)
    block["tail"] = read_rows(lead_ref, lead.edge + lead.edges * n, lead.edges, n)
    return block


def write_block(lay, ref, block):
    n = lay.lines
    write_pieces(lay, ref, block["first"])
    write_pieces(lay, ref, block["last"], lay.total)
    if not lay.leads:
        return
    for e, name in enumerate(("near", "cross", "far")):
        ref[pl.ds(lay.couple + e * n, n), :] = block[name][0]
        if lay.groups > 1:
            write_pair(ref, lay.packed + 2 * e, block[name][1])
    if lay.groups > 1:
        ref[pl.ds(lay.packed + 6, 2), :] = jnp.zeros((2, LANES), jnp.float32)
    write_rows(ref, lay.edge, block["head"], n)
    write_rows(ref, lay.edge + lay.edges * n, block["tail"], n)


def pick(upper, low, high):
    if isinstance(low, list):
        return [pick(upper, a, b) for a, b in zip(low, high)]
    return jnp.where(jnp.full(low.shape, upper, jnp.int32) == 1, high, low)


def write_side(lay, ref, block, upper):
    n = lay.lines
    write_pieces(lay, ref, pick(upper, block["last"], block["first"]))
    if not lay.leads:
        return
    pair = pick(upper, block["far"], block["near"])
    ref[pl.ds(lay.side_couple, n), :] = pair[0]
    if lay.groups > 1:
        ref[pl.ds(lay.side_packed, TILE), :] = pair[1]
    write_rows(ref, lay.side_edge, pick(upper, block["tail"], block["head"]), n)


def read_side(lay, ref, lead, lead_ref):
    n = lead.lines
    couple = [lead_ref[pl.ds(lead.side_couple, n), :]]
    if lead.groups > 1:
        couple.append(lead_ref[pl.ds(lead.side_packed, TILE), :])
    return read_pieces(lay, ref), couple, read_rows(lead_ref, lead.side_edge, lead.edges, n)


def ordered(upper, own, other):
    low = {name: pick(upper, own[name], other[name]) for name in own}
    high = {name: pick(upper, other[name], own[name]) for name in own}
    return low, high


def joint(low, high):
    return [1.0 / (1.0 - far * near) for far, near in zip(low["far"], high["near"])]


def merge(lay, low, high):
    shrink = joint(low, high)
    groups = range(len(shrink))
    to_low = [low["cross"][g] * shrink[g] for g in groups]
    to_high = [high["cross"][g] * shrink[g] for g in groups]
    span = range(len(lay.sizes))
    of = lay.group
    block = {
        "first": [
            low["first"][i]
            + to_low[of(i)] * (high["first"][i] + high["near"][of(i)] * low["last"][i])
            for i in span
        ],
        "last": [
            high["last"][i]
            + to_high[of(i)] * (low["last"][i] + low["far"][of(i)] * high["first"][i])
            for i in span
        ],
    }
    block["near"] = [low["near"][g] + to_low[g] * low["cross"][g] * high["near"][g] for g in groups]
    block["cross"] = [to_low[g] * high["cross"][g] for g in groups]
    block["far"] = [high["far"][g] + to_high[g] * high["cross"][g] * low["far"][g] for g in groups]
    block["head"] = low["head"]
    block["tail"] = high["tail"]
    return block


def inner(lay, low, high, before, after):
    shrink = joint(low, high)
    low_last, high_first = [], []
    for i in range(len(lay.sizes)):
        g = lay.group(i)
        left = low["last"][i] + low["cross"][g] * before[i]
        right = high["first"][i] + high["cross"][g] * after[i]
        low_last.append((left + low["far"][g] * right) * shrink[g])
        high_first.append((right + high["near"][g] * left) * shrink[g])
    return low_last, high_first


def merge_kernel(lay, lead, bit, top, me_ref, own, other, *refs):
    out, *side = refs[-2:] if top else refs[-1:]
    lead_own, lead_other = (own, other) if lay.leads else refs[:2]
    upper = (me_ref[0] >> bit) & 1
    low, high = ordered(
        upper, read_block(lay, own, lead, lead_own), read_block(lay, other, lead, lead_other)
    )
    block = merge(lay, low, high)
    write_block(lay, out, block)
    if top:
        write_side(lay, side[0], block, (me_ref[0] >> (bit + 1)) & 1)


def first_merge_kernel(lay, bit, top, me_ref, own, slim, apart, *refs):
    out, joined, *side = refs[-3:] if top else refs[-2:]
    joined[pl.ds(0, lay.couple), :] = slim[pl.ds(0, lay.couple), :]
    joined[pl.ds(lay.packed, TILE), :] = slim[pl.ds(lay.couple, TILE), :]
    joined[pl.ds(lay.couple, 3 * lay.lines), :] = apart[pl.ds(0, 3 * lay.lines), :]
    edges = 2 * lay.edges * lay.lines
    joined[pl.ds(lay.edge, edges), :] = apart[pl.ds(3 * lay.lines, edges), :]
    merge_kernel(lay, lay, bit, top, me_ref, own, joined, out, *side)


def solve_lines(lay, lead, levels, me, refs):
    owns, gots = refs[:levels], refs[levels : 2 * levels]
    lead_owns, lead_gots = owns, gots
    if not lay.leads:
        lead_owns, lead_gots = refs[2 * levels : 3 * levels], refs[3 * levels : 4 * levels]
    top = levels - 1
    upper = (me >> top) & 1
    own = read_block(lay, owns[top], lead, lead_owns[top])
    met, met_couple, met_edge = read_side(lay, gots[top], lead, lead_gots[top])
    facing = pick(upper, own["last"], own["first"])
    couple = pick(upper, own["far"], own["near"])
    shrink = [1.0 / (1.0 - a * b) for a, b in zip(met_couple, couple)]
    found = []
    for i in range(len(lay.sizes)):
        g = lay.group(i)
        found.append((met[i] + met_couple[g] * facing[i]) * shrink[g])
    zeros = [jnp.zeros_like(v) for v in found]
    blank = [jnp.zeros_like(v) for v in met_edge]
    state = (
        pick(upper, zeros, found), pick(upper, found, zeros),
        pick(upper, blank, met_edge), pick(upper, met_edge, blank),
    )
    partner = None
    for level in reversed(range(top)):
        upper = (me >> level) & 1
        low, high = ordered(
            upper,
            read_block(lay, owns[level], lead, lead_owns[level]),
            read_block(lay, gots[level], lead, lead_gots[level]),
        )
        before, after, behind, ahead = state
        low_last, high_first = inner(lay, low, high, before, after)
        lower = (before, high_first, behind, high["head"])
        higher = (low_last, after, low["tail"], ahead)
        state = tuple(pick(upper, a, b) for a, b in zip(lower, higher))
        partner = tuple(pick(upper, a, b) for a, b in zip(higher, lower))
    return state, partner


def write_answer(lay, ref, state):
    before, after, behind, ahead = state
    write_pieces(lay, ref, before)
    write_pieces(lay, ref, after, lay.total)
    if lay.leads:
        write_rows(ref, 2 * lay.total, behind + ahead, lay.lines)


def solve_kernel(lay, lead, levels, me_ref, *refs):
    state, partner = solve_lines(lay, lead, levels, me_ref[0], refs[:-2])
    write_answer(lay, refs[-2], state)
    write_answer(lay, refs[-1], partner)


def corners(weights):
    one = jnp.ones_like(weights[0])
    value, slope, chain = one, one, [one]
    for weight in weights:
        value, slope = growing_step(value, slope, weight)
        chain.append(value)
    back, fall, backs = one, one, []
    for weight in reversed(weights):
        backs.append(back)
        back, fall = growing_step(back, fall, weight)
    backs.reverse()
    return chain, backs, 1.0 / value


def post(mine, keep, send, row, cells):
    half = cells.shape[0] // 2
    low, high = cells[:half], cells[half:]
    keep[pl.ds(row, half), :] = pick(mine, low, high)
    send[pl.ds(row, half), :] = pick(mine, high, low)


def z_part(dims, lay, me_ref, cot, phi, psi, w, left, right, arrived, turned, az, keep, send):
    nx, ny = dims
    tiles = nx * ny // LANES
    sums = sum_matrix()
    mine = me_ref[0] & 1
    for c in range(len(lay.sizes)):
        arrived(c)
        for t in range(tiles):
            span = pl.ds(t * LANES, LANES)
            cells, up, down = cot[c, span, :], phi[span, :], psi[span, :]
            wide = jnp.concatenate([up * cells, down * cells], axis=1)
            found = jnp.dot(
                jnp.concatenate(split3(wide), axis=0), sums, preferred_element_type=jnp.float32
            )
            found = found[:LANES] + (found[LANES : 2 * LANES] + found[2 * LANES :])
            az[c, span, :] = w[span, :] * (down * found[:, :LANES] + up * found[:, LANES:])
        first = jnp.zeros((nx, LANES), jnp.float32)
        last = jnp.zeros((nx, LANES), jnp.float32)
        for y in range(ny):
            cells = az[c, pl.ds(y, nx, stride=ny), :]
            span = pl.ds(y * nx, nx)
            turned[c, span, :] = cells
            first = first + left[span, :] * cells
            last = last + right[span, :] * cells
        post(mine, keep, send, lay.offsets[c], first)
        post(mine, keep, send, lay.total + lay.offsets[c], last)


def carried(maps, state):
    return maps[0] * state[0] + maps[1] * state[1], maps[2] * state[0] + maps[3] * state[1]


def z_continuants(tiles, wt, pht, pst, maps, ends):
    deep = LANES // TILE
    lines = tiles * TILE
    one = jnp.ones((lines, LANES), jnp.float32)
    zero = jnp.zeros((lines, LANES), jnp.float32)

    def at(k, t):
        return pl.ds(t * LANES + k, TILE, stride=deep)

    weights = [
        jnp.concatenate([wt[at(k, t), :] for t in range(tiles)], axis=0) for k in range(deep)
    ]
    found = []
    for order in (range(deep), reversed(range(deep))):
        pair = [(one, zero), (zero, one)]
        values = {}
        for k in order:
            values[k] = (pair[0][0], pair[1][0])
            pair = [growing_step(*state, weights[k]) for state in pair]
        base = len(found) * 4 * lines
        found.append(values)
        for i, entry in enumerate((pair[0][0], pair[1][0], pair[0][1], pair[1][1])):
            maps[pl.ds(base + i * lines, lines), :] = entry
    state = (jnp.ones((tiles, LANES), jnp.float32),) * 2
    for side, order in enumerate((range(TILE), reversed(range(TILE)))):
        for s in order:
            for i in range(2):
                ends[pl.ds((2 * side + i) * lines + s, tiles, stride=TILE), :] = state[i]
            rows = [pl.ds((4 * side + i) * lines + s, tiles, stride=TILE) for i in range(4)]
            state = carried([maps[row, :] for row in rows], state)
        state = (1.0 / state[0],) * 2
    for values, target, side in ((found[0], pht, 0), (found[1], pst, 1)):
        first, second = (ends[pl.ds((2 * side + i) * lines, lines), :] for i in range(2))
        for k in range(deep):
            cells = values[k][0] * first + values[k][1] * second
            for t in range(tiles):
                target[at(k, t), :] = cells[t * TILE : (t + 1) * TILE]


def lead_z_kernel(
    dims, lay, me_ref, cot_any, diff_any, phase_any, cour_any, upw_any,
    keep, send, turned, w, left, right, phi, psi, later,
    az, cot, diff, phase, cour, upw, wt, pht, pst, maps, ends, in_sems, sems,
):
    nx, ny = dims
    tiles = nx * ny // LANES
    half = nx // 2
    count = len(lay.sizes)
    ahead = pltpu.make_async_copy(cot_any.at[pl.ds(count, later.shape[0])], later, sems.at[4])
    small = [(diff_any, diff), (phase_any, phase), (cour_any.at[1], cour), (upw_any.at[1], upw)]
    for i, (source, target) in enumerate(small):
        pltpu.make_async_copy(source, target, sems.at[i]).start()
    for c in range(count):
        pltpu.make_async_copy(cot_any.at[c], cot.at[c], in_sems.at[c]).start()
    ahead.start()

    for i, (source, target) in enumerate(small[:2]):
        pltpu.make_async_copy(source, target, sems.at[i]).wait()
    w[...] = weight_of(diff[...], phase[...])
    for t in range(tiles):
        span = pl.ds(t * LANES, LANES)
        wt[span, :] = w[span, :].T
    z_continuants(tiles, wt, pht, pst, maps, ends)
    for t in range(tiles):
        span = pl.ds(t * LANES, LANES)
        phi[span, :] = pht[span, :].T
        psi[span, :] = pst[span, :].T

    chain, backs, total = corners([w[pl.ds(y, nx, stride=ny), :] for y in range(ny)])
    for y in range(ny):
        span = pl.ds(y * nx, nx)
        left[span, :] = backs[y] * total
        right[span, :] = chain[y] * total
    mine = me_ref[0] & 1
    post(mine, keep, send, lay.couple, backs[0] * total)
    post(mine, keep, send, lay.couple + half, total)
    post(mine, keep, send, lay.couple + 2 * half, chain[ny - 1] * total)
    for i, (source, target) in enumerate(small[2:]):
        pltpu.make_async_copy(source, target, sems.at[2 + i]).wait()
    for e, y in enumerate((0, ny - 1)):
        edge = pl.ds(y, nx, stride=ny)
        weight = w[edge, :]
        up = cour[edge, :] * upw[edge, :].astype(jnp.float32)
        flow = up if e == 0 else cour[edge, :] - up
        post(mine, keep, send, lay.edge + 2 * e * half, weight)
        post(mine, keep, send, lay.edge + (2 * e + 1) * half, weight * flow)

    def arrived(c):
        pltpu.make_async_copy(cot_any.at[c], cot.at[c], in_sems.at[c]).wait()

    z_part(dims, lay, me_ref, cot, phi, psi, w, left, right, arrived, turned, az, keep, send)
    ahead.wait()


def next_z_kernel(dims, lay, me_ref, cot, phi, psi, w, left, right, keep, send, turned, az):
    z_part(
        dims, lay, me_ref, cot, phi, psi, w, left, right, lambda c: None, turned, az, keep, send
    )


def coef_kernel(dims, w, courant, upwind, after, block, inv, wy, xinv, seam, left, right, flows):
    del after
    nx, ny = dims
    rows = nx * ny
    one = jnp.ones((ny, LANES), jnp.float32)
    value, slope, back, fall = one, one, one, one
    for k in range(nx):
        low, high = pl.ds(k * ny, ny), pl.ds((nx - 1 - k) * ny, ny)
        right[low, :] = value
        left[high, :] = back
        new_value, slope = growing_step(value, slope, w[low, :])
        new_back, fall = growing_step(back, fall, w[high, :])
        if k < nx // 2:
            up, down = value / new_value, back / new_back
            xinv[low, :] = up
            xinv[high, :] = down
        end, value = value, new_value
        corner, back = back, new_back
    seam[...] = 1.0 / (1.0 - up * down)
    total = 1.0 / value
    block[pl.ds(0, ny), :] = corner * total
    block[pl.ds(ny, ny), :] = total
    block[pl.ds(2 * ny, ny), :] = end * total
    value = jnp.ones((nx, LANES), jnp.float32)
    slope = value
    for y in range(ny):
        weight = w[pl.ds(y, nx, stride=ny), :]
        wy[pl.ds(y * nx, nx), :] = weight
        new_value, slope = growing_step(value, slope, weight)
        inv[pl.ds(y * nx, nx), :] = value / new_value
        value = new_value

    lane = lax.broadcasted_iota(jnp.int32, (ny, LANES), 1)

    def plane(x, carry):
        span = pl.ds(x * ny, ny)
        scale = w[span, :] * total
        left[span, :] = left[span, :] * scale
        right[span, :] = right[span, :] * scale
        own = one
        for d in range(3):
            flow = courant[d, span, :]
            up = flow * upwind[d, span, :].astype(jnp.float32)
            down = flow - up
            own = own + (down - up)
            if d == 2:
                up = jnp.where(lane == 0, 0.0, up)
                down = jnp.where(lane == LANES - 1, 0.0, down)
            flows[pl.ds((1 + 2 * d) * rows + x * ny, ny), :] = up
            flows[pl.ds((2 + 2 * d) * rows + x * ny, ny), :] = down
        flows[span, :] = own
        return carry

    lax.fori_loop(0, nx, plane, 0, unroll=4)
    first, last = pl.ds(0, ny), pl.ds(rows - ny, ny)
    block[pl.ds(3 * ny, ny), :] = w[first, :] * flows[pl.ds(rows, ny), :]
    block[pl.ds(4 * ny, ny), :] = w[last, :] * flows[pl.ds(2 * rows + rows - ny, ny), :]


def sides(before, after, x):
    return two_sides(before[pl.ds(x, 1), :], after[pl.ds(x, 1), :])


def y_kernel(dims, ylay, xlay, me_ref, az, own, got, w, wy, inv, xinv, seam, *refs):
    nx, ny = dims
    half = nx // 2
    comps = len(ylay.sizes)
    if xlay.leads:
        part, block, slim, field, ghost, ginv, gseam, gleft, gright, before, after, ay, joined = refs
    else:
        before, after, ginv, gseam, gleft, gright, block, field, ghost, fleft, fright, ay, joined = refs
        for x in range(nx):
            here = pl.ds(x * TILE, TILE)
            scale = sides(before, after, nx + x)
            fleft[here, :] = gleft[here, :] * scale
            fright[here, :] = gright[here, :] * scale
    mine = me_ref[0] & 1
    span = ylay.answer_rows
    joined[pl.ds(pl.multiple_of(mine * span, TILE), span), :] = own[...]
    joined[pl.ds(pl.multiple_of((1 - mine) * span, TILE), span), :] = got[...]
    if xlay.leads:
        for h in range(2):
            for e in range(2):
                where = pl.ds(e * nx + h * half, half)
                row = h * span + 2 * ylay.total + e * half
                before[where, :] = joined[pl.ds(row, half), :]
                after[where, :] = joined[pl.ds(row + 2 * half, half), :]
        one = jnp.ones((TILE, LANES), jnp.float32)
        value, slope, back, fall = one, one, one, one
        for k in range(nx):
            low, high = pl.ds(k * TILE, TILE), pl.ds((nx - 1 - k) * TILE, TILE)
            gright[low, :] = value
            gleft[high, :] = back
            new_value, slope = growing_step(value, slope, sides(before, after, k))
            new_back, fall = growing_step(back, fall, sides(before, after, nx - 1 - k))
            if k < nx // 2:
                up, down = value / new_value, back / new_back
                ginv[low, :] = up
                ginv[high, :] = down
            end, value = value, new_value
            corner, back = back, new_back
        gseam[...] = 1.0 / (1.0 - up * down)
        total = 1.0 / value
        for x in range(nx):
            here = pl.ds(x * TILE, TILE)
            gleft[here, :] = gleft[here, :] * total
            gright[here, :] = gright[here, :] * total

    ghost[...] = jnp.zeros(ghost.shape, jnp.float32)
    for c in range(comps):
        for h in range(2):
            piece = pl.ds(h * half, half)
            fb = joined[pl.ds(h * span + c * half, half), :]
            fa = joined[pl.ds(h * span + ylay.total + c * half, half), :]
            ghost[pl.ds(h * half * TILE + c, half, stride=TILE), :] = before[piece, :] * fb
            ghost[pl.ds(h * half * TILE + SIDE + c, half, stride=TILE), :] = after[piece, :] * fa
            swept, chain = fb, []
            for y in range(ny):
                cells = az[c, pl.ds(y * nx + h * half, half), :]
                swept = (cells + swept) * inv[pl.ds(y * nx + h * half, half), :]
                chain.append(swept)
            later = fa
            for y in reversed(range(ny)):
                row = pl.ds(y * nx + h * half, half)
                later = chain[y] + inv[row, :] * later
                ay[c, pl.ds(h * half * ny + y, half, stride=ny), :] = later * wy[row, :]

    def load(i, x):
        return ghost[pl.ds(x * TILE, TILE), :] if i == comps else ay[i, pl.ds(x * ny, ny), :]

    def keep(i, x, cells):
        if i == comps:
            ghost[pl.ds(x * TILE, TILE), :] = cells
        else:
            ay[i, pl.ds(x * ny, ny), :] = cells

    def pivot(i, x):
        return ginv[pl.ds(x * TILE, TILE), :] if i == comps else xinv[pl.ds(x * ny, ny), :]

    def finish(i, x, cells):
        if i == comps:
            ghost[pl.ds(x * TILE, TILE), :] = cells * sides(before, after, nx + x)
        else:
            here = pl.ds(x * ny, ny)
            field[i, here, :] = cells * w[here, :]

    pieces = range(comps + 1)
    middle = nx // 2
    lows = [jnp.zeros((n, LANES), jnp.float32) for n in xlay.sizes]
    highs = list(lows)
    for k in range(middle):
        x, mirror = k, nx - 1 - k
        for i in pieces:
            lows[i] = (load(i, x) + lows[i]) * pivot(i, x)
            highs[i] = (load(i, mirror) + highs[i]) * pivot(i, mirror)
            if k + 1 < middle:
                keep(i, x, lows[i])
                keep(i, mirror, highs[i])
    for i in pieces:
        joint_scale = gseam[...] if i == comps else seam[...]
        highs[i] = (highs[i] + pivot(i, middle) * lows[i]) * joint_scale
        lows[i] = lows[i] + pivot(i, middle - 1) * highs[i]
        finish(i, middle - 1, lows[i])
        finish(i, middle, highs[i])
    for k in range(1, middle):
        x, mirror = middle - 1 - k, middle + k
        for i in pieces:
            lows[i] = load(i, x) + pivot(i, x) * lows[i]
            highs[i] = load(i, mirror) + pivot(i, mirror) * highs[i]
            finish(i, x, lows[i])
            finish(i, mirror, highs[i])
    solved, lasts = lows, highs
    record = {"first": solved, "last": lasts}
    if xlay.leads:
        pieces = [part[pl.ds(i * ny, ny), :] for i in range(5)]
        record["near"] = [pieces[0], corner * total]
        record["cross"] = [pieces[1], total]
        record["far"] = [pieces[2], end * total]
        record["head"], record["tail"] = pieces[3:4], pieces[4:5]
    write_block(xlay, block, record)
    if xlay.leads:
        slim[pl.ds(0, xlay.couple), :] = block[pl.ds(0, xlay.couple), :]
        slim[pl.ds(xlay.couple, TILE), :] = block[pl.ds(xlay.packed, TILE), :]


def x_kernel(dims, lay, lead, levels, shift, start, me_ref, *refs):
    nx, ny = dims
    count = (2 if lay.leads else 4) * levels
    state, _ = solve_lines(lay, lead, levels, me_ref[0] >> shift, refs[:count])
    left, right, gleft, gright, flows, inputs, ghost, *rest = refs[count:]
    out_any, out, field, fluxes, sems = rest[-5:]
    rows = nx * ny
    tiles = ny // TILE
    comps = len(lay.sizes) - 1
    starts, nexts, (near,), (far,) = state

    def fill(x, carry):
        span, above = pl.ds(x * ny, ny), pl.ds((x + 1) * ny, ny)
        lower, upper = left[span, :], right[span, :]
        for c in range(comps):
            field[c, above, :] = inputs[c, span, :] + lower * starts[c] + upper * nexts[c]
        here = pl.ds(x * TILE, TILE)
        fluxes[here, :] = ghost[here, :] + gleft[here, :] * starts[comps] + gright[here, :] * nexts[comps]
        return carry

    lax.fori_loop(0, nx, fill, 0, unroll=8)
    blank = jnp.zeros((comps, ny, LANES), jnp.float32)
    field[:, pl.ds(0, ny), :] = blank
    field[:, pl.ds((nx + 1) * ny, ny), :] = blank

    line = lax.broadcasted_iota(jnp.int32, (TILE, LANES), 0)

    def advect(x, carry):
        before = jnp.maximum(x - 1, 0)
        beyond = jnp.minimum(x + 1, nx - 1)

        def flow(kind, plane, t):
            begin = pl.multiple_of(kind * rows + plane * ny + t * TILE, TILE)
            return flows[pl.ds(begin, TILE), :]

        own = [flow(0, x, t) for t in range(tiles)]
        ahead_x = [flow(1, beyond, t) for t in range(tiles)]
        behind_x = [flow(2, before, t) for t in range(tiles)]
        ahead_y = [flow(3, x, t) for t in range(tiles)]
        behind_y = [flow(4, x, t) for t in range(tiles)]
        ahead_z = [flow(5, x, t) for t in range(tiles)]
        behind_z = [flow(6, x, t) for t in range(tiles)]
        for c in range(comps):

            def cells(plane, t):
                begin = pl.multiple_of((plane + 1) * ny + t * TILE, TILE)
                return field[c, pl.ds(begin, TILE), :]

            grad = [cells(x, t) for t in range(tiles)]
            ups = [pltpu.roll(ahead_y[t] * grad[t], TILE - 1, 0) for t in range(tiles)]
            downs = [pltpu.roll(behind_y[t] * grad[t], 1, 0) for t in range(tiles)]
            lowest = fluxes[pl.ds(x * TILE + c, 1), :]
            highest = fluxes[pl.ds(x * TILE + SIDE + c, 1), :]
            for t in range(tiles):
                part = own[t] * grad[t]
                part = part + ahead_x[t] * cells(x + 1, t) - behind_x[t] * cells(x - 1, t)
                enter = ups[t + 1] if t + 1 < tiles else jnp.broadcast_to(highest, (TILE, LANES))
                part = part + jnp.where(line == TILE - 1, enter, ups[t])
                enter = downs[t - 1] if t > 0 else jnp.broadcast_to(lowest, (TILE, LANES))
                part = part - jnp.where(line == 0, enter, downs[t])
                part = part + pltpu.roll(ahead_z[t] * grad[t], LANES - 1, 1)
                part = part - pltpu.roll(behind_z[t] * grad[t], 1, 1)
                out[c, pl.ds(pl.multiple_of(x * ny + t * TILE, TILE), TILE), :] = part
        return carry

    parts = 8
    share = nx // parts

    def copy(part):
        span = pl.ds(part * share * ny, share * ny)
        target = out_any.at[pl.ds(start, comps), span, :]
        return pltpu.make_async_copy(out.at[:, span, :], target, sems.at[part])

    top, bottom = pl.ds(0, ny), pl.ds(rows - ny, ny)
    for part in range(parts):
        lax.fori_loop(part * share, (part + 1) * share, advect, 0, unroll=share)
        for c in range(comps):
            if part == 0:
                out[c, top, :] = out[c, top, :] - near * starts[c]
            if part == parts - 1:
                out[c, bottom, :] = out[c, bottom, :] + far * nexts[c]
        copy(part).start()
    for part in range(parts):
        copy(part).wait()


def call(
    kernel, name, operands, outs, scratch=(), spaces=None, out_spaces=None, mebibytes=4, aliases=None
):
    params = pltpu.CompilerParams(vmem_limit_bytes=mebibytes * 1024 * 1024)
    memory = {"v": pltpu.VMEM, "k": pltpu.VMEM, "h": pltpu.HBM, "s": pltpu.SMEM}
    held = {"h": pltpu.HBM, "k": pltpu.VMEM}
    spaces = spaces or "s" + "v" * (len(operands) - 1)
    out_spaces = out_spaces or "v" * len(outs)
    operands = [
        pltpu.with_memory_space_constraint(o, held[s]) if s in held else o
        for o, s in zip(operands, spaces)
    ]
    return pl.pallas_call(
        kernel,
        name=name,
        out_shape=[
            held[s](shape, jnp.float32) if s in held else jax.ShapeDtypeStruct(shape, jnp.float32)
            for shape, s in zip(outs, out_spaces)
        ],
        in_specs=[pl.BlockSpec(memory_space=memory[s]) for s in spaces],
        out_specs=[pl.BlockSpec(memory_space=memory[s]) for s in out_spaces],
        scratch_shapes=list(scratch),
        input_output_aliases=aliases or {},
        compiler_params=params,
        cost_estimate=pl.CostEstimate(flops=10**9, bytes_accessed=10**7, transcendentals=0),
    )(*operands)


def exchange(rows, axis, bit):
    count = lax.axis_size(axis)
    return lax.ppermute(rows, axis, [(i, i ^ (1 << bit)) for i in range(count)])


class Ladder:
    def __init__(self, lay, axis, shift, me, send, keep, lead=None):
        self.lay, self.axis, self.shift, self.me, self.lead = lay, axis, shift, me, lead
        self.levels = (lax.axis_size(axis) - 1).bit_length()
        self.owns, self.gots, self.outgoing = [keep], [], send

    def send(self):
        self.gots.append(exchange(self.outgoing, self.axis, len(self.gots)))

    def merge(self, beside=(), apart=None):
        level = len(self.owns) - 1
        top = level == self.levels - 2
        lay, bit = self.lay, self.shift + level
        leader = self.lead or self
        operands = (self.me, self.owns[-1], self.gots[-1])
        if not lay.leads:
            operands += (leader.owns[level], leader.gots[level])
        shapes = [(lay.rows, LANES)] + ([(lay.side_rows, LANES)] if top else [])
        kernel = functools.partial(merge_kernel, lay, leader.lay, bit, top)
        if apart is not None:
            kernel = functools.partial(first_merge_kernel, lay, bit, top)
            operands += (apart,)
            shapes = shapes[:1] + shapes
        found = call(kernel, "merge_" + self.axis, operands + tuple(beside), shapes)
        self.owns.append(found[0])
        self.outgoing = found[-1] if top else found[0]
        if apart is not None:
            self.gots[0] = found[1]

    def records(self):
        found = (*self.owns, *self.gots)
        return found if self.lay.leads else found + (*self.lead.owns, *self.lead.gots)


def on_device(cotangent, diffusion, phase, courant, upwind):
    comps, nx, ny, nz = cotangent.shape
    shift = (lax.axis_size("gy") - 1).bit_length()
    rows = nx * ny
    half = nx // 2
    size = comps // 2
    starts = (0, size)
    counts = (size, comps - size)
    ylays = [Layout([half] * n, 1, 2, half, g == 0) for g, n in enumerate(counts)]
    xlays = [Layout([ny] * n + [TILE], 2, 1, ny, g == 0) for g, n in enumerate(counts)]
    me = lax.axis_index(("gx", "gy")).astype(jnp.int32).reshape(1)

    def vmem(*shape, dtype=jnp.float32):
        return pltpu.VMEM(shape, dtype)

    flat = (rows, nz)
    cot = cotangent.reshape(comps, rows, nz)
    cour = courant.reshape(3, rows, nz)
    upw = upwind.reshape(3, rows, nz)
    n = counts[0]
    keep, send, az, w, left, right, phi, psi, cot_next = call(
        functools.partial(lead_z_kernel, (nx, ny), ylays[0]),
        "z_solve_lead",
        (me, cot, diffusion.reshape(flat), phase.reshape(flat), cour, upw),
        [(ylays[0].rows, nz)] * 2 + [(n, rows, nz)] + [flat] * 5 + [(counts[1], rows, nz)],
        [
            vmem(n, rows, nz), vmem(n, rows, nz), vmem(*flat), vmem(*flat, dtype=jnp.int32),
            vmem(*flat), vmem(*flat, dtype=jnp.int32),
            vmem(*flat), vmem(*flat), vmem(*flat),
            vmem(rows // LANES * 8 * TILE, nz), vmem(rows // LANES * 4 * TILE, nz),
            pltpu.SemaphoreType.DMA((n,)), pltpu.SemaphoreType.DMA((5,)),
        ],
        spaces="shhhhh",
        mebibytes=12,
    )
    lead = Ladder(ylays[0], "gy", 0, me, send, keep)
    lead.send()
    azs = [az]
    n = counts[1]
    keep, send, az = call(
        functools.partial(next_z_kernel, (nx, ny), ylays[1]),
        "z_solve_next",
        (me, cot_next, phi, psi, w, left, right),
        [(ylays[1].rows, nz)] * 2 + [(n, rows, nz)],
        [vmem(n, rows, nz)],
        mebibytes=8,
    )
    azs.append(az)
    follow = Ladder(ylays[1], "gy", 0, me, send, keep, lead)
    follow.send()
    beside = (send,)
    for level in range(lead.levels - 1):
        lead.merge(beside)
        lead.send()
        follow.merge()
        follow.send()
        beside = (follow.outgoing,)
        if level == 0:
            part, inv, wy, xinv, seam, xleft, xright, flows = call(
                functools.partial(coef_kernel, (nx, ny)),
                "x_coefficients",
                (w, cour, upw, lead.owns[1]),
                [(5 * ny, nz), flat, flat, flat, (ny, nz), flat, flat, (7 * rows, nz)],
                spaces="vvvv",
                mebibytes=8,
            )
            beside = (part, follow.outgoing)
            apart = exchange(part, "gx", 0)
    ladders, mets, answers = (lead, follow), [], []
    for g, ladder in enumerate(ladders):
        answer, passed = call(
            functools.partial(solve_kernel, ylays[g], ylays[0], ladder.levels),
            "y_reduced",
            (me,) + ladder.records() + (beside + (apart,) if g == 0 else ()),
            [(ylays[g].answer_rows, nz)] * 2,
        )
        answers.append(answer)
        mets.append(exchange(passed, "gy", 0))
    fields, ghosts, climbs = [], [], []
    for g in range(2):
        common = (me, azs[g], answers[g], mets[g], w, wy, inv, xinv, seam)
        edge = (nx * TILE, nz)
        outs = [(counts[g], rows, nz), edge]
        scratch = [vmem(counts[g], rows, nz), vmem(2 * ylays[g].answer_rows, nz)]
        body = functools.partial(y_kernel, (nx, ny), ylays[g], xlays[g])
        if g == 0:
            block, slim, field, ghost, ginv, gseam, gleft, gright, before, after = call(
                body,
                "y_solve_lead",
                common + (part,),
                [(xlays[0].rows, nz), (xlays[0].couple + TILE, nz)]
                + outs + [edge, (TILE, nz), edge, edge] + [(2 * nx, nz)] * 2,
                scratch,
                mebibytes=6,
            )
            climbs.append(Ladder(xlays[0], "gx", shift, me, slim, block))
        else:
            block, field, ghost, gleft, gright = call(
                body,
                "y_solve_next",
                common + (before, after, ginv, gseam, gleft, gright),
                [(xlays[1].rows, nz)] + outs + [edge] * 2,
                scratch,
                mebibytes=6,
            )
            climbs.append(Ladder(xlays[1], "gx", shift, me, block, block, climbs[0]))
        fields.append(field)
        ghosts.append(ghost)
        climbs[g].send()
    beside = (block,)
    for level in range(climbs[0].levels - 1):
        for ladder in climbs:
            leads = ladder.lay.leads
            ladder.merge(beside if leads else (), apart if leads and level == 0 else None)
            ladder.send()
        beside = (climbs[1].outgoing,)
    grad = None
    for g, ladder in enumerate(climbs):
        operands = (me, *ladder.records(), xleft, xright, gleft, gright, flows, fields[g], ghosts[g])
        spaces = "s" + "v" * (len(operands) - 1)
        aliases = None
        if g:
            aliases = {len(operands): 0}
            operands, spaces = operands + (grad,), spaces + "h"
        (grad,) = call(
            functools.partial(
                x_kernel, (nx, ny), xlays[g], xlays[0], ladder.levels, shift, starts[g]
            ),
            "x_solve",
            operands,
            [(comps, rows, nz)],
            [
                vmem(counts[g], rows, nz), vmem(counts[g], rows + 2 * ny, nz), vmem(nx * TILE, nz),
                pltpu.SemaphoreType.DMA((8,)),
            ],
            spaces=spaces,
            out_spaces="h",
            mebibytes=8,
            aliases=aliases,
        )
    return grad.reshape(comps, nx, ny, nz)


def solution(mesh):
    placed = (
        P(None, "gx", "gy", None),
        P("gx", "gy", None),
        P("gx", "gy", None),
        P(None, "gx", "gy", None),
        P(None, "gx", "gy", None),
    )
    return jax.shard_map(
        on_device, mesh=mesh, in_specs=placed, out_specs=P(None, "gx", "gy", None), check_vma=False
    )
```

```python
import functools

import jax
import jax.numpy as jnp
from jax import lax
from jax.experimental import pallas as pl
from jax.experimental.pallas import tpu as pltpu
from jax.sharding import PartitionSpec as P

COMPS = 6
LANES = 128
TILE = 8
SIDE = TILE // 2


def weight_of(diffusion, phase):
    return 1.0 / (diffusion * (1.0 + 3.0 * phase.astype(jnp.float32)))


def growing_step(value, slope, weight):
    slope = slope + weight * value
    return value + slope, slope


def split3(cells):
    high = cells.astype(jnp.bfloat16)
    rest = cells - high.astype(jnp.float32)
    middle = rest.astype(jnp.bfloat16)
    low = (rest - middle.astype(jnp.float32)).astype(jnp.bfloat16)
    return high, middle, low


def sum_matrix():
    row = lax.broadcasted_iota(jnp.int32, (2 * LANES, 2 * LANES), 0)
    col = lax.broadcasted_iota(jnp.int32, (2 * LANES, 2 * LANES), 1)
    before = (row < LANES) & (col < LANES) & (row <= col)
    after = (row >= LANES) & (col >= LANES) & (row > col)
    return jnp.where(before | after, 1.0, 0.0).astype(jnp.bfloat16)


class Layout:
    def __init__(self, sizes, groups, edges, lines, leads):
        self.sizes, self.groups, self.edges, self.lines, self.leads = sizes, groups, edges, lines, leads
        self.offsets = [sum(sizes[:i]) for i in range(len(sizes))]
        self.total = sum(sizes)
        packed = TILE if groups > 1 else 0
        self.couple = 2 * self.total
        self.packed = self.couple + 3 * lines
        self.edge = self.packed + packed
        self.side_couple = self.total
        self.side_packed = self.side_couple + lines
        self.side_edge = self.side_packed + packed
        extra = 2 * edges * lines
        self.rows = self.edge + extra if leads else self.couple
        self.side_rows = self.side_edge + extra // 2 if leads else self.total
        self.answer_rows = 2 * self.total + (extra if leads else 0)

    def group(self, piece):
        return 1 if self.groups > 1 and piece == len(self.sizes) - 1 else 0


def read_pieces(lay, ref, base=0):
    return [ref[pl.ds(base + o, n), :] for o, n in zip(lay.offsets, lay.sizes)]


def write_pieces(lay, ref, values, base=0):
    for o, n, value in zip(lay.offsets, lay.sizes, values):
        ref[pl.ds(base + o, n), :] = value


def read_rows(ref, base, count, lines):
    return [ref[pl.ds(base + i * lines, lines), :] for i in range(count)]


def write_rows(ref, base, values, lines):
    for i, value in enumerate(values):
        ref[pl.ds(base + i * lines, lines), :] = value


def two_sides(low, high):
    return jnp.concatenate(
        [jnp.broadcast_to(low, (SIDE, LANES)), jnp.broadcast_to(high, (SIDE, LANES))], axis=0
    )


def read_pair(ref, row):
    return two_sides(ref[pl.ds(row, 1), :], ref[pl.ds(row + 1, 1), :])


def write_pair(ref, row, value):
    ref[pl.ds(row, 1), :] = value[:1]
    ref[pl.ds(row + 1, 1), :] = value[SIDE : SIDE + 1]


def read_block(lay, ref, lead, lead_ref):
    n = lead.lines
    block = {"first": read_pieces(lay, ref), "last": read_pieces(lay, ref, lay.total)}
    for e, name in enumerate(("near", "cross", "far")):
        entry = [lead_ref[pl.ds(lead.couple + e * n, n), :]]
        if lead.groups > 1:
            entry.append(read_pair(lead_ref, lead.packed + 2 * e))
        block[name] = entry
    block["head"] = read_rows(lead_ref, lead.edge, lead.edges, n)
    block["tail"] = read_rows(lead_ref, lead.edge + lead.edges * n, lead.edges, n)
    return block


def write_block(lay, ref, block):
    n = lay.lines
    write_pieces(lay, ref, block["first"])
    write_pieces(lay, ref, block["last"], lay.total)
    if not lay.leads:
        return
    for e, name in enumerate(("near", "cross", "far")):
        ref[pl.ds(lay.couple + e * n, n), :] = block[name][0]
        if lay.groups > 1:
            write_pair(ref, lay.packed + 2 * e, block[name][1])
    if lay.groups > 1:
        ref[pl.ds(lay.packed + 6, 2), :] = jnp.zeros((2, LANES), jnp.float32)
    write_rows(ref, lay.edge, block["head"], n)
    write_rows(ref, lay.edge + lay.edges * n, block["tail"], n)


def pick(upper, low, high):
    if isinstance(low, list):
        return [pick(upper, a, b) for a, b in zip(low, high)]
    return jnp.where(jnp.full(low.shape, upper, jnp.int32) == 1, high, low)


def write_side(lay, ref, block, upper):
    n = lay.lines
    write_pieces(lay, ref, pick(upper, block["last"], block["first"]))
    if not lay.leads:
        return
    pair = pick(upper, block["far"], block["near"])
    ref[pl.ds(lay.side_couple, n), :] = pair[0]
    if lay.groups > 1:
        ref[pl.ds(lay.side_packed, TILE), :] = pair[1]
    write_rows(ref, lay.side_edge, pick(upper, block["tail"], block["head"]), n)


def read_side(lay, ref, lead, lead_ref):
    n = lead.lines
    couple = [lead_ref[pl.ds(lead.side_couple, n), :]]
    if lead.groups > 1:
        couple.append(lead_ref[pl.ds(lead.side_packed, TILE), :])
    return read_pieces(lay, ref), couple, read_rows(lead_ref, lead.side_edge, lead.edges, n)


def ordered(upper, own, other):
    low = {name: pick(upper, own[name], other[name]) for name in own}
    high = {name: pick(upper, other[name], own[name]) for name in own}
    return low, high


def joint(low, high):
    return [1.0 / (1.0 - far * near) for far, near in zip(low["far"], high["near"])]


def merge(lay, low, high):
    shrink = joint(low, high)
    groups = range(len(shrink))
    to_low = [low["cross"][g] * shrink[g] for g in groups]
    to_high = [high["cross"][g] * shrink[g] for g in groups]
    span = range(len(lay.sizes))
    of = lay.group
    block = {
        "first": [
            low["first"][i]
            + to_low[of(i)] * (high["first"][i] + high["near"][of(i)] * low["last"][i])
            for i in span
        ],
        "last": [
            high["last"][i]
            + to_high[of(i)] * (low["last"][i] + low["far"][of(i)] * high["first"][i])
            for i in span
        ],
    }
    block["near"] = [low["near"][g] + to_low[g] * low["cross"][g] * high["near"][g] for g in groups]
    block["cross"] = [to_low[g] * high["cross"][g] for g in groups]
    block["far"] = [high["far"][g] + to_high[g] * high["cross"][g] * low["far"][g] for g in groups]
    block["head"] = low["head"]
    block["tail"] = high["tail"]
    return block


def inner(lay, low, high, before, after):
    shrink = joint(low, high)
    low_last, high_first = [], []
    for i in range(len(lay.sizes)):
        g = lay.group(i)
        left = low["last"][i] + low["cross"][g] * before[i]
        right = high["first"][i] + high["cross"][g] * after[i]
        low_last.append((left + low["far"][g] * right) * shrink[g])
        high_first.append((right + high["near"][g] * left) * shrink[g])
    return low_last, high_first


def merge_kernel(lay, lead, bit, top, me_ref, own, other, *refs):
    out, *side = refs[-2:] if top else refs[-1:]
    lead_own, lead_other = (own, other) if lay.leads else refs[:2]
    upper = (me_ref[0] >> bit) & 1
    low, high = ordered(
        upper, read_block(lay, own, lead, lead_own), read_block(lay, other, lead, lead_other)
    )
    block = merge(lay, low, high)
    write_block(lay, out, block)
    if top:
        write_side(lay, side[0], block, (me_ref[0] >> (bit + 1)) & 1)


def first_merge_kernel(lay, bit, top, me_ref, own, slim, apart, *refs):
    out, joined, *side = refs[-3:] if top else refs[-2:]
    joined[pl.ds(0, lay.couple), :] = slim[pl.ds(0, lay.couple), :]
    joined[pl.ds(lay.packed, TILE), :] = slim[pl.ds(lay.couple, TILE), :]
    joined[pl.ds(lay.couple, 3 * lay.lines), :] = apart[pl.ds(0, 3 * lay.lines), :]
    edges = 2 * lay.edges * lay.lines
    joined[pl.ds(lay.edge, edges), :] = apart[pl.ds(3 * lay.lines, edges), :]
    merge_kernel(lay, lay, bit, top, me_ref, own, joined, out, *side)


def solve_lines(lay, lead, levels, me, refs):
    owns, gots = refs[:levels], refs[levels : 2 * levels]
    lead_owns, lead_gots = owns, gots
    if not lay.leads:
        lead_owns, lead_gots = refs[2 * levels : 3 * levels], refs[3 * levels : 4 * levels]
    top = levels - 1
    upper = (me >> top) & 1
    own = read_block(lay, owns[top], lead, lead_owns[top])
    met, met_couple, met_edge = read_side(lay, gots[top], lead, lead_gots[top])
    facing = pick(upper, own["last"], own["first"])
    couple = pick(upper, own["far"], own["near"])
    shrink = [1.0 / (1.0 - a * b) for a, b in zip(met_couple, couple)]
    found = []
    for i in range(len(lay.sizes)):
        g = lay.group(i)
        found.append((met[i] + met_couple[g] * facing[i]) * shrink[g])
    zeros = [jnp.zeros_like(v) for v in found]
    blank = [jnp.zeros_like(v) for v in met_edge]
    state = (
        pick(upper, zeros, found), pick(upper, found, zeros),
        pick(upper, blank, met_edge), pick(upper, met_edge, blank),
    )
    partner = None
    for level in reversed(range(top)):
        upper = (me >> level) & 1
        low, high = ordered(
            upper,
            read_block(lay, owns[level], lead, lead_owns[level]),
            read_block(lay, gots[level], lead, lead_gots[level]),
        )
        before, after, behind, ahead = state
        low_last, high_first = inner(lay, low, high, before, after)
        lower = (before, high_first, behind, high["head"])
        higher = (low_last, after, low["tail"], ahead)
        state = tuple(pick(upper, a, b) for a, b in zip(lower, higher))
        partner = tuple(pick(upper, a, b) for a, b in zip(higher, lower))
    return state, partner


def write_answer(lay, ref, state):
    before, after, behind, ahead = state
    write_pieces(lay, ref, before)
    write_pieces(lay, ref, after, lay.total)
    if lay.leads:
        write_rows(ref, 2 * lay.total, behind + ahead, lay.lines)


def solve_kernel(lay, lead, levels, me_ref, *refs):
    state, partner = solve_lines(lay, lead, levels, me_ref[0], refs[:-2])
    write_answer(lay, refs[-2], state)
    write_answer(lay, refs[-1], partner)


def corners(weights):
    one = jnp.ones_like(weights[0])
    value, slope, chain = one, one, [one]
    for weight in weights:
        value, slope = growing_step(value, slope, weight)
        chain.append(value)
    back, fall, backs = one, one, []
    for weight in reversed(weights):
        backs.append(back)
        back, fall = growing_step(back, fall, weight)
    backs.reverse()
    return chain, backs, 1.0 / value


def post(mine, keep, send, row, cells):
    half = cells.shape[0] // 2
    low, high = cells[:half], cells[half:]
    keep[pl.ds(row, half), :] = pick(mine, low, high)
    send[pl.ds(row, half), :] = pick(mine, high, low)


def z_part(dims, lay, me_ref, cot, phi, psi, w, left, right, arrived, turned, az, keep, send):
    nx, ny = dims
    tiles = nx * ny // LANES
    sums = sum_matrix()
    mine = me_ref[0] & 1
    for c in range(len(lay.sizes)):
        arrived(c)
        for t in range(tiles):
            span = pl.ds(t * LANES, LANES)
            cells, up, down = cot[c, span, :], phi[span, :], psi[span, :]
            wide = jnp.concatenate([up * cells, down * cells], axis=1)
            found = jnp.dot(
                jnp.concatenate(split3(wide), axis=0), sums, preferred_element_type=jnp.float32
            )
            found = found[:LANES] + (found[LANES : 2 * LANES] + found[2 * LANES :])
            az[c, span, :] = w[span, :] * (down * found[:, :LANES] + up * found[:, LANES:])
        first = jnp.zeros((nx, LANES), jnp.float32)
        last = jnp.zeros((nx, LANES), jnp.float32)
        for y in range(ny):
            cells = az[c, pl.ds(y, nx, stride=ny), :]
            span = pl.ds(y * nx, nx)
            turned[c, span, :] = cells
            first = first + left[span, :] * cells
            last = last + right[span, :] * cells
        post(mine, keep, send, lay.offsets[c], first)
        post(mine, keep, send, lay.total + lay.offsets[c], last)


def carried(maps, state):
    return maps[0] * state[0] + maps[1] * state[1], maps[2] * state[0] + maps[3] * state[1]


def z_continuants(tiles, wt, pht, pst, maps, ends):
    deep = LANES // TILE
    lines = tiles * TILE
    one = jnp.ones((lines, LANES), jnp.float32)
    zero = jnp.zeros((lines, LANES), jnp.float32)

    def at(k, t):
        return pl.ds(t * LANES + k, TILE, stride=deep)

    weights = [
        jnp.concatenate([wt[at(k, t), :] for t in range(tiles)], axis=0) for k in range(deep)
    ]
    found = []
    for order in (range(deep), reversed(range(deep))):
        pair = [(one, zero), (zero, one)]
        values = {}
        for k in order:
            values[k] = (pair[0][0], pair[1][0])
            pair = [growing_step(*state, weights[k]) for state in pair]
        base = len(found) * 4 * lines
        found.append(values)
        for i, entry in enumerate((pair[0][0], pair[1][0], pair[0][1], pair[1][1])):
            maps[pl.ds(base + i * lines, lines), :] = entry
    state = (jnp.ones((tiles, LANES), jnp.float32),) * 2
    for side, order in enumerate((range(TILE), reversed(range(TILE)))):
        for s in order:
            for i in range(2):
                ends[pl.ds((2 * side + i) * lines + s, tiles, stride=TILE), :] = state[i]
            rows = [pl.ds((4 * side + i) * lines + s, tiles, stride=TILE) for i in range(4)]
            state = carried([maps[row, :] for row in rows], state)
        state = (1.0 / state[0],) * 2
    for values, target, side in ((found[0], pht, 0), (found[1], pst, 1)):
        first, second = (ends[pl.ds((2 * side + i) * lines, lines), :] for i in range(2))
        for k in range(deep):
            cells = values[k][0] * first + values[k][1] * second
            for t in range(tiles):
                target[at(k, t), :] = cells[t * TILE : (t + 1) * TILE]


def lead_z_kernel(
    dims, lay, me_ref, cot_any, diff_any, phase_any, cour_any, upw_any,
    keep, send, turned, w, left, right, phi, psi, later,
    az, cot, diff, phase, cour, upw, wt, pht, pst, maps, ends, in_sems, sems,
):
    nx, ny = dims
    tiles = nx * ny // LANES
    half = nx // 2
    count = len(lay.sizes)
    ahead = pltpu.make_async_copy(cot_any.at[pl.ds(count, later.shape[0])], later, sems.at[4])
    small = [(diff_any, diff), (phase_any, phase), (cour_any.at[1], cour), (upw_any.at[1], upw)]
    for i, (source, target) in enumerate(small):
        pltpu.make_async_copy(source, target, sems.at[i]).start()
    for c in range(count):
        pltpu.make_async_copy(cot_any.at[c], cot.at[c], in_sems.at[c]).start()
    ahead.start()

    for i, (source, target) in enumerate(small[:2]):
        pltpu.make_async_copy(source, target, sems.at[i]).wait()
    w[...] = weight_of(diff[...], phase[...])
    for t in range(tiles):
        span = pl.ds(t * LANES, LANES)
        wt[span, :] = w[span, :].T
    z_continuants(tiles, wt, pht, pst, maps, ends)
    for t in range(tiles):
        span = pl.ds(t * LANES, LANES)
        phi[span, :] = pht[span, :].T
        psi[span, :] = pst[span, :].T

    chain, backs, total = corners([w[pl.ds(y, nx, stride=ny), :] for y in range(ny)])
    for y in range(ny):
        span = pl.ds(y * nx, nx)
        left[span, :] = backs[y] * total
        right[span, :] = chain[y] * total
    mine = me_ref[0] & 1
    post(mine, keep, send, lay.couple, backs[0] * total)
    post(mine, keep, send, lay.couple + half, total)
    post(mine, keep, send, lay.couple + 2 * half, chain[ny - 1] * total)
    for i, (source, target) in enumerate(small[2:]):
        pltpu.make_async_copy(source, target, sems.at[2 + i]).wait()
    for e, y in enumerate((0, ny - 1)):
        edge = pl.ds(y, nx, stride=ny)
        weight = w[edge, :]
        up = cour[edge, :] * upw[edge, :].astype(jnp.float32)
        flow = up if e == 0 else cour[edge, :] - up
        post(mine, keep, send, lay.edge + 2 * e * half, weight)
        post(mine, keep, send, lay.edge + (2 * e + 1) * half, weight * flow)

    def arrived(c):
        pltpu.make_async_copy(cot_any.at[c], cot.at[c], in_sems.at[c]).wait()

    z_part(dims, lay, me_ref, cot, phi, psi, w, left, right, arrived, turned, az, keep, send)
    ahead.wait()


def next_z_kernel(dims, lay, me_ref, cot, phi, psi, w, left, right, keep, send, turned, az):
    z_part(
        dims, lay, me_ref, cot, phi, psi, w, left, right, lambda c: None, turned, az, keep, send
    )


def coef_kernel(dims, w, courant, upwind, after, block, inv, wy, xinv, seam, left, right, flows):
    del after
    nx, ny = dims
    rows = nx * ny
    one = jnp.ones((ny, LANES), jnp.float32)
    value, slope, back, fall = one, one, one, one
    for k in range(nx):
        low, high = pl.ds(k * ny, ny), pl.ds((nx - 1 - k) * ny, ny)
        right[low, :] = value
        left[high, :] = back
        new_value, slope = growing_step(value, slope, w[low, :])
        new_back, fall = growing_step(back, fall, w[high, :])
        if k < nx // 2:
            up, down = value / new_value, back / new_back
            xinv[low, :] = up
            xinv[high, :] = down
        end, value = value, new_value
        corner, back = back, new_back
    seam[...] = 1.0 / (1.0 - up * down)
    total = 1.0 / value
    block[pl.ds(0, ny), :] = corner * total
    block[pl.ds(ny, ny), :] = total
    block[pl.ds(2 * ny, ny), :] = end * total
    value = jnp.ones((nx, LANES), jnp.float32)
    slope = value
    for y in range(ny):
        weight = w[pl.ds(y, nx, stride=ny), :]
        wy[pl.ds(y * nx, nx), :] = weight
        new_value, slope = growing_step(value, slope, weight)
        inv[pl.ds(y * nx, nx), :] = value / new_value
        value = new_value

    lane = lax.broadcasted_iota(jnp.int32, (ny, LANES), 1)

    def plane(x, carry):
        span = pl.ds(x * ny, ny)
        scale = w[span, :] * total
        left[span, :] = left[span, :] * scale
        right[span, :] = right[span, :] * scale
        own = one
        for d in range(3):
            flow = courant[d, span, :]
            up = flow * upwind[d, span, :].astype(jnp.float32)
            down = flow - up
            own = own + (down - up)
            if d == 2:
                up = jnp.where(lane == 0, 0.0, up)
                down = jnp.where(lane == LANES - 1, 0.0, down)
            flows[pl.ds((1 + 2 * d) * rows + x * ny, ny), :] = up
            flows[pl.ds((2 + 2 * d) * rows + x * ny, ny), :] = down
        flows[span, :] = own
        return carry

    lax.fori_loop(0, nx, plane, 0, unroll=4)
    first, last = pl.ds(0, ny), pl.ds(rows - ny, ny)
    block[pl.ds(3 * ny, ny), :] = w[first, :] * flows[pl.ds(rows, ny), :]
    block[pl.ds(4 * ny, ny), :] = w[last, :] * flows[pl.ds(2 * rows + rows - ny, ny), :]


def sides(before, after, x):
    return two_sides(before[pl.ds(x, 1), :], after[pl.ds(x, 1), :])


def y_kernel(dims, ylay, xlay, me_ref, az, own, got, w, wy, inv, xinv, seam, *refs):
    nx, ny = dims
    half = nx // 2
    comps = len(ylay.sizes)
    if xlay.leads:
        part, block, slim, field, ghost, ginv, gseam, gleft, gright, before, after, ay, joined = refs
    else:
        before, after, ginv, gseam, gleft, gright, block, field, ghost, fleft, fright, ay, joined = refs
        for x in range(nx):
            here = pl.ds(x * TILE, TILE)
            scale = sides(before, after, nx + x)
            fleft[here, :] = gleft[here, :] * scale
            fright[here, :] = gright[here, :] * scale
    mine = me_ref[0] & 1
    span = ylay.answer_rows
    joined[pl.ds(pl.multiple_of(mine * span, TILE), span), :] = own[...]
    joined[pl.ds(pl.multiple_of((1 - mine) * span, TILE), span), :] = got[...]
    if xlay.leads:
        for h in range(2):
            for e in range(2):
                where = pl.ds(e * nx + h * half, half)
                row = h * span + 2 * ylay.total + e * half
                before[where, :] = joined[pl.ds(row, half), :]
                after[where, :] = joined[pl.ds(row + 2 * half, half), :]
        one = jnp.ones((TILE, LANES), jnp.float32)
        value, slope, back, fall = one, one, one, one
        for k in range(nx):
            low, high = pl.ds(k * TILE, TILE), pl.ds((nx - 1 - k) * TILE, TILE)
            gright[low, :] = value
            gleft[high, :] = back
            new_value, slope = growing_step(value, slope, sides(before, after, k))
            new_back, fall = growing_step(back, fall, sides(before, after, nx - 1 - k))
            if k < nx // 2:
                up, down = value / new_value, back / new_back
                ginv[low, :] = up
                ginv[high, :] = down
            end, value = value, new_value
            corner, back = back, new_back
        gseam[...] = 1.0 / (1.0 - up * down)
        total = 1.0 / value
        for x in range(nx):
            here = pl.ds(x * TILE, TILE)
            gleft[here, :] = gleft[here, :] * total
            gright[here, :] = gright[here, :] * total

    ghost[...] = jnp.zeros(ghost.shape, jnp.float32)
    for c in range(comps):
        for h in range(2):
            piece = pl.ds(h * half, half)
            fb = joined[pl.ds(h * span + c * half, half), :]
            fa = joined[pl.ds(h * span + ylay.total + c * half, half), :]
            ghost[pl.ds(h * half * TILE + c, half, stride=TILE), :] = before[piece, :] * fb
            ghost[pl.ds(h * half * TILE + SIDE + c, half, stride=TILE), :] = after[piece, :] * fa
            swept, chain = fb, []
            for y in range(ny):
                cells = az[c, pl.ds(y * nx + h * half, half), :]
                swept = (cells + swept) * inv[pl.ds(y * nx + h * half, half), :]
                chain.append(swept)
            later = fa
            for y in reversed(range(ny)):
                row = pl.ds(y * nx + h * half, half)
                later = chain[y] + inv[row, :] * later
                ay[c, pl.ds(h * half * ny + y, half, stride=ny), :] = later * wy[row, :]

    def load(i, x):
        return ghost[pl.ds(x * TILE, TILE), :] if i == comps else ay[i, pl.ds(x * ny, ny), :]

    def keep(i, x, cells):
        if i == comps:
            ghost[pl.ds(x * TILE, TILE), :] = cells
        else:
            ay[i, pl.ds(x * ny, ny), :] = cells

    def pivot(i, x):
        return ginv[pl.ds(x * TILE, TILE), :] if i == comps else xinv[pl.ds(x * ny, ny), :]

    def finish(i, x, cells):
        if i == comps:
            ghost[pl.ds(x * TILE, TILE), :] = cells * sides(before, after, nx + x)
        else:
            here = pl.ds(x * ny, ny)
            field[i, here, :] = cells * w[here, :]

    pieces = range(comps + 1)
    middle = nx // 2
    lows = [jnp.zeros((n, LANES), jnp.float32) for n in xlay.sizes]
    highs = list(lows)
    for k in range(middle):
        x, mirror = k, nx - 1 - k
        for i in pieces:
            lows[i] = (load(i, x) + lows[i]) * pivot(i, x)
            highs[i] = (load(i, mirror) + highs[i]) * pivot(i, mirror)
            if k + 1 < middle:
                keep(i, x, lows[i])
                keep(i, mirror, highs[i])
    for i in pieces:
        joint_scale = gseam[...] if i == comps else seam[...]
        highs[i] = (highs[i] + pivot(i, middle) * lows[i]) * joint_scale
        lows[i] = lows[i] + pivot(i, middle - 1) * highs[i]
        finish(i, middle - 1, lows[i])
        finish(i, middle, highs[i])
    for k in range(1, middle):
        x, mirror = middle - 1 - k, middle + k
        for i in pieces:
            lows[i] = load(i, x) + pivot(i, x) * lows[i]
            highs[i] = load(i, mirror) + pivot(i, mirror) * highs[i]
            finish(i, x, lows[i])
            finish(i, mirror, highs[i])
    solved, lasts = lows, highs
    record = {"first": solved, "last": lasts}
    if xlay.leads:
        pieces = [part[pl.ds(i * ny, ny), :] for i in range(5)]
        record["near"] = [pieces[0], corner * total]
        record["cross"] = [pieces[1], total]
        record["far"] = [pieces[2], end * total]
        record["head"], record["tail"] = pieces[3:4], pieces[4:5]
    write_block(xlay, block, record)
    if xlay.leads:
        slim[pl.ds(0, xlay.couple), :] = block[pl.ds(0, xlay.couple), :]
        slim[pl.ds(xlay.couple, TILE), :] = block[pl.ds(xlay.packed, TILE), :]


def x_kernel(dims, lay, lead, levels, shift, start, me_ref, *refs):
    nx, ny = dims
    count = (2 if lay.leads else 4) * levels
    state, _ = solve_lines(lay, lead, levels, me_ref[0] >> shift, refs[:count])
    left, right, gleft, gright, flows, inputs, ghost, *rest = refs[count:]
    out_any, out, field, fluxes, sems = rest[-5:]
    rows = nx * ny
    tiles = ny // TILE
    comps = len(lay.sizes) - 1
    starts, nexts, (near,), (far,) = state

    def fill(x, carry):
        span, above = pl.ds(x * ny, ny), pl.ds((x + 1) * ny, ny)
        lower, upper = left[span, :], right[span, :]
        for c in range(comps):
            field[c, above, :] = inputs[c, span, :] + lower * starts[c] + upper * nexts[c]
        here = pl.ds(x * TILE, TILE)
        fluxes[here, :] = ghost[here, :] + gleft[here, :] * starts[comps] + gright[here, :] * nexts[comps]
        return carry

    lax.fori_loop(0, nx, fill, 0, unroll=8)
    blank = jnp.zeros((comps, ny, LANES), jnp.float32)
    field[:, pl.ds(0, ny), :] = blank
    field[:, pl.ds((nx + 1) * ny, ny), :] = blank

    line = lax.broadcasted_iota(jnp.int32, (TILE, LANES), 0)

    def advect(x, carry):
        before = jnp.maximum(x - 1, 0)
        beyond = jnp.minimum(x + 1, nx - 1)

        def flow(kind, plane, t):
            begin = pl.multiple_of(kind * rows + plane * ny + t * TILE, TILE)
            return flows[pl.ds(begin, TILE), :]

        own = [flow(0, x, t) for t in range(tiles)]
        ahead_x = [flow(1, beyond, t) for t in range(tiles)]
        behind_x = [flow(2, before, t) for t in range(tiles)]
        ahead_y = [flow(3, x, t) for t in range(tiles)]
        behind_y = [flow(4, x, t) for t in range(tiles)]
        ahead_z = [flow(5, x, t) for t in range(tiles)]
        behind_z = [flow(6, x, t) for t in range(tiles)]
        for c in range(comps):

            def cells(plane, t):
                begin = pl.multiple_of((plane + 1) * ny + t * TILE, TILE)
                return field[c, pl.ds(begin, TILE), :]

            grad = [cells(x, t) for t in range(tiles)]
            ups = [pltpu.roll(ahead_y[t] * grad[t], TILE - 1, 0) for t in range(tiles)]
            downs = [pltpu.roll(behind_y[t] * grad[t], 1, 0) for t in range(tiles)]
            lowest = fluxes[pl.ds(x * TILE + c, 1), :]
            highest = fluxes[pl.ds(x * TILE + SIDE + c, 1), :]
            for t in range(tiles):
                part = own[t] * grad[t]
                part = part + ahead_x[t] * cells(x + 1, t) - behind_x[t] * cells(x - 1, t)
                enter = ups[t + 1] if t + 1 < tiles else jnp.broadcast_to(highest, (TILE, LANES))
                part = part + jnp.where(line == TILE - 1, enter, ups[t])
                enter = downs[t - 1] if t > 0 else jnp.broadcast_to(lowest, (TILE, LANES))
                part = part - jnp.where(line == 0, enter, downs[t])
                part = part + pltpu.roll(ahead_z[t] * grad[t], LANES - 1, 1)
                part = part - pltpu.roll(behind_z[t] * grad[t], 1, 1)
                out[c, pl.ds(pl.multiple_of(x * ny + t * TILE, TILE), TILE), :] = part
        return carry

    parts = 8
    share = nx // parts

    def copy(part):
        span = pl.ds(part * share * ny, share * ny)
        target = out_any.at[pl.ds(start, comps), span, :]
        return pltpu.make_async_copy(out.at[:, span, :], target, sems.at[part])

    top, bottom = pl.ds(0, ny), pl.ds(rows - ny, ny)
    for part in range(parts):
        lax.fori_loop(part * share, (part + 1) * share, advect, 0, unroll=share)
        for c in range(comps):
            if part == 0:
                out[c, top, :] = out[c, top, :] - near * starts[c]
            if part == parts - 1:
                out[c, bottom, :] = out[c, bottom, :] + far * nexts[c]
        copy(part).start()
    for part in range(parts):
        copy(part).wait()


def call(
    kernel, name, operands, outs, scratch=(), spaces=None, out_spaces=None, mebibytes=4, aliases=None
):
    params = pltpu.CompilerParams(vmem_limit_bytes=mebibytes * 1024 * 1024)
    memory = {"v": pltpu.VMEM, "k": pltpu.VMEM, "h": pltpu.HBM, "s": pltpu.SMEM}
    held = {"h": pltpu.HBM, "k": pltpu.VMEM}
    spaces = spaces or "s" + "v" * (len(operands) - 1)
    out_spaces = out_spaces or "v" * len(outs)
    operands = [
        pltpu.with_memory_space_constraint(o, held[s]) if s in held else o
        for o, s in zip(operands, spaces)
    ]
    return pl.pallas_call(
        kernel,
        name=name,
        out_shape=[
            held[s](shape, jnp.float32) if s in held else jax.ShapeDtypeStruct(shape, jnp.float32)
            for shape, s in zip(outs, out_spaces)
        ],
        in_specs=[pl.BlockSpec(memory_space=memory[s]) for s in spaces],
        out_specs=[pl.BlockSpec(memory_space=memory[s]) for s in out_spaces],
        scratch_shapes=list(scratch),
        input_output_aliases=aliases or {},
        compiler_params=params,
        cost_estimate=pl.CostEstimate(flops=10**9, bytes_accessed=10**7, transcendentals=0),
    )(*operands)


def exchange(rows, axis, bit):
    count = lax.axis_size(axis)
    return lax.ppermute(rows, axis, [(i, i ^ (1 << bit)) for i in range(count)])


class Ladder:
    def __init__(self, lay, axis, shift, me, send, keep, lead=None):
        self.lay, self.axis, self.shift, self.me, self.lead = lay, axis, shift, me, lead
        self.levels = (lax.axis_size(axis) - 1).bit_length()
        self.owns, self.gots, self.outgoing = [keep], [], send

    def send(self):
        self.gots.append(exchange(self.outgoing, self.axis, len(self.gots)))

    def merge(self, beside=(), apart=None):
        level = len(self.owns) - 1
        top = level == self.levels - 2
        lay, bit = self.lay, self.shift + level
        leader = self.lead or self
        operands = (self.me, self.owns[-1], self.gots[-1])
        if not lay.leads:
            operands += (leader.owns[level], leader.gots[level])
        shapes = [(lay.rows, LANES)] + ([(lay.side_rows, LANES)] if top else [])
        kernel = functools.partial(merge_kernel, lay, leader.lay, bit, top)
        if apart is not None:
            kernel = functools.partial(first_merge_kernel, lay, bit, top)
            operands += (apart,)
            shapes = shapes[:1] + shapes
        found = call(kernel, "merge_" + self.axis, operands + tuple(beside), shapes)
        self.owns.append(found[0])
        self.outgoing = found[-1] if top else found[0]
        if apart is not None:
            self.gots[0] = found[1]

    def records(self):
        found = (*self.owns, *self.gots)
        return found if self.lay.leads else found + (*self.lead.owns, *self.lead.gots)


def on_device(cotangent, diffusion, phase, courant, upwind):
    comps, nx, ny, nz = cotangent.shape
    shift = (lax.axis_size("gy") - 1).bit_length()
    rows = nx * ny
    half = nx // 2
    size = comps // 3
    starts = (0, size)
    counts = (size, comps - size)
    ylays = [Layout([half] * n, 1, 2, half, g == 0) for g, n in enumerate(counts)]
    xlays = [Layout([ny] * n + [TILE], 2, 1, ny, g == 0) for g, n in enumerate(counts)]
    me = lax.axis_index(("gx", "gy")).astype(jnp.int32).reshape(1)

    def vmem(*shape, dtype=jnp.float32):
        return pltpu.VMEM(shape, dtype)

    flat = (rows, nz)
    cot = cotangent.reshape(comps, rows, nz)
    cour = courant.reshape(3, rows, nz)
    upw = upwind.reshape(3, rows, nz)
    n = counts[0]
    keep, send, az, w, left, right, phi, psi, cot_next = call(
        functools.partial(lead_z_kernel, (nx, ny), ylays[0]),
        "z_solve_lead",
        (me, cot, diffusion.reshape(flat), phase.reshape(flat), cour, upw),
        [(ylays[0].rows, nz)] * 2 + [(n, rows, nz)] + [flat] * 5 + [(counts[1], rows, nz)],
        [
            vmem(n, rows, nz), vmem(n, rows, nz), vmem(*flat), vmem(*flat, dtype=jnp.int32),
            vmem(*flat), vmem(*flat, dtype=jnp.int32),
            vmem(*flat), vmem(*flat), vmem(*flat),
            vmem(rows // LANES * 8 * TILE, nz), vmem(rows // LANES * 4 * TILE, nz),
            pltpu.SemaphoreType.DMA((n,)), pltpu.SemaphoreType.DMA((5,)),
        ],
        spaces="shhhhh",
        mebibytes=12,
    )
    lead = Ladder(ylays[0], "gy", 0, me, send, keep)
    lead.send()
    azs = [az]
    n = counts[1]
    keep, send, az = call(
        functools.partial(next_z_kernel, (nx, ny), ylays[1]),
        "z_solve_next",
        (me, cot_next, phi, psi, w, left, right),
        [(ylays[1].rows, nz)] * 2 + [(n, rows, nz)],
        [vmem(n, rows, nz)],
        mebibytes=8,
    )
    azs.append(az)
    follow = Ladder(ylays[1], "gy", 0, me, send, keep, lead)
    follow.send()
    beside = (send,)
    for level in range(lead.levels - 1):
        lead.merge(beside)
        lead.send()
        follow.merge((lead.outgoing,))
        follow.send()
        beside = (follow.outgoing,)
        if level == 0:
            part, inv, wy, xinv, seam, xleft, xright, flows = call(
                functools.partial(coef_kernel, (nx, ny)),
                "x_coefficients",
                (w, cour, upw, lead.owns[1]),
                [(5 * ny, nz), flat, flat, flat, (ny, nz), flat, flat, (7 * rows, nz)],
                spaces="vvvv",
                mebibytes=8,
            )
            beside = (part, follow.outgoing)
            apart = exchange(part, "gx", 0)
    ladders, mets, answers = (lead, follow), [], []
    for g, ladder in enumerate(ladders):
        answer, passed = call(
            functools.partial(solve_kernel, ylays[g], ylays[0], ladder.levels),
            "y_reduced",
            (me,) + ladder.records() + (beside + (apart,) if g == 0 else ()),
            [(ylays[g].answer_rows, nz)] * 2,
        )
        answers.append(answer)
        mets.append(exchange(passed, "gy", 0))
    fields, ghosts, climbs = [], [], []
    for g in range(2):
        common = (me, azs[g], answers[g], mets[g], w, wy, inv, xinv, seam)
        edge = (nx * TILE, nz)
        outs = [(counts[g], rows, nz), edge]
        scratch = [vmem(counts[g], rows, nz), vmem(2 * ylays[g].answer_rows, nz)]
        body = functools.partial(y_kernel, (nx, ny), ylays[g], xlays[g])
        if g == 0:
            block, slim, field, ghost, ginv, gseam, gleft, gright, before, after = call(
                body,
                "y_solve_lead",
                common + (part,),
                [(xlays[0].rows, nz), (xlays[0].couple + TILE, nz)]
                + outs + [edge, (TILE, nz), edge, edge] + [(2 * nx, nz)] * 2,
                scratch,
                mebibytes=6,
            )
            climbs.append(Ladder(xlays[0], "gx", shift, me, slim, block))
        else:
            block, field, ghost, gleft, gright = call(
                body,
                "y_solve_next",
                common + (before, after, ginv, gseam, gleft, gright),
                [(xlays[1].rows, nz)] + outs + [edge] * 2,
                scratch,
                mebibytes=6,
            )
            climbs.append(Ladder(xlays[1], "gx", shift, me, block, block, climbs[0]))
        fields.append(field)
        ghosts.append(ghost)
        climbs[g].send()
    beside = (block,)
    for level in range(climbs[0].levels - 1):
        for ladder in climbs:
            leads = ladder.lay.leads
            ladder.merge(beside if leads else (), apart if leads and level == 0 else None)
            ladder.send()
        beside = (climbs[1].outgoing,)
    grad = None
    for g, ladder in enumerate(climbs):
        operands = (me, *ladder.records(), xleft, xright, gleft, gright, flows, fields[g], ghosts[g])
        spaces = "s" + "v" * (len(operands) - 1)
        aliases = None
        if g:
            aliases = {len(operands): 0}
            operands, spaces = operands + (grad,), spaces + "h"
        (grad,) = call(
            functools.partial(
                x_kernel, (nx, ny), xlays[g], xlays[0], ladder.levels, shift, starts[g]
            ),
            "x_solve",
            operands,
            [(comps, rows, nz)],
            [
                vmem(counts[g], rows, nz), vmem(counts[g], rows + 2 * ny, nz), vmem(nx * TILE, nz),
                pltpu.SemaphoreType.DMA((8,)),
            ],
            spaces=spaces,
            out_spaces="h",
            mebibytes=8,
            aliases=aliases,
        )
    return grad.reshape(comps, nx, ny, nz)


def solution(mesh):
    placed = (
        P(None, "gx", "gy", None),
        P("gx", "gy", None),
        P("gx", "gy", None),
        P(None, "gx", "gy", None),
        P(None, "gx", "gy", None),
    )
    return jax.shard_map(
        on_device, mesh=mesh, in_specs=placed, out_specs=P(None, "gx", "gy", None), check_vma=False
    )
```

```python
import functools

import jax
import jax.numpy as jnp
from jax import lax
from jax.experimental import pallas as pl
from jax.experimental.pallas import tpu as pltpu
from jax.sharding import PartitionSpec as P

COMPS = 6
LANES = 128
TILE = 8
SIDE = TILE // 2


def weight_of(diffusion, phase):
    return 1.0 / (diffusion * (1.0 + 3.0 * phase.astype(jnp.float32)))


def growing_step(value, slope, weight):
    slope = slope + weight * value
    return value + slope, slope


def split3(cells):
    high = cells.astype(jnp.bfloat16)
    rest = cells - high.astype(jnp.float32)
    middle = rest.astype(jnp.bfloat16)
    low = (rest - middle.astype(jnp.float32)).astype(jnp.bfloat16)
    return high, middle, low


def sum_matrix():
    row = lax.broadcasted_iota(jnp.int32, (2 * LANES, 2 * LANES), 0)
    col = lax.broadcasted_iota(jnp.int32, (2 * LANES, 2 * LANES), 1)
    before = (row < LANES) & (col < LANES) & (row <= col)
    after = (row >= LANES) & (col >= LANES) & (row > col)
    return jnp.where(before | after, 1.0, 0.0).astype(jnp.bfloat16)


class Layout:
    def __init__(self, sizes, groups, edges, lines, leads):
        self.sizes, self.groups, self.edges, self.lines, self.leads = sizes, groups, edges, lines, leads
        self.offsets = [sum(sizes[:i]) for i in range(len(sizes))]
        self.total = sum(sizes)
        packed = TILE if groups > 1 else 0
        self.couple = 2 * self.total
        self.packed = self.couple + 3 * lines
        self.edge = self.packed + packed
        self.side_couple = self.total
        self.side_packed = self.side_couple + lines
        self.side_edge = self.side_packed + packed
        extra = 2 * edges * lines
        self.rows = self.edge + extra if leads else self.couple
        self.side_rows = self.side_edge + extra // 2 if leads else self.total
        self.answer_rows = 2 * self.total + (extra if leads else 0)

    def group(self, piece):
        return 1 if self.groups > 1 and piece == len(self.sizes) - 1 else 0


def read_pieces(lay, ref, base=0):
    return [ref[pl.ds(base + o, n), :] for o, n in zip(lay.offsets, lay.sizes)]


def write_pieces(lay, ref, values, base=0):
    for o, n, value in zip(lay.offsets, lay.sizes, values):
        ref[pl.ds(base + o, n), :] = value


def read_rows(ref, base, count, lines):
    return [ref[pl.ds(base + i * lines, lines), :] for i in range(count)]


def write_rows(ref, base, values, lines):
    for i, value in enumerate(values):
        ref[pl.ds(base + i * lines, lines), :] = value


def two_sides(low, high):
    return jnp.concatenate(
        [jnp.broadcast_to(low, (SIDE, LANES)), jnp.broadcast_to(high, (SIDE, LANES))], axis=0
    )


def read_pair(ref, row):
    return two_sides(ref[pl.ds(row, 1), :], ref[pl.ds(row + 1, 1), :])


def write_pair(ref, row, value):
    ref[pl.ds(row, 1), :] = value[:1]
    ref[pl.ds(row + 1, 1), :] = value[SIDE : SIDE + 1]


def read_block(lay, ref, lead, lead_ref):
    n = lead.lines
    block = {"first": read_pieces(lay, ref), "last": read_pieces(lay, ref, lay.total)}
    for e, name in enumerate(("near", "cross", "far")):
        entry = [lead_ref[pl.ds(lead.couple + e * n, n), :]]
        if lead.groups > 1:
            entry.append(read_pair(lead_ref, lead.packed + 2 * e))
        block[name] = entry
    block["head"] = read_rows(lead_ref, lead.edge, lead.edges, n)
    block["tail"] = read_rows(lead_ref, lead.edge + lead.edges * n, lead.edges, n)
    return block


def write_block(lay, ref, block):
    n = lay.lines
    write_pieces(lay, ref, block["first"])
    write_pieces(lay, ref, block["last"], lay.total)
    if not lay.leads:
        return
    for e, name in enumerate(("near", "cross", "far")):
        ref[pl.ds(lay.couple + e * n, n), :] = block[name][0]
        if lay.groups > 1:
            write_pair(ref, lay.packed + 2 * e, block[name][1])
    if lay.groups > 1:
        ref[pl.ds(lay.packed + 6, 2), :] = jnp.zeros((2, LANES), jnp.float32)
    write_rows(ref, lay.edge, block["head"], n)
    write_rows(ref, lay.edge + lay.edges * n, block["tail"], n)


def pick(upper, low, high):
    if isinstance(low, list):
        return [pick(upper, a, b) for a, b in zip(low, high)]
    return jnp.where(jnp.full(low.shape, upper, jnp.int32) == 1, high, low)


def write_side(lay, ref, block, upper):
    n = lay.lines
    write_pieces(lay, ref, pick(upper, block["last"], block["first"]))
    if not lay.leads:
        return
    pair = pick(upper, block["far"], block["near"])
    ref[pl.ds(lay.side_couple, n), :] = pair[0]
    if lay.groups > 1:
        ref[pl.ds(lay.side_packed, TILE), :] = pair[1]
    write_rows(ref, lay.side_edge, pick(upper, block["tail"], block["head"]), n)


def read_side(lay, ref, lead, lead_ref):
    n = lead.lines
    couple = [lead_ref[pl.ds(lead.side_couple, n), :]]
    if lead.groups > 1:
        couple.append(lead_ref[pl.ds(lead.side_packed, TILE), :])
    return read_pieces(lay, ref), couple, read_rows(lead_ref, lead.side_edge, lead.edges, n)


def ordered(upper, own, other):
    low = {name: pick(upper, own[name], other[name]) for name in own}
    high = {name: pick(upper, other[name], own[name]) for name in own}
    return low, high


def joint(low, high):
    return [1.0 / (1.0 - far * near) for far, near in zip(low["far"], high["near"])]


def merge(lay, low, high):
    shrink = joint(low, high)
    groups = range(len(shrink))
    to_low = [low["cross"][g] * shrink[g] for g in groups]
    to_high = [high["cross"][g] * shrink[g] for g in groups]
    span = range(len(lay.sizes))
    of = lay.group
    block = {
        "first": [
            low["first"][i]
            + to_low[of(i)] * (high["first"][i] + high["near"][of(i)] * low["last"][i])
            for i in span
        ],
        "last": [
            high["last"][i]
            + to_high[of(i)] * (low["last"][i] + low["far"][of(i)] * high["first"][i])
            for i in span
        ],
    }
    block["near"] = [low["near"][g] + to_low[g] * low["cross"][g] * high["near"][g] for g in groups]
    block["cross"] = [to_low[g] * high["cross"][g] for g in groups]
    block["far"] = [high["far"][g] + to_high[g] * high["cross"][g] * low["far"][g] for g in groups]
    block["head"] = low["head"]
    block["tail"] = high["tail"]
    return block


def inner(lay, low, high, before, after):
    shrink = joint(low, high)
    low_last, high_first = [], []
    for i in range(len(lay.sizes)):
        g = lay.group(i)
        left = low["last"][i] + low["cross"][g] * before[i]
        right = high["first"][i] + high["cross"][g] * after[i]
        low_last.append((left + low["far"][g] * right) * shrink[g])
        high_first.append((right + high["near"][g] * left) * shrink[g])
    return low_last, high_first


def merge_kernel(lay, lead, bit, top, me_ref, own, other, *refs):
    out, *side = refs[-2:] if top else refs[-1:]
    lead_own, lead_other = (own, other) if lay.leads else refs[:2]
    upper = (me_ref[0] >> bit) & 1
    low, high = ordered(
        upper, read_block(lay, own, lead, lead_own), read_block(lay, other, lead, lead_other)
    )
    block = merge(lay, low, high)
    write_block(lay, out, block)
    if top:
        write_side(lay, side[0], block, (me_ref[0] >> (bit + 1)) & 1)


def first_merge_kernel(lay, bit, top, me_ref, own, slim, apart, *refs):
    out, joined, *side = refs[-3:] if top else refs[-2:]
    joined[pl.ds(0, lay.couple), :] = slim[pl.ds(0, lay.couple), :]
    joined[pl.ds(lay.packed, TILE), :] = slim[pl.ds(lay.couple, TILE), :]
    joined[pl.ds(lay.couple, 3 * lay.lines), :] = apart[pl.ds(0, 3 * lay.lines), :]
    edges = 2 * lay.edges * lay.lines
    joined[pl.ds(lay.edge, edges), :] = apart[pl.ds(3 * lay.lines, edges), :]
    merge_kernel(lay, lay, bit, top, me_ref, own, joined, out, *side)


def solve_lines(lay, lead, levels, me, refs):
    owns, gots = refs[:levels], refs[levels : 2 * levels]
    lead_owns, lead_gots = owns, gots
    if not lay.leads:
        lead_owns, lead_gots = refs[2 * levels : 3 * levels], refs[3 * levels : 4 * levels]
    top = levels - 1
    upper = (me >> top) & 1
    own = read_block(lay, owns[top], lead, lead_owns[top])
    met, met_couple, met_edge = read_side(lay, gots[top], lead, lead_gots[top])
    facing = pick(upper, own["last"], own["first"])
    couple = pick(upper, own["far"], own["near"])
    shrink = [1.0 / (1.0 - a * b) for a, b in zip(met_couple, couple)]
    found = []
    for i in range(len(lay.sizes)):
        g = lay.group(i)
        found.append((met[i] + met_couple[g] * facing[i]) * shrink[g])
    zeros = [jnp.zeros_like(v) for v in found]
    blank = [jnp.zeros_like(v) for v in met_edge]
    state = (
        pick(upper, zeros, found), pick(upper, found, zeros),
        pick(upper, blank, met_edge), pick(upper, met_edge, blank),
    )
    partner = None
    for level in reversed(range(top)):
        upper = (me >> level) & 1
        low, high = ordered(
            upper,
            read_block(lay, owns[level], lead, lead_owns[level]),
            read_block(lay, gots[level], lead, lead_gots[level]),
        )
        before, after, behind, ahead = state
        low_last, high_first = inner(lay, low, high, before, after)
        lower = (before, high_first, behind, high["head"])
        higher = (low_last, after, low["tail"], ahead)
        state = tuple(pick(upper, a, b) for a, b in zip(lower, higher))
        partner = tuple(pick(upper, a, b) for a, b in zip(higher, lower))
    return state, partner


def write_answer(lay, ref, state):
    before, after, behind, ahead = state
    write_pieces(lay, ref, before)
    write_pieces(lay, ref, after, lay.total)
    if lay.leads:
        write_rows(ref, 2 * lay.total, behind + ahead, lay.lines)


def solve_kernel(lay, lead, levels, me_ref, *refs):
    state, partner = solve_lines(lay, lead, levels, me_ref[0], refs[:-2])
    write_answer(lay, refs[-2], state)
    write_answer(lay, refs[-1], partner)


def corners(weights):
    one = jnp.ones_like(weights[0])
    value, slope, chain = one, one, [one]
    for weight in weights:
        value, slope = growing_step(value, slope, weight)
        chain.append(value)
    back, fall, backs = one, one, []
    for weight in reversed(weights):
        backs.append(back)
        back, fall = growing_step(back, fall, weight)
    backs.reverse()
    return chain, backs, 1.0 / value


def post(mine, keep, send, row, cells):
    half = cells.shape[0] // 2
    low, high = cells[:half], cells[half:]
    keep[pl.ds(row, half), :] = pick(mine, low, high)
    send[pl.ds(row, half), :] = pick(mine, high, low)


def z_part(
    dims, lay, me_ref, sums, cot, phi, psi, w, left, right, arrived, turned, az, keep, send
):
    nx, ny = dims
    tiles = nx * ny // LANES
    mine = me_ref[0] & 1
    for c in range(len(lay.sizes)):
        arrived(c)
        for t in range(tiles):
            span = pl.ds(t * LANES, LANES)
            cells, up, down = cot[c, span, :], phi[span, :], psi[span, :]
            wide = jnp.concatenate([up * cells, down * cells], axis=1)
            found = jnp.dot(
                jnp.concatenate(split3(wide), axis=0), sums, preferred_element_type=jnp.float32
            )
            found = found[:LANES] + (found[LANES : 2 * LANES] + found[2 * LANES :])
            az[c, span, :] = w[span, :] * (down * found[:, :LANES] + up * found[:, LANES:])
        first = jnp.zeros((nx, LANES), jnp.float32)
        last = jnp.zeros((nx, LANES), jnp.float32)
        for y in range(ny):
            cells = az[c, pl.ds(y, nx, stride=ny), :]
            span = pl.ds(y * nx, nx)
            turned[c, span, :] = cells
            first = first + left[span, :] * cells
            last = last + right[span, :] * cells
        post(mine, keep, send, lay.offsets[c], first)
        post(mine, keep, send, lay.total + lay.offsets[c], last)


def carried(maps, state):
    return maps[0] * state[0] + maps[1] * state[1], maps[2] * state[0] + maps[3] * state[1]


def z_continuants(tiles, wt, pht, pst, maps, ends):
    deep = LANES // TILE
    lines = tiles * TILE
    one = jnp.ones((lines, LANES), jnp.float32)
    zero = jnp.zeros((lines, LANES), jnp.float32)

    def at(k, t):
        return pl.ds(t * LANES + k, TILE, stride=deep)

    weights = [
        jnp.concatenate([wt[at(k, t), :] for t in range(tiles)], axis=0) for k in range(deep)
    ]
    found = []
    for order in (range(deep), reversed(range(deep))):
        pair = [(one, zero), (zero, one)]
        values = {}
        for k in order:
            values[k] = (pair[0][0], pair[1][0])
            pair = [growing_step(*state, weights[k]) for state in pair]
        base = len(found) * 4 * lines
        found.append(values)
        for i, entry in enumerate((pair[0][0], pair[1][0], pair[0][1], pair[1][1])):
            maps[pl.ds(base + i * lines, lines), :] = entry
    state = (jnp.ones((tiles, LANES), jnp.float32),) * 2
    for side, order in enumerate((range(TILE), reversed(range(TILE)))):
        for s in order:
            for i in range(2):
                ends[pl.ds((2 * side + i) * lines + s, tiles, stride=TILE), :] = state[i]
            rows = [pl.ds((4 * side + i) * lines + s, tiles, stride=TILE) for i in range(4)]
            state = carried([maps[row, :] for row in rows], state)
        state = (1.0 / state[0],) * 2
    for values, target, side in ((found[0], pht, 0), (found[1], pst, 1)):
        first, second = (ends[pl.ds((2 * side + i) * lines, lines), :] for i in range(2))
        for k in range(deep):
            cells = values[k][0] * first + values[k][1] * second
            for t in range(tiles):
                target[at(k, t), :] = cells[t * TILE : (t + 1) * TILE]


def lead_z_kernel(
    dims, lay, me_ref, cot_any, diff_any, phase_any, cour_any, upw_any,
    keep, send, turned, w, left, right, phi, psi, later,
    az, cot, diff, phase, cour, upw, wt, pht, pst, maps, ends, in_sems, sems,
):
    nx, ny = dims
    tiles = nx * ny // LANES
    half = nx // 2
    count = len(lay.sizes)
    ahead = pltpu.make_async_copy(cot_any.at[pl.ds(count, later.shape[0])], later, sems.at[4])
    small = [(diff_any, diff), (phase_any, phase), (cour_any.at[1], cour), (upw_any.at[1], upw)]
    for i, (source, target) in enumerate(small):
        pltpu.make_async_copy(source, target, sems.at[i]).start()
    for c in range(count):
        pltpu.make_async_copy(cot_any.at[c], cot.at[c], in_sems.at[c]).start()
    ahead.start()
    sums = sum_matrix()

    for i, (source, target) in enumerate(small[:2]):
        pltpu.make_async_copy(source, target, sems.at[i]).wait()
    w[...] = weight_of(diff[...], phase[...])
    for t in range(tiles):
        span = pl.ds(t * LANES, LANES)
        wt[span, :] = w[span, :].T
    z_continuants(tiles, wt, pht, pst, maps, ends)
    for t in range(tiles):
        span = pl.ds(t * LANES, LANES)
        phi[span, :] = pht[span, :].T
        psi[span, :] = pst[span, :].T

    chain, backs, total = corners([w[pl.ds(y, nx, stride=ny), :] for y in range(ny)])
    for y in range(ny):
        span = pl.ds(y * nx, nx)
        left[span, :] = backs[y] * total
        right[span, :] = chain[y] * total
    mine = me_ref[0] & 1
    post(mine, keep, send, lay.couple, backs[0] * total)
    post(mine, keep, send, lay.couple + half, total)
    post(mine, keep, send, lay.couple + 2 * half, chain[ny - 1] * total)
    for i, (source, target) in enumerate(small[2:]):
        pltpu.make_async_copy(source, target, sems.at[2 + i]).wait()
    for e, y in enumerate((0, ny - 1)):
        edge = pl.ds(y, nx, stride=ny)
        weight = w[edge, :]
        up = cour[edge, :] * upw[edge, :].astype(jnp.float32)
        flow = up if e == 0 else cour[edge, :] - up
        post(mine, keep, send, lay.edge + 2 * e * half, weight)
        post(mine, keep, send, lay.edge + (2 * e + 1) * half, weight * flow)

    def arrived(c):
        pltpu.make_async_copy(cot_any.at[c], cot.at[c], in_sems.at[c]).wait()

    z_part(dims, lay, me_ref, sums, cot, phi, psi, w, left, right, arrived, turned, az, keep, send)
    ahead.wait()


def next_z_kernel(dims, lay, me_ref, cot, phi, psi, w, left, right, keep, send, turned, az):
    z_part(
        dims, lay, me_ref, sum_matrix(), cot, phi, psi, w, left, right, lambda c: None, turned, az, keep, send
    )


def coef_kernel(dims, w, courant, upwind, after, block, inv, wy, xinv, seam, left, right, flows):
    del after
    nx, ny = dims
    rows = nx * ny
    one = jnp.ones((ny, LANES), jnp.float32)
    value, slope, back, fall = one, one, one, one
    for k in range(nx):
        low, high = pl.ds(k * ny, ny), pl.ds((nx - 1 - k) * ny, ny)
        right[low, :] = value
        left[high, :] = back
        new_value, slope = growing_step(value, slope, w[low, :])
        new_back, fall = growing_step(back, fall, w[high, :])
        if k < nx // 2:
            up, down = value / new_value, back / new_back
            xinv[low, :] = up
            xinv[high, :] = down
        end, value = value, new_value
        corner, back = back, new_back
    seam[...] = 1.0 / (1.0 - up * down)
    total = 1.0 / value
    block[pl.ds(0, ny), :] = corner * total
    block[pl.ds(ny, ny), :] = total
    block[pl.ds(2 * ny, ny), :] = end * total
    value = jnp.ones((nx, LANES), jnp.float32)
    slope = value
    for y in range(ny):
        weight = w[pl.ds(y, nx, stride=ny), :]
        wy[pl.ds(y * nx, nx), :] = weight
        new_value, slope = growing_step(value, slope, weight)
        inv[pl.ds(y * nx, nx), :] = value / new_value
        value = new_value

    lane = lax.broadcasted_iota(jnp.int32, (ny, LANES), 1)

    def plane(x, carry):
        span = pl.ds(x * ny, ny)
        scale = w[span, :] * total
        left[span, :] = left[span, :] * scale
        right[span, :] = right[span, :] * scale
        own = one
        for d in range(3):
            flow = courant[d, span, :]
            up = flow * upwind[d, span, :].astype(jnp.float32)
            down = flow - up
            own = own + (down - up)
            if d == 2:
                up = jnp.where(lane == 0, 0.0, up)
                down = jnp.where(lane == LANES - 1, 0.0, down)
            flows[pl.ds((1 + 2 * d) * rows + x * ny, ny), :] = up
            flows[pl.ds((2 + 2 * d) * rows + x * ny, ny), :] = down
        flows[span, :] = own
        return carry

    lax.fori_loop(0, nx, plane, 0, unroll=4)
    first, last = pl.ds(0, ny), pl.ds(rows - ny, ny)
    block[pl.ds(3 * ny, ny), :] = w[first, :] * flows[pl.ds(rows, ny), :]
    block[pl.ds(4 * ny, ny), :] = w[last, :] * flows[pl.ds(2 * rows + rows - ny, ny), :]


def sides(before, after, x):
    return two_sides(before[pl.ds(x, 1), :], after[pl.ds(x, 1), :])


def y_kernel(dims, ylay, xlay, me_ref, az, own, got, w, wy, inv, xinv, seam, *refs):
    nx, ny = dims
    half = nx // 2
    comps = len(ylay.sizes)
    if xlay.leads:
        part, block, slim, field, ghost, ginv, gseam, gleft, gright, before, after, ay, joined = refs
    else:
        before, after, ginv, gseam, gleft, gright, block, field, ghost, fleft, fright, ay, joined = refs
        for x in range(nx):
            here = pl.ds(x * TILE, TILE)
            scale = sides(before, after, nx + x)
            fleft[here, :] = gleft[here, :] * scale
            fright[here, :] = gright[here, :] * scale
    mine = me_ref[0] & 1
    span = ylay.answer_rows
    joined[pl.ds(pl.multiple_of(mine * span, TILE), span), :] = own[...]
    joined[pl.ds(pl.multiple_of((1 - mine) * span, TILE), span), :] = got[...]
    if xlay.leads:
        for h in range(2):
            for e in range(2):
                where = pl.ds(e * nx + h * half, half)
                row = h * span + 2 * ylay.total + e * half
                before[where, :] = joined[pl.ds(row, half), :]
                after[where, :] = joined[pl.ds(row + 2 * half, half), :]
        one = jnp.ones((TILE, LANES), jnp.float32)
        value, slope, back, fall = one, one, one, one
        for k in range(nx):
            low, high = pl.ds(k * TILE, TILE), pl.ds((nx - 1 - k) * TILE, TILE)
            gright[low, :] = value
            gleft[high, :] = back
            new_value, slope = growing_step(value, slope, sides(before, after, k))
            new_back, fall = growing_step(back, fall, sides(before, after, nx - 1 - k))
            if k < nx // 2:
                up, down = value / new_value, back / new_back
                ginv[low, :] = up
                ginv[high, :] = down
            end, value = value, new_value
            corner, back = back, new_back
        gseam[...] = 1.0 / (1.0 - up * down)
        total = 1.0 / value
        for x in range(nx):
            here = pl.ds(x * TILE, TILE)
            gleft[here, :] = gleft[here, :] * total
            gright[here, :] = gright[here, :] * total

    ghost[...] = jnp.zeros(ghost.shape, jnp.float32)
    for c in range(comps):
        for h in range(2):
            piece = pl.ds(h * half, half)
            fb = joined[pl.ds(h * span + c * half, half), :]
            fa = joined[pl.ds(h * span + ylay.total + c * half, half), :]
            ghost[pl.ds(h * half * TILE + c, half, stride=TILE), :] = before[piece, :] * fb
            ghost[pl.ds(h * half * TILE + SIDE + c, half, stride=TILE), :] = after[piece, :] * fa
            swept, chain = fb, []
            for y in range(ny):
                cells = az[c, pl.ds(y * nx + h * half, half), :]
                swept = (cells + swept) * inv[pl.ds(y * nx + h * half, half), :]
                chain.append(swept)
            later = fa
            for y in reversed(range(ny)):
                row = pl.ds(y * nx + h * half, half)
                later = chain[y] + inv[row, :] * later
                ay[c, pl.ds(h * half * ny + y, half, stride=ny), :] = later * wy[row, :]

    def load(i, x):
        return ghost[pl.ds(x * TILE, TILE), :] if i == comps else ay[i, pl.ds(x * ny, ny), :]

    def keep(i, x, cells):
        if i == comps:
            ghost[pl.ds(x * TILE, TILE), :] = cells
        else:
            ay[i, pl.ds(x * ny, ny), :] = cells

    def pivot(i, x):
        return ginv[pl.ds(x * TILE, TILE), :] if i == comps else xinv[pl.ds(x * ny, ny), :]

    def finish(i, x, cells):
        if i == comps:
            ghost[pl.ds(x * TILE, TILE), :] = cells * sides(before, after, nx + x)
        else:
            here = pl.ds(x * ny, ny)
            field[i, here, :] = cells * w[here, :]

    pieces = range(comps + 1)
    middle = nx // 2
    lows = [jnp.zeros((n, LANES), jnp.float32) for n in xlay.sizes]
    highs = list(lows)
    for k in range(middle):
        x, mirror = k, nx - 1 - k
        for i in pieces:
            lows[i] = (load(i, x) + lows[i]) * pivot(i, x)
            highs[i] = (load(i, mirror) + highs[i]) * pivot(i, mirror)
            if k + 1 < middle:
                keep(i, x, lows[i])
                keep(i, mirror, highs[i])
    for i in pieces:
        joint_scale = gseam[...] if i == comps else seam[...]
        highs[i] = (highs[i] + pivot(i, middle) * lows[i]) * joint_scale
        lows[i] = lows[i] + pivot(i, middle - 1) * highs[i]
        finish(i, middle - 1, lows[i])
        finish(i, middle, highs[i])
    for k in range(1, middle):
        x, mirror = middle - 1 - k, middle + k
        for i in pieces:
            lows[i] = load(i, x) + pivot(i, x) * lows[i]
            highs[i] = load(i, mirror) + pivot(i, mirror) * highs[i]
            finish(i, x, lows[i])
            finish(i, mirror, highs[i])
    solved, lasts = lows, highs
    record = {"first": solved, "last": lasts}
    if xlay.leads:
        pieces = [part[pl.ds(i * ny, ny), :] for i in range(5)]
        record["near"] = [pieces[0], corner * total]
        record["cross"] = [pieces[1], total]
        record["far"] = [pieces[2], end * total]
        record["head"], record["tail"] = pieces[3:4], pieces[4:5]
    write_block(xlay, block, record)
    if xlay.leads:
        slim[pl.ds(0, xlay.couple), :] = block[pl.ds(0, xlay.couple), :]
        slim[pl.ds(xlay.couple, TILE), :] = block[pl.ds(xlay.packed, TILE), :]


def x_kernel(dims, lay, lead, levels, shift, start, me_ref, *refs):
    nx, ny = dims
    count = (2 if lay.leads else 4) * levels
    state, _ = solve_lines(lay, lead, levels, me_ref[0] >> shift, refs[:count])
    left, right, gleft, gright, flows, inputs, ghost, *rest = refs[count:]
    out_any, out, field, fluxes, sems = rest[-5:]
    rows = nx * ny
    tiles = ny // TILE
    comps = len(lay.sizes) - 1
    starts, nexts, (near,), (far,) = state

    def fill(x, carry):
        span, above = pl.ds(x * ny, ny), pl.ds((x + 1) * ny, ny)
        lower, upper = left[span, :], right[span, :]
        for c in range(comps):
            field[c, above, :] = inputs[c, span, :] + lower * starts[c] + upper * nexts[c]
        here = pl.ds(x * TILE, TILE)
        fluxes[here, :] = ghost[here, :] + gleft[here, :] * starts[comps] + gright[here, :] * nexts[comps]
        return carry

    lax.fori_loop(0, nx, fill, 0, unroll=8)
    blank = jnp.zeros((comps, ny, LANES), jnp.float32)
    field[:, pl.ds(0, ny), :] = blank
    field[:, pl.ds((nx + 1) * ny, ny), :] = blank

    line = lax.broadcasted_iota(jnp.int32, (TILE, LANES), 0)

    def advect(x, carry):
        before = jnp.maximum(x - 1, 0)
        beyond = jnp.minimum(x + 1, nx - 1)

        def flow(kind, plane, t):
            begin = pl.multiple_of(kind * rows + plane * ny + t * TILE, TILE)
            return flows[pl.ds(begin, TILE), :]

        own = [flow(0, x, t) for t in range(tiles)]
        ahead_x = [flow(1, beyond, t) for t in range(tiles)]
        behind_x = [flow(2, before, t) for t in range(tiles)]
        ahead_y = [flow(3, x, t) for t in range(tiles)]
        behind_y = [flow(4, x, t) for t in range(tiles)]
        ahead_z = [flow(5, x, t) for t in range(tiles)]
        behind_z = [flow(6, x, t) for t in range(tiles)]
        for c in range(comps):

            def cells(plane, t):
                begin = pl.multiple_of((plane + 1) * ny + t * TILE, TILE)
                return field[c, pl.ds(begin, TILE), :]

            grad = [cells(x, t) for t in range(tiles)]
            ups = [pltpu.roll(ahead_y[t] * grad[t], TILE - 1, 0) for t in range(tiles)]
            downs = [pltpu.roll(behind_y[t] * grad[t], 1, 0) for t in range(tiles)]
            lowest = fluxes[pl.ds(x * TILE + c, 1), :]
            highest = fluxes[pl.ds(x * TILE + SIDE + c, 1), :]
            for t in range(tiles):
                part = own[t] * grad[t]
                part = part + ahead_x[t] * cells(x + 1, t) - behind_x[t] * cells(x - 1, t)
                enter = ups[t + 1] if t + 1 < tiles else jnp.broadcast_to(highest, (TILE, LANES))
                part = part + jnp.where(line == TILE - 1, enter, ups[t])
                enter = downs[t - 1] if t > 0 else jnp.broadcast_to(lowest, (TILE, LANES))
                part = part - jnp.where(line == 0, enter, downs[t])
                part = part + pltpu.roll(ahead_z[t] * grad[t], LANES - 1, 1)
                part = part - pltpu.roll(behind_z[t] * grad[t], 1, 1)
                out[c, pl.ds(pl.multiple_of(x * ny + t * TILE, TILE), TILE), :] = part
        return carry

    parts = 8
    share = nx // parts

    def copy(part):
        span = pl.ds(part * share * ny, share * ny)
        target = out_any.at[pl.ds(start, comps), span, :]
        return pltpu.make_async_copy(out.at[:, span, :], target, sems.at[part])

    top, bottom = pl.ds(0, ny), pl.ds(rows - ny, ny)
    for part in range(parts):
        lax.fori_loop(part * share, (part + 1) * share, advect, 0, unroll=share)
        for c in range(comps):
            if part == 0:
                out[c, top, :] = out[c, top, :] - near * starts[c]
            if part == parts - 1:
                out[c, bottom, :] = out[c, bottom, :] + far * nexts[c]
        copy(part).start()
    for part in range(parts):
        copy(part).wait()


def call(
    kernel, name, operands, outs, scratch=(), spaces=None, out_spaces=None, mebibytes=4, aliases=None
):
    params = pltpu.CompilerParams(vmem_limit_bytes=mebibytes * 1024 * 1024)
    memory = {"v": pltpu.VMEM, "k": pltpu.VMEM, "h": pltpu.HBM, "s": pltpu.SMEM}
    held = {"h": pltpu.HBM, "k": pltpu.VMEM}
    spaces = spaces or "s" + "v" * (len(operands) - 1)
    out_spaces = out_spaces or "v" * len(outs)
    operands = [
        pltpu.with_memory_space_constraint(o, held[s]) if s in held else o
        for o, s in zip(operands, spaces)
    ]
    return pl.pallas_call(
        kernel,
        name=name,
        out_shape=[
            held[s](shape, jnp.float32) if s in held else jax.ShapeDtypeStruct(shape, jnp.float32)
            for shape, s in zip(outs, out_spaces)
        ],
        in_specs=[pl.BlockSpec(memory_space=memory[s]) for s in spaces],
        out_specs=[pl.BlockSpec(memory_space=memory[s]) for s in out_spaces],
        scratch_shapes=list(scratch),
        input_output_aliases=aliases or {},
        compiler_params=params,
        cost_estimate=pl.CostEstimate(flops=10**9, bytes_accessed=10**7, transcendentals=0),
    )(*operands)


def exchange(rows, axis, bit):
    count = lax.axis_size(axis)
    return lax.ppermute(rows, axis, [(i, i ^ (1 << bit)) for i in range(count)])


class Ladder:
    def __init__(self, lay, axis, shift, me, send, keep, lead=None):
        self.lay, self.axis, self.shift, self.me, self.lead = lay, axis, shift, me, lead
        self.levels = (lax.axis_size(axis) - 1).bit_length()
        self.owns, self.gots, self.outgoing = [keep], [], send

    def send(self):
        self.gots.append(exchange(self.outgoing, self.axis, len(self.gots)))

    def merge(self, beside=(), apart=None):
        level = len(self.owns) - 1
        top = level == self.levels - 2
        lay, bit = self.lay, self.shift + level
        leader = self.lead or self
        operands = (self.me, self.owns[-1], self.gots[-1])
        if not lay.leads:
            operands += (leader.owns[level], leader.gots[level])
        shapes = [(lay.rows, LANES)] + ([(lay.side_rows, LANES)] if top else [])
        kernel = functools.partial(merge_kernel, lay, leader.lay, bit, top)
        if apart is not None:
            kernel = functools.partial(first_merge_kernel, lay, bit, top)
            operands += (apart,)
            shapes = shapes[:1] + shapes
        found = call(kernel, "merge_" + self.axis, operands + tuple(beside), shapes)
        self.owns.append(found[0])
        self.outgoing = found[-1] if top else found[0]
        if apart is not None:
            self.gots[0] = found[1]

    def records(self):
        found = (*self.owns, *self.gots)
        return found if self.lay.leads else found + (*self.lead.owns, *self.lead.gots)


def on_device(cotangent, diffusion, phase, courant, upwind):
    comps, nx, ny, nz = cotangent.shape
    shift = (lax.axis_size("gy") - 1).bit_length()
    rows = nx * ny
    half = nx // 2
    size = comps // 3
    starts = (0, size)
    counts = (size, comps - size)
    ylays = [Layout([half] * n, 1, 2, half, g == 0) for g, n in enumerate(counts)]
    xlays = [Layout([ny] * n + [TILE], 2, 1, ny, g == 0) for g, n in enumerate(counts)]
    me = lax.axis_index(("gx", "gy")).astype(jnp.int32).reshape(1)

    def vmem(*shape, dtype=jnp.float32):
        return pltpu.VMEM(shape, dtype)

    flat = (rows, nz)
    cot = cotangent.reshape(comps, rows, nz)
    cour = courant.reshape(3, rows, nz)
    upw = upwind.reshape(3, rows, nz)
    n = counts[0]
    keep, send, az, w, left, right, phi, psi, cot_next = call(
        functools.partial(lead_z_kernel, (nx, ny), ylays[0]),
        "z_solve_lead",
        (me, cot, diffusion.reshape(flat), phase.reshape(flat), cour, upw),
        [(ylays[0].rows, nz)] * 2 + [(n, rows, nz)] + [flat] * 5 + [(counts[1], rows, nz)],
        [
            vmem(n, rows, nz), vmem(n, rows, nz), vmem(*flat), vmem(*flat, dtype=jnp.int32),
            vmem(*flat), vmem(*flat, dtype=jnp.int32),
            vmem(*flat), vmem(*flat), vmem(*flat),
            vmem(rows // LANES * 8 * TILE, nz), vmem(rows // LANES * 4 * TILE, nz),
            pltpu.SemaphoreType.DMA((n,)), pltpu.SemaphoreType.DMA((5,)),
        ],
        spaces="shhhhh",
        mebibytes=12,
    )
    lead = Ladder(ylays[0], "gy", 0, me, send, keep)
    lead.send()
    azs = [az]
    n = counts[1]
    keep, send, az = call(
        functools.partial(next_z_kernel, (nx, ny), ylays[1]),
        "z_solve_next",
        (me, cot_next, phi, psi, w, left, right),
        [(ylays[1].rows, nz)] * 2 + [(n, rows, nz)],
        [vmem(n, rows, nz)],
        mebibytes=8,
    )
    azs.append(az)
    follow = Ladder(ylays[1], "gy", 0, me, send, keep, lead)
    follow.send()
    beside = (send,)
    for level in range(lead.levels - 1):
        lead.merge(beside)
        lead.send()
        follow.merge((lead.outgoing,))
        follow.send()
        beside = (follow.outgoing,)
        if level == 0:
            part, inv, wy, xinv, seam, xleft, xright, flows = call(
                functools.partial(coef_kernel, (nx, ny)),
                "x_coefficients",
                (w, cour, upw, lead.owns[1]),
                [(5 * ny, nz), flat, flat, flat, (ny, nz), flat, flat, (7 * rows, nz)],
                spaces="vvvv",
                mebibytes=8,
            )
            beside = (part, follow.outgoing)
            apart = exchange(part, "gx", 0)
    ladders, mets, answers = (lead, follow), [], []
    for g, ladder in enumerate(ladders):
        answer, passed = call(
            functools.partial(solve_kernel, ylays[g], ylays[0], ladder.levels),
            "y_reduced",
            (me,) + ladder.records() + (beside + (apart,) if g == 0 else ()),
            [(ylays[g].answer_rows, nz)] * 2,
        )
        answers.append(answer)
        mets.append(exchange(passed, "gy", 0))
    fields, ghosts, climbs = [], [], []
    for g in range(2):
        common = (me, azs[g], answers[g], mets[g], w, wy, inv, xinv, seam)
        edge = (nx * TILE, nz)
        outs = [(counts[g], rows, nz), edge]
        scratch = [vmem(counts[g], rows, nz), vmem(2 * ylays[g].answer_rows, nz)]
        body = functools.partial(y_kernel, (nx, ny), ylays[g], xlays[g])
        if g == 0:
            block, slim, field, ghost, ginv, gseam, gleft, gright, before, after = call(
                body,
                "y_solve_lead",
                common + (part,),
                [(xlays[0].rows, nz), (xlays[0].couple + TILE, nz)]
                + outs + [edge, (TILE, nz), edge, edge] + [(2 * nx, nz)] * 2,
                scratch,
                mebibytes=6,
            )
            climbs.append(Ladder(xlays[0], "gx", shift, me, slim, block))
        else:
            block, field, ghost, gleft, gright = call(
                body,
                "y_solve_next",
                common + (before, after, ginv, gseam, gleft, gright),
                [(xlays[1].rows, nz)] + outs + [edge] * 2,
                scratch,
                mebibytes=6,
            )
            climbs.append(Ladder(xlays[1], "gx", shift, me, block, block, climbs[0]))
        fields.append(field)
        ghosts.append(ghost)
        climbs[g].send()
    beside = (block,)
    for level in range(climbs[0].levels - 1):
        for ladder in climbs:
            leads = ladder.lay.leads
            ladder.merge(beside if leads else (), apart if leads and level == 0 else None)
            ladder.send()
        beside = (climbs[1].outgoing,)
    grad = None
    for g, ladder in enumerate(climbs):
        operands = (me, *ladder.records(), xleft, xright, gleft, gright, flows, fields[g], ghosts[g])
        spaces = "s" + "v" * (len(operands) - 1)
        aliases = None
        if g:
            aliases = {len(operands): 0}
            operands, spaces = operands + (grad,), spaces + "h"
        (grad,) = call(
            functools.partial(
                x_kernel, (nx, ny), xlays[g], xlays[0], ladder.levels, shift, starts[g]
            ),
            "x_solve",
            operands,
            [(comps, rows, nz)],
            [
                vmem(counts[g], rows, nz), vmem(counts[g], rows + 2 * ny, nz), vmem(nx * TILE, nz),
                pltpu.SemaphoreType.DMA((8,)),
            ],
            spaces=spaces,
            out_spaces="h",
            mebibytes=8,
            aliases=aliases,
        )
    return grad.reshape(comps, nx, ny, nz)


def solution(mesh):
    placed = (
        P(None, "gx", "gy", None),
        P("gx", "gy", None),
        P("gx", "gy", None),
        P(None, "gx", "gy", None),
        P(None, "gx", "gy", None),
    )
    return jax.shard_map(
        on_device, mesh=mesh, in_specs=placed, out_specs=P(None, "gx", "gy", None), check_vma=False
    )
```

```python
import functools

import jax
import jax.numpy as jnp
from jax import lax
from jax.experimental import pallas as pl
from jax.experimental.pallas import tpu as pltpu
from jax.sharding import PartitionSpec as P

COMPS = 6
LANES = 128
TILE = 8
SIDE = TILE // 2


def weight_of(diffusion, phase):
    return 1.0 / (diffusion * (1.0 + 3.0 * phase.astype(jnp.float32)))


def growing_step(value, slope, weight):
    slope = slope + weight * value
    return value + slope, slope


def split3(cells):
    high = cells.astype(jnp.bfloat16)
    rest = cells - high.astype(jnp.float32)
    middle = rest.astype(jnp.bfloat16)
    low = (rest - middle.astype(jnp.float32)).astype(jnp.bfloat16)
    return high, middle, low


def sum_matrix():
    row = lax.broadcasted_iota(jnp.int32, (2 * LANES, 2 * LANES), 0)
    col = lax.broadcasted_iota(jnp.int32, (2 * LANES, 2 * LANES), 1)
    before = (row < LANES) & (col < LANES) & (row <= col)
    after = (row >= LANES) & (col >= LANES) & (row > col)
    return jnp.where(before | after, 1.0, 0.0).astype(jnp.bfloat16)


class Layout:
    def __init__(self, sizes, groups, edges, lines, leads):
        self.sizes, self.groups, self.edges, self.lines, self.leads = sizes, groups, edges, lines, leads
        self.offsets = [sum(sizes[:i]) for i in range(len(sizes))]
        self.total = sum(sizes)
        packed = TILE if groups > 1 else 0
        self.couple = 2 * self.total
        self.packed = self.couple + 3 * lines
        self.edge = self.packed + packed
        self.side_couple = self.total
        self.side_packed = self.side_couple + lines
        self.side_edge = self.side_packed + packed
        extra = 2 * edges * lines
        self.rows = self.edge + extra if leads else self.couple
        self.side_rows = self.side_edge + extra // 2 if leads else self.total
        self.answer_rows = 2 * self.total + (extra if leads else 0)

    def group(self, piece):
        return 1 if self.groups > 1 and piece == len(self.sizes) - 1 else 0


def read_pieces(lay, ref, base=0):
    return [ref[pl.ds(base + o, n), :] for o, n in zip(lay.offsets, lay.sizes)]


def write_pieces(lay, ref, values, base=0):
    for o, n, value in zip(lay.offsets, lay.sizes, values):
        ref[pl.ds(base + o, n), :] = value


def read_rows(ref, base, count, lines):
    return [ref[pl.ds(base + i * lines, lines), :] for i in range(count)]


def write_rows(ref, base, values, lines):
    for i, value in enumerate(values):
        ref[pl.ds(base + i * lines, lines), :] = value


def two_sides(low, high):
    return jnp.concatenate(
        [jnp.broadcast_to(low, (SIDE, LANES)), jnp.broadcast_to(high, (SIDE, LANES))], axis=0
    )


def read_pair(ref, row):
    return two_sides(ref[pl.ds(row, 1), :], ref[pl.ds(row + 1, 1), :])


def write_pair(ref, row, value):
    ref[pl.ds(row, 1), :] = value[:1]
    ref[pl.ds(row + 1, 1), :] = value[SIDE : SIDE + 1]


def read_block(lay, ref, lead, lead_ref):
    n = lead.lines
    block = {"first": read_pieces(lay, ref), "last": read_pieces(lay, ref, lay.total)}
    for e, name in enumerate(("near", "cross", "far")):
        entry = [lead_ref[pl.ds(lead.couple + e * n, n), :]]
        if lead.groups > 1:
            entry.append(read_pair(lead_ref, lead.packed + 2 * e))
        block[name] = entry
    block["head"] = read_rows(lead_ref, lead.edge, lead.edges, n)
    block["tail"] = read_rows(lead_ref, lead.edge + lead.edges * n, lead.edges, n)
    return block


def write_block(lay, ref, block):
    n = lay.lines
    write_pieces(lay, ref, block["first"])
    write_pieces(lay, ref, block["last"], lay.total)
    if not lay.leads:
        return
    for e, name in enumerate(("near", "cross", "far")):
        ref[pl.ds(lay.couple + e * n, n), :] = block[name][0]
        if lay.groups > 1:
            write_pair(ref, lay.packed + 2 * e, block[name][1])
    if lay.groups > 1:
        ref[pl.ds(lay.packed + 6, 2), :] = jnp.zeros((2, LANES), jnp.float32)
    write_rows(ref, lay.edge, block["head"], n)
    write_rows(ref, lay.edge + lay.edges * n, block["tail"], n)


def pick(upper, low, high):
    if isinstance(low, list):
        return [pick(upper, a, b) for a, b in zip(low, high)]
    return jnp.where(jnp.full(low.shape, upper, jnp.int32) == 1, high, low)


def write_side(lay, ref, block, upper):
    n = lay.lines
    write_pieces(lay, ref, pick(upper, block["last"], block["first"]))
    if not lay.leads:
        return
    pair = pick(upper, block["far"], block["near"])
    ref[pl.ds(lay.side_couple, n), :] = pair[0]
    if lay.groups > 1:
        ref[pl.ds(lay.side_packed, TILE), :] = pair[1]
    write_rows(ref, lay.side_edge, pick(upper, block["tail"], block["head"]), n)


def read_side(lay, ref, lead, lead_ref):
    n = lead.lines
    couple = [lead_ref[pl.ds(lead.side_couple, n), :]]
    if lead.groups > 1:
        couple.append(lead_ref[pl.ds(lead.side_packed, TILE), :])
    return read_pieces(lay, ref), couple, read_rows(lead_ref, lead.side_edge, lead.edges, n)


def ordered(upper, own, other):
    low = {name: pick(upper, own[name], other[name]) for name in own}
    high = {name: pick(upper, other[name], own[name]) for name in own}
    return low, high


def joint(low, high):
    return [1.0 / (1.0 - far * near) for far, near in zip(low["far"], high["near"])]


def merge(lay, low, high):
    shrink = joint(low, high)
    groups = range(len(shrink))
    to_low = [low["cross"][g] * shrink[g] for g in groups]
    to_high = [high["cross"][g] * shrink[g] for g in groups]
    span = range(len(lay.sizes))
    of = lay.group
    block = {
        "first": [
            low["first"][i]
            + to_low[of(i)] * (high["first"][i] + high["near"][of(i)] * low["last"][i])
            for i in span
        ],
        "last": [
            high["last"][i]
            + to_high[of(i)] * (low["last"][i] + low["far"][of(i)] * high["first"][i])
            for i in span
        ],
    }
    block["near"] = [low["near"][g] + to_low[g] * low["cross"][g] * high["near"][g] for g in groups]
    block["cross"] = [to_low[g] * high["cross"][g] for g in groups]
    block["far"] = [high["far"][g] + to_high[g] * high["cross"][g] * low["far"][g] for g in groups]
    block["head"] = low["head"]
    block["tail"] = high["tail"]
    return block


def inner(lay, low, high, before, after):
    shrink = joint(low, high)
    low_last, high_first = [], []
    for i in range(len(lay.sizes)):
        g = lay.group(i)
        left = low["last"][i] + low["cross"][g] * before[i]
        right = high["first"][i] + high["cross"][g] * after[i]
        low_last.append((left + low["far"][g] * right) * shrink[g])
        high_first.append((right + high["near"][g] * left) * shrink[g])
    return low_last, high_first


def merge_kernel(lay, lead, bit, top, me_ref, own, other, *refs):
    out, *side = refs[-2:] if top else refs[-1:]
    lead_own, lead_other = (own, other) if lay.leads else refs[:2]
    upper = (me_ref[0] >> bit) & 1
    low, high = ordered(
        upper, read_block(lay, own, lead, lead_own), read_block(lay, other, lead, lead_other)
    )
    block = merge(lay, low, high)
    write_block(lay, out, block)
    if top:
        write_side(lay, side[0], block, (me_ref[0] >> (bit + 1)) & 1)


def first_merge_kernel(lay, bit, top, me_ref, own, slim, apart, *refs):
    out, joined, *side = refs[-3:] if top else refs[-2:]
    joined[pl.ds(0, lay.couple), :] = slim[pl.ds(0, lay.couple), :]
    joined[pl.ds(lay.packed, TILE), :] = slim[pl.ds(lay.couple, TILE), :]
    joined[pl.ds(lay.couple, 3 * lay.lines), :] = apart[pl.ds(0, 3 * lay.lines), :]
    edges = 2 * lay.edges * lay.lines
    joined[pl.ds(lay.edge, edges), :] = apart[pl.ds(3 * lay.lines, edges), :]
    merge_kernel(lay, lay, bit, top, me_ref, own, joined, out, *side)


def solve_lines(lay, lead, levels, me, refs):
    owns, gots = refs[:levels], refs[levels : 2 * levels]
    lead_owns, lead_gots = owns, gots
    if not lay.leads:
        lead_owns, lead_gots = refs[2 * levels : 3 * levels], refs[3 * levels : 4 * levels]
    top = levels - 1
    upper = (me >> top) & 1
    own = read_block(lay, owns[top], lead, lead_owns[top])
    met, met_couple, met_edge = read_side(lay, gots[top], lead, lead_gots[top])
    facing = pick(upper, own["last"], own["first"])
    couple = pick(upper, own["far"], own["near"])
    shrink = [1.0 / (1.0 - a * b) for a, b in zip(met_couple, couple)]
    found = []
    for i in range(len(lay.sizes)):
        g = lay.group(i)
        found.append((met[i] + met_couple[g] * facing[i]) * shrink[g])
    zeros = [jnp.zeros_like(v) for v in found]
    blank = [jnp.zeros_like(v) for v in met_edge]
    state = (
        pick(upper, zeros, found), pick(upper, found, zeros),
        pick(upper, blank, met_edge), pick(upper, met_edge, blank),
    )
    partner = None
    for level in reversed(range(top)):
        upper = (me >> level) & 1
        low, high = ordered(
            upper,
            read_block(lay, owns[level], lead, lead_owns[level]),
            read_block(lay, gots[level], lead, lead_gots[level]),
        )
        before, after, behind, ahead = state
        low_last, high_first = inner(lay, low, high, before, after)
        lower = (before, high_first, behind, high["head"])
        higher = (low_last, after, low["tail"], ahead)
        state = tuple(pick(upper, a, b) for a, b in zip(lower, higher))
        partner = tuple(pick(upper, a, b) for a, b in zip(higher, lower))
    return state, partner


def write_answer(lay, ref, state):
    before, after, behind, ahead = state
    write_pieces(lay, ref, before)
    write_pieces(lay, ref, after, lay.total)
    if lay.leads:
        write_rows(ref, 2 * lay.total, behind + ahead, lay.lines)


def solve_kernel(lay, lead, levels, me_ref, *refs):
    state, partner = solve_lines(lay, lead, levels, me_ref[0], refs[:-2])
    write_answer(lay, refs[-2], state)
    write_answer(lay, refs[-1], partner)


def corners(weights):
    one = jnp.ones_like(weights[0])
    value, slope, chain = one, one, [one]
    for weight in weights:
        value, slope = growing_step(value, slope, weight)
        chain.append(value)
    back, fall, backs = one, one, []
    for weight in reversed(weights):
        backs.append(back)
        back, fall = growing_step(back, fall, weight)
    backs.reverse()
    return chain, backs, 1.0 / value


def post(mine, keep, send, row, cells):
    half = cells.shape[0] // 2
    low, high = cells[:half], cells[half:]
    keep[pl.ds(row, half), :] = pick(mine, low, high)
    send[pl.ds(row, half), :] = pick(mine, high, low)


def z_part(
    dims, lay, me_ref, sums, cot, phi, psi, w, left, right, arrived, turned, az, keep, send
):
    nx, ny = dims
    tiles = nx * ny // LANES
    mine = me_ref[0] & 1
    for c in range(len(lay.sizes)):
        arrived(c)
        for t in range(tiles):
            span = pl.ds(t * LANES, LANES)
            cells, up, down = cot[c, span, :], phi[span, :], psi[span, :]
            wide = jnp.concatenate([up * cells, down * cells], axis=1)
            found = jnp.dot(
                jnp.concatenate(split3(wide), axis=0), sums, preferred_element_type=jnp.float32
            )
            found = found[:LANES] + (found[LANES : 2 * LANES] + found[2 * LANES :])
            az[c, span, :] = w[span, :] * (down * found[:, :LANES] + up * found[:, LANES:])
        first = jnp.zeros((nx, LANES), jnp.float32)
        last = jnp.zeros((nx, LANES), jnp.float32)
        for y in range(ny):
            cells = az[c, pl.ds(y, nx, stride=ny), :]
            span = pl.ds(y * nx, nx)
            turned[c, span, :] = cells
            first = first + left[span, :] * cells
            last = last + right[span, :] * cells
        post(mine, keep, send, lay.offsets[c], first)
        post(mine, keep, send, lay.total + lay.offsets[c], last)


def carried(maps, state):
    return maps[0] * state[0] + maps[1] * state[1], maps[2] * state[0] + maps[3] * state[1]


def z_continuants(tiles, wt, pht, pst, maps, ends):
    deep = LANES // TILE
    lines = tiles * TILE
    one = jnp.ones((lines, LANES), jnp.float32)
    zero = jnp.zeros((lines, LANES), jnp.float32)

    def at(k, t):
        return pl.ds(t * LANES + k, TILE, stride=deep)

    weights = [
        jnp.concatenate([wt[at(k, t), :] for t in range(tiles)], axis=0) for k in range(deep)
    ]
    found = []
    for order in (range(deep), reversed(range(deep))):
        pair = [(one, zero), (zero, one)]
        values = {}
        for k in order:
            values[k] = (pair[0][0], pair[1][0])
            pair = [growing_step(*state, weights[k]) for state in pair]
        base = len(found) * 4 * lines
        found.append(values)
        for i, entry in enumerate((pair[0][0], pair[1][0], pair[0][1], pair[1][1])):
            maps[pl.ds(base + i * lines, lines), :] = entry
    state = (jnp.ones((tiles, LANES), jnp.float32),) * 2
    for side, order in enumerate((range(TILE), reversed(range(TILE)))):
        for s in order:
            for i in range(2):
                ends[pl.ds((2 * side + i) * lines + s, tiles, stride=TILE), :] = state[i]
            rows = [pl.ds((4 * side + i) * lines + s, tiles, stride=TILE) for i in range(4)]
            state = carried([maps[row, :] for row in rows], state)
        state = (1.0 / state[0],) * 2
    for values, target, side in ((found[0], pht, 0), (found[1], pst, 1)):
        first, second = (ends[pl.ds((2 * side + i) * lines, lines), :] for i in range(2))
        for k in range(deep):
            cells = values[k][0] * first + values[k][1] * second
            for t in range(tiles):
                target[at(k, t), :] = cells[t * TILE : (t + 1) * TILE]


def lead_z_kernel(
    dims, lay, me_ref, cot_any, diff_any, phase_any, cour_any, upw_any,
    keep, send, turned, w, left, right, phi, psi, later,
    az, cot, diff, phase, cour, upw, wt, pht, pst, maps, ends, in_sems, sems,
):
    nx, ny = dims
    tiles = nx * ny // LANES
    half = nx // 2
    count = len(lay.sizes)
    ahead = pltpu.make_async_copy(cot_any.at[pl.ds(count, later.shape[0])], later, sems.at[4])
    small = [(diff_any, diff), (phase_any, phase), (cour_any.at[1], cour), (upw_any.at[1], upw)]
    for i, (source, target) in enumerate(small):
        pltpu.make_async_copy(source, target, sems.at[i]).start()
    for c in range(count):
        pltpu.make_async_copy(cot_any.at[c], cot.at[c], in_sems.at[c]).start()
    ahead.start()
    sums = sum_matrix()

    for i, (source, target) in enumerate(small[:2]):
        pltpu.make_async_copy(source, target, sems.at[i]).wait()
    w[...] = weight_of(diff[...], phase[...])
    for t in range(tiles):
        span = pl.ds(t * LANES, LANES)
        wt[span, :] = w[span, :].T
    z_continuants(tiles, wt, pht, pst, maps, ends)
    for t in range(tiles):
        span = pl.ds(t * LANES, LANES)
        phi[span, :] = pht[span, :].T
        psi[span, :] = pst[span, :].T

    chain, backs, total = corners([w[pl.ds(y, nx, stride=ny), :] for y in range(ny)])
    for y in range(ny):
        span = pl.ds(y * nx, nx)
        left[span, :] = backs[y] * total
        right[span, :] = chain[y] * total
    mine = me_ref[0] & 1
    post(mine, keep, send, lay.couple, backs[0] * total)
    post(mine, keep, send, lay.couple + half, total)
    post(mine, keep, send, lay.couple + 2 * half, chain[ny - 1] * total)
    for i, (source, target) in enumerate(small[2:]):
        pltpu.make_async_copy(source, target, sems.at[2 + i]).wait()
    for e, y in enumerate((0, ny - 1)):
        edge = pl.ds(y, nx, stride=ny)
        weight = w[edge, :]
        up = cour[edge, :] * upw[edge, :].astype(jnp.float32)
        flow = up if e == 0 else cour[edge, :] - up
        post(mine, keep, send, lay.edge + 2 * e * half, weight)
        post(mine, keep, send, lay.edge + (2 * e + 1) * half, weight * flow)

    def arrived(c):
        pltpu.make_async_copy(cot_any.at[c], cot.at[c], in_sems.at[c]).wait()

    z_part(dims, lay, me_ref, sums, cot, phi, psi, w, left, right, arrived, turned, az, keep, send)
    ahead.wait()


def next_z_kernel(dims, lay, me_ref, cot, phi, psi, w, left, right, keep, send, turned, az):
    z_part(
        dims, lay, me_ref, sum_matrix(), cot, phi, psi, w, left, right, lambda c: None, turned, az, keep, send
    )


def coef_kernel(dims, w, courant, upwind, after, block, inv, wy, xinv, seam, left, right, flows):
    del after
    nx, ny = dims
    rows = nx * ny
    one = jnp.ones((ny, LANES), jnp.float32)
    value, slope, back, fall = one, one, one, one
    for k in range(nx):
        low, high = pl.ds(k * ny, ny), pl.ds((nx - 1 - k) * ny, ny)
        right[low, :] = value
        left[high, :] = back
        new_value, slope = growing_step(value, slope, w[low, :])
        new_back, fall = growing_step(back, fall, w[high, :])
        if k < nx // 2:
            up, down = value / new_value, back / new_back
            xinv[low, :] = up
            xinv[high, :] = down
        end, value = value, new_value
        corner, back = back, new_back
    seam[...] = 1.0 / (1.0 - up * down)
    total = 1.0 / value
    block[pl.ds(0, ny), :] = corner * total
    block[pl.ds(ny, ny), :] = total
    block[pl.ds(2 * ny, ny), :] = end * total
    value = jnp.ones((nx, LANES), jnp.float32)
    slope = value
    for y in range(ny):
        weight = w[pl.ds(y, nx, stride=ny), :]
        wy[pl.ds(y * nx, nx), :] = weight
        new_value, slope = growing_step(value, slope, weight)
        inv[pl.ds(y * nx, nx), :] = value / new_value
        value = new_value

    lane = lax.broadcasted_iota(jnp.int32, (ny, LANES), 1)

    def plane(x, carry):
        span = pl.ds(x * ny, ny)
        scale = w[span, :] * total
        left[span, :] = left[span, :] * scale
        right[span, :] = right[span, :] * scale
        own = one
        for d in range(3):
            flow = courant[d, span, :]
            up = flow * upwind[d, span, :].astype(jnp.float32)
            down = flow - up
            own = own + (down - up)
            if d == 2:
                up = jnp.where(lane == 0, 0.0, up)
                down = jnp.where(lane == LANES - 1, 0.0, down)
            flows[pl.ds((1 + 2 * d) * rows + x * ny, ny), :] = up
            flows[pl.ds((2 + 2 * d) * rows + x * ny, ny), :] = down
        flows[span, :] = own
        return carry

    lax.fori_loop(0, nx, plane, 0, unroll=4)
    first, last = pl.ds(0, ny), pl.ds(rows - ny, ny)
    block[pl.ds(3 * ny, ny), :] = w[first, :] * flows[pl.ds(rows, ny), :]
    block[pl.ds(4 * ny, ny), :] = w[last, :] * flows[pl.ds(2 * rows + rows - ny, ny), :]


def sides(before, after, x):
    return two_sides(before[pl.ds(x, 1), :], after[pl.ds(x, 1), :])


def y_kernel(dims, ylay, xlay, me_ref, az, own, got, w, wy, inv, xinv, seam, *refs):
    nx, ny = dims
    half = nx // 2
    comps = len(ylay.sizes)
    if xlay.leads:
        part, block, slim, field, ghost, ginv, gseam, gleft, gright, before, after, ay, joined = refs
    else:
        before, after, ginv, gseam, gleft, gright, block, field, ghost, fleft, fright, ay, joined = refs
        for x in range(nx):
            here = pl.ds(x * TILE, TILE)
            scale = sides(before, after, nx + x)
            fleft[here, :] = gleft[here, :] * scale
            fright[here, :] = gright[here, :] * scale
    mine = me_ref[0] & 1
    span = ylay.answer_rows
    joined[pl.ds(pl.multiple_of(mine * span, TILE), span), :] = own[...]
    joined[pl.ds(pl.multiple_of((1 - mine) * span, TILE), span), :] = got[...]
    if xlay.leads:
        for h in range(2):
            for e in range(2):
                where = pl.ds(e * nx + h * half, half)
                row = h * span + 2 * ylay.total + e * half
                before[where, :] = joined[pl.ds(row, half), :]
                after[where, :] = joined[pl.ds(row + 2 * half, half), :]
        one = jnp.ones((TILE, LANES), jnp.float32)
        value, slope, back, fall = one, one, one, one
        for k in range(nx):
            low, high = pl.ds(k * TILE, TILE), pl.ds((nx - 1 - k) * TILE, TILE)
            gright[low, :] = value
            gleft[high, :] = back
            new_value, slope = growing_step(value, slope, sides(before, after, k))
            new_back, fall = growing_step(back, fall, sides(before, after, nx - 1 - k))
            if k < nx // 2:
                up, down = value / new_value, back / new_back
                ginv[low, :] = up
                ginv[high, :] = down
            end, value = value, new_value
            corner, back = back, new_back
        gseam[...] = 1.0 / (1.0 - up * down)
        total = 1.0 / value
        for x in range(nx):
            here = pl.ds(x * TILE, TILE)
            gleft[here, :] = gleft[here, :] * total
            gright[here, :] = gright[here, :] * total

    ghost[...] = jnp.zeros(ghost.shape, jnp.float32)
    for c in range(comps):
        for h in range(2):
            piece = pl.ds(h * half, half)
            fb = joined[pl.ds(h * span + c * half, half), :]
            fa = joined[pl.ds(h * span + ylay.total + c * half, half), :]
            ghost[pl.ds(h * half * TILE + c, half, stride=TILE), :] = before[piece, :] * fb
            ghost[pl.ds(h * half * TILE + SIDE + c, half, stride=TILE), :] = after[piece, :] * fa
            swept, chain = fb, []
            for y in range(ny):
                cells = az[c, pl.ds(y * nx + h * half, half), :]
                swept = (cells + swept) * inv[pl.ds(y * nx + h * half, half), :]
                chain.append(swept)
            later = fa
            for y in reversed(range(ny)):
                row = pl.ds(y * nx + h * half, half)
                later = chain[y] + inv[row, :] * later
                ay[c, pl.ds(h * half * ny + y, half, stride=ny), :] = later * wy[row, :]

    def load(i, x):
        return ghost[pl.ds(x * TILE, TILE), :] if i == comps else ay[i, pl.ds(x * ny, ny), :]

    def keep(i, x, cells):
        if i == comps:
            ghost[pl.ds(x * TILE, TILE), :] = cells
        else:
            ay[i, pl.ds(x * ny, ny), :] = cells

    def pivot(i, x):
        return ginv[pl.ds(x * TILE, TILE), :] if i == comps else xinv[pl.ds(x * ny, ny), :]

    def finish(i, x, cells):
        if i == comps:
            ghost[pl.ds(x * TILE, TILE), :] = cells * sides(before, after, nx + x)
        else:
            here = pl.ds(x * ny, ny)
            field[i, here, :] = cells * w[here, :]

    pieces = range(comps + 1)
    middle = nx // 2
    lows = [jnp.zeros((n, LANES), jnp.float32) for n in xlay.sizes]
    highs = list(lows)
    for k in range(middle):
        x, mirror = k, nx - 1 - k
        for i in pieces:
            lows[i] = (load(i, x) + lows[i]) * pivot(i, x)
            highs[i] = (load(i, mirror) + highs[i]) * pivot(i, mirror)
            if k + 1 < middle:
                keep(i, x, lows[i])
                keep(i, mirror, highs[i])
    for i in pieces:
        joint_scale = gseam[...] if i == comps else seam[...]
        highs[i] = (highs[i] + pivot(i, middle) * lows[i]) * joint_scale
        lows[i] = lows[i] + pivot(i, middle - 1) * highs[i]
        finish(i, middle - 1, lows[i])
        finish(i, middle, highs[i])
    for k in range(1, middle):
        x, mirror = middle - 1 - k, middle + k
        for i in pieces:
            lows[i] = load(i, x) + pivot(i, x) * lows[i]
            highs[i] = load(i, mirror) + pivot(i, mirror) * highs[i]
            finish(i, x, lows[i])
            finish(i, mirror, highs[i])
    solved, lasts = lows, highs
    record = {"first": solved, "last": lasts}
    if xlay.leads:
        pieces = [part[pl.ds(i * ny, ny), :] for i in range(5)]
        record["near"] = [pieces[0], corner * total]
        record["cross"] = [pieces[1], total]
        record["far"] = [pieces[2], end * total]
        record["head"], record["tail"] = pieces[3:4], pieces[4:5]
    write_block(xlay, block, record)
    if xlay.leads:
        slim[pl.ds(0, xlay.couple), :] = block[pl.ds(0, xlay.couple), :]
        slim[pl.ds(xlay.couple, TILE), :] = block[pl.ds(xlay.packed, TILE), :]


def x_kernel(dims, lay, lead, levels, shift, start, me_ref, *refs):
    nx, ny = dims
    count = (2 if lay.leads else 4) * levels
    state, _ = solve_lines(lay, lead, levels, me_ref[0] >> shift, refs[:count])
    left, right, gleft, gright, flows, inputs, ghost, *rest = refs[count:]
    out_any, out, field, fluxes, sems = rest[-5:]
    rows = nx * ny
    tiles = ny // TILE
    comps = len(lay.sizes) - 1
    starts, nexts, (near,), (far,) = state

    def fill(x, carry):
        span, above = pl.ds(x * ny, ny), pl.ds((x + 1) * ny, ny)
        lower, upper = left[span, :], right[span, :]
        for c in range(comps):
            field[c, above, :] = inputs[c, span, :] + lower * starts[c] + upper * nexts[c]
        here = pl.ds(x * TILE, TILE)
        fluxes[here, :] = ghost[here, :] + gleft[here, :] * starts[comps] + gright[here, :] * nexts[comps]
        return carry

    lax.fori_loop(0, nx, fill, 0, unroll=8)
    blank = jnp.zeros((comps, ny, LANES), jnp.float32)
    field[:, pl.ds(0, ny), :] = blank
    field[:, pl.ds((nx + 1) * ny, ny), :] = blank

    line = lax.broadcasted_iota(jnp.int32, (TILE, LANES), 0)

    def advect(x, carry):
        before = jnp.maximum(x - 1, 0)
        beyond = jnp.minimum(x + 1, nx - 1)

        def flow(kind, plane, t):
            begin = pl.multiple_of(kind * rows + plane * ny + t * TILE, TILE)
            return flows[pl.ds(begin, TILE), :]

        own = [flow(0, x, t) for t in range(tiles)]
        ahead_x = [flow(1, beyond, t) for t in range(tiles)]
        behind_x = [flow(2, before, t) for t in range(tiles)]
        ahead_y = [flow(3, x, t) for t in range(tiles)]
        behind_y = [flow(4, x, t) for t in range(tiles)]
        ahead_z = [flow(5, x, t) for t in range(tiles)]
        behind_z = [flow(6, x, t) for t in range(tiles)]
        for c in range(comps):

            def cells(plane, t):
                begin = pl.multiple_of((plane + 1) * ny + t * TILE, TILE)
                return field[c, pl.ds(begin, TILE), :]

            grad = [cells(x, t) for t in range(tiles)]
            ups = [pltpu.roll(ahead_y[t] * grad[t], TILE - 1, 0) for t in range(tiles)]
            downs = [pltpu.roll(behind_y[t] * grad[t], 1, 0) for t in range(tiles)]
            lowest = fluxes[pl.ds(x * TILE + c, 1), :]
            highest = fluxes[pl.ds(x * TILE + SIDE + c, 1), :]
            for t in range(tiles):
                part = own[t] * grad[t]
                part = part + ahead_x[t] * cells(x + 1, t) - behind_x[t] * cells(x - 1, t)
                enter = ups[t + 1] if t + 1 < tiles else jnp.broadcast_to(highest, (TILE, LANES))
                part = part + jnp.where(line == TILE - 1, enter, ups[t])
                enter = downs[t - 1] if t > 0 else jnp.broadcast_to(lowest, (TILE, LANES))
                part = part - jnp.where(line == 0, enter, downs[t])
                part = part + pltpu.roll(ahead_z[t] * grad[t], LANES - 1, 1)
                part = part - pltpu.roll(behind_z[t] * grad[t], 1, 1)
                out[c, pl.ds(pl.multiple_of(x * ny + t * TILE, TILE), TILE), :] = part
        return carry

    parts = 16
    share = nx // parts

    def copy(part):
        span = pl.ds(part * share * ny, share * ny)
        target = out_any.at[pl.ds(start, comps), span, :]
        return pltpu.make_async_copy(out.at[:, span, :], target, sems.at[part])

    top, bottom = pl.ds(0, ny), pl.ds(rows - ny, ny)
    for part in range(parts):
        lax.fori_loop(part * share, (part + 1) * share, advect, 0, unroll=share)
        for c in range(comps):
            if part == 0:
                out[c, top, :] = out[c, top, :] - near * starts[c]
            if part == parts - 1:
                out[c, bottom, :] = out[c, bottom, :] + far * nexts[c]
        copy(part).start()
    for part in range(parts):
        copy(part).wait()


def call(
    kernel, name, operands, outs, scratch=(), spaces=None, out_spaces=None, mebibytes=4, aliases=None
):
    params = pltpu.CompilerParams(vmem_limit_bytes=mebibytes * 1024 * 1024)
    memory = {"v": pltpu.VMEM, "k": pltpu.VMEM, "h": pltpu.HBM, "s": pltpu.SMEM}
    held = {"h": pltpu.HBM, "k": pltpu.VMEM}
    spaces = spaces or "s" + "v" * (len(operands) - 1)
    out_spaces = out_spaces or "v" * len(outs)
    operands = [
        pltpu.with_memory_space_constraint(o, held[s]) if s in held else o
        for o, s in zip(operands, spaces)
    ]
    return pl.pallas_call(
        kernel,
        name=name,
        out_shape=[
            held[s](shape, jnp.float32) if s in held else jax.ShapeDtypeStruct(shape, jnp.float32)
            for shape, s in zip(outs, out_spaces)
        ],
        in_specs=[pl.BlockSpec(memory_space=memory[s]) for s in spaces],
        out_specs=[pl.BlockSpec(memory_space=memory[s]) for s in out_spaces],
        scratch_shapes=list(scratch),
        input_output_aliases=aliases or {},
        compiler_params=params,
        cost_estimate=pl.CostEstimate(flops=10**9, bytes_accessed=10**7, transcendentals=0),
    )(*operands)


def exchange(rows, axis, bit):
    count = lax.axis_size(axis)
    return lax.ppermute(rows, axis, [(i, i ^ (1 << bit)) for i in range(count)])


class Ladder:
    def __init__(self, lay, axis, shift, me, send, keep, lead=None):
        self.lay, self.axis, self.shift, self.me, self.lead = lay, axis, shift, me, lead
        self.levels = (lax.axis_size(axis) - 1).bit_length()
        self.owns, self.gots, self.outgoing = [keep], [], send

    def send(self):
        self.gots.append(exchange(self.outgoing, self.axis, len(self.gots)))

    def merge(self, beside=(), apart=None):
        level = len(self.owns) - 1
        top = level == self.levels - 2
        lay, bit = self.lay, self.shift + level
        leader = self.lead or self
        operands = (self.me, self.owns[-1], self.gots[-1])
        if not lay.leads:
            operands += (leader.owns[level], leader.gots[level])
        shapes = [(lay.rows, LANES)] + ([(lay.side_rows, LANES)] if top else [])
        kernel = functools.partial(merge_kernel, lay, leader.lay, bit, top)
        if apart is not None:
            kernel = functools.partial(first_merge_kernel, lay, bit, top)
            operands += (apart,)
            shapes = shapes[:1] + shapes
        found = call(kernel, "merge_" + self.axis, operands + tuple(beside), shapes)
        self.owns.append(found[0])
        self.outgoing = found[-1] if top else found[0]
        if apart is not None:
            self.gots[0] = found[1]

    def records(self):
        found = (*self.owns, *self.gots)
        return found if self.lay.leads else found + (*self.lead.owns, *self.lead.gots)


def on_device(cotangent, diffusion, phase, courant, upwind):
    comps, nx, ny, nz = cotangent.shape
    shift = (lax.axis_size("gy") - 1).bit_length()
    rows = nx * ny
    half = nx // 2
    size = comps // 3
    starts = (0, size)
    counts = (size, comps - size)
    ylays = [Layout([half] * n, 1, 2, half, g == 0) for g, n in enumerate(counts)]
    xlays = [Layout([ny] * n + [TILE], 2, 1, ny, g == 0) for g, n in enumerate(counts)]
    me = lax.axis_index(("gx", "gy")).astype(jnp.int32).reshape(1)

    def vmem(*shape, dtype=jnp.float32):
        return pltpu.VMEM(shape, dtype)

    flat = (rows, nz)
    cot = cotangent.reshape(comps, rows, nz)
    cour = courant.reshape(3, rows, nz)
    upw = upwind.reshape(3, rows, nz)
    n = counts[0]
    keep, send, az, w, left, right, phi, psi, cot_next = call(
        functools.partial(lead_z_kernel, (nx, ny), ylays[0]),
        "z_solve_lead",
        (me, cot, diffusion.reshape(flat), phase.reshape(flat), cour, upw),
        [(ylays[0].rows, nz)] * 2 + [(n, rows, nz)] + [flat] * 5 + [(counts[1], rows, nz)],
        [
            vmem(n, rows, nz), vmem(n, rows, nz), vmem(*flat), vmem(*flat, dtype=jnp.int32),
            vmem(*flat), vmem(*flat, dtype=jnp.int32),
            vmem(*flat), vmem(*flat), vmem(*flat),
            vmem(rows // LANES * 8 * TILE, nz), vmem(rows // LANES * 4 * TILE, nz),
            pltpu.SemaphoreType.DMA((n,)), pltpu.SemaphoreType.DMA((5,)),
        ],
        spaces="shhhhh",
        mebibytes=12,
    )
    lead = Ladder(ylays[0], "gy", 0, me, send, keep)
    lead.send()
    azs = [az]
    n = counts[1]
    keep, send, az = call(
        functools.partial(next_z_kernel, (nx, ny), ylays[1]),
        "z_solve_next",
        (me, cot_next, phi, psi, w, left, right),
        [(ylays[1].rows, nz)] * 2 + [(n, rows, nz)],
        [vmem(n, rows, nz)],
        mebibytes=8,
    )
    azs.append(az)
    follow = Ladder(ylays[1], "gy", 0, me, send, keep, lead)
    follow.send()
    beside = (send,)
    for level in range(lead.levels - 1):
        lead.merge(beside)
        lead.send()
        follow.merge((lead.outgoing,))
        follow.send()
        beside = (follow.outgoing,)
        if level == 0:
            part, inv, wy, xinv, seam, xleft, xright, flows = call(
                functools.partial(coef_kernel, (nx, ny)),
                "x_coefficients",
                (w, cour, upw, lead.owns[1]),
                [(5 * ny, nz), flat, flat, flat, (ny, nz), flat, flat, (7 * rows, nz)],
                spaces="vvvv",
                mebibytes=8,
            )
            beside = (part, follow.outgoing)
            apart = exchange(part, "gx", 0)
    ladders, mets, answers = (lead, follow), [], []
    for g, ladder in enumerate(ladders):
        answer, passed = call(
            functools.partial(solve_kernel, ylays[g], ylays[0], ladder.levels),
            "y_reduced",
            (me,) + ladder.records() + (beside + (apart,) if g == 0 else ()),
            [(ylays[g].answer_rows, nz)] * 2,
        )
        answers.append(answer)
        mets.append(exchange(passed, "gy", 0))
    fields, ghosts, climbs = [], [], []
    for g in range(2):
        common = (me, azs[g], answers[g], mets[g], w, wy, inv, xinv, seam)
        edge = (nx * TILE, nz)
        outs = [(counts[g], rows, nz), edge]
        scratch = [vmem(counts[g], rows, nz), vmem(2 * ylays[g].answer_rows, nz)]
        body = functools.partial(y_kernel, (nx, ny), ylays[g], xlays[g])
        if g == 0:
            block, slim, field, ghost, ginv, gseam, gleft, gright, before, after = call(
                body,
                "y_solve_lead",
                common + (part,),
                [(xlays[0].rows, nz), (xlays[0].couple + TILE, nz)]
                + outs + [edge, (TILE, nz), edge, edge] + [(2 * nx, nz)] * 2,
                scratch,
                mebibytes=6,
            )
            climbs.append(Ladder(xlays[0], "gx", shift, me, slim, block))
        else:
            block, field, ghost, gleft, gright = call(
                body,
                "y_solve_next",
                common + (before, after, ginv, gseam, gleft, gright),
                [(xlays[1].rows, nz)] + outs + [edge] * 2,
                scratch,
                mebibytes=6,
            )
            climbs.append(Ladder(xlays[1], "gx", shift, me, block, block, climbs[0]))
        fields.append(field)
        ghosts.append(ghost)
        climbs[g].send()
    beside = (block,)
    for level in range(climbs[0].levels - 1):
        for ladder in climbs:
            leads = ladder.lay.leads
            ladder.merge(beside if leads else (), apart if leads and level == 0 else None)
            ladder.send()
        beside = (climbs[1].outgoing,)
    grad = None
    for g, ladder in enumerate(climbs):
        operands = (me, *ladder.records(), xleft, xright, gleft, gright, flows, fields[g], ghosts[g])
        spaces = "s" + "v" * (len(operands) - 1)
        aliases = None
        if g:
            aliases = {len(operands): 0}
            operands, spaces = operands + (grad,), spaces + "h"
        (grad,) = call(
            functools.partial(
                x_kernel, (nx, ny), xlays[g], xlays[0], ladder.levels, shift, starts[g]
            ),
            "x_solve",
            operands,
            [(comps, rows, nz)],
            [
                vmem(counts[g], rows, nz), vmem(counts[g], rows + 2 * ny, nz), vmem(nx * TILE, nz),
                pltpu.SemaphoreType.DMA((16,)),
            ],
            spaces=spaces,
            out_spaces="h",
            mebibytes=8,
            aliases=aliases,
        )
    return grad.reshape(comps, nx, ny, nz)


def solution(mesh):
    placed = (
        P(None, "gx", "gy", None),
        P("gx", "gy", None),
        P("gx", "gy", None),
        P(None, "gx", "gy", None),
        P(None, "gx", "gy", None),
    )
    return jax.shard_map(
        on_device, mesh=mesh, in_specs=placed, out_specs=P(None, "gx", "gy", None), check_vma=False
    )
```
